32 devices in a mesh: dp: 4 (over y, core), ctx: 2 (over x), tensor: 4 (over z).
Axes of the slice: x: 2, y: 2, z: 4, core: 2. Of those that a mesh axis runs over, the one named last changes fastest.
Arguments:
- stream: bfloat16 [4, 1024, 2048], P('dp', 'ctx'), may hold values from -6 to 6
- cotangent: bfloat16 [4, 1024, 2048], P('dp', 'ctx'), may hold values from -6 to 6
- prefixes: int32 [4], P('dp'), may hold values from 102 to 512
- attention_gain: float32 [2, 2048], replicated, may hold values from 0.5 to 1.5
- query_weight: bfloat16 [2, 2048, 2048], P(None, None, 'tensor'), may hold values from -0.125 to 0.125
- key_weight: bfloat16 [2, 2048, 1024], P(None, None, 'tensor'), may hold values from -0.125 to 0.125
- value_weight: bfloat16 [2, 2048, 1024], P(None, None, 'tensor'), may hold values from -0.125 to 0.125
- gate_heads: bfloat16 [2, 2048, 16], P(None, None, 'tensor'), may hold values from -0.25 to 0.25
- query_gain: float32 [2, 128], replicated, may hold values from 0.5 to 1.5
- key_gain: float32 [2, 128], replicated, may hold values from 0.5 to 1.5
- output_weight: bfloat16 [2, 2048, 2048], P(None, 'tensor'), may hold values from -0.75 to 0.75
- feed_gain: float32 [2, 2048], replicated, may hold values from 0.5 to 1.5
- gate_weight: bfloat16 [2, 2048, 6144], P(None, None, 'tensor'), may hold values from -0.125 to 0.125
- up_weight: bfloat16 [2, 2048, 6144], P(None, None, 'tensor'), may hold values from -0.125 to 0.125
- down_weight: bfloat16 [2, 6144, 2048], P(None, 'tensor'), may hold values from -0.15625 to 0.15625
Outputs:
- result: bfloat16 [4, 1024, 2048], P('dp', 'ctx')
- stream_grad: float32 [4, 1024, 2048], P('dp', 'ctx')
- attention_gain_grad: float32 [2, 2048], P(None, ('dp', 'ctx'))
- query_weight_grad: float32 [2, 2048, 2048], P(None, ('dp', 'ctx'), 'tensor')
- key_weight_grad: float32 [2, 2048, 1024], P(None, ('dp', 'ctx'), 'tensor')
- value_weight_grad: float32 [2, 2048, 1024], P(None, ('dp', 'ctx'), 'tensor')
- gate_heads_grad: float32 [2, 2048, 16], P(None, ('dp', 'ctx'), 'tensor')
- query_gain_grad: float32 [2, 128], P(None, ('dp', 'ctx'))
- key_gain_grad: float32 [2, 128], P(None, ('dp', 'ctx'))
- output_weight_grad: float32 [2, 2048, 2048], P(None, 'tensor', ('dp', 'ctx'))
- feed_gain_grad: float32 [2, 2048], P(None, ('dp', 'ctx'))
- gate_weight_grad: float32 [2, 2048, 6144], P(None, ('dp', 'ctx'), 'tensor')
- up_weight_grad: float32 [2, 2048, 6144], P(None, ('dp', 'ctx'), 'tensor')
- down_weight_grad: float32 [2, 6144, 2048], P(None, 'tensor', ('dp', 'ctx'))
The draws below stay inside these ranges and needn't reach their ends.
Inputs may be any that keep to these rules, and one draw needn't show every extreme that they name: `prefixes`: tokens from the start of each sequence that attend both ways.
All inputs are finite; a program needn't handle non-finite values.
Results may differ from the reference program's by a relative error of at most 0.035.
Values may be sent and summed in bfloat16 or wider, within the bound.
A program may use at most 256 MiB of HBM per device.

```python
import jax
import jax.numpy as jnp
from jax import lax

D = 2048
H = 16
KVH = 8
HD = 128
FF = 6144
LEN = 1024
LAYERS = 2
SEQS = 4
QD = 2048
KD = 1024


def touch_ends(values, stream_key, smallest, high):
    longest = values.shape.index(max(values.shape))
    spots = []
    for shift in (0, 1):
        where = [jax.random.randint(jax.random.fold_in(stream_key, axis), (), 0, length) for axis, length in enumerate(values.shape)]
        where[longest] = (where[longest] + shift) % values.shape[longest]
        spots.append(tuple(where))
    return values.at[spots[0]].set(smallest).at[spots[1]].set(high)


def block_levels(key, shape, pieces, low, top_value):
    def one(position, shards_of):
        steps = jax.random.uniform(jax.random.fold_in(jax.random.fold_in(key, 6), position), (shards_of,), jnp.float32, low / len(pieces), top_value / len(pieces))
        return jnp.repeat(jnp.exp(steps), shape[position] // shards_of).reshape((-1,) + (1,) * (len(shape) - position - 1))

    level = one(*pieces[0])
    for cut in pieces[1:]:
        level = level * one(*cut)
    return level


def gaussian(key, extent, spread, most, split=(), kind=jnp.bfloat16):
    level = block_levels(key, extent, split, -0.22, 0.18) if split else 1.0
    values = jax.random.normal(key, extent, jnp.float32) * spread * level
    return jnp.minimum(jnp.maximum(values, -most), most).astype(kind)


def setup_inputs(seed: int = 0) -> dict:
    streams_of = jax.random.split(jax.random.key(seed), 16)
    return {
        "stream": gaussian(streams_of[0], (SEQS, LEN, D), 1.0, 6.0, ((0, 4), (1, 2))),
        "cotangent": gaussian(streams_of[1], (SEQS, LEN, D), 1.0, 6.0, ((0, 4), (1, 2))),
        "prefixes": touch_ends(jax.random.randint(streams_of[2], (SEQS,), LEN // 10, LEN // 2 + 1), jax.random.fold_in(streams_of[2], 1), LEN // 10, (LEN // 2 + 1) - 1).astype(jnp.int32),
        "attention_gain": jnp.clip(1.0 + 0.1 * jax.random.normal(streams_of[3], (LAYERS, D), jnp.float32), 0.5, 1.5),
        "query_weight": gaussian(streams_of[4], (LAYERS, D, QD), D ** -0.5, 0.125, ((2, 4),)),
        "key_weight": gaussian(streams_of[5], (LAYERS, D, KD), D ** -0.5, 0.125, ((2, 4),)),
        "value_weight": gaussian(streams_of[6], (LAYERS, D, KD), D ** -0.5, 0.125, ((2, 4),)),
        "gate_heads": gaussian(streams_of[7], (LAYERS, D, H), (D // 4) ** -0.5, 0.25, ((2, 4),)),
        "query_gain": jnp.clip(1.0 + 0.1 * jax.random.normal(streams_of[8], (LAYERS, HD), jnp.float32), 0.5, 1.5),
        "key_gain": jnp.clip(1.0 + 0.1 * jax.random.normal(streams_of[9], (LAYERS, HD), jnp.float32), 0.5, 1.5),
        "output_weight": gaussian(streams_of[10], (LAYERS, QD, D), (QD // 32) ** -0.5, 0.75, ((1, 4),)),
        "feed_gain": jnp.clip(1.0 + 0.1 * jax.random.normal(streams_of[11], (LAYERS, D), jnp.float32), 0.5, 1.5),
        "gate_weight": gaussian(streams_of[12], (LAYERS, D, FF), D ** -0.5, 0.125, ((2, 4),)),
        "up_weight": gaussian(streams_of[13], (LAYERS, D, FF), D ** -0.5, 0.125, ((2, 4),)),
        "down_weight": gaussian(streams_of[14], (LAYERS, FF, D), (FF // 4) ** -0.5, 0.15625, ((1, 4),)),
    }


@jax.custom_vjp
def low(v):
    return lax.optimization_barrier(v.astype(jnp.bfloat16)).astype(jnp.float32)

@jax.custom_vjp
def low_back(v):
    return v

def low_keep(v):
    return (low(v), None)

def low_pass(kept, grad):
    return (grad,)

def back_keep(v):
    return (v, None)

def back_low(kept, grad):
    return (low(grad),)
low.defvjp(low_keep, low_pass)
low_back.defvjp(back_keep, back_low)
epsilon = 1e-06
theta = 1000000.0
masked = -1000000000.0

def rms_scale(values, gain):
    return values * lax.rsqrt(lax.optimization_barrier(jnp.mean(values * values, axis=-1, keepdims=True)) + epsilon) * gain

def rotary_tables(positions, width):
    counter = jnp.arange(width // 2, dtype=jnp.float32)
    frequency = theta ** (-2.0 * counter / width)
    angles = positions.astype(jnp.float32)[:, None] * frequency[None, :]
    return (jnp.cos(angles), jnp.sin(angles))

def rotate(values, cos_table, sin_table):
    width = values.shape[-1]
    leading = values[..., :width // 2]
    trailing = values[..., width // 2:]
    cos_part = cos_table[:, None, :]
    sin_part = sin_table[:, None, :]
    return jnp.concatenate([leading * cos_part - trailing * sin_part, trailing * cos_part + leading * sin_part], axis=-1)

def rotated_norm(raw, gain, cos_table, sin_table):
    return rotate(rms_scale(raw, gain), cos_table, sin_table)

def swiglu(gate_pre, up_pre):
    return jax.nn.silu(gate_pre) * up_pre

def gated(attended, logits):
    return attended * jax.nn.sigmoid(logits)[:, :, None]

def project(left, right):
    return jnp.dot(left, right, precision=lax.Precision.HIGHEST)

def attend(inputs):
    query, keys, values, prefix = inputs
    group_size = H // KVH
    keys = jnp.repeat(keys, group_size, axis=1)
    values = jnp.repeat(values, group_size, axis=1)
    scores = jnp.einsum('qhd,khd->hqk', query, keys, precision=lax.Precision.HIGHEST) * HD ** (-0.5)
    scores = low_back(scores)
    places = jnp.arange(LEN, dtype=jnp.int32)
    visible = (places[None, :] <= places[:, None]) | (places[None, :] < prefix)
    scores = jnp.where(visible[None], scores, masked)
    weights = low(jax.nn.softmax(scores, axis=-1))
    return low_back(jnp.einsum('hqk,khd->qhd', weights, values, precision=lax.Precision.HIGHEST))

def block(current, params, prefixes, cos_table, sin_table):
    attention_gain, query_weight, key_weight, value_weight, gate_heads, query_gain, key_gain, output_weight, feed_gain, gate_weight, up_weight, down_weight = params
    flat_rows = current.reshape(SEQS * LEN, D)
    normed = low(rms_scale(flat_rows, attention_gain))
    query_raw = low_back(project(normed, query_weight)).reshape(-1, H, HD)
    key_raw = low_back(project(normed, key_weight)).reshape(-1, KVH, HD)
    values = low(low_back(project(normed, value_weight))).reshape(SEQS, LEN, KVH, HD)
    logits = low_back(project(normed, gate_heads))
    query_rot = low(rotated_norm(query_raw, query_gain, cos_table, sin_table)).reshape(SEQS, LEN, H, HD)
    key_rot = low(rotated_norm(key_raw, key_gain, cos_table, sin_table)).reshape(SEQS, LEN, KVH, HD)
    attended = lax.map(jax.checkpoint(attend), (query_rot, key_rot, values, prefixes)).reshape(-1, H, HD)
    mixed_heads = low(gated(attended, logits).reshape(-1, QD))
    middle = flat_rows + low_back(project(mixed_heads, output_weight))
    normed_two = low(rms_scale(middle, feed_gain))
    gate_pre = low_back(project(normed_two, gate_weight))
    up_pre = low_back(project(normed_two, up_weight))
    hidden = low(swiglu(gate_pre, up_pre))
    layer_out = middle + low_back(project(hidden, down_weight))
    return layer_out.reshape(SEQS, LEN, D)

def reference(stream, cotangent, prefixes, attention_gain, query_weight, key_weight, value_weight, gate_heads, query_gain, key_gain, output_weight, feed_gain, gate_weight, up_weight, down_weight):
    weights_in = (attention_gain, query_weight, key_weight, value_weight, gate_heads, query_gain, key_gain, output_weight, feed_gain, gate_weight, up_weight, down_weight)
    floats = tuple((entry.astype(jnp.float32) for entry in weights_in))
    positions = jnp.tile(jnp.arange(LEN, dtype=jnp.int32), SEQS)
    cos_table, sin_table = rotary_tables(positions, HD)

    def forward(inputs, *params):
        current = inputs
        for depth in range(LAYERS):
            current = block(current, tuple((entry[depth] for entry in params)), prefixes, cos_table, sin_table)
        return current
    result, pullback = jax.vjp(forward, stream.astype(jnp.float32), *floats)
    gradients = pullback(cotangent.astype(jnp.float32))
    return (result.astype(jnp.bfloat16), gradients[0], gradients[1], gradients[2], gradients[3], gradients[4], gradients[5], gradients[6], gradients[7], gradients[8], gradients[9], gradients[10], gradients[11], gradients[12])
```

```python
from functools import partial

import jax
import jax.numpy as jnp
from jax import lax
from jax.experimental import pallas as pl
from jax.experimental.pallas import tpu as pltpu
from jax.sharding import PartitionSpec as P

HD = 128
LAYERS = 2
LANES = 128

epsilon = 1e-06
theta = 1000000.0
masked = -1000000000.0

BF = jnp.bfloat16
F32 = jnp.float32
ANY = pl.BlockSpec(memory_space=pl.ANY)
WHOLE = pl.BlockSpec(memory_space=pltpu.VMEM)
MESH = pl.DeviceIdType.MESH

BLOCKS = 8
PIECES = 2
LAG = 4
STRIP = 16
VMEM_LIMIT = 62 * 1024 * 1024


def rms_scale(values, gain):
    return values * lax.rsqrt(jnp.mean(values * values, axis=-1, keepdims=True) + epsilon) * gain


def rotary_tables(positions, width):
    counter = jnp.arange(width // 2, dtype=jnp.float32)
    frequency = theta ** (-2.0 * counter / width)
    angles = positions.astype(jnp.float32)[:, None] * frequency[None, :]
    return (jnp.cos(angles), jnp.sin(angles))


def rotate(values, cos_table, sin_table):
    width = values.shape[-1]
    leading = values[..., : width // 2]
    trailing = values[..., width // 2 :]
    cos_part = cos_table[:, None, :]
    sin_part = sin_table[:, None, :]
    return jnp.concatenate(
        [leading * cos_part - trailing * sin_part, trailing * cos_part + leading * sin_part],
        axis=-1,
    )


def rotated_norm(raw, gain, cos_table, sin_table):
    return rotate(rms_scale(raw, gain), cos_table, sin_table)


def gated(attended, logits):
    return attended * jax.nn.sigmoid(logits)[:, :, None]


def matmul(left, right):
    return jnp.dot(left, right, preferred_element_type=F32)


def weight_product(left, right):
    return lax.dot_general(left, right, (((0,), (0,)), ((), ())), preferred_element_type=F32)


def back_product(gradient, weight):
    return lax.dot_general(gradient, weight, (((1,), (1,)), ((), ())), preferred_element_type=F32)


def masked_scores(query, keys, prefix, query_pos, key_pos):
    scale = query.shape[-1] ** (-0.5)
    scores = jnp.einsum("qkgd,tkd->kgqt", query, keys, preferred_element_type=F32) * scale
    visible = (key_pos[None, :] <= query_pos[:, None]) | (key_pos[None, :] < prefix)
    return jnp.where(visible, scores, masked)


def attend_forward(inputs, query_pos, key_pos):
    query, keys, values, prefix = inputs
    scores = masked_scores(query, keys, prefix, query_pos, key_pos)
    highest = jnp.max(scores, axis=-1, keepdims=True)
    logsum = highest + jnp.log(jnp.sum(jnp.exp(scores - highest), axis=-1, keepdims=True))
    weights = jnp.exp(scores - logsum).astype(BF)
    attended = jnp.einsum("kgqt,tkd->qkgd", weights, values, preferred_element_type=F32)
    return (attended, logsum)


def attend_backward(inputs, query_pos, key_pos):
    query, keys, values, prefix, logsum, out_grad = inputs
    scale = query.shape[-1] ** (-0.5)
    weights = jnp.exp(masked_scores(query, keys, prefix, query_pos, key_pos) - logsum)
    weight_grad = jnp.einsum("qkgd,tkd->kgqt", out_grad, values, preferred_element_type=F32)
    score_grad = weights * (weight_grad - jnp.sum(weights * weight_grad, axis=-1, keepdims=True))
    score_low = score_grad.astype(BF)
    query_grad = jnp.einsum("kgqt,tkd->qkgd", score_low, keys, preferred_element_type=F32) * scale
    key_grad = jnp.einsum("kgqt,qkgd->tkd", score_low, query, preferred_element_type=F32) * scale
    value_grad = jnp.einsum(
        "kgqt,qkgd->tkd", weights.astype(BF), out_grad, preferred_element_type=F32
    )
    return (query_grad, key_grad, value_grad)


def tile_of(width):
    for size in (512, 384, 256, 128):
        if width % size == 0:
            return size
    return width


def loop(count, body):
    def step(i, carry):
        body(i)
        return carry

    lax.fori_loop(0, count, step, 0)


class Chain:
    def __init__(self, size):
        self.size = size
        self.spot = lax.axis_index("tensor")
        half = size // 2
        on_left = self.spot < half
        self.end = (self.spot == 0) | (self.spot == size - 1)
        self.mid = (self.spot == half - 1) | (self.spot == half)
        self.first_mid = self.spot == half - 1
        self.inward = jnp.where(on_left, self.spot + 1, self.spot - 1)
        self.outward = jnp.where(on_left, self.spot - 1, self.spot + 1)

    def greet(self):
        barrier = pltpu.get_barrier_semaphore()
        pl.semaphore_signal(barrier, inc=1, device_id={"tensor": self.inward}, device_id_type=MESH)

        @pl.when(jnp.logical_not(self.end))
        def _():
            pl.semaphore_signal(
                barrier, inc=1, device_id={"tensor": self.outward}, device_id_type=MESH
            )
            pl.semaphore_wait(barrier, 2)

        @pl.when(self.end)
        def _():
            pl.semaphore_wait(barrier, 1)


class Sum:
    def __init__(self, chain, refs, rows, width):
        self.chain = chain
        self.part, self.landed, self.spread, self.s_in, self.r_in, self.s_out, self.r_out = refs
        self.block = rows // BLOCKS
        self.piece = width // PIECES

    @staticmethod
    def scratch(rows, width):
        return [
            pltpu.VMEM((rows, width), BF),
            pltpu.VMEM((2, rows, width), BF),
            pltpu.VMEM((rows, width), BF),
            pltpu.SemaphoreType.DMA((BLOCKS, PIECES)),
            pltpu.SemaphoreType.DMA((2, BLOCKS, PIECES)),
            pltpu.SemaphoreType.DMA((BLOCKS,)),
            pltpu.SemaphoreType.DMA((BLOCKS,)),
        ]

    def rows(self, r):
        return pl.ds(pl.multiple_of(r * self.block, self.block), self.block)

    def cols(self, p):
        return pl.ds(pl.multiple_of(p * self.piece, self.piece), self.piece)

    def hop(self, r, p, slot):
        where = (self.rows(r), self.cols(p))
        return pltpu.make_async_remote_copy(
            src_ref=self.part.at[where],
            dst_ref=self.landed.at[(slot,) + where],
            send_sem=self.s_in.at[r, p],
            recv_sem=self.r_in.at[slot, r, p],
            device_id={"tensor": self.chain.inward},
            device_id_type=MESH,
        )

    def out_hop(self, r):
        return pltpu.make_async_remote_copy(
            src_ref=self.spread.at[self.rows(r)],
            dst_ref=self.spread.at[self.rows(r)],
            send_sem=self.s_out.at[r],
            recv_sem=self.r_out.at[r],
            device_id={"tensor": self.chain.outward},
            device_id_type=MESH,
        )

    def offer(self, r, p):
        @pl.when(self.chain.end)
        def _():
            self.hop(r, p, 0).start()

    def relay(self, r):
        @pl.when(jnp.logical_not(self.chain.end))
        def _():
            for p in range(PIECES):
                self.hop(r, p, 0).wait_recv()

                def strip(i, p=p):
                    at = pl.ds(pl.multiple_of(r * self.block + i * STRIP, STRIP), STRIP)
                    col = self.cols(p)
                    total = self.part[at, col].astype(F32) + self.landed[0, at, col].astype(F32)
                    self.part[at, col] = total.astype(BF)

                loop(self.block // STRIP, strip)

                @pl.when(self.chain.mid)
                def _(p=p):
                    self.hop(r, p, 1).start()

                @pl.when(jnp.logical_not(self.chain.mid))
                def _(p=p):
                    self.hop(r, p, 0).start()

    def finish(self, r, make):
        @pl.when(self.chain.mid)
        def _():
            for p in range(PIECES):
                self.hop(r, p, 1).wait_recv()

            def strip(i):
                at = pl.ds(pl.multiple_of(r * self.block + i * STRIP, STRIP), STRIP)
                total = self.part[at, :].astype(F32) + self.landed[1, at, :].astype(F32)
                self.spread[at, :] = make(at, total)

            loop(self.block // STRIP, strip)
            self.out_hop(r).start()

        @pl.when(jnp.logical_not(self.chain.mid))
        def _():
            self.out_hop(r).wait_recv()

            @pl.when(jnp.logical_not(self.chain.end))
            def _():
                self.out_hop(r).start()

    def close(self):
        def block(r):
            for p in range(PIECES):
                self.hop(r, p, 0).wait_send()

            @pl.when(jnp.logical_not(self.chain.end))
            def _():
                self.out_hop(r).wait_send()

        loop(BLOCKS, block)


class Small:
    def __init__(self, chain, ref, send, receive):
        self.chain = chain
        self.copy = pltpu.make_async_remote_copy(
            src_ref=ref,
            dst_ref=ref,
            send_sem=send,
            recv_sem=receive,
            device_id={"tensor": chain.outward},
            device_id_type=MESH,
        )

    @staticmethod
    def scratch(width):
        return [
            pltpu.VMEM((8, width), F32),
            pltpu.SemaphoreType.DMA(()),
            pltpu.SemaphoreType.DMA(()),
        ]

    def run(self):
        @pl.when(jnp.logical_not(self.chain.mid))
        def _():
            self.copy.wait_recv()

        @pl.when(jnp.logical_not(self.chain.end))
        def _():
            self.copy.start()
            self.copy.wait_send()


def two_sums(first, second, start, made_one, between, made_two, after):
    loop(BLOCKS, start)

    def step(s):
        @pl.when(s < BLOCKS)
        def _():
            first.relay(s)

        @pl.when((s >= 1) & (s <= BLOCKS))
        def _():
            first.finish(s - 1, made_one)
            between(s - 1)

        @pl.when((s >= LAG) & (s < BLOCKS + LAG))
        def _():
            second.relay(s - LAG)

        @pl.when(s >= LAG + 1)
        def _():
            second.finish(s - LAG - 1, made_two)
            after(s - LAG - 1)

    loop(BLOCKS + LAG + 1, step)


def one_sum(first, start, made, after):
    loop(BLOCKS, start)

    def step(s):
        @pl.when(s < BLOCKS)
        def _():
            first.relay(s)

        @pl.when(s >= 1)
        def _():
            first.finish(s - 1, made)
            after(s - 1)

    loop(BLOCKS + 1, step)


def rows_of(r, block):
    return pl.ds(pl.multiple_of(r * block, block), block)


def columns(j, width):
    return pl.ds(pl.multiple_of(j * width, width), width)


def back_norm(value, gain, grad):
    spread = lax.rsqrt(jnp.mean(value * value, axis=-1, keepdims=True) + epsilon)
    scaled = grad * gain
    pulled = jnp.mean(scaled * value, axis=-1, keepdims=True)
    terms = grad * value * spread
    return spread * scaled - value * (spread * spread * spread * pulled), terms


def fold(terms):
    folded = terms[:8]
    for k in range(8, terms.shape[0], 8):
        folded = folded + terms[k : k + 8]
    return folded


def load_all(pairs, sems):
    copies = [pltpu.make_async_copy(src, dst, sems.at[k]) for k, (src, dst) in enumerate(pairs)]
    for copy in copies:
        copy.start()
    return copies


def forward_kernel(
    size, depth, rows, width,
    mixed, stream, wo, feed_gain, wg, wu, wd, next_gain, wq, wk, wv, gh,
    middle_o, two_o, slope_o, silu_o, hidden_o, x_o, normed_o, q_o, k_o, v_o, logit_o,
    *scratch,
):
    (wo_v, wg_v, wu_v, wd_v, wq_v, wk_v, wv_v, x_v, middle_v, stage_v,
     slope_v, silu_v, hidden_v, q_v, k_v, v_v, logit_v, load_sem, out_sem) = scratch[:19]
    chain = Chain(size)
    one = Sum(chain, scratch[19:26], rows, width)
    two = Sum(chain, scratch[26:33], rows, width)
    block = one.block
    loads = load_all(
        [(wo.at[depth], wo_v), (stream, x_v), (wg.at[depth], wg_v), (wu.at[depth], wu_v),
         (wd.at[depth], wd_v), (wq.at[depth + 1], wq_v), (wk.at[depth + 1], wk_v),
         (wv.at[depth + 1], wv_v)],
        load_sem,
    )
    chain.greet()
    loads[0].wait()
    units = wg_v.shape[1]
    tile = tile_of(units)
    piece = one.piece
    gain_one = feed_gain[depth : depth + 1, :]
    gain_two = next_gain[depth + 1 : depth + 2, :]

    def out(k, r, src, dst):
        at = rows_of(r, block)
        return pltpu.make_async_copy(src.at[at], dst.at[at], out_sem.at[k, r])

    def staged(r):
        return pltpu.make_async_copy(
            stage_v.at[lax.rem(r, 2)], x_o.at[rows_of(r, block)], out_sem.at[5, r]
        )

    def start(r):
        at = rows_of(r, block)
        for p in range(PIECES):
            col = one.cols(p)
            one.part[at, col] = matmul(mixed[at, :], wo_v[:, col]).astype(BF)
            one.offer(r, p)

        @pl.when(r == 0)
        def _():
            loads[1].wait()

    def made_one(at, total):
        value = x_v[at, :].astype(F32) + total
        middle_v[at, :] = value
        return rms_scale(value, gain_one).astype(BF)

    def between(r):
        @pl.when(r == 0)
        def _():
            for copy in loads[2:5]:
                copy.wait()

        at = rows_of(r, block)

        @pl.when(chain.mid)
        def _():
            out(0, r, middle_v, middle_o).start()

        out(1, r, one.spread, two_o).start()

        def units_of(j):
            col = columns(j, tile)
            gate = matmul(one.spread[at, :], wg_v[:, col])
            up = matmul(one.spread[at, :], wu_v[:, col])
            sig = jax.nn.sigmoid(gate)
            act = gate * sig
            hidden_v[at, col] = (act * up).astype(BF)
            silu_v[at, col] = act.astype(BF)
            slope_v[at, col] = (up * (sig * (1.0 + gate * (1.0 - sig)))).astype(BF)

        loop(units // tile, units_of)
        for p in range(PIECES):
            col = two.cols(p)
            two.part[at, col] = matmul(hidden_v[at, :], wd_v[:, col]).astype(BF)
            two.offer(r, p)
        out(2, r, slope_v, slope_o).start()
        out(3, r, silu_v, silu_o).start()
        out(4, r, hidden_v, hidden_o).start()

    def made_two(at, total):
        value = middle_v[at, :] + total
        r = at.start // block
        stage_v[lax.rem(r, 2), pl.ds(pl.multiple_of(lax.rem(at.start, block), STRIP), STRIP), :] = value
        return rms_scale(value, gain_two).astype(BF)

    def after(r):
        @pl.when(r == 0)
        def _():
            for copy in loads[5:]:
                copy.wait()

        at = rows_of(r, block)

        @pl.when(chain.mid)
        def _():
            staged(r).start()

        out(6, r, two.spread, normed_o).start()
        q_v[at, :] = matmul(two.spread[at, :], wq_v[...])
        k_v[at, :] = matmul(two.spread[at, :], wk_v[...])
        v_v[at, :] = matmul(two.spread[at, :], wv_v[...]).astype(BF)
        logit_v[at, :] = matmul(two.spread[at, :], gh[...])
        out(7, r, q_v, q_o).start()
        out(8, r, k_v, k_o).start()
        out(9, r, v_v, v_o).start()
        out(10, r, logit_v, logit_o).start()

        @pl.when(chain.mid)
        def _():
            staged(r).wait()

    two_sums(one, two, start, made_one, between, made_two, after)
    one.close()
    two.close()

    def drain(r):
        @pl.when(chain.mid)
        def _():
            out(0, r, middle_v, middle_o).wait()

        for k, src, dst in (
            (1, one.spread, two_o), (2, slope_v, slope_o), (3, silu_v, silu_o),
            (4, hidden_v, hidden_o), (6, two.spread, normed_o), (7, q_v, q_o),
            (8, k_v, k_o), (9, v_v, v_o), (10, logit_v, logit_o),
        ):
            out(k, r, src, dst).wait()

    loop(BLOCKS, drain)


def turn_kernel(
    size, depth, rows, width,
    mixed, x_in, cot, wo, feed_gain, wg, wu, wd,
    two_o, hidden_o, down_o, gate_o, up_o, grad_o, low_o, mixed_o, gain_o,
    *scratch,
):
    (wo_v, wg_v, wu_v, wd_v, middle_v, cot_v, hidden_v, gate_v, up_v, mixed_v, down_v,
     load_sem, out_sem) = scratch[:13]
    chain = Chain(size)
    one = Sum(chain, scratch[13:20], rows, width)
    two = Sum(chain, scratch[20:27], rows, width)
    gain_v = scratch[27]
    small = Small(chain, *scratch[27:30])
    block = one.block
    loads = load_all(
        [(wo.at[depth], wo_v), (x_in, middle_v), (wg.at[depth], wg_v), (wu.at[depth], wu_v),
         (wd.at[depth], wd_v), (cot, cot_v)],
        load_sem,
    )
    chain.greet()
    loads[0].wait()
    units = wg_v.shape[1]
    tile = tile_of(units)
    gain_one = feed_gain[depth : depth + 1, :]

    def out(k, r, src, dst):
        at = rows_of(r, block)
        return pltpu.make_async_copy(src.at[at], dst.at[at], out_sem.at[k, r])

    def start(r):
        at = rows_of(r, block)
        for p in range(PIECES):
            col = one.cols(p)
            one.part[at, col] = matmul(mixed[at, :], wo_v[:, col]).astype(BF)
            one.offer(r, p)

        @pl.when(r == 0)
        def _():
            loads[1].wait()

    def made_one(at, total):
        value = middle_v[at, :] + total
        middle_v[at, :] = value
        return rms_scale(value, gain_one).astype(BF)

    def between(r):
        @pl.when(r == 0)
        def _():
            for copy in loads[2:]:
                copy.wait()

        at = rows_of(r, block)
        out(0, r, one.spread, two_o).start()

        def units_of(j):
            col = columns(j, tile)
            gate = matmul(one.spread[at, :], wg_v[:, col])
            up = matmul(one.spread[at, :], wu_v[:, col])
            pulled = back_product(cot_v[at, :], wd_v[col, :])
            sig = jax.nn.sigmoid(gate)
            act = gate * sig
            hidden_v[at, col] = (act * up).astype(BF)
            gate_v[at, col] = (pulled * up * (sig * (1.0 + gate * (1.0 - sig)))).astype(BF)
            up_v[at, col] = (pulled * act).astype(BF)

        loop(units // tile, units_of)
        for p in range(PIECES):
            col = two.cols(p)
            two.part[at, col] = (
                back_product(gate_v[at, :], wg_v[col, :]) + back_product(up_v[at, :], wu_v[col, :])
            ).astype(BF)
            two.offer(r, p)
        out(1, r, hidden_v, hidden_o).start()
        out(2, r, gate_v, gate_o).start()
        out(3, r, up_v, up_o).start()
        for p in range(PIECES):
            col = two.cols(p)
            partial_sum = matmul(hidden_v[at, :], wd_v[:, col])

            @pl.when(chain.first_mid)
            def _(col=col, partial_sum=partial_sum):
                down_v[at, col] = (partial_sum + middle_v[at, col]).astype(BF)

            @pl.when(jnp.logical_not(chain.first_mid))
            def _(col=col, partial_sum=partial_sum):
                down_v[at, col] = partial_sum.astype(BF)

        out(4, r, down_v, down_o).start()

    @pl.when(chain.mid)
    def _():
        gain_v[...] = jnp.zeros_like(gain_v)

    def made_two(at, total):
        pulled, terms = back_norm(middle_v[at, :], gain_one, total)
        gain_v[...] += fold(terms)
        value = cot_v[at, :].astype(F32) + pulled
        middle_v[at, :] = value
        return value.astype(BF)

    def after(r):
        at = rows_of(r, block)

        @pl.when(chain.mid)
        def _():
            out(5, r, middle_v, grad_o).start()

        out(6, r, two.spread, low_o).start()
        mixed_v[at, :] = back_product(two.spread[at, :], wo_v[...])
        out(7, r, mixed_v, mixed_o).start()

    two_sums(one, two, start, made_one, between, made_two, after)
    small.run()
    gain_out = pltpu.make_async_copy(gain_v, gain_o, out_sem.at[8, 0])
    gain_out.start()
    one.close()
    two.close()

    def drain(r):
        @pl.when(chain.mid)
        def _():
            out(5, r, middle_v, grad_o).wait()

        for k, src, dst in (
            (0, one.spread, two_o), (1, hidden_v, hidden_o), (2, gate_v, gate_o),
            (3, up_v, up_o), (4, down_v, down_o), (6, two.spread, low_o), (7, mixed_v, mixed_o),
        ):
            out(k, r, src, dst).wait()

    loop(BLOCKS, drain)
    gain_out.wait()


def back_kernel(
    size, depth, rows, width,
    q_low, k_low, v_low, l_low, gh, x_in, grad_in, attention_gain, wq, wk, wv,
    wd, wg, wu, slope_in, silu_in, middle_in, feed_gain, wo,
    gate_o, up_o, first_o, grad_o, low_o, mixed_o, gain_o, feed_gain_o,
    *scratch,
):
    (wq_v, wk_v, wv_v, wd_v, wg_v, wu_v, wo_v, x_v, grad_v, middle_v, slope_v, silu_v,
     gate_v, up_v, mixed_v, load_sem, out_sem) = scratch[:17]
    chain = Chain(size)
    one = Sum(chain, scratch[17:24], rows, width)
    two = Sum(chain, scratch[24:31], rows, width)
    gain_v = scratch[31]
    small = Small(chain, *scratch[31:34])
    feed_v = scratch[34]
    small_two = Small(chain, *scratch[34:37])
    block = one.block
    below = depth - 1
    loads = load_all(
        [(wq.at[depth], wq_v), (wk.at[depth], wk_v), (wv.at[depth], wv_v), (x_in, x_v),
         (grad_in, grad_v), (wd.at[below], wd_v), (wg.at[below], wg_v), (wu.at[below], wu_v),
         (slope_in, slope_v), (silu_in, silu_v), (middle_in, middle_v), (wo.at[below], wo_v)],
        load_sem,
    )
    chain.greet()
    for copy in loads[:3]:
        copy.wait()
    units = wg_v.shape[1]
    tile = tile_of(units)
    gain_one = attention_gain[depth : depth + 1, :]
    gain_two = feed_gain[below : below + 1, :]

    def out(k, r, src, dst):
        at = rows_of(r, block)
        return pltpu.make_async_copy(src.at[at], dst.at[at], out_sem.at[k, r])

    def start(r):
        at = rows_of(r, block)
        for p in range(PIECES):
            col = one.cols(p)
            one.part[at, col] = (
                back_product(q_low[at, :], wq_v[col, :])
                + back_product(k_low[at, :], wk_v[col, :])
                + back_product(v_low[at, :], wv_v[col, :])
                + back_product(l_low[at, :], gh[col, :])
            ).astype(BF)
            one.offer(r, p)

        @pl.when(r == 0)
        def _():
            for copy in loads[3:5]:
                copy.wait()

    @pl.when(chain.mid)
    def _():
        gain_v[...] = jnp.zeros_like(gain_v)
        feed_v[...] = jnp.zeros_like(feed_v)

    def made_one(at, total):
        pulled, terms = back_norm(x_v[at, :], gain_one, total)
        gain_v[...] += fold(terms)
        value = grad_v[at, :] + pulled
        grad_v[at, :] = value
        return value.astype(BF)

    def between(r):
        @pl.when(r == 0)
        def _():
            for copy in loads[5:]:
                copy.wait()

        at = rows_of(r, block)
        out(0, r, one.spread, first_o).start()

        def units_of(j):
            col = columns(j, tile)
            pulled = back_product(one.spread[at, :], wd_v[col, :])
            gate_v[at, col] = (pulled * slope_v[at, col].astype(F32)).astype(BF)
            up_v[at, col] = (pulled * silu_v[at, col].astype(F32)).astype(BF)

        loop(units // tile, units_of)
        for p in range(PIECES):
            col = two.cols(p)
            two.part[at, col] = (
                back_product(gate_v[at, :], wg_v[col, :]) + back_product(up_v[at, :], wu_v[col, :])
            ).astype(BF)
            two.offer(r, p)
        out(1, r, gate_v, gate_o).start()
        out(2, r, up_v, up_o).start()

    def made_two(at, total):
        pulled, terms = back_norm(middle_v[at, :], gain_two, total)
        feed_v[...] += fold(terms)
        value = grad_v[at, :] + pulled
        grad_v[at, :] = value
        return value.astype(BF)

    def after(r):
        at = rows_of(r, block)

        @pl.when(chain.mid)
        def _():
            out(5, r, grad_v, grad_o).start()

        out(3, r, two.spread, low_o).start()
        mixed_v[at, :] = back_product(two.spread[at, :], wo_v[...])
        out(4, r, mixed_v, mixed_o).start()

    two_sums(one, two, start, made_one, between, made_two, after)
    small.run()
    small_two.run()
    gain_out = pltpu.make_async_copy(gain_v, gain_o, out_sem.at[6, 0])
    feed_out = pltpu.make_async_copy(feed_v, feed_gain_o, out_sem.at[7, 0])
    gain_out.start()
    feed_out.start()
    one.close()
    two.close()

    def drain(r):
        @pl.when(chain.mid)
        def _():
            out(5, r, grad_v, grad_o).wait()

        for k, src, dst in (
            (0, one.spread, first_o), (1, gate_v, gate_o), (2, up_v, up_o),
            (3, two.spread, low_o), (4, mixed_v, mixed_o),
        ):
            out(k, r, src, dst).wait()

    loop(BLOCKS, drain)
    gain_out.wait()
    feed_out.wait()


def last_kernel(
    size, depth, rows, width,
    q_low, k_low, v_low, l_low, gh, x_in, grad_in, attention_gain, wq, wk, wv,
    grad_o, gain_o,
    *scratch,
):
    (wq_v, wk_v, wv_v, x_v, grad_v, load_sem, out_sem) = scratch[:7]
    chain = Chain(size)
    one = Sum(chain, scratch[7:14], rows, width)
    gain_v = scratch[14]
    small = Small(chain, *scratch[14:17])
    block = one.block
    loads = load_all(
        [(wq.at[depth], wq_v), (wk.at[depth], wk_v), (wv.at[depth], wv_v), (x_in, x_v),
         (grad_in, grad_v)],
        load_sem,
    )
    chain.greet()
    for copy in loads[:3]:
        copy.wait()
    gain_one = attention_gain[depth : depth + 1, :]

    def out(k, r, src, dst):
        at = rows_of(r, block)
        return pltpu.make_async_copy(src.at[at], dst.at[at], out_sem.at[k, r])

    def start(r):
        at = rows_of(r, block)
        for p in range(PIECES):
            col = one.cols(p)
            one.part[at, col] = (
                back_product(q_low[at, :], wq_v[col, :])
                + back_product(k_low[at, :], wk_v[col, :])
                + back_product(v_low[at, :], wv_v[col, :])
                + back_product(l_low[at, :], gh[col, :])
            ).astype(BF)
            one.offer(r, p)

        @pl.when(r == 0)
        def _():
            for copy in loads[3:]:
                copy.wait()

    @pl.when(chain.mid)
    def _():
        gain_v[...] = jnp.zeros_like(gain_v)

    def made_one(at, total):
        pulled, terms = back_norm(x_v[at, :].astype(F32), gain_one, total)
        gain_v[...] += fold(terms)
        return (grad_v[at, :] + pulled).astype(BF)

    def after(r):
        out(0, r, one.spread, grad_o).start()

    one_sum(one, start, made_one, after)
    small.run()
    gain_out = pltpu.make_async_copy(gain_v, gain_o, out_sem.at[1, 0])
    gain_out.start()
    one.close()

    def drain(r):
        out(0, r, one.spread, grad_o).wait()

    loop(BLOCKS, drain)
    gain_out.wait()


def call(kernel, collective_id, in_specs, outs, scratch, flops):
    return pl.pallas_call(
        kernel,
        out_shape=tuple(jax.ShapeDtypeStruct(shape, kind) for shape, kind in outs),
        in_specs=in_specs,
        out_specs=tuple(ANY for _ in outs),
        scratch_shapes=scratch,
        cost_estimate=pl.CostEstimate(flops=flops, bytes_accessed=40_000_000, transcendentals=0),
        compiler_params=pltpu.CompilerParams(
            collective_id=collective_id, has_side_effects=True, vmem_limit_bytes=VMEM_LIMIT
        ),
    )


def dma(*shape):
    return pltpu.SemaphoreType.DMA(shape)


def shards(
    size,
    stream,
    cotangent,
    prefixes,
    attention_gain,
    query_weight,
    key_weight,
    value_weight,
    gate_heads,
    query_gain,
    key_gain,
    output_weight,
    feed_gain,
    gate_weight,
    up_weight,
    down_weight,
):
    seq_count, row_count, width = stream.shape
    rows = seq_count * row_count
    block = rows // BLOCKS
    heads_wide = query_weight.shape[2]
    keys_wide = key_weight.shape[2]
    units = gate_weight.shape[2]
    gates = gate_heads.shape[2]
    halves = lax.axis_size("ctx")
    offset = lax.axis_index("ctx") * row_count
    query_pos = offset + jnp.arange(row_count, dtype=jnp.int32)
    key_pos = jnp.arange(row_count * halves, dtype=jnp.int32)
    cos_table, sin_table = rotary_tables(query_pos, HD)
    stream_flat = stream.reshape(rows, width)
    cot_flat = cotangent.reshape(rows, width)
    heads_padded = [
        jnp.pad(gate_heads[depth], ((0, 0), (0, LANES - gates))) for depth in range(LAYERS)
    ]
    sum_scratch = Sum.scratch(rows, width)

    def attention(depth, q_raw, k_raw, values, logits):
        q_raw = q_raw.reshape(seq_count, row_count, -1, HD)
        k_raw = k_raw.reshape(seq_count, row_count, -1, HD)
        values = values.reshape(seq_count, row_count, -1, HD)
        query_rot = rotated_norm(q_raw, query_gain[depth], cos_table, sin_table).astype(BF)
        key_rot = rotated_norm(k_raw, key_gain[depth], cos_table, sin_table).astype(BF)
        key_full = lax.all_gather(key_rot, "ctx", axis=1, tiled=True)
        value_full = lax.all_gather(values, "ctx", axis=1, tiled=True)
        key_heads = key_rot.shape[2]
        grouped = query_rot.reshape(seq_count, row_count, key_heads, -1, HD)
        attended, logsum = lax.map(
            partial(attend_forward, query_pos=query_pos, key_pos=key_pos),
            (grouped, key_full, value_full, prefixes),
        )
        attended = attended.reshape(rows, -1, HD)
        mixed = gated(attended, logits).reshape(rows, -1).astype(BF)
        return mixed, (q_raw, k_raw, logits, grouped, key_full, value_full, logsum, attended)

    def attention_back(depth, mixed_grad, saved):
        q_raw, k_raw, logits, grouped, key_full, value_full, logsum, attended = saved
        unused, gate_pull = jax.vjp(gated, attended, logits)
        attended_grad, logits_grad = gate_pull(mixed_grad.reshape(attended.shape))
        attended_low = attended_grad.astype(BF).reshape(grouped.shape)
        logits_low = logits_grad.astype(BF)
        query_grad, key_grad, value_grad = lax.map(
            partial(attend_backward, query_pos=query_pos, key_pos=key_pos),
            (grouped, key_full, value_full, prefixes, logsum, attended_low),
        )
        key_grad = lax.psum_scatter(
            key_grad.astype(BF), "ctx", scatter_dimension=1, tiled=True
        ).astype(F32)
        value_grad = lax.psum_scatter(
            value_grad.astype(BF), "ctx", scatter_dimension=1, tiled=True
        ).astype(F32)
        rotation = partial(rotated_norm, cos_table=cos_table, sin_table=sin_table)
        unused, query_pull = jax.vjp(rotation, q_raw, query_gain[depth])
        query_raw_grad, grad_query_gain = query_pull(query_grad.reshape(q_raw.shape))
        unused, key_pull = jax.vjp(rotation, k_raw, key_gain[depth])
        key_raw_grad, grad_key_gain = key_pull(key_grad)
        query_low = query_raw_grad.astype(BF).reshape(rows, -1)
        key_low = key_raw_grad.astype(BF).reshape(rows, -1)
        value_low = value_grad.astype(BF).reshape(rows, -1)
        return query_low, key_low, value_low, logits_low, grad_query_gain, grad_key_gain

    normed_zero = rms_scale(stream_flat.astype(F32), attention_gain[0]).astype(BF)
    mixed_zero, saved_zero = attention(
        0,
        matmul(normed_zero, query_weight[0]),
        matmul(normed_zero, key_weight[0]),
        matmul(normed_zero, value_weight[0]).astype(BF),
        matmul(normed_zero, gate_heads[0]),
    )
    middle_zero, two_zero, slope, silu, hidden_zero, x_one, normed_one, q_raw, k_raw, values, logits = call(
        partial(forward_kernel, size, 0, rows, width),
        0,
        [WHOLE, ANY, ANY, WHOLE, ANY, ANY, ANY, WHOLE, ANY, ANY, ANY, WHOLE],
        [
            ((rows, width), F32), ((rows, width), BF), ((rows, units), BF), ((rows, units), BF),
            ((rows, units), BF), ((rows, width), F32), ((rows, width), BF),
            ((rows, heads_wide), F32), ((rows, keys_wide), F32), ((rows, keys_wide), BF),
            ((rows, LANES), F32),
        ],
        [
            pltpu.VMEM((heads_wide, width), BF), pltpu.VMEM((width, units), BF),
            pltpu.VMEM((width, units), BF), pltpu.VMEM((units, width), BF),
            pltpu.VMEM((width, heads_wide), BF), pltpu.VMEM((width, keys_wide), BF),
            pltpu.VMEM((width, keys_wide), BF), pltpu.VMEM((rows, width), BF),
            pltpu.VMEM((rows, width), F32), pltpu.VMEM((2, block, width), F32),
            pltpu.VMEM((rows, units), BF), pltpu.VMEM((rows, units), BF),
            pltpu.VMEM((rows, units), BF), pltpu.VMEM((rows, heads_wide), F32),
            pltpu.VMEM((rows, keys_wide), F32), pltpu.VMEM((rows, keys_wide), BF),
            pltpu.VMEM((rows, LANES), F32), dma(8), dma(11, BLOCKS),
        ]
        + sum_scratch + sum_scratch,
        13_000_000_000,
    )(
        mixed_zero, stream_flat, output_weight, feed_gain, gate_weight, up_weight, down_weight,
        attention_gain, query_weight, key_weight, value_weight, heads_padded[1],
    )
    mixed_one, saved_one = attention(1, q_raw, k_raw, values, logits[:, :gates])
    two_one, hidden_one, down_part, gate_low, up_low, grad, low, mixed_grad, feed_one = call(
        partial(turn_kernel, size, 1, rows, width),
        1,
        [WHOLE, ANY, ANY, ANY, WHOLE, ANY, ANY, ANY],
        [
            ((rows, width), BF), ((rows, units), BF), ((rows, width), BF), ((rows, units), BF),
            ((rows, units), BF), ((rows, width), F32), ((rows, width), BF),
            ((rows, heads_wide), F32), ((8, width), F32),
        ],
        [
            pltpu.VMEM((heads_wide, width), BF), pltpu.VMEM((width, units), BF),
            pltpu.VMEM((width, units), BF), pltpu.VMEM((units, width), BF),
            pltpu.VMEM((rows, width), F32), pltpu.VMEM((rows, width), BF),
            pltpu.VMEM((rows, units), BF),
            pltpu.VMEM((rows, units), BF), pltpu.VMEM((rows, units), BF),
            pltpu.VMEM((rows, heads_wide), F32), pltpu.VMEM((rows, width), BF),
            dma(6), dma(9, BLOCKS),
        ]
        + sum_scratch + sum_scratch + Small.scratch(width),
        24_000_000_000,
    )(mixed_one, x_one, cot_flat, output_weight, feed_gain, gate_weight, up_weight, down_weight)
    result = lax.psum(down_part, "tensor")
    q_low, k_low, v_low, l_low, q_gain_one, k_gain_one = attention_back(1, mixed_grad, saved_one)

    grads = [[None] * 12 for _ in range(LAYERS)]

    def scatter(value, dimension):
        return lax.psum_scatter(
            value.astype(BF), ("dp", "ctx"), scatter_dimension=dimension, tiled=True
        ).astype(F32)

    def feed_grads(depth, hidden, low_in, two, gate, up):
        grads[depth][11] = scatter(weight_product(hidden, low_in), 1)
        grads[depth][9] = scatter(weight_product(two, gate), 0)
        grads[depth][10] = scatter(weight_product(two, up), 0)

    def head_grads(depth, mixed, low_in, normed, q, k, v, l):
        grads[depth][7] = scatter(weight_product(mixed, low_in), 1)
        grads[depth][1] = scatter(weight_product(normed, q), 0)
        grads[depth][2] = scatter(weight_product(normed, k), 0)
        grads[depth][3] = scatter(weight_product(normed, v), 0)
        grads[depth][4] = scatter(weight_product(normed, l), 0)

    feed_grads(1, hidden_one, cot_flat, two_one, gate_low, up_low)
    head_grads(1, mixed_one, low, normed_one, q_low, k_low, v_low, l_low)

    def padded(l):
        return jnp.pad(l, ((0, 0), (0, LANES - gates)))

    gate_low, up_low, first_low, grad, low, mixed_grad, gain_one, feed_zero = call(
        partial(back_kernel, size, 1, rows, width),
        2,
        [WHOLE] * 5 + [ANY, ANY, WHOLE] + [ANY] * 9 + [WHOLE, ANY],
        [
            ((rows, units), BF), ((rows, units), BF), ((rows, width), BF), ((rows, width), F32),
            ((rows, width), BF), ((rows, heads_wide), F32), ((8, width), F32), ((8, width), F32),
        ],
        [
            pltpu.VMEM((width, heads_wide), BF), pltpu.VMEM((width, keys_wide), BF),
            pltpu.VMEM((width, keys_wide), BF), pltpu.VMEM((units, width), BF),
            pltpu.VMEM((width, units), BF), pltpu.VMEM((width, units), BF),
            pltpu.VMEM((heads_wide, width), BF), pltpu.VMEM((rows, width), F32),
            pltpu.VMEM((rows, width), F32), pltpu.VMEM((rows, width), F32),
            pltpu.VMEM((rows, units), BF), pltpu.VMEM((rows, units), BF),
            pltpu.VMEM((rows, units), BF),
            pltpu.VMEM((rows, units), BF), pltpu.VMEM((rows, heads_wide), F32),
            dma(12), dma(8, BLOCKS),
        ]
        + sum_scratch + sum_scratch + Small.scratch(width) + Small.scratch(width),
        13_000_000_000,
    )(
        q_low, k_low, v_low, padded(l_low), heads_padded[1], x_one, grad, attention_gain,
        query_weight, key_weight, value_weight, down_weight, gate_weight, up_weight, slope, silu,
        middle_zero, feed_gain, output_weight,
    )
    feed_grads(0, hidden_zero, first_low, two_zero, gate_low, up_low)
    q_low, k_low, v_low, l_low, q_gain_zero, k_gain_zero = attention_back(0, mixed_grad, saved_zero)
    head_grads(0, mixed_zero, low, normed_zero, q_low, k_low, v_low, l_low)
    stream_low, gain_zero = call(
        partial(last_kernel, size, 0, rows, width),
        3,
        [WHOLE] * 5 + [ANY, ANY, WHOLE, ANY, ANY, ANY],
        [((rows, width), BF), ((8, width), F32)],
        [
            pltpu.VMEM((width, heads_wide), BF), pltpu.VMEM((width, keys_wide), BF),
            pltpu.VMEM((width, keys_wide), BF), pltpu.VMEM((rows, width), BF),
            pltpu.VMEM((rows, width), F32), dma(5), dma(2, BLOCKS),
        ]
        + sum_scratch + Small.scratch(width),
        4_000_000_000,
    )(
        q_low, k_low, v_low, padded(l_low), heads_padded[0], stream_flat, grad, attention_gain,
        query_weight, key_weight, value_weight,
    )
    grads[1][0], grads[0][0] = gain_one.sum(0), gain_zero.sum(0)
    grads[1][8], grads[0][8] = feed_one.sum(0), feed_zero.sum(0)
    grads[1][5], grads[0][5] = q_gain_one, q_gain_zero
    grads[1][6], grads[0][6] = k_gain_one, k_gain_zero
    stacked = [jnp.stack([grads[depth][entry] for depth in range(LAYERS)]) for entry in range(12)]
    stacked[5] = lax.psum(stacked[5], "tensor")
    stacked[6] = lax.psum(stacked[6], "tensor")
    for entry in (0, 5, 6, 8):
        stacked[entry] = lax.psum_scatter(
            stacked[entry], ("dp", "ctx"), scatter_dimension=1, tiled=True
        )
    return (
        result.reshape(seq_count, row_count, width),
        stream_low.astype(F32).reshape(seq_count, row_count, width),
        *stacked,
    )


def solution(mesh):
    return jax.shard_map(
        partial(shards, mesh.shape["tensor"]),
        mesh=mesh,
        in_specs=(
            P("dp", "ctx", None),
            P("dp", "ctx", None),
            P("dp"),
            P(),
            P(None, None, "tensor"),
            P(None, None, "tensor"),
            P(None, None, "tensor"),
            P(None, None, "tensor"),
            P(),
            P(),
            P(None, "tensor", None),
            P(),
            P(None, None, "tensor"),
            P(None, None, "tensor"),
            P(None, "tensor", None),
        ),
        out_specs=(
            P("dp", "ctx", None),
            P("dp", "ctx", None),
            P(None, ("dp", "ctx")),
            P(None, ("dp", "ctx"), "tensor"),
            P(None, ("dp", "ctx"), "tensor"),
            P(None, ("dp", "ctx"), "tensor"),
            P(None, ("dp", "ctx"), "tensor"),
            P(None, ("dp", "ctx")),
            P(None, ("dp", "ctx")),
            P(None, "tensor", ("dp", "ctx")),
            P(None, ("dp", "ctx")),
            P(None, ("dp", "ctx"), "tensor"),
            P(None, ("dp", "ctx"), "tensor"),
            P(None, "tensor", ("dp", "ctx")),
        ),
        check_vma=False,
    )
```

```python
from functools import partial

import jax
import jax.numpy as jnp
from jax import lax
from jax.experimental import pallas as pl
from jax.experimental.pallas import tpu as pltpu
from jax.sharding import PartitionSpec as P

HD = 128
LAYERS = 2
LANES = 128

epsilon = 1e-06
theta = 1000000.0
masked = -1000000000.0

BF = jnp.bfloat16
F32 = jnp.float32
ANY = pl.BlockSpec(memory_space=pl.ANY)
WHOLE = pl.BlockSpec(memory_space=pltpu.VMEM)
MESH = pl.DeviceIdType.MESH

BLOCKS = 8
PIECES = 2
GROUP = 4
STRIP = 16
VMEM_LIMIT = 63 * 1024 * 1024


def rms_scale(values, gain):
    return values * lax.rsqrt(jnp.mean(values * values, axis=-1, keepdims=True) + epsilon) * gain


def rotary_tables(positions, width):
    counter = jnp.arange(width // 2, dtype=jnp.float32)
    frequency = theta ** (-2.0 * counter / width)
    angles = positions.astype(jnp.float32)[:, None] * frequency[None, :]
    return (jnp.cos(angles), jnp.sin(angles))


def rotate(values, cos_table, sin_table):
    width = values.shape[-1]
    leading = values[..., : width // 2]
    trailing = values[..., width // 2 :]
    cos_part = cos_table[:, None, :]
    sin_part = sin_table[:, None, :]
    return jnp.concatenate(
        [leading * cos_part - trailing * sin_part, trailing * cos_part + leading * sin_part],
        axis=-1,
    )


def rotated_norm(raw, gain, cos_table, sin_table):
    return rotate(rms_scale(raw, gain), cos_table, sin_table)


def gated(attended, logits):
    return attended * jax.nn.sigmoid(logits)[:, :, None]


def matmul(left, right):
    return jnp.dot(left, right, preferred_element_type=F32)


def weight_product(left, right):
    return lax.dot_general(left, right, (((0,), (0,)), ((), ())), preferred_element_type=F32)


def back_product(gradient, weight):
    return lax.dot_general(gradient, weight, (((1,), (1,)), ((), ())), preferred_element_type=F32)


def masked_scores(query, keys, prefix, query_pos, key_pos):
    scale = query.shape[-1] ** (-0.5)
    scores = jnp.einsum("qkgd,tkd->kgqt", query, keys, preferred_element_type=F32) * scale
    visible = (key_pos[None, :] <= query_pos[:, None]) | (key_pos[None, :] < prefix)
    return jnp.where(visible, scores, masked)


def attend_forward(inputs, query_pos, key_pos):
    query, keys, values, prefix = inputs
    scores = masked_scores(query, keys, prefix, query_pos, key_pos)
    highest = jnp.max(scores, axis=-1, keepdims=True)
    logsum = highest + jnp.log(jnp.sum(jnp.exp(scores - highest), axis=-1, keepdims=True))
    weights = jnp.exp(scores - logsum).astype(BF)
    attended = jnp.einsum("kgqt,tkd->qkgd", weights, values, preferred_element_type=F32)
    return (attended, logsum)


def attend_backward(inputs, query_pos, key_pos):
    query, keys, values, prefix, logsum, out_grad = inputs
    scale = query.shape[-1] ** (-0.5)
    weights = jnp.exp(masked_scores(query, keys, prefix, query_pos, key_pos) - logsum)
    weight_grad = jnp.einsum("qkgd,tkd->kgqt", out_grad, values, preferred_element_type=F32)
    score_grad = weights * (weight_grad - jnp.sum(weights * weight_grad, axis=-1, keepdims=True))
    score_low = score_grad.astype(BF)
    query_grad = jnp.einsum("kgqt,tkd->qkgd", score_low, keys, preferred_element_type=F32) * scale
    key_grad = jnp.einsum("kgqt,qkgd->tkd", score_low, query, preferred_element_type=F32) * scale
    value_grad = jnp.einsum(
        "kgqt,qkgd->tkd", weights.astype(BF), out_grad, preferred_element_type=F32
    )
    return (query_grad, key_grad, value_grad)


def loop(count, body):
    def step(i, carry):
        body(i)
        return carry

    lax.fori_loop(0, count, step, 0)


def rows_of(r, block):
    return pl.ds(pl.multiple_of(r * block, block), block)


def columns(j, width):
    return pl.ds(pl.multiple_of(j * width, width), width)


def greet(targets, extra, has_extra):
    barrier = pltpu.get_barrier_semaphore()
    for target in targets:
        pl.semaphore_signal(barrier, inc=1, device_id=target, device_id_type=MESH)

    @pl.when(has_extra)
    def _():
        pl.semaphore_signal(barrier, inc=1, device_id=extra, device_id_type=MESH)
        pl.semaphore_wait(barrier, len(targets) + 1)

    @pl.when(jnp.logical_not(has_extra))
    def _():
        pl.semaphore_wait(barrier, len(targets))


class Chain:
    def __init__(self, size):
        self.size = size
        self.spot = lax.axis_index("tensor")
        half = size // 2
        on_left = self.spot < half
        self.end = (self.spot == 0) | (self.spot == size - 1)
        self.inner = jnp.logical_not(self.end)
        self.mid = (self.spot == half - 1) | (self.spot == half)
        self.outer = jnp.logical_not(self.mid)
        self.first_mid = self.spot == half - 1
        self.inward = {"tensor": jnp.where(on_left, self.spot + 1, self.spot - 1)}
        self.outward = {"tensor": jnp.where(on_left, self.spot - 1, self.spot + 1)}

    def greet(self, others=()):
        greet([self.inward, *others], self.outward, self.inner)


class Sum:
    def __init__(self, chain, refs, rows, width):
        self.chain = chain
        self.part, self.landed, self.spread, self.s_in, self.r_in, self.s_out, self.r_out = refs
        self.block = rows // BLOCKS
        self.piece = width // PIECES

    @staticmethod
    def scratch(rows, width):
        return [
            pltpu.VMEM((rows, width), BF),
            pltpu.VMEM((2, rows, width), BF),
            pltpu.VMEM((rows, width), BF),
            pltpu.SemaphoreType.DMA((BLOCKS, PIECES)),
            pltpu.SemaphoreType.DMA((2, BLOCKS, PIECES)),
            pltpu.SemaphoreType.DMA((BLOCKS,)),
            pltpu.SemaphoreType.DMA((BLOCKS,)),
        ]

    def hop(self, r, p, slot):
        where = (rows_of(r, self.block), columns(p, self.piece))
        return pltpu.make_async_remote_copy(
            src_ref=self.part.at[where],
            dst_ref=self.landed.at[(slot,) + where],
            send_sem=self.s_in.at[r, p],
            recv_sem=self.r_in.at[slot, r, p],
            device_id=self.chain.inward,
            device_id_type=MESH,
        )

    def out_hop(self, r):
        at = rows_of(r, self.block)
        return pltpu.make_async_remote_copy(
            src_ref=self.spread.at[at],
            dst_ref=self.spread.at[at],
            send_sem=self.s_out.at[r],
            recv_sem=self.r_out.at[r],
            device_id=self.chain.outward,
            device_id_type=MESH,
        )

    def offer(self, g):
        @pl.when(self.chain.end)
        def _():
            def one(k):
                for p in range(PIECES):
                    self.hop(g * GROUP + k, p, 0).start()

            loop(GROUP, one)

    def relay(self, r):
        @pl.when(self.chain.inner)
        def _():
            for p in range(PIECES):
                self.hop(r, p, 0).wait_recv()
                col = columns(p, self.piece)

                def strip(i, col=col):
                    at = pl.ds(pl.multiple_of(r * self.block + i * STRIP, STRIP), STRIP)
                    total = self.part[at, col].astype(F32) + self.landed[0, at, col].astype(F32)
                    self.part[at, col] = total.astype(BF)

                loop(self.block // STRIP, strip)

                @pl.when(self.chain.mid)
                def _(p=p):
                    self.hop(r, p, 1).start()

                @pl.when(self.chain.outer)
                def _(p=p):
                    self.hop(r, p, 0).start()

    def finish(self, r, make):
        @pl.when(self.chain.mid)
        def _():
            for p in range(PIECES):
                self.hop(r, p, 1).wait_recv()

            def strip(i):
                at = pl.ds(pl.multiple_of(r * self.block + i * STRIP, STRIP), STRIP)
                total = self.part[at, :].astype(F32) + self.landed[1, at, :].astype(F32)
                self.spread[at, :] = make(at, total)

            loop(self.block // STRIP, strip)
            self.out_hop(r).start()

    def receive(self, g):
        @pl.when(self.chain.outer)
        def _():
            def one(k):
                self.out_hop(g * GROUP + k).wait_recv()

                @pl.when(self.chain.inner)
                def _():
                    self.out_hop(g * GROUP + k).start()

            loop(GROUP, one)

    def close(self):
        def block(r):
            for p in range(PIECES):
                self.hop(r, p, 0).wait_send()

            @pl.when(self.chain.inner)
            def _():
                self.out_hop(r).wait_send()

        loop(BLOCKS, block)


PARTS = GROUP
GROUPS = BLOCKS // GROUP
STEPS = 2 * BLOCKS + 1


def two_sums(s, first, second, made_one, between, ahead, made_two, after):
    @pl.when(s < BLOCKS)
    def _():
        first.relay(s)

    @pl.when((s >= 1) & (s <= BLOCKS))
    def _():
        first.finish(s - 1, made_one)

    @pl.when((s >= GROUP) & (s < BLOCKS + GROUP))
    def _():
        part = lax.rem(s - GROUP, PARTS)
        group = lax.div(s - GROUP, PARTS)

        @pl.when(part == 0)
        def _():
            first.receive(group)

        between(group, part)

    @pl.when((s >= BLOCKS) & (s < 2 * BLOCKS))
    def _():
        second.relay(s - BLOCKS)

    @pl.when((s >= BLOCKS + 1) & (s < STEPS))
    def _():
        @pl.when(lax.rem(s - BLOCKS - 1, GROUP) == 0)
        def _():
            ahead(lax.div(s - BLOCKS - 1, GROUP))

        second.finish(s - BLOCKS - 1, made_two)

        @pl.when(lax.rem(s - BLOCKS, GROUP) == 0)
        def _():
            group = lax.div(s - BLOCKS, GROUP) - 1
            second.receive(group)
            after(group)


def back_norm(value, gain, grad):
    spread = lax.rsqrt(jnp.mean(value * value, axis=-1, keepdims=True) + epsilon)
    scaled = grad * gain
    pulled = jnp.mean(scaled * value, axis=-1, keepdims=True)
    terms = grad * value * spread
    return spread * scaled - value * (spread * spread * spread * pulled), terms


def fold(terms):
    folded = terms[:8]
    for k in range(8, terms.shape[0], 8):
        folded = folded + terms[k : k + 8]
    return folded


def load_all(pairs, sems):
    copies = [pltpu.make_async_copy(src, dst, sems.at[k]) for k, (src, dst) in enumerate(pairs)]
    for copy in copies:
        copy.start()
    return copies


def wait_all(copies):
    for copy in copies:
        copy.wait()


def wide(width):
    return 512 if width % 512 == 0 else 256


def fill(target, at, make):
    width = target.shape[1]
    tile = wide(width)

    def one(p):
        col = columns(p, tile)
        target[at, col] = make(col).astype(target.dtype)

    loop(width // tile, one)


def flip(value, bit):
    return value + bit * (1 - 2 * lax.rem(lax.div(value, bit), 2))


class Plane:
    def __init__(self, dp_size, ctx_size):
        self.count = dp_size * ctx_size
        self.ctx_size = ctx_size
        self.me = lax.axis_index("dp") * ctx_size + lax.axis_index("ctx")
        bits = [1 << k for k in range(self.count.bit_length() - 1)]
        near = [bit for bit in bits if bit >= ctx_size][:1]
        rest = [bit for bit in bits if bit not in near]
        self.bits = bits
        self.orders = (near + rest, near + rest[1:] + rest[:1])

    def partner(self, bit):
        other = flip(self.me, bit)
        return {"dp": lax.div(other, self.ctx_size), "ctx": lax.rem(other, self.ctx_size)}

    def partners(self):
        return [self.partner(bit) for bit in self.bits]


class Scatter:
    SLOTS = (2, 4, 4, 4)
    KEPT = (1, 3, 3, 3)
    RESULTS = 2
    LAGS = (0, 1, 4, 7, 10, 13)

    def __init__(self, plane, refs, groups, share, tile):
        self.plane = plane
        self.groups = groups
        self.share, self.tile = share, tile
        self.stages = len(plane.bits)
        self.units = sum(group[4] for group in groups)
        self.refs = [refs[6 * k : 6 * k + 6] for k in range(self.stages)]
        self.made, self.out_sem, self.load_sem = refs[6 * self.stages :]
        self.steps = self.units + self.LAGS[self.stages]

    @classmethod
    def scratch(cls, count, share, tile):
        found = []
        blocks = count // 2
        for k in range(count.bit_length() - 1):
            slots = cls.SLOTS[k]
            found += [
                pltpu.VMEM((depth, blocks, share, tile), BF) for depth in (slots, cls.KEPT[k], slots)
            ]
            found += [
                pltpu.SemaphoreType.DMA((slots,)),
                pltpu.SemaphoreType.DMA((slots,)),
                pltpu.SemaphoreType.REGULAR((slots,)),
            ]
            blocks //= 2
        return found + [
            pltpu.VMEM((cls.RESULTS, share, tile), BF),
            pltpu.SemaphoreType.DMA((cls.RESULTS,)),
            pltpu.SemaphoreType.DMA((2,)),
        ]

    def partner(self, stage, u):
        odd = lax.rem(u, 2) == 1
        even_one, odd_one = (self.plane.partner(order[stage]) for order in self.plane.orders)
        return {axis: jnp.where(odd, odd_one[axis], even_one[axis]) for axis in even_one}

    def copy(self, stage, u):
        send, unused, land, s_sem, r_sem, unused_credit = self.refs[stage]
        slot = lax.rem(u, self.SLOTS[stage])
        return pltpu.make_async_remote_copy(
            src_ref=send.at[slot],
            dst_ref=land.at[slot],
            send_sem=s_sem.at[slot],
            recv_sem=r_sem.at[slot],
            device_id=self.partner(stage, u),
            device_id_type=MESH,
        )

    def ready(self, stage, u):
        @pl.when(u >= self.SLOTS[stage])
        def _():
            self.copy(stage, u - self.SLOTS[stage]).wait_send()

    def push(self, stage, u):
        @pl.when(u >= self.SLOTS[stage])
        def _():
            pl.semaphore_wait(self.refs[stage][5].at[lax.rem(u, self.SLOTS[stage])], 1)

        self.copy(stage, u).start()

    def product(self, u):
        send, keep = self.refs[0][:2]
        slot, spot = lax.rem(u, self.SLOTS[0]), lax.rem(u, self.KEPT[0])
        odd = lax.rem(u, 2)
        orders = self.plane.orders
        blocks = self.plane.count // 2
        first = 0
        for whole, parts, by_rows, unused, count, loads in self.groups:

            @pl.when((u >= first) & (u < first + count))
            def _(whole=whole, parts=parts, by_rows=by_rows, first=first, loads=loads):
                if loads:

                    @pl.when(u == first)
                    def _():
                        wait_all(load_all(loads, self.load_sem))

                col = columns(u - first, self.tile)

                def one(i):
                    far = lax.rem(i, 2)
                    j = lax.div(i, 2)
                    owner = flip(self.plane.me, orders[0][0]) * far + self.plane.me * (1 - far)
                    rest = j
                    for bits in reversed(tuple(zip(*orders))[1:]):
                        low = lax.rem(rest, 2)
                        rest = lax.div(rest, 2)
                        turned = flip(owner, bits[0]) * (1 - odd) + flip(owner, bits[1]) * odd
                        owner = turned * low + owner * (1 - low)
                    at = columns(owner, self.share)
                    if by_rows:
                        made = weight_product(whole[:, at], parts[:, col])
                    else:
                        made = weight_product(parts[:, col], whole[:, at])
                    made = made.astype(BF)

                    @pl.when(far == 1)
                    def _():
                        send[slot, j] = made

                    @pl.when(far == 0)
                    def _():
                        keep[spot, j] = made

                loop(2 * blocks, one)

            first += count

    def merge(self, stage, u):
        unused, keep, land = self.refs[stage][:3]
        slots = self.SLOTS[stage]
        slot, spot = lax.rem(u, slots), lax.rem(u, self.KEPT[stage])
        self.copy(stage, u).wait_recv()
        half = (self.plane.count // 2) >> (stage + 1)
        last = stage == self.stages - 1
        if not last:
            self.ready(stage + 1, u)
            send_on, keep_on = self.refs[stage + 1][:2]
            slot_on = lax.rem(u, self.SLOTS[stage + 1])
            spot_on = lax.rem(u, self.KEPT[stage + 1])

            def one(j):
                far = keep[spot, half + j].astype(F32) + land[slot, half + j].astype(F32)
                send_on[slot_on, j] = far.astype(BF)
                near = keep[spot, j].astype(F32) + land[slot, j].astype(F32)
                keep_on[spot_on, j] = near.astype(BF)

            loop(half, one)
            self.push(stage + 1, u)
        else:
            place = lax.rem(u, self.RESULTS)

            @pl.when(u >= self.RESULTS)
            def _():
                self.results(u - self.RESULTS, lambda copy: copy.wait())

            total = keep[spot, 0].astype(F32) + land[slot, 0].astype(F32)
            self.made[place] = total.astype(BF)
            self.results(u, lambda copy: copy.start())

        @pl.when(u + slots < self.units)
        def _():
            pl.semaphore_signal(
                self.refs[stage][5].at[slot],
                inc=1,
                device_id=self.partner(stage, u),
                device_id_type=MESH,
            )

    def results(self, u, act):
        place = lax.rem(u, self.RESULTS)
        first = 0
        for unused, unused_parts, by_rows, out, count, unused_loads in self.groups:

            @pl.when((u >= first) & (u < first + count))
            def _(by_rows=by_rows, out=out, first=first):
                if by_rows:
                    at = (slice(None), columns(u - first, self.tile))
                else:
                    at = (rows_of(u - first, self.tile), slice(None))
                act(pltpu.make_async_copy(self.made.at[place], out.at[at], self.out_sem.at[place]))

            first += count

    def tick(self, i):
        for stage in reversed(range(self.stages)):
            u = i - self.LAGS[stage + 1]

            @pl.when((u >= 0) & (u < self.units))
            def _(stage=stage, u=u):
                self.merge(stage, u)

        @pl.when(i < self.units)
        def _():
            self.ready(0, i)
            self.product(i)
            self.push(0, i)

    def close(self):
        for stage in range(self.stages):
            for k in range(max(0, self.units - self.SLOTS[stage]), self.units):
                self.copy(stage, jnp.int32(k)).wait_send()
        for k in range(max(0, self.units - self.RESULTS), self.units):
            self.results(jnp.int32(k), lambda copy: copy.wait())


class Total:
    def __init__(self, plane, size, refs, own):
        self.plane, self.own = plane, own
        self.value, self.land, self.s_sem, self.r_sem = refs
        spot = lax.axis_index("tensor")
        bits = [1 << k for k in range(size.bit_length() - 1)]
        self.targets = [plane.partner(bit) for bit in plane.bits]
        self.across = [{"tensor": flip(spot, bit)} for bit in bits]
        self.stages = len(self.targets) + len(bits)

    @staticmethod
    def scratch(rows, width, stages):
        return [
            pltpu.VMEM((stages, rows, width), F32),
            pltpu.VMEM((stages, rows, width), F32),
            pltpu.SemaphoreType.DMA((stages,)),
            pltpu.SemaphoreType.DMA((stages,)),
        ]

    def copy(self, k):
        count = len(self.targets)
        rows = slice(None) if k < count else pl.ds(0, self.own)
        return pltpu.make_async_remote_copy(
            src_ref=self.value.at[k, rows],
            dst_ref=self.land.at[k, rows],
            send_sem=self.s_sem.at[k],
            recv_sem=self.r_sem.at[k],
            device_id=(self.targets + self.across)[k],
            device_id_type=MESH,
        )

    def start(self, k):
        if k > 0:
            self.copy(k - 1).wait_recv()
            rows = slice(None) if k - 1 < len(self.targets) else pl.ds(0, self.own)
            if k - 1 >= len(self.targets):
                self.value[k] = self.value[k - 1]
            self.value[k, rows] = self.value[k - 1, rows] + self.land[k - 1, rows]
        self.copy(k).start()

    def finish(self, target):
        last = self.stages - 1
        self.copy(last).wait_recv()
        rows = pl.ds(0, self.own)
        target[...] = self.value[last]
        target[rows] = self.value[last, rows] + self.land[last, rows]
        for k in range(self.stages):
            self.copy(k).wait_send()


def forward_kernel(
    size, depth, rows, width,
    mixed, stream, wo, feed_gain, wg, wu, wd, next_gain, wq, wk, wv, gh,
    middle_o, two_o, slope_o, silu_o, hidden_o, x_o, normed_o, q_o, k_o, v_o, logit_o,
    *scratch,
):
    (wo_v, wg_v, wu_v, wd_v, wq_v, wk_v, wv_v, x_v, middle_v, slope_v, silu_v, hidden_v, q_v, k_v,
     v_v, logit_v, load_sem, out_sem) = scratch[:18]
    chain = Chain(size)
    one = Sum(chain, scratch[18:25], rows, width)
    two = Sum(chain, scratch[25:32], rows, width)
    span = one.block * GROUP
    loads = load_all(
        [(wo.at[depth], wo_v), (stream, x_v), (wg.at[depth], wg_v), (wu.at[depth], wu_v),
         (wd.at[depth], wd_v), (wq.at[depth + 1], wq_v), (wk.at[depth + 1], wk_v),
         (wv.at[depth + 1], wv_v)],
        load_sem,
    )
    chain.greet()
    tile = wg_v.shape[1] // (PARTS - 1)
    gain_one = feed_gain[depth : depth + 1, :]
    gain_two = next_gain[depth + 1 : depth + 2, :]

    def out(k, g, src, dst):
        at = rows_of(g, span)
        return pltpu.make_async_copy(src.at[at], dst.at[at], out_sem.at[k, g])

    loads[0].wait()

    def start(g):
        at = rows_of(g, span)
        fill(one.part, at, lambda col: matmul(mixed[at, :], wo_v[:, col]))
        one.offer(g)

    loop(GROUPS, start)
    wait_all(loads[1:5])

    def made_one(at, total):
        value = x_v[at, :].astype(F32) + total
        middle_v[at, :] = value
        return rms_scale(value, gain_one).astype(BF)

    def between(g, part):
        at = rows_of(g, span)

        @pl.when(part == 0)
        def _():
            out(1, g, one.spread, two_o).start()

            @pl.when(chain.mid)
            def _():
                out(0, g, middle_v, middle_o).start()

        @pl.when(part < PARTS - 1)
        def _():
            col = columns(part, tile)
            gate = matmul(one.spread[at, :], wg_v[:, col])
            up = matmul(one.spread[at, :], wu_v[:, col])
            sig = jax.nn.sigmoid(gate)
            act = gate * sig
            hidden_v[at, col] = (act * up).astype(BF)
            silu_v[at, col] = act.astype(BF)
            slope_v[at, col] = (up * (sig * (1.0 + gate * (1.0 - sig)))).astype(BF)

        @pl.when(part == PARTS - 1)
        def _():
            fill(two.part, at, lambda col: matmul(hidden_v[at, :], wd_v[:, col]))
            two.offer(g)
            out(2, g, slope_v, slope_o).start()
            out(3, g, silu_v, silu_o).start()
            out(4, g, hidden_v, hidden_o).start()

    def ahead(g):
        @pl.when(g == 0)
        def _():
            wait_all(loads[5:])

        @pl.when(chain.mid)
        def _():
            out(0, g, middle_v, middle_o).wait()

    def made_two(at, total):
        value = middle_v[at, :] + total
        middle_v[at, :] = value
        return rms_scale(value, gain_two).astype(BF)

    def after(g):
        at = rows_of(g, span)

        @pl.when(chain.mid)
        def _():
            out(5, g, middle_v, x_o).start()

        q_v[at, :] = matmul(two.spread[at, :], wq_v[...])
        out(7, g, q_v, q_o).start()
        k_v[at, :] = matmul(two.spread[at, :], wk_v[...])
        out(8, g, k_v, k_o).start()
        v_v[at, :] = matmul(two.spread[at, :], wv_v[...]).astype(BF)
        out(9, g, v_v, v_o).start()
        logit_v[at, :] = matmul(two.spread[at, :], gh[...])
        out(10, g, logit_v, logit_o).start()
        out(6, g, two.spread, normed_o).start()

    loop(STEPS, lambda s: two_sums(s, one, two, made_one, between, ahead, made_two, after))
    one.close()
    two.close()

    def drain(g):
        @pl.when(chain.mid)
        def _():
            out(5, g, middle_v, x_o).wait()

        for k, src, dst in (
            (1, one.spread, two_o), (2, slope_v, slope_o), (3, silu_v, silu_o),
            (4, hidden_v, hidden_o), (6, two.spread, normed_o), (7, q_v, q_o),
            (8, k_v, k_o), (9, v_v, v_o), (10, logit_v, logit_o),
        ):
            out(k, g, src, dst).wait()

    loop(GROUPS, drain)


def turn_kernel(
    size, depth, rows, width,
    mixed, x_in, cot, wo, feed_gain, wg, wu, wd,
    two_o, hidden_o, down_o, gate_o, up_o, grad_o, low_o, mixed_o, gain_o,
    *scratch,
):
    (wo_v, wg_v, wu_v, wd_v, middle_v, cot_v, hidden_v, gate_v, up_v, mixed_v, down_v, gain_v,
     load_sem, out_sem) = scratch[:14]
    chain = Chain(size)
    one = Sum(chain, scratch[14:21], rows, width)
    two = Sum(chain, scratch[21:28], rows, width)
    span = one.block * GROUP
    loads = load_all(
        [(wo.at[depth], wo_v), (x_in, middle_v), (cot, cot_v), (wg.at[depth], wg_v),
         (wu.at[depth], wu_v), (wd.at[depth], wd_v)],
        load_sem,
    )
    chain.greet()
    tile = wg_v.shape[1] // (PARTS - 1)
    gain_one = feed_gain[depth : depth + 1, :]

    def out(k, g, src, dst):
        at = rows_of(g, span)
        return pltpu.make_async_copy(src.at[at], dst.at[at], out_sem.at[k, g])

    loads[0].wait()

    def start(g):
        at = rows_of(g, span)
        fill(one.part, at, lambda col: matmul(mixed[at, :], wo_v[:, col]))
        one.offer(g)

    loop(GROUPS, start)
    gain_v[...] = jnp.zeros_like(gain_v)
    wait_all(loads[1:])

    def made_one(at, total):
        value = middle_v[at, :] + total
        middle_v[at, :] = value
        return rms_scale(value, gain_one).astype(BF)

    def between(g, part):
        at = rows_of(g, span)

        @pl.when(part == 0)
        def _():
            out(0, g, one.spread, two_o).start()

        @pl.when(part < PARTS - 1)
        def _():
            col = columns(part, tile)
            gate = matmul(one.spread[at, :], wg_v[:, col])
            sig = jax.nn.sigmoid(gate)
            act = gate * sig
            slope = sig * (1.0 + gate * (1.0 - sig))
            up = matmul(one.spread[at, :], wu_v[:, col])
            hidden_v[at, col] = (act * up).astype(BF)
            pulled = back_product(cot_v[at, :], wd_v[col, :])
            gate_v[at, col] = (pulled * up * slope).astype(BF)
            up_v[at, col] = (pulled * act).astype(BF)

        @pl.when(part == PARTS - 1)
        def _():
            fill(
                two.part,
                at,
                lambda col: back_product(gate_v[at, :], wg_v[col, :])
                + back_product(up_v[at, :], wu_v[col, :]),
            )
            two.offer(g)
            out(1, g, hidden_v, hidden_o).start()
            out(2, g, gate_v, gate_o).start()
            out(3, g, up_v, up_o).start()

    def ahead(g):
        at = rows_of(g, span)
        share = jnp.where(chain.first_mid, 1.0, 0.0)

        @pl.when(chain.first_mid)
        def _():
            fill(down_v, at, lambda col: matmul(hidden_v[at, :], wd_v[:, col]) + middle_v[at, col])

        @pl.when(jnp.logical_not(chain.first_mid))
        def _():
            fill(down_v, at, lambda col: matmul(hidden_v[at, :], wd_v[:, col]))

        out(4, g, down_v, down_o).start()

    def made_two(at, total):
        pulled, terms = back_norm(middle_v[at, :], gain_one, total)
        gain_v[...] += fold(terms)
        value = cot_v[at, :].astype(F32) + pulled
        middle_v[at, :] = value
        return value.astype(BF)

    def after(g):
        at = rows_of(g, span)

        @pl.when(chain.mid)
        def _():
            out(5, g, middle_v, grad_o).start()

        out(6, g, two.spread, low_o).start()
        mixed_v[at, :] = back_product(two.spread[at, :], wo_v[...])
        out(7, g, mixed_v, mixed_o).start()

    loop(STEPS, lambda s: two_sums(s, one, two, made_one, between, ahead, made_two, after))

    @pl.when(jnp.logical_not(chain.first_mid))
    def _():
        gain_v[...] = jnp.zeros_like(gain_v)

    gain_out = pltpu.make_async_copy(gain_v, gain_o, out_sem.at[8, 0])
    gain_out.start()
    one.close()
    two.close()

    def drain(g):
        @pl.when(chain.mid)
        def _():
            out(5, g, middle_v, grad_o).wait()

        for k, src, dst in (
            (0, one.spread, two_o), (1, hidden_v, hidden_o), (2, gate_v, gate_o),
            (3, up_v, up_o), (4, down_v, down_o), (6, two.spread, low_o), (7, mixed_v, mixed_o),
        ):
            out(k, g, src, dst).wait()

    loop(GROUPS, drain)
    gain_out.wait()


def back_kernel(
    size, plane_sizes, depth, rows, width,
    q_low, k_low, v_low, l_low, gh, x_in, grad_in, attention_gain, wq, wk, wv,
    wd, wg, wu, slope_in, silu_in, middle_in, feed_gain, wo,
    two_in, gate_in, up_in, cot_in, hidden_in, normed_in, low_in, mixed_in,
    gate_o, up_o, first_o, grad_o, low_o, mixed_o, gain_o, feed_gain_o,
    *rest,
):
    made, scratch = rest[:7], rest[7:]
    (wq_v, wk_v, wv_v, wd_v, wg_v, wu_v, wo_v, x_v, grad_v, slope_v, silu_v, gate_v, up_v, mixed_v,
     gain_v, feed_v, whole_v, parts_v, load_sem, row_sem, tile_sem, out_sem) = scratch[:22]
    chain = Chain(size)
    one = Sum(chain, scratch[22:29], rows, width)
    two = Sum(chain, scratch[29:36], rows, width)
    plane = Plane(*plane_sizes)
    share = width // plane.count
    unit = min(256, wk_v.shape[1])
    units_wide, heads_wide, keys_wide = wg_v.shape[1], wq_v.shape[1], wk_v.shape[1]
    parts_heads = parts_v.at[:, pl.ds(0, heads_wide)]
    scatter = Scatter(
        plane, scratch[36:],
        [
            (whole_v, parts_v, True, made[0], units_wide // unit, [(two_in, whole_v), (gate_in, parts_v)]),
            (whole_v, parts_v, True, made[1], units_wide // unit, [(up_in, parts_v)]),
            (whole_v, parts_v, False, made[2], units_wide // unit, [(cot_in, whole_v), (hidden_in, parts_v)]),
            (whole_v, q_low, True, made[3], heads_wide // unit, [(normed_in, whole_v)]),
            (whole_v, k_low, True, made[4], keys_wide // unit, []),
            (whole_v, v_low, True, made[5], keys_wide // unit, []),
            (whole_v, parts_v, False, made[6], heads_wide // unit, [(low_in, whole_v), (mixed_in, parts_heads)]),
        ],
        share, unit,
    )
    span = one.block * GROUP
    below = depth - 1
    loads = load_all(
        [(wq.at[depth], wq_v), (wk.at[depth], wk_v), (wv.at[depth], wv_v), (grad_in, grad_v),
         (wd.at[below], wd_v), (wg.at[below], wg_v), (wu.at[below], wu_v), (wo.at[below], wo_v)],
        load_sem,
    )

    def row_load(src, g, k):
        return pltpu.make_async_copy(src.at[rows_of(g, span)], x_v, row_sem.at[k])

    tile = wg_v.shape[1] // (PARTS - 1)

    def tile_load(src, dst, g, part, k):
        col = columns(part, tile)
        return pltpu.make_async_copy(
            src.at[rows_of(g, span), col], dst.at[:, col], tile_sem.at[k, part]
        )

    row_load(x_in, 0, 0).start()

    def first_tiles(part):
        tile_load(slope_in, slope_v, 0, part, 0).start()
        tile_load(silu_in, silu_v, 0, part, 1).start()

    loop(PARTS - 1, first_tiles)
    chain.greet(plane.partners())
    wait_all(loads[:3])
    gain_one = attention_gain[depth : depth + 1, :]
    gain_two = feed_gain[below : below + 1, :]

    def out(k, g, src, dst, whole=True):
        at = rows_of(g, span)
        return pltpu.make_async_copy(src.at[at] if whole else src, dst.at[at], out_sem.at[k, g])

    def start(g):
        at = rows_of(g, span)
        fill(
            one.part,
            at,
            lambda col: back_product(q_low[at, :], wq_v[col, :])
            + back_product(k_low[at, :], wk_v[col, :])
            + back_product(v_low[at, :], wv_v[col, :])
            + back_product(l_low[at, :], gh[col, :]),
        )
        one.offer(g)

    loop(GROUPS, start)
    gain_v[...] = jnp.zeros_like(gain_v)
    feed_v[...] = jnp.zeros_like(feed_v)
    wait_all(loads[3:])
    row_load(x_in, 0, 0).wait()

    def local(at):
        return pl.ds(pl.multiple_of(lax.rem(at.start, span), STRIP), STRIP)

    def made_one(at, total):
        pulled, terms = back_norm(x_v[local(at), :], gain_one, total)
        gain_v[...] += fold(terms)
        value = grad_v[at, :] + pulled
        grad_v[at, :] = value
        return value.astype(BF)

    def between(g, part):
        at = rows_of(g, span)

        @pl.when(part == 0)
        def _():
            out(0, g, one.spread, first_o).start()

            @pl.when(g < GROUPS - 1)
            def _():
                copy = row_load(x_in, g + 1, 1)
                copy.start()
                copy.wait()

            @pl.when(g > 0)
            def _():
                out(1, g - 1, gate_v, gate_o, False).wait()
                out(2, g - 1, up_v, up_o, False).wait()

        @pl.when(part < PARTS - 1)
        def _():
            col = columns(part, tile)
            tile_load(slope_in, slope_v, g, part, 0).wait()
            tile_load(silu_in, silu_v, g, part, 1).wait()
            pulled = back_product(one.spread[at, :], wd_v[col, :])
            gate_v[:, col] = (pulled * slope_v[:, col].astype(F32)).astype(BF)
            up_v[:, col] = (pulled * silu_v[:, col].astype(F32)).astype(BF)

            @pl.when(g < GROUPS - 1)
            def _():
                tile_load(slope_in, slope_v, g + 1, part, 0).start()
                tile_load(silu_in, silu_v, g + 1, part, 1).start()

        @pl.when(part == PARTS - 1)
        def _():
            fill(
                two.part,
                at,
                lambda col: back_product(gate_v[...], wg_v[col, :])
                + back_product(up_v[...], wu_v[col, :]),
            )
            two.offer(g)
            out(1, g, gate_v, gate_o, False).start()
            out(2, g, up_v, up_o, False).start()

    def ahead(g):
        copy = row_load(middle_in, g, 2)
        copy.start()
        copy.wait()

    def made_two(at, total):
        pulled, terms = back_norm(x_v[local(at), :], gain_two, total)
        feed_v[...] += fold(terms)
        value = grad_v[at, :] + pulled
        grad_v[at, :] = value
        return value.astype(BF)

    def after(g):
        at = rows_of(g, span)

        @pl.when(chain.mid)
        def _():
            out(5, g, grad_v, grad_o).start()

        out(3, g, two.spread, low_o).start()

        @pl.when(g > 0)
        def _():
            out(4, g - 1, mixed_v, mixed_o, False).wait()

        mixed_v[...] = back_product(two.spread[at, :], wo_v[...])
        out(4, g, mixed_v, mixed_o, False).start()

    pace = 3

    def step(s):
        two_sums(s, one, two, made_one, between, ahead, made_two, after)
        begin = lax.div(s * pace, 2)
        stop = lax.div((s + 1) * pace, 2)
        lax.fori_loop(begin, stop, lambda i, carry: (scatter.tick(i), carry)[1], 0)

    loop(max(STEPS, (2 * scatter.steps + pace - 1) // pace), step)

    @pl.when(jnp.logical_not(chain.first_mid))
    def _():
        gain_v[...] = jnp.zeros_like(gain_v)
        feed_v[...] = jnp.zeros_like(feed_v)

    gain_out = pltpu.make_async_copy(gain_v, gain_o, out_sem.at[6, 0])
    feed_out = pltpu.make_async_copy(feed_v, feed_gain_o, out_sem.at[7, 0])
    gain_out.start()
    feed_out.start()
    one.close()
    two.close()
    scatter.close()

    def drain(g):
        out(0, g, one.spread, first_o).wait()
        out(3, g, two.spread, low_o).wait()

        @pl.when(chain.mid)
        def _():
            out(5, g, grad_v, grad_o).wait()

    loop(GROUPS, drain)
    out(1, GROUPS - 1, gate_v, gate_o, False).wait()
    out(2, GROUPS - 1, up_v, up_o, False).wait()
    out(4, GROUPS - 1, mixed_v, mixed_o, False).wait()
    gain_out.wait()
    feed_out.wait()


def last_kernel(
    size, plane_sizes, depth, rows, width,
    q_low, k_low, v_low, l_low, gh, smalls, x_in, grad_in, attention_gain, wq, wk, wv,
    two_in, gate_in, up_in, first_in, hidden_in, normed_in, low_in, mixed_in,
    grad_o, total_o,
    *rest,
):
    made, scratch = rest[:7], rest[7:]
    (wq_v, wk_v, wv_v, x_v, grad_v, gain_v, whole_v, parts_v, total_v, load_sem, out_sem) = scratch[:11]
    chain = Chain(size)
    one = Sum(chain, scratch[11:18], rows, width)
    plane = Plane(*plane_sizes)
    total = Total(plane, size, scratch[18:22], 8)
    share = width // plane.count
    units_wide, heads_wide, keys_wide = parts_v.shape[1], wq_v.shape[1], wk_v.shape[1]
    unit = min(256, keys_wide)
    parts_heads = parts_v.at[:, pl.ds(0, heads_wide)]
    scatter = Scatter(
        plane, scratch[22:],
        [
            (whole_v, parts_v, True, made[0], units_wide // unit, [(two_in, whole_v), (gate_in, parts_v)]),
            (whole_v, parts_v, True, made[1], units_wide // unit, [(up_in, parts_v)]),
            (whole_v, parts_v, False, made[2], units_wide // unit, [(first_in, whole_v), (hidden_in, parts_v)]),
            (whole_v, q_low, True, made[3], heads_wide // unit, [(normed_in, whole_v)]),
            (whole_v, k_low, True, made[4], keys_wide // unit, []),
            (whole_v, v_low, True, made[5], keys_wide // unit, []),
            (whole_v, parts_v, False, made[6], heads_wide // unit, [(low_in, whole_v), (mixed_in, parts_heads)]),
        ],
        share, unit,
    )
    span = one.block * GROUP
    loads = load_all(
        [(wq.at[depth], wq_v), (wk.at[depth], wk_v), (wv.at[depth], wv_v), (x_in, x_v),
         (grad_in, grad_v)],
        load_sem,
    )
    chain.greet([*plane.partners(), *total.across])
    wait_all(loads[:3])
    gain_one = attention_gain[depth : depth + 1, :]

    def out(g):
        at = rows_of(g, span)
        return pltpu.make_async_copy(one.spread.at[at], grad_o.at[at], out_sem.at[g])

    def start(g):
        at = rows_of(g, span)
        fill(
            one.part,
            at,
            lambda col: back_product(q_low[at, :], wq_v[col, :])
            + back_product(k_low[at, :], wk_v[col, :])
            + back_product(v_low[at, :], wv_v[col, :])
            + back_product(l_low[at, :], gh[col, :]),
        )
        one.offer(g)

    loop(GROUPS, start)
    gain_v[...] = jnp.zeros_like(gain_v)
    wait_all(loads[3:])

    def made_one(at, total_sum):
        pulled, terms = back_norm(x_v[at, :].astype(F32), gain_one, total_sum)
        gain_v[...] += fold(terms)
        return (grad_v[at, :] + pulled).astype(BF)

    first_total = 2 * BLOCKS + 1

    def step(i):
        scatter.tick(i)
        s = lax.div(i, 2)

        @pl.when(lax.rem(i, 2) == 1)
        def _():
            @pl.when(s < BLOCKS)
            def _():
                one.relay(s)

            @pl.when((s >= 1) & (s <= BLOCKS))
            def _():
                one.finish(s - 1, made_one)

                @pl.when(lax.rem(s, GROUP) == 0)
                def _():
                    group = lax.div(s, GROUP) - 1
                    one.receive(group)
                    out(group).start()

        @pl.when(i == first_total)
        def _():
            total.value[0] = smalls[...]

            @pl.when(chain.first_mid)
            def _():
                total.value[0, pl.ds(0, 1)] = jnp.sum(gain_v[...], axis=0, keepdims=True)

        for k in range(total.stages):

            @pl.when(i == first_total + 1 + k)
            def _(k=k):
                total.start(k)

    loop(max(scatter.steps, first_total + 2 + total.stages), step)
    total.finish(total_v)
    total_out = pltpu.make_async_copy(total_v, total_o, out_sem.at[GROUPS])
    total_out.start()
    one.close()
    scatter.close()
    loop(GROUPS, lambda g: out(g).wait())
    total_out.wait()


def call(kernel, collective_id, in_specs, outs, scratch, flops):
    return pl.pallas_call(
        kernel,
        out_shape=tuple(jax.ShapeDtypeStruct(shape, kind) for shape, kind in outs),
        in_specs=in_specs,
        out_specs=tuple(ANY for _ in outs),
        scratch_shapes=scratch,
        cost_estimate=pl.CostEstimate(flops=flops, bytes_accessed=40_000_000, transcendentals=0),
        compiler_params=pltpu.CompilerParams(
            collective_id=collective_id, has_side_effects=True, vmem_limit_bytes=VMEM_LIMIT
        ),
    )


def dma(*shape):
    return pltpu.SemaphoreType.DMA(shape)


def shards(
    size,
    stream,
    cotangent,
    prefixes,
    attention_gain,
    query_weight,
    key_weight,
    value_weight,
    gate_heads,
    query_gain,
    key_gain,
    output_weight,
    feed_gain,
    gate_weight,
    up_weight,
    down_weight,
):
    seq_count, row_count, width = stream.shape
    rows = seq_count * row_count
    span = rows // GROUPS
    dp_size = lax.axis_size("dp")
    plane_sizes = (dp_size, lax.axis_size("ctx"))
    plane_count = plane_sizes[0] * plane_sizes[1]
    heads_wide = query_weight.shape[2]
    keys_wide = key_weight.shape[2]
    units = gate_weight.shape[2]
    gates = gate_heads.shape[2]
    share = width // plane_count
    unit = min(256, keys_wide)
    halves = lax.axis_size("ctx")
    offset = lax.axis_index("ctx") * row_count
    query_pos = offset + jnp.arange(row_count, dtype=jnp.int32)
    key_pos = jnp.arange(row_count * halves, dtype=jnp.int32)
    cos_table, sin_table = rotary_tables(query_pos, HD)
    stream_flat = stream.reshape(rows, width)
    cot_flat = cotangent.reshape(rows, width)
    heads_padded = [
        jnp.pad(gate_heads[depth], ((0, 0), (0, LANES - gates))) for depth in range(LAYERS)
    ]
    sum_scratch = Sum.scratch(rows, width)

    def attention(depth, q_raw, k_raw, values, logits):
        q_raw = q_raw.reshape(seq_count, row_count, -1, HD)
        k_raw = k_raw.reshape(seq_count, row_count, -1, HD)
        values = values.reshape(seq_count, row_count, -1, HD)
        query_rot = rotated_norm(q_raw, query_gain[depth], cos_table, sin_table).astype(BF)
        key_rot = rotated_norm(k_raw, key_gain[depth], cos_table, sin_table).astype(BF)
        key_full = lax.all_gather(key_rot, "ctx", axis=1, tiled=True)
        value_full = lax.all_gather(values, "ctx", axis=1, tiled=True)
        key_heads = key_rot.shape[2]
        grouped = query_rot.reshape(seq_count, row_count, key_heads, -1, HD)
        attended, logsum = lax.map(
            partial(attend_forward, query_pos=query_pos, key_pos=key_pos),
            (grouped, key_full, value_full, prefixes),
        )
        attended = attended.reshape(rows, -1, HD)
        mixed = gated(attended, logits).reshape(rows, -1).astype(BF)
        return mixed, (q_raw, k_raw, logits, grouped, key_full, value_full, logsum, attended)

    def attention_back(depth, mixed_grad, saved):
        q_raw, k_raw, logits, grouped, key_full, value_full, logsum, attended = saved
        unused, gate_pull = jax.vjp(gated, attended, logits)
        attended_grad, logits_grad = gate_pull(mixed_grad.reshape(attended.shape))
        attended_low = attended_grad.astype(BF).reshape(grouped.shape)
        logits_low = logits_grad.astype(BF)
        query_grad, key_grad, value_grad = lax.map(
            partial(attend_backward, query_pos=query_pos, key_pos=key_pos),
            (grouped, key_full, value_full, prefixes, logsum, attended_low),
        )
        key_grad = lax.psum_scatter(
            key_grad.astype(BF), "ctx", scatter_dimension=1, tiled=True
        ).astype(F32)
        value_grad = lax.psum_scatter(
            value_grad.astype(BF), "ctx", scatter_dimension=1, tiled=True
        ).astype(F32)
        rotation = partial(rotated_norm, cos_table=cos_table, sin_table=sin_table)
        unused, query_pull = jax.vjp(rotation, q_raw, query_gain[depth])
        query_raw_grad, grad_query_gain = query_pull(query_grad.reshape(q_raw.shape))
        unused, key_pull = jax.vjp(rotation, k_raw, key_gain[depth])
        key_raw_grad, grad_key_gain = key_pull(key_grad)
        query_low = query_raw_grad.astype(BF).reshape(rows, -1)
        key_low = key_raw_grad.astype(BF).reshape(rows, -1)
        value_low = value_grad.astype(BF).reshape(rows, -1)
        return query_low, key_low, value_low, logits_low, grad_query_gain, grad_key_gain

    made_shapes = [
        ((share, units), BF), ((share, units), BF), ((units, share), BF),
        ((share, heads_wide), BF), ((share, keys_wide), BF), ((share, keys_wide), BF),
        ((heads_wide, share), BF),
    ]
    scatter_scratch = Scatter.scratch(plane_count, share, unit)

    def padded(l):
        return jnp.pad(l, ((0, 0), (0, LANES - gates)))

    normed_zero = rms_scale(stream_flat.astype(F32), attention_gain[0]).astype(BF)
    mixed_zero, saved_zero = attention(
        0,
        matmul(normed_zero, query_weight[0]),
        matmul(normed_zero, key_weight[0]),
        matmul(normed_zero, value_weight[0]).astype(BF),
        matmul(normed_zero, gate_heads[0]),
    )
    middle_zero, two_zero, slope, silu, hidden_zero, x_one, normed_one, q_raw, k_raw, values, logits = call(
        partial(forward_kernel, size, 0, rows, width),
        0,
        [WHOLE, ANY, ANY, WHOLE, ANY, ANY, ANY, WHOLE, ANY, ANY, ANY, WHOLE],
        [
            ((rows, width), F32), ((rows, width), BF), ((rows, units), BF), ((rows, units), BF),
            ((rows, units), BF), ((rows, width), F32), ((rows, width), BF),
            ((rows, heads_wide), F32), ((rows, keys_wide), F32), ((rows, keys_wide), BF),
            ((rows, LANES), F32),
        ],
        [
            pltpu.VMEM((heads_wide, width), BF), pltpu.VMEM((width, units), BF),
            pltpu.VMEM((width, units), BF), pltpu.VMEM((units, width), BF),
            pltpu.VMEM((width, heads_wide), BF), pltpu.VMEM((width, keys_wide), BF),
            pltpu.VMEM((width, keys_wide), BF), pltpu.VMEM((rows, width), BF),
            pltpu.VMEM((rows, width), F32), pltpu.VMEM((rows, units), BF),
            pltpu.VMEM((rows, units), BF), pltpu.VMEM((rows, units), BF),
            pltpu.VMEM((rows, heads_wide), F32), pltpu.VMEM((rows, keys_wide), F32),
            pltpu.VMEM((rows, keys_wide), BF), pltpu.VMEM((rows, LANES), F32),
            dma(8), dma(11, GROUPS),
        ]
        + sum_scratch + sum_scratch,
        13_000_000_000,
    )(
        mixed_zero, stream_flat, output_weight, feed_gain, gate_weight, up_weight, down_weight,
        attention_gain, query_weight, key_weight, value_weight, heads_padded[1],
    )
    mixed_one, saved_one = attention(1, q_raw, k_raw, values, logits[:, :gates])
    two_one, hidden_one, down_part, gate_low, up_low, grad, low, mixed_grad, feed_one = call(
        partial(turn_kernel, size, 1, rows, width),
        1,
        [WHOLE, ANY, ANY, ANY, WHOLE, ANY, ANY, ANY],
        [
            ((rows, width), BF), ((rows, units), BF), ((rows, width), BF), ((rows, units), BF),
            ((rows, units), BF), ((rows, width), F32), ((rows, width), BF),
            ((rows, heads_wide), F32), ((8, width), F32),
        ],
        [
            pltpu.VMEM((heads_wide, width), BF), pltpu.VMEM((width, units), BF),
            pltpu.VMEM((width, units), BF), pltpu.VMEM((units, width), BF),
            pltpu.VMEM((rows, width), F32), pltpu.VMEM((rows, width), BF),
            pltpu.VMEM((rows, units), BF), pltpu.VMEM((rows, units), BF),
            pltpu.VMEM((rows, units), BF), pltpu.VMEM((rows, heads_wide), F32),
            pltpu.VMEM((rows, width), BF), pltpu.VMEM((8, width), F32),
            dma(6), dma(9, GROUPS),
        ]
        + sum_scratch + sum_scratch,
        24_000_000_000,
    )(mixed_one, x_one, cot_flat, output_weight, feed_gain, gate_weight, up_weight, down_weight)
    result = lax.psum(down_part, "tensor")
    q_low, k_low, v_low, l_low, q_gain_one, k_gain_one = attention_back(1, mixed_grad, saved_one)
    heads_one = weight_product(l_low, normed_one)
    gate_low, up_low, first_low, grad, low, mixed_grad, gain_one, feed_zero, *made_one = call(
        partial(back_kernel, size, plane_sizes, 1, rows, width),
        2,
        [WHOLE] * 5 + [ANY, ANY, WHOLE] + [ANY] * 9 + [WHOLE] + [ANY] * 9,
        [
            ((rows, units), BF), ((rows, units), BF), ((rows, width), BF), ((rows, width), F32),
            ((rows, width), BF), ((rows, heads_wide), F32), ((8, width), F32), ((8, width), F32),
            *made_shapes,
        ],
        [
            pltpu.VMEM((width, heads_wide), BF), pltpu.VMEM((width, keys_wide), BF),
            pltpu.VMEM((width, keys_wide), BF), pltpu.VMEM((units, width), BF),
            pltpu.VMEM((width, units), BF), pltpu.VMEM((width, units), BF),
            pltpu.VMEM((heads_wide, width), BF), pltpu.VMEM((span, width), F32),
            pltpu.VMEM((rows, width), F32), pltpu.VMEM((span, units), BF),
            pltpu.VMEM((span, units), BF), pltpu.VMEM((span, units), BF),
            pltpu.VMEM((span, units), BF), pltpu.VMEM((span, heads_wide), F32),
            pltpu.VMEM((8, width), F32), pltpu.VMEM((8, width), F32),
            pltpu.VMEM((rows, width), BF), pltpu.VMEM((rows, units), BF),
            dma(8), dma(3), dma(2, PARTS - 1), dma(8, GROUPS),
        ]
        + sum_scratch + sum_scratch + scatter_scratch,
        26_000_000_000,
    )(
        q_low, k_low, v_low, padded(l_low), heads_padded[1], x_one, grad, attention_gain,
        query_weight, key_weight, value_weight, down_weight, gate_weight, up_weight, slope, silu,
        middle_zero, feed_gain, output_weight,
        two_one, gate_low, up_low, cot_flat, hidden_one, normed_one, low, mixed_one,
    )
    q_low, k_low, v_low, l_low, q_gain_zero, k_gain_zero = attention_back(0, mixed_grad, saved_zero)
    heads_zero = weight_product(l_low, normed_zero)
    head_gains = jnp.concatenate([q_gain_zero, k_gain_zero, q_gain_one, k_gain_one])
    below_rows = -(-LAYERS * gates // 8) * 8
    smalls = jnp.concatenate(
        [
            jnp.zeros((1, width), F32),
            gain_one.sum(0, keepdims=True),
            feed_zero.sum(0, keepdims=True),
            feed_one.sum(0, keepdims=True),
            jnp.pad(head_gains, (0, width - head_gains.shape[0]))[None],
            jnp.zeros((3, width), F32),
            heads_zero,
            heads_one,
            jnp.zeros((below_rows - LAYERS * gates, width), F32),
        ]
    )
    stages = plane_count.bit_length() - 1 + size.bit_length() - 1
    stream_low, totals, *made_zero = call(
        partial(last_kernel, size, plane_sizes, 0, rows, width),
        3,
        [WHOLE] * 6 + [ANY, ANY, WHOLE] + [ANY] * 11,
        [((rows, width), BF), ((8 + below_rows, width), F32), *made_shapes],
        [
            pltpu.VMEM((width, heads_wide), BF), pltpu.VMEM((width, keys_wide), BF),
            pltpu.VMEM((width, keys_wide), BF), pltpu.VMEM((rows, width), BF),
            pltpu.VMEM((rows, width), F32), pltpu.VMEM((8, width), F32),
            pltpu.VMEM((rows, width), BF), pltpu.VMEM((rows, units), BF),
            pltpu.VMEM((8 + below_rows, width), F32), dma(5), dma(GROUPS + 1),
        ]
        + sum_scratch + Total.scratch(8 + below_rows, width, stages) + scatter_scratch,
        16_000_000_000,
    )(
        q_low, k_low, v_low, padded(l_low), heads_padded[0], smalls, stream_flat, grad,
        attention_gain, query_weight, key_weight, value_weight,
        two_zero, gate_low, up_low, first_low, hidden_zero, normed_zero, low, mixed_zero,
    )
    here = lax.axis_index("dp") * halves + lax.axis_index("ctx")

    def own(array, wide_share):
        return lax.dynamic_slice_in_dim(array, here * wide_share, wide_share, array.ndim - 1)

    gains = own(totals[:4], share)
    head_gains = own(totals[4, : 4 * HD].reshape(2, 2, HD), HD // plane_count)
    heads = own(totals[8 : 8 + LAYERS * gates].reshape(LAYERS, gates, width), share)
    weights = [
        jnp.stack([made_zero[entry], made_one[entry]]).astype(F32) for entry in range(7)
    ]
    return (
        result.reshape(seq_count, row_count, width),
        stream_low.astype(F32).reshape(seq_count, row_count, width),
        gains[0:2],
        weights[3],
        weights[4],
        weights[5],
        heads.transpose(0, 2, 1),
        head_gains[:, 0],
        head_gains[:, 1],
        weights[6],
        gains[2:4],
        weights[0],
        weights[1],
        weights[2],
    )


def solution(mesh):
    return jax.shard_map(
        partial(shards, mesh.shape["tensor"]),
        mesh=mesh,
        in_specs=(
            P("dp", "ctx", None),
            P("dp", "ctx", None),
            P("dp"),
            P(),
            P(None, None, "tensor"),
            P(None, None, "tensor"),
            P(None, None, "tensor"),
            P(None, None, "tensor"),
            P(),
            P(),
            P(None, "tensor", None),
            P(),
            P(None, None, "tensor"),
            P(None, None, "tensor"),
            P(None, "tensor", None),
        ),
        out_specs=(
            P("dp", "ctx", None),
            P("dp", "ctx", None),
            P(None, ("dp", "ctx")),
            P(None, ("dp", "ctx"), "tensor"),
            P(None, ("dp", "ctx"), "tensor"),
            P(None, ("dp", "ctx"), "tensor"),
            P(None, ("dp", "ctx"), "tensor"),
            P(None, ("dp", "ctx")),
            P(None, ("dp", "ctx")),
            P(None, "tensor", ("dp", "ctx")),
            P(None, ("dp", "ctx")),
            P(None, ("dp", "ctx"), "tensor"),
            P(None, ("dp", "ctx"), "tensor"),
            P(None, "tensor", ("dp", "ctx")),
        ),
        check_vma=False,
    )
```

```python
from functools import partial

import jax
import jax.numpy as jnp
from jax import lax
from jax.experimental import pallas as pl
from jax.experimental.pallas import tpu as pltpu
from jax.sharding import PartitionSpec as P

HD = 128
LAYERS = 2
LANES = 128

epsilon = 1e-06
theta = 1000000.0
masked = -1000000000.0

BF = jnp.bfloat16
F32 = jnp.float32
ANY = pl.BlockSpec(memory_space=pl.ANY)
WHOLE = pl.BlockSpec(memory_space=pltpu.VMEM)
MESH = pl.DeviceIdType.MESH

BLOCKS = 8
PIECES = 2
GROUP = 4
STRIP = 16
VMEM_LIMIT = 63 * 1024 * 1024


def rms_scale(values, gain):
    return values * lax.rsqrt(jnp.mean(values * values, axis=-1, keepdims=True) + epsilon) * gain


def rotary_tables(positions, width):
    counter = jnp.arange(width // 2, dtype=jnp.float32)
    frequency = theta ** (-2.0 * counter / width)
    angles = positions.astype(jnp.float32)[:, None] * frequency[None, :]
    return (jnp.cos(angles), jnp.sin(angles))


def matmul(left, right):
    return jnp.dot(left, right, preferred_element_type=F32)


def weight_product(left, right):
    return lax.dot_general(left, right, (((0,), (0,)), ((), ())), preferred_element_type=F32)


def back_product(gradient, weight):
    return lax.dot_general(gradient, weight, (((1,), (1,)), ((), ())), preferred_element_type=F32)


def loop(count, body):
    def step(i, carry):
        body(i)
        return carry

    lax.fori_loop(0, count, step, 0)


def rows_of(r, block):
    return pl.ds(pl.multiple_of(r * block, block), block)


def columns(j, width):
    return pl.ds(pl.multiple_of(j * width, width), width)


def greet(targets, extra, has_extra):
    barrier = pltpu.get_barrier_semaphore()
    for target in targets:
        pl.semaphore_signal(barrier, inc=1, device_id=target, device_id_type=MESH)

    @pl.when(has_extra)
    def _():
        pl.semaphore_signal(barrier, inc=1, device_id=extra, device_id_type=MESH)
        pl.semaphore_wait(barrier, len(targets) + 1)

    @pl.when(jnp.logical_not(has_extra))
    def _():
        pl.semaphore_wait(barrier, len(targets))


class Chain:
    def __init__(self, size):
        self.size = size
        self.spot = lax.axis_index("tensor")
        half = size // 2
        on_left = self.spot < half
        self.end = (self.spot == 0) | (self.spot == size - 1)
        self.inner = jnp.logical_not(self.end)
        self.mid = (self.spot == half - 1) | (self.spot == half)
        self.outer = jnp.logical_not(self.mid)
        self.first_mid = self.spot == half - 1
        self.inward = {"tensor": jnp.where(on_left, self.spot + 1, self.spot - 1)}
        self.outward = {"tensor": jnp.where(on_left, self.spot - 1, self.spot + 1)}

    def greet(self, others=()):
        greet([self.inward, *others], self.outward, self.inner)


class Sum:
    def __init__(self, chain, refs, landed, rows, width):
        self.chain = chain
        self.part, self.spread, self.s_in, self.r_in, self.s_out, self.r_out, self.r_cross = refs
        self.landed, self.cross = landed
        self.block = rows // BLOCKS
        self.piece = width // PIECES

    @staticmethod
    def scratch(rows, width):
        return [
            pltpu.VMEM((rows, width), BF),
            pltpu.VMEM((rows, width), BF),
            pltpu.SemaphoreType.DMA((BLOCKS, PIECES)),
            pltpu.SemaphoreType.DMA((BLOCKS, PIECES)),
            pltpu.SemaphoreType.DMA((BLOCKS,)),
            pltpu.SemaphoreType.DMA((BLOCKS,)),
            pltpu.SemaphoreType.DMA((BLOCKS, PIECES)),
        ]

    def hop(self, r, p, across):
        where = (rows_of(r, self.block), columns(p, self.piece))
        return pltpu.make_async_remote_copy(
            src_ref=self.part.at[where],
            dst_ref=self.landed.at[(self.cross if across else 0,) + where],
            send_sem=self.s_in.at[r, p],
            recv_sem=(self.r_cross if across else self.r_in).at[r, p],
            device_id=self.chain.inward,
            device_id_type=MESH,
        )

    def out_hop(self, r):
        at = rows_of(r, self.block)
        return pltpu.make_async_remote_copy(
            src_ref=self.spread.at[at],
            dst_ref=self.spread.at[at],
            send_sem=self.s_out.at[r],
            recv_sem=self.r_out.at[r],
            device_id=self.chain.outward,
            device_id_type=MESH,
        )

    def offer(self, g):
        @pl.when(self.chain.end)
        def _():
            def one(k):
                for p in range(PIECES):
                    self.hop(g * GROUP + k, p, False).start()

            loop(GROUP, one)

    def relay(self, r):
        @pl.when(self.chain.inner)
        def _():
            for p in range(PIECES):
                self.hop(r, p, False).wait_recv()
                col = columns(p, self.piece)

                def strip(i, col=col):
                    at = pl.ds(pl.multiple_of(r * self.block + i * STRIP, STRIP), STRIP)
                    total = self.part[at, col].astype(F32) + self.landed[0, at, col].astype(F32)
                    self.part[at, col] = total.astype(BF)

                loop(self.block // STRIP, strip)

                @pl.when(self.chain.mid)
                def _(p=p):
                    self.hop(r, p, True).start()

                @pl.when(self.chain.outer)
                def _(p=p):
                    self.hop(r, p, False).start()

    def finish(self, r, make):
        @pl.when(self.chain.mid)
        def _():
            for p in range(PIECES):
                self.hop(r, p, True).wait_recv()

            def strip(i):
                at = pl.ds(pl.multiple_of(r * self.block + i * STRIP, STRIP), STRIP)
                total = self.part[at, :].astype(F32) + self.landed[self.cross, at, :].astype(F32)
                self.spread[at, :] = make(at, total)

            loop(self.block // STRIP, strip)
            self.out_hop(r).start()

    def receive(self, g):
        @pl.when(self.chain.outer)
        def _():
            def one(k):
                self.out_hop(g * GROUP + k).wait_recv()

                @pl.when(self.chain.inner)
                def _():
                    self.out_hop(g * GROUP + k).start()

            loop(GROUP, one)

    def close(self):
        def block(r):
            for p in range(PIECES):
                self.hop(r, p, False).wait_send()

            @pl.when(self.chain.inner)
            def _():
                self.out_hop(r).wait_send()

        loop(BLOCKS, block)


PARTS = GROUP
GROUPS = BLOCKS // GROUP
STEPS = 2 * BLOCKS + 1


def two_sums(s, first, second, made_one, between, ahead, made_two, after):
    @pl.when(s < BLOCKS)
    def _():
        first.relay(s)

    @pl.when((s >= 1) & (s <= BLOCKS))
    def _():
        first.finish(s - 1, made_one)

    @pl.when((s >= GROUP) & (s < BLOCKS + GROUP))
    def _():
        part = lax.rem(s - GROUP, PARTS)
        group = lax.div(s - GROUP, PARTS)

        @pl.when(part == 0)
        def _():
            first.receive(group)

        between(group, part)

    @pl.when((s >= BLOCKS) & (s < 2 * BLOCKS))
    def _():
        second.relay(s - BLOCKS)

    @pl.when((s >= BLOCKS + 1) & (s < STEPS))
    def _():
        @pl.when(lax.rem(s - BLOCKS - 1, GROUP) == 0)
        def _():
            ahead(lax.div(s - BLOCKS - 1, GROUP))

        second.finish(s - BLOCKS - 1, made_two)

        @pl.when(lax.rem(s - BLOCKS, GROUP) == 0)
        def _():
            group = lax.div(s - BLOCKS, GROUP) - 1
            second.receive(group)
            after(group)


def back_norm(value, gain, grad):
    spread = lax.rsqrt(jnp.mean(value * value, axis=-1, keepdims=True) + epsilon)
    scaled = grad * gain
    pulled = jnp.mean(scaled * value, axis=-1, keepdims=True)
    terms = grad * value * spread
    return spread * scaled - value * (spread * spread * spread * pulled), terms


def fold(terms):
    folded = terms[:8]
    for k in range(8, terms.shape[0], 8):
        folded = folded + terms[k : k + 8]
    return folded


def load_all(pairs, sems):
    copies = [pltpu.make_async_copy(src, dst, sems.at[k]) for k, (src, dst) in enumerate(pairs)]
    for copy in copies:
        copy.start()
    return copies


def wait_all(copies):
    for copy in copies:
        copy.wait()


def wide(width):
    return 512 if width % 512 == 0 else 256


def fill(target, at, make):
    width = target.shape[1]
    tile = wide(width)

    def one(p):
        col = columns(p, tile)
        target[at, col] = make(col).astype(target.dtype)

    loop(width // tile, one)


def flip(value, bit):
    return value + bit * (1 - 2 * lax.rem(lax.div(value, bit), 2))


class Plane:
    def __init__(self, dp_size, ctx_size):
        self.count = dp_size * ctx_size
        self.ctx_size = ctx_size
        self.me = lax.axis_index("dp") * ctx_size + lax.axis_index("ctx")
        bits = [1 << k for k in range(self.count.bit_length() - 1)]
        near = [bit for bit in bits if bit >= ctx_size][:1]
        rest = [bit for bit in bits if bit not in near]
        self.bits = bits
        self.orders = (near + rest, near + rest[1:] + rest[:1])

    def partner(self, bit):
        other = flip(self.me, bit)
        return {"dp": lax.div(other, self.ctx_size), "ctx": lax.rem(other, self.ctx_size)}

    def partners(self):
        return [self.partner(bit) for bit in self.bits]


class Scatter:
    SLOTS = (2, 4, 4, 4)
    KEPT = (2, 3, 3, 3)
    RESULTS = 2
    LAGS = (0, 1, 4, 7, 10, 13)

    def __init__(self, plane, refs, groups, share, tile):
        self.plane = plane
        self.groups = groups
        self.share, self.tile = share, tile
        self.stages = len(plane.bits)
        self.units = sum(group[4] for group in groups)
        self.refs = [refs[6 * k : 6 * k + 6] for k in range(self.stages)]
        self.made, self.out_sem, self.load_sem = refs[6 * self.stages :]
        self.steps = self.units + self.LAGS[self.stages]

    @classmethod
    def scratch(cls, count, share, tile):
        found = []
        blocks = count // 2
        for k in range(count.bit_length() - 1):
            slots = cls.SLOTS[k]
            found += [
                pltpu.VMEM((depth, blocks, share, tile), BF) for depth in (slots, cls.KEPT[k], slots)
            ]
            found += [
                pltpu.SemaphoreType.DMA((slots,)),
                pltpu.SemaphoreType.DMA((slots,)),
                pltpu.SemaphoreType.REGULAR((slots,)),
            ]
            blocks //= 2
        return found + [
            pltpu.VMEM((cls.RESULTS, share, tile), BF),
            pltpu.SemaphoreType.DMA((cls.RESULTS,)),
            pltpu.SemaphoreType.DMA((2,)),
        ]

    def partner(self, stage, u):
        odd = lax.rem(u, 2) == 1
        even_one, odd_one = (self.plane.partner(order[stage]) for order in self.plane.orders)
        return {axis: jnp.where(odd, odd_one[axis], even_one[axis]) for axis in even_one}

    def copy(self, stage, u):
        send, unused, land, s_sem, r_sem, unused_credit = self.refs[stage]
        slot = lax.rem(u, self.SLOTS[stage])
        return pltpu.make_async_remote_copy(
            src_ref=send.at[slot],
            dst_ref=land.at[slot],
            send_sem=s_sem.at[slot],
            recv_sem=r_sem.at[slot],
            device_id=self.partner(stage, u),
            device_id_type=MESH,
        )

    def ready(self, stage, u):
        @pl.when(u >= self.SLOTS[stage])
        def _():
            self.copy(stage, u - self.SLOTS[stage]).wait_send()

    def push(self, stage, u):
        @pl.when(u >= self.SLOTS[stage])
        def _():
            pl.semaphore_wait(self.refs[stage][5].at[lax.rem(u, self.SLOTS[stage])], 1)

        self.copy(stage, u).start()

    def product(self, u):
        send, keep = self.refs[0][:2]
        slot, spot = lax.rem(u, self.SLOTS[0]), lax.rem(u, self.KEPT[0])
        odd = lax.rem(u, 2)
        orders = self.plane.orders
        blocks = self.plane.count // 2
        first = 0
        for whole, parts, by_rows, unused, count, loads in self.groups:

            @pl.when((u >= first) & (u < first + count))
            def _(whole=whole, parts=parts, by_rows=by_rows, first=first, loads=loads):
                if loads:

                    @pl.when(u == first)
                    def _():
                        wait_all(load_all(loads, self.load_sem))

                col = columns(u - first, self.tile)

                def one(i):
                    far = lax.rem(i, 2)
                    j = lax.div(i, 2)
                    owner = flip(self.plane.me, orders[0][0]) * far + self.plane.me * (1 - far)
                    rest = j
                    for bits in reversed(tuple(zip(*orders))[1:]):
                        low = lax.rem(rest, 2)
                        rest = lax.div(rest, 2)
                        turned = flip(owner, bits[0]) * (1 - odd) + flip(owner, bits[1]) * odd
                        owner = turned * low + owner * (1 - low)
                    at = columns(owner, self.share)
                    if by_rows:
                        made = weight_product(whole[:, at], parts[:, col])
                    else:
                        made = weight_product(parts[:, col], whole[:, at])
                    made = made.astype(BF)

                    @pl.when(far == 1)
                    def _():
                        send[slot, j] = made

                    @pl.when(far == 0)
                    def _():
                        keep[spot, j] = made

                loop(2 * blocks, one)

            first += count

    def merge(self, stage, u):
        unused, keep, land = self.refs[stage][:3]
        slots = self.SLOTS[stage]
        slot, spot = lax.rem(u, slots), lax.rem(u, self.KEPT[stage])
        self.copy(stage, u).wait_recv()
        half = (self.plane.count // 2) >> (stage + 1)
        last = stage == self.stages - 1
        if not last:
            self.ready(stage + 1, u)
            send_on, keep_on = self.refs[stage + 1][:2]
            slot_on = lax.rem(u, self.SLOTS[stage + 1])
            spot_on = lax.rem(u, self.KEPT[stage + 1])

            def one(j):
                far = keep[spot, half + j].astype(F32) + land[slot, half + j].astype(F32)
                send_on[slot_on, j] = far.astype(BF)
                near = keep[spot, j].astype(F32) + land[slot, j].astype(F32)
                keep_on[spot_on, j] = near.astype(BF)

            loop(half, one)
            self.push(stage + 1, u)
        else:
            place = lax.rem(u, self.RESULTS)

            @pl.when(u >= self.RESULTS)
            def _():
                self.results(u - self.RESULTS, lambda copy: copy.wait())

            total = keep[spot, 0].astype(F32) + land[slot, 0].astype(F32)
            self.made[place] = total.astype(BF)
            self.results(u, lambda copy: copy.start())

        @pl.when(u + slots < self.units)
        def _():
            pl.semaphore_signal(
                self.refs[stage][5].at[slot],
                inc=1,
                device_id=self.partner(stage, u),
                device_id_type=MESH,
            )

    def results(self, u, act):
        place = lax.rem(u, self.RESULTS)
        first = 0
        for unused, unused_parts, by_rows, out, count, unused_loads in self.groups:

            @pl.when((u >= first) & (u < first + count))
            def _(by_rows=by_rows, out=out, first=first):
                if by_rows:
                    at = (slice(None), columns(u - first, self.tile))
                else:
                    at = (rows_of(u - first, self.tile), slice(None))
                act(pltpu.make_async_copy(self.made.at[place], out.at[at], self.out_sem.at[place]))

            first += count

    def tick(self, i):
        @pl.when(i < self.units)
        def _():
            self.ready(0, i)
            self.product(i)
            self.push(0, i)

        for stage in reversed(range(self.stages)):
            u = i - self.LAGS[stage + 1]

            @pl.when((u >= 0) & (u < self.units))
            def _(stage=stage, u=u):
                self.merge(stage, u)

    def close(self):
        for stage in range(self.stages):
            for k in range(max(0, self.units - self.SLOTS[stage]), self.units):
                self.copy(stage, jnp.int32(k)).wait_send()
        for k in range(max(0, self.units - self.RESULTS), self.units):
            self.results(jnp.int32(k), lambda copy: copy.wait())


class Total:
    def __init__(self, plane, size, refs, own):
        self.plane, self.own = plane, own
        self.value, self.land, self.s_sem, self.r_sem = refs
        spot = lax.axis_index("tensor")
        bits = [1 << k for k in range(size.bit_length() - 1)]
        self.targets = [plane.partner(bit) for bit in plane.bits]
        self.across = [{"tensor": flip(spot, bit)} for bit in bits]
        self.stages = len(self.targets) + len(bits)

    @staticmethod
    def scratch(rows, width, stages):
        return [
            pltpu.VMEM((stages, rows, width), F32),
            pltpu.VMEM((stages, rows, width), F32),
            pltpu.SemaphoreType.DMA((stages,)),
            pltpu.SemaphoreType.DMA((stages,)),
        ]

    def copy(self, k):
        count = len(self.targets)
        rows = slice(None) if k < count else pl.ds(0, self.own)
        return pltpu.make_async_remote_copy(
            src_ref=self.value.at[k, rows],
            dst_ref=self.land.at[k, rows],
            send_sem=self.s_sem.at[k],
            recv_sem=self.r_sem.at[k],
            device_id=(self.targets + self.across)[k],
            device_id_type=MESH,
        )

    def start(self, k):
        if k > 0:
            self.copy(k - 1).wait_recv()
            rows = slice(None) if k - 1 < len(self.targets) else pl.ds(0, self.own)
            if k - 1 >= len(self.targets):
                self.value[k] = self.value[k - 1]
            self.value[k, rows] = self.value[k - 1, rows] + self.land[k - 1, rows]
        self.copy(k).start()

    def finish(self, target):
        last = self.stages - 1
        self.copy(last).wait_recv()
        rows = pl.ds(0, self.own)
        target[...] = self.value[last]
        target[rows] = self.value[last, rows] + self.land[last, rows]
        for k in range(self.stages):
            self.copy(k).wait_send()


def turned(value):
    return pltpu.roll(value, HD // 2, 1)


def head_at(h):
    return pl.ds(h * HD, HD)


def head_norm(raw, gain, cos, sin):
    scaled = rms_scale(raw, gain)
    return scaled * cos + turned(scaled) * sin


def head_norm_back(raw, gain, cos, sin, grad):
    return back_norm(raw, gain, grad * cos - turned(grad) * sin)


def seen(rows, first_row, columns_wide, offset, prefix):
    query = first_row + lax.broadcasted_iota(jnp.int32, (rows, columns_wide), 0)
    key = lax.broadcasted_iota(jnp.int32, (rows, columns_wide), 1)
    return (key <= query) | (key + offset < prefix)


def attend(prefix, q_raw, k_raw, v, logits, query_gain, key_gain, cos, sin,
           mixed_o, q_o, keys_o, values_o, norm_o, attended_o, scratch, half):
    high, low, out, send_sem, land_sem = scratch
    rows = q_raw.shape[0]
    span = rows // GROUPS
    key_heads = k_raw.shape[1] // HD
    shared = q_raw.shape[1] // k_raw.shape[1]
    scale = HD ** (-0.5)

    def copy(j, which):
        ref = (keys_o, values_o)[which]
        return pltpu.make_async_remote_copy(
            src_ref=ref.at[0, j],
            dst_ref=ref.at[1, j],
            send_sem=send_sem.at[j, which],
            recv_sem=land_sem.at[j, which],
            device_id={"ctx": 1 - half},
            device_id_type=MESH,
        )

    for j in range(key_heads):

        def key_rows(g, j=j):
            at = rows_of(g, span)
            made = head_norm(k_raw[at, head_at(j)], key_gain, cos[at, :], sin[at, :])
            keys_o[0, j, at, :] = made.astype(BF)
            values_o[0, j, at, :] = v[at, head_at(j)]

        loop(GROUPS, key_rows)

        @pl.when(half == 0)
        def _(j=j):
            copy(j, 0).start()
            copy(j, 1).start()

    def own(g):
        at = rows_of(g, span)
        mask = seen(span, g * span, rows, half * rows, prefix)
        for h in range(key_heads * shared):
            j = h // shared
            query = head_norm(q_raw[at, head_at(h)], query_gain, cos[at, :], sin[at, :]).astype(BF)
            q_o[at, head_at(h)] = query
            scores = jnp.where(mask, back_product(query, keys_o[0, j]) * scale, masked)
            top = jnp.max(scores, axis=1, keepdims=True)
            weights = jnp.exp(scores - top)
            high[h, at, :] = top
            low[h, at, :] = jnp.sum(weights, axis=1, keepdims=True)
            out[at, head_at(h)] = matmul(weights.astype(BF), values_o[0, j])

    loop(GROUPS, own)

    @pl.when(half == 1)
    def _():
        for h in range(key_heads * shared):
            j = h // shared
            if h % shared == 0:
                copy(j, 0).wait_recv()
                copy(j, 1).wait_recv()

            def other(g, h=h, j=j):
                at = rows_of(g, span)
                scores = back_product(q_o[at, head_at(h)], keys_o[1, j]) * scale
                before = high[h, at, :]
                top = jnp.maximum(before, jnp.max(scores, axis=1, keepdims=True))
                weights = jnp.exp(scores - top)
                shrink = jnp.exp(before - top)
                high[h, at, :] = top
                low[h, at, :] = low[h, at, :] * shrink + jnp.sum(weights, axis=1, keepdims=True)
                out[at, head_at(h)] = out[at, head_at(h)] * shrink + matmul(
                    weights.astype(BF), values_o[1, j]
                )

            loop(GROUPS, other)

    def close(g):
        at = rows_of(g, span)
        open_gate = jax.nn.sigmoid(logits[at, :])
        for h in range(key_heads * shared):
            total = low[h, at, :]
            norm_o[h, at, :] = high[h, at, :] + jnp.log(total)
            attended = out[at, head_at(h)] * (1.0 / total)
            attended_o[at, head_at(h)] = attended
            mixed_o[at, head_at(h)] = (attended * open_gate[:, h : h + 1]).astype(BF)

    loop(GROUPS, close)

    @pl.when(half == 0)
    def _():
        for j in range(key_heads):
            copy(j, 0).wait_send()
            copy(j, 1).wait_send()


def attend_scratch(rows, heads_wide, keys_wide):
    return [
        pltpu.VMEM((heads_wide // HD, rows, 1), F32),
        pltpu.VMEM((heads_wide // HD, rows, 1), F32),
        pltpu.VMEM((rows, heads_wide), F32),
        pltpu.SemaphoreType.DMA((keys_wide // HD, 2)),
        pltpu.SemaphoreType.DMA((keys_wide // HD, 2)),
    ]


def greet_half(half):
    greet([{"ctx": 1 - half}], {"ctx": 1 - half}, half < 0)


def attend_kernel(
    depth, prefix, q_raw, k_raw, v, logits, query_gain, key_gain, cos, sin,
    mixed_o, q_o, keys_o, values_o, norm_o, attended_o, *scratch,
):
    half = lax.axis_index("ctx")
    greet_half(half)
    attend(prefix[0], q_raw, k_raw, v, logits, query_gain[depth : depth + 1, :],
           key_gain[depth : depth + 1, :], cos, sin,
           mixed_o, q_o, keys_o, values_o, norm_o, attended_o, scratch, half)


def first_kernel(
    depth, prefix, stream, gain, wq, wk, wv, gh, query_gain, key_gain, cos, sin,
    mixed_o, q_o, keys_o, values_o, norm_o, attended_o, normed_o, q_raw, k_raw, logits,
    v, wq_v, wk_v, wv_v, load_sem, *scratch,
):
    half = lax.axis_index("ctx")
    loads = load_all([(wk.at[depth], wk_v), (wv.at[depth], wv_v), (wq.at[depth], wq_v)], load_sem)
    greet_half(half)
    rows = stream.shape[0]
    span = rows // GROUPS

    def strip(i):
        at = rows_of(i, STRIP)
        value = stream[at, :].astype(F32)
        normed_o[at, :] = rms_scale(value, gain[depth : depth + 1, :]).astype(BF)

    loop(rows // STRIP, strip)
    wait_all(loads)

    def project(g):
        at = rows_of(g, span)
        k_raw[at, :] = matmul(normed_o[at, :], wk_v[...])
        v[at, :] = matmul(normed_o[at, :], wv_v[...]).astype(BF)
        q_raw[at, :] = matmul(normed_o[at, :], wq_v[...])
        logits[at, :] = matmul(normed_o[at, :], gh[depth])

    loop(GROUPS, project)
    attend(prefix[0], q_raw, k_raw, v, logits, query_gain[depth : depth + 1, :],
           key_gain[depth : depth + 1, :], cos, sin,
           mixed_o, q_o, keys_o, values_o, norm_o, attended_o, scratch, half)


def attend_back_kernel(
    depth, prefix, mixed_grad, logits, attended, q_rot, keys, values, norm, q_raw, k_raw,
    query_gain, key_gain, cos, sin, normed,
    q_o, k_o, v_o, l_o, heads_o, q_gain_o, k_gain_o,
    grad_low, inner, q_grad, k_grad, v_grad, given, landed, send_sem, land_sem,
):
    half = lax.axis_index("ctx")
    greet_half(half)
    rows = q_raw.shape[0]
    span = rows // GROUPS
    key_heads = k_raw.shape[1] // HD
    shared = q_raw.shape[1] // k_raw.shape[1]
    heads = key_heads * shared
    scale = HD ** (-0.5)
    query_gain_here = query_gain[depth : depth + 1, :]
    key_gain_here = key_gain[depth : depth + 1, :]

    def copy(j):
        return pltpu.make_async_remote_copy(
            src_ref=given.at[j],
            dst_ref=landed.at[j],
            send_sem=send_sem.at[j],
            recv_sem=land_sem.at[j],
            device_id={"ctx": 1 - half},
            device_id_type=MESH,
        )

    def gate_back(g):
        at = rows_of(g, span)
        open_gate = jax.nn.sigmoid(logits[at, :])
        lane = lax.broadcasted_iota(jnp.int32, (span, LANES), 1)
        pulled = jnp.zeros((span, LANES), F32)
        for h in range(heads):
            grad = mixed_grad[at, head_at(h)]
            here = attended[at, head_at(h)]
            low_grad = (grad * open_gate[:, h : h + 1]).astype(BF)
            grad_low[at, head_at(h)] = low_grad
            inner[h, at, :] = jnp.sum(low_grad.astype(F32) * here, axis=1, keepdims=True)
            pulled = jnp.where(lane == h, jnp.sum(grad * here, axis=1, keepdims=True), pulled)
        l_o[at, :] = (pulled * (open_gate * (1.0 - open_gate))).astype(BF)

    loop(GROUPS, gate_back)
    heads_o[...] = weight_product(l_o[...], normed[...])[: heads_o.shape[0], :]

    def back(j, side, mask_of, first):
        k_grad[j] = jnp.zeros((rows, HD), F32)
        v_grad[j] = jnp.zeros((rows, HD), F32)

        def block(g):
            at = rows_of(g, span)
            for h in range(j * shared, (j + 1) * shared):
                query = q_rot[at, head_at(h)]
                pulled = grad_low[at, head_at(h)]
                scores = back_product(query, keys[side, j]) * scale
                if mask_of is not None:
                    scores = jnp.where(mask_of(g), scores, masked)
                weights = jnp.exp(scores - norm[h, at, :])
                slope = back_product(pulled, values[side, j])
                score_low = (weights * (slope - inner[h, at, :])).astype(BF)
                moved = matmul(score_low, keys[side, j])
                if first:
                    q_grad[at, head_at(h)] = moved
                else:
                    q_grad[at, head_at(h)] += moved
                k_grad[j] += weight_product(score_low, query)
                v_grad[j] += weight_product(weights.astype(BF), pulled)

        loop(GROUPS, block)

    @pl.when(half == 1)
    def _():
        for j in range(key_heads):
            back(j, 1, None, True)
            given[j, 0] = (k_grad[j] * scale).astype(BF)
            given[j, 1] = v_grad[j].astype(BF)
            copy(j).start()

    @pl.when(half == 0)
    def _():
        q_grad[...] = jnp.zeros_like(q_grad)

    for j in range(key_heads):
        back(j, 0, lambda g: seen(span, g * span, rows, half * rows, prefix[0]), False)

    q_gain_o[...] = jnp.zeros_like(q_gain_o)
    k_gain_o[...] = jnp.zeros_like(k_gain_o)

    def query_rows(g):
        at = rows_of(g, span)
        for h in range(heads):
            pulled, terms = head_norm_back(
                q_raw[at, head_at(h)], query_gain_here, cos[at, :], sin[at, :],
                q_grad[at, head_at(h)] * scale,
            )
            q_o[at, head_at(h)] = pulled.astype(BF)
            q_gain_o[...] += jnp.sum(terms.reshape(span // 8, 8, HD), axis=0)

    loop(GROUPS, query_rows)

    for j in range(key_heads):

        @pl.when(half == 0)
        def _(j=j):
            copy(j).wait_recv()

        def key_rows(g, j=j):
            at = rows_of(g, span)
            k_total = k_grad[j, at, :] * scale
            v_total = v_grad[j, at, :]
            k_grad[j, at, :] = k_total
            v_o[at, head_at(j)] = v_total.astype(BF)

            @pl.when(half == 0)
            def _():
                k_grad[j, at, :] = k_total + landed[j, 0, at, :].astype(F32)
                v_o[at, head_at(j)] = (v_total + landed[j, 1, at, :].astype(F32)).astype(BF)

            pulled, terms = head_norm_back(
                k_raw[at, head_at(j)], key_gain_here, cos[at, :], sin[at, :], k_grad[j, at, :]
            )
            k_o[at, head_at(j)] = pulled.astype(BF)
            k_gain_o[...] += jnp.sum(terms.reshape(span // 8, 8, HD), axis=0)

        loop(GROUPS, key_rows)

    @pl.when(half == 1)
    def _():
        for j in range(key_heads):
            copy(j).wait_send()


def forward_kernel(
    size, depth, rows, width,
    mixed, stream, wo, feed_gain, wg, wu, wd, next_gain, wq, wk, wv, gh,
    middle_o, two_o, slope_o, silu_o, hidden_o, x_o, normed_o, q_o, k_o, v_o, logit_o,
    *scratch,
):
    (wo_v, wg_v, wu_v, wd_v, wq_v, wk_v, wv_v, x_v, middle_v, slope_v, silu_v, hidden_v, q_v, k_v,
     v_v, logit_v, load_sem, out_sem) = scratch[:18]
    chain = Chain(size)
    landed = scratch[18]
    one = Sum(chain, scratch[19:26], (landed, 1), rows, width)
    two = Sum(chain, scratch[26:33], (landed, 2), rows, width)
    span = one.block * GROUP
    loads = load_all(
        [(wo.at[depth], wo_v), (stream, x_v), (wg.at[depth], wg_v), (wu.at[depth], wu_v),
         (wd.at[depth], wd_v), (wq.at[depth + 1], wq_v), (wk.at[depth + 1], wk_v),
         (wv.at[depth + 1], wv_v)],
        load_sem,
    )
    chain.greet()
    tile = wg_v.shape[1] // (PARTS - 1)
    gain_one = feed_gain[depth : depth + 1, :]
    gain_two = next_gain[depth + 1 : depth + 2, :]

    def out(k, g, src, dst):
        at = rows_of(g, span)
        return pltpu.make_async_copy(src.at[at], dst.at[at], out_sem.at[k, g])

    loads[0].wait()

    def start(g):
        at = rows_of(g, span)
        fill(one.part, at, lambda col: matmul(mixed[at, :], wo_v[:, col]))
        one.offer(g)

    loop(GROUPS, start)
    wait_all(loads[1:5])

    def made_one(at, total):
        value = x_v[at, :].astype(F32) + total
        middle_v[at, :] = value
        return rms_scale(value, gain_one).astype(BF)

    def between(g, part):
        at = rows_of(g, span)

        @pl.when(part == 0)
        def _():
            out(1, g, one.spread, two_o).start()

            @pl.when(chain.mid)
            def _():
                out(0, g, middle_v, middle_o).start()

        @pl.when(part < PARTS - 1)
        def _():
            col = columns(part, tile)
            gate = matmul(one.spread[at, :], wg_v[:, col])
            up = matmul(one.spread[at, :], wu_v[:, col])
            sig = jax.nn.sigmoid(gate)
            act = gate * sig
            hidden_v[at, col] = (act * up).astype(BF)
            silu_v[at, col] = act.astype(BF)
            slope_v[at, col] = (up * (sig * (1.0 + gate * (1.0 - sig)))).astype(BF)

        @pl.when(part == PARTS - 1)
        def _():
            fill(two.part, at, lambda col: matmul(hidden_v[at, :], wd_v[:, col]))
            two.offer(g)
            out(2, g, slope_v, slope_o).start()
            out(3, g, silu_v, silu_o).start()
            out(4, g, hidden_v, hidden_o).start()

    def ahead(g):
        @pl.when(g == 0)
        def _():
            wait_all(loads[5:])

        @pl.when(chain.mid)
        def _():
            out(0, g, middle_v, middle_o).wait()

    def made_two(at, total):
        value = middle_v[at, :] + total
        middle_v[at, :] = value
        return rms_scale(value, gain_two).astype(BF)

    def after(g):
        at = rows_of(g, span)

        @pl.when(chain.mid)
        def _():
            out(5, g, middle_v, x_o).start()

        q_v[at, :] = matmul(two.spread[at, :], wq_v[...])
        out(7, g, q_v, q_o).start()
        k_v[at, :] = matmul(two.spread[at, :], wk_v[...])
        out(8, g, k_v, k_o).start()
        v_v[at, :] = matmul(two.spread[at, :], wv_v[...]).astype(BF)
        out(9, g, v_v, v_o).start()
        logit_v[at, :] = matmul(two.spread[at, :], gh[depth + 1])
        out(10, g, logit_v, logit_o).start()
        out(6, g, two.spread, normed_o).start()

    loop(STEPS, lambda s: two_sums(s, one, two, made_one, between, ahead, made_two, after))
    one.close()
    two.close()

    def drain(g):
        @pl.when(chain.mid)
        def _():
            out(5, g, middle_v, x_o).wait()

        for k, src, dst in (
            (1, one.spread, two_o), (2, slope_v, slope_o), (3, silu_v, silu_o),
            (4, hidden_v, hidden_o), (6, two.spread, normed_o), (7, q_v, q_o),
            (8, k_v, k_o), (9, v_v, v_o), (10, logit_v, logit_o),
        ):
            out(k, g, src, dst).wait()

    loop(GROUPS, drain)


def turn_kernel(
    size, depth, rows, width,
    mixed, x_in, cot, wo, feed_gain, wg, wu, wd,
    two_o, hidden_o, down_o, gate_o, up_o, grad_o, low_o, mixed_o, gain_o,
    *scratch,
):
    (wo_v, wg_v, wu_v, wd_v, middle_v, cot_v, hidden_v, gate_v, up_v, mixed_v, down_v, gain_v,
     load_sem, out_sem) = scratch[:14]
    chain = Chain(size)
    landed = scratch[14]
    one = Sum(chain, scratch[15:22], (landed, 1), rows, width)
    two = Sum(chain, scratch[22:29], (landed, 2), rows, width)
    span = one.block * GROUP
    loads = load_all(
        [(wo.at[depth], wo_v), (x_in, middle_v), (cot, cot_v), (wg.at[depth], wg_v),
         (wu.at[depth], wu_v), (wd.at[depth], wd_v)],
        load_sem,
    )
    chain.greet()
    tile = wg_v.shape[1] // (PARTS - 1)
    gain_one = feed_gain[depth : depth + 1, :]

    def out(k, g, src, dst):
        at = rows_of(g, span)
        return pltpu.make_async_copy(src.at[at], dst.at[at], out_sem.at[k, g])

    loads[0].wait()

    def start(g):
        at = rows_of(g, span)
        fill(one.part, at, lambda col: matmul(mixed[at, :], wo_v[:, col]))
        one.offer(g)

    loop(GROUPS, start)
    gain_v[...] = jnp.zeros_like(gain_v)
    wait_all(loads[1:])

    def made_one(at, total):
        value = middle_v[at, :] + total
        middle_v[at, :] = value
        return rms_scale(value, gain_one).astype(BF)

    def between(g, part):
        at = rows_of(g, span)

        @pl.when(part == 0)
        def _():
            out(0, g, one.spread, two_o).start()

        @pl.when(part < PARTS - 1)
        def _():
            col = columns(part, tile)
            gate = matmul(one.spread[at, :], wg_v[:, col])
            sig = jax.nn.sigmoid(gate)
            act = gate * sig
            slope = sig * (1.0 + gate * (1.0 - sig))
            up = matmul(one.spread[at, :], wu_v[:, col])
            hidden_v[at, col] = (act * up).astype(BF)
            pulled = back_product(cot_v[at, :], wd_v[col, :])
            gate_v[at, col] = (pulled * up * slope).astype(BF)
            up_v[at, col] = (pulled * act).astype(BF)

        @pl.when(part == PARTS - 1)
        def _():
            fill(
                two.part,
                at,
                lambda col: back_product(gate_v[at, :], wg_v[col, :])
                + back_product(up_v[at, :], wu_v[col, :]),
            )
            two.offer(g)
            out(1, g, hidden_v, hidden_o).start()
            out(2, g, gate_v, gate_o).start()
            out(3, g, up_v, up_o).start()

    def ahead(g):
        at = rows_of(g, span)
        share = jnp.where(chain.first_mid, 1.0, 0.0)

        @pl.when(chain.first_mid)
        def _():
            fill(down_v, at, lambda col: matmul(hidden_v[at, :], wd_v[:, col]) + middle_v[at, col])

        @pl.when(jnp.logical_not(chain.first_mid))
        def _():
            fill(down_v, at, lambda col: matmul(hidden_v[at, :], wd_v[:, col]))

        out(4, g, down_v, down_o).start()

    def made_two(at, total):
        pulled, terms = back_norm(middle_v[at, :], gain_one, total)
        gain_v[...] += fold(terms)
        value = cot_v[at, :].astype(F32) + pulled
        middle_v[at, :] = value
        return value.astype(BF)

    def after(g):
        at = rows_of(g, span)

        @pl.when(chain.mid)
        def _():
            out(5, g, middle_v, grad_o).start()

        out(6, g, two.spread, low_o).start()
        mixed_v[at, :] = back_product(two.spread[at, :], wo_v[...])
        out(7, g, mixed_v, mixed_o).start()

    loop(STEPS, lambda s: two_sums(s, one, two, made_one, between, ahead, made_two, after))

    @pl.when(jnp.logical_not(chain.first_mid))
    def _():
        gain_v[...] = jnp.zeros_like(gain_v)

    gain_out = pltpu.make_async_copy(gain_v, gain_o, out_sem.at[8, 0])
    gain_out.start()
    one.close()
    two.close()

    def drain(g):
        @pl.when(chain.mid)
        def _():
            out(5, g, middle_v, grad_o).wait()

        for k, src, dst in (
            (0, one.spread, two_o), (1, hidden_v, hidden_o), (2, gate_v, gate_o),
            (3, up_v, up_o), (4, down_v, down_o), (6, two.spread, low_o), (7, mixed_v, mixed_o),
        ):
            out(k, g, src, dst).wait()

    loop(GROUPS, drain)
    gain_out.wait()


def back_kernel(
    size, plane_sizes, depth, rows, width,
    q_low, k_low, v_low, l_low, gh, x_in, grad_in, attention_gain, wq, wk, wv,
    wd, wg, wu, slope_in, silu_in, middle_in, feed_gain, wo,
    two_in, gate_in, up_in, cot_in, hidden_in, normed_in, low_in, mixed_in,
    gate_o, up_o, first_o, grad_o, low_o, mixed_o, gain_o, feed_gain_o,
    *rest,
):
    made, scratch = rest[:7], rest[7:]
    (wq_v, wk_v, wv_v, wd_v, wg_v, wu_v, wo_v, x_v, grad_v, slope_v, silu_v, gate_v, up_v, mixed_v,
     gain_v, feed_v, whole_v, parts_v, gh_v, load_sem, row_sem, tile_sem, out_sem) = scratch[:23]
    chain = Chain(size)
    landed = scratch[23]
    one = Sum(chain, scratch[24:31], (landed, 1), rows, width)
    two = Sum(chain, scratch[31:38], (landed, 2), rows, width)
    plane = Plane(*plane_sizes)
    share = width // plane.count
    unit = min(256, wk_v.shape[1])
    units_wide, heads_wide, keys_wide = wg_v.shape[1], wq_v.shape[1], wk_v.shape[1]
    parts_heads = parts_v.at[:, pl.ds(0, heads_wide)]
    scatter = Scatter(
        plane, scratch[38:],
        [
            (whole_v, parts_v, True, made[0], units_wide // unit, [(two_in, whole_v), (gate_in, parts_v)]),
            (whole_v, parts_v, True, made[1], units_wide // unit, [(up_in, parts_v)]),
            (whole_v, parts_v, False, made[2], units_wide // unit, [(cot_in, whole_v), (hidden_in, parts_v)]),
            (whole_v, q_low, True, made[3], heads_wide // unit, [(normed_in, whole_v)]),
            (whole_v, k_low, True, made[4], keys_wide // unit, []),
            (whole_v, v_low, True, made[5], keys_wide // unit, []),
            (whole_v, parts_v, False, made[6], heads_wide // unit, [(low_in, whole_v), (mixed_in, parts_heads)]),
        ],
        share, unit,
    )
    span = one.block * GROUP
    below = depth - 1
    loads = load_all(
        [(wq.at[depth], wq_v), (wk.at[depth], wk_v), (wv.at[depth], wv_v), (gh.at[depth], gh_v),
         (grad_in, grad_v),
         (wd.at[below], wd_v), (wg.at[below], wg_v), (wu.at[below], wu_v), (wo.at[below], wo_v)],
        load_sem,
    )

    def row_load(src, g, k):
        return pltpu.make_async_copy(src.at[rows_of(g, span)], x_v, row_sem.at[k])

    tile = wg_v.shape[1] // (PARTS - 1)

    def tile_load(src, dst, g, part, k):
        col = columns(part, tile)
        return pltpu.make_async_copy(
            src.at[rows_of(g, span), col], dst.at[:, col], tile_sem.at[k, part]
        )

    row_load(x_in, 0, 0).start()

    def first_tiles(part):
        tile_load(slope_in, slope_v, 0, part, 0).start()
        tile_load(silu_in, silu_v, 0, part, 1).start()

    loop(PARTS - 1, first_tiles)
    chain.greet(plane.partners())
    wait_all(loads[:4])
    gain_one = attention_gain[depth : depth + 1, :]
    gain_two = feed_gain[below : below + 1, :]

    def out(k, g, src, dst, whole=True):
        at = rows_of(g, span)
        return pltpu.make_async_copy(src.at[at] if whole else src, dst.at[at], out_sem.at[k, g])

    def start(g):
        at = rows_of(g, span)
        fill(
            one.part,
            at,
            lambda col: back_product(q_low[at, :], wq_v[col, :])
            + back_product(k_low[at, :], wk_v[col, :])
            + back_product(v_low[at, :], wv_v[col, :])
            + back_product(l_low[at, :], gh_v[col, :]),
        )
        one.offer(g)

    loop(GROUPS, start)
    gain_v[...] = jnp.zeros_like(gain_v)
    feed_v[...] = jnp.zeros_like(feed_v)
    wait_all(loads[4:])
    row_load(x_in, 0, 0).wait()

    def local(at):
        return pl.ds(pl.multiple_of(lax.rem(at.start, span), STRIP), STRIP)

    def made_one(at, total):
        pulled, terms = back_norm(x_v[local(at), :], gain_one, total)
        gain_v[...] += fold(terms)
        value = grad_v[at, :] + pulled
        grad_v[at, :] = value
        return value.astype(BF)

    def between(g, part):
        at = rows_of(g, span)

        @pl.when(part == 0)
        def _():
            out(0, g, one.spread, first_o).start()

            @pl.when(g < GROUPS - 1)
            def _():
                copy = row_load(x_in, g + 1, 1)
                copy.start()
                copy.wait()

            @pl.when(g > 0)
            def _():
                out(1, g - 1, gate_v, gate_o, False).wait()
                out(2, g - 1, up_v, up_o, False).wait()

        @pl.when(part < PARTS - 1)
        def _():
            col = columns(part, tile)
            tile_load(slope_in, slope_v, g, part, 0).wait()
            tile_load(silu_in, silu_v, g, part, 1).wait()
            pulled = back_product(one.spread[at, :], wd_v[col, :])
            gate_v[:, col] = (pulled * slope_v[:, col].astype(F32)).astype(BF)
            up_v[:, col] = (pulled * silu_v[:, col].astype(F32)).astype(BF)

            @pl.when(g < GROUPS - 1)
            def _():
                tile_load(slope_in, slope_v, g + 1, part, 0).start()
                tile_load(silu_in, silu_v, g + 1, part, 1).start()

        @pl.when(part == PARTS - 1)
        def _():
            fill(
                two.part,
                at,
                lambda col: back_product(gate_v[...], wg_v[col, :])
                + back_product(up_v[...], wu_v[col, :]),
            )
            two.offer(g)
            out(1, g, gate_v, gate_o, False).start()
            out(2, g, up_v, up_o, False).start()

    def ahead(g):
        copy = row_load(middle_in, g, 2)
        copy.start()
        copy.wait()

    def made_two(at, total):
        pulled, terms = back_norm(x_v[local(at), :], gain_two, total)
        feed_v[...] += fold(terms)
        value = grad_v[at, :] + pulled
        grad_v[at, :] = value
        return value.astype(BF)

    def after(g):
        at = rows_of(g, span)

        @pl.when(chain.mid)
        def _():
            out(5, g, grad_v, grad_o).start()

        out(3, g, two.spread, low_o).start()

        @pl.when(g > 0)
        def _():
            out(4, g - 1, mixed_v, mixed_o, False).wait()

        mixed_v[...] = back_product(two.spread[at, :], wo_v[...])
        out(4, g, mixed_v, mixed_o, False).start()

    pace = 3

    def step(s):
        two_sums(s, one, two, made_one, between, ahead, made_two, after)
        begin = lax.div(s * pace, 2)
        stop = lax.div((s + 1) * pace, 2)
        lax.fori_loop(begin, stop, lambda i, carry: (scatter.tick(i), carry)[1], 0)

    loop(max(STEPS, (2 * scatter.steps + pace - 1) // pace), step)

    @pl.when(jnp.logical_not(chain.first_mid))
    def _():
        gain_v[...] = jnp.zeros_like(gain_v)
        feed_v[...] = jnp.zeros_like(feed_v)

    gain_out = pltpu.make_async_copy(gain_v, gain_o, out_sem.at[6, 0])
    feed_out = pltpu.make_async_copy(feed_v, feed_gain_o, out_sem.at[7, 0])
    gain_out.start()
    feed_out.start()
    one.close()
    two.close()
    scatter.close()

    def drain(g):
        out(0, g, one.spread, first_o).wait()
        out(3, g, two.spread, low_o).wait()

        @pl.when(chain.mid)
        def _():
            out(5, g, grad_v, grad_o).wait()

    loop(GROUPS, drain)
    out(1, GROUPS - 1, gate_v, gate_o, False).wait()
    out(2, GROUPS - 1, up_v, up_o, False).wait()
    out(4, GROUPS - 1, mixed_v, mixed_o, False).wait()
    gain_out.wait()
    feed_out.wait()


def last_kernel(
    size, plane_sizes, depth, rows, width,
    q_low, k_low, v_low, l_low, gh, gain_rows, head_gains, heads_below, x_in, grad_in,
    attention_gain, wq, wk, wv, down_in,
    two_in, gate_in, up_in, first_in, hidden_in, normed_in, low_in, mixed_in,
    grad_o, result_o, total_o,
    *rest,
):
    made, scratch = rest[:7], rest[7:]
    (wq_v, wk_v, wv_v, x_v, grad_v, gain_v, whole_v, parts_v, total_v, load_sem, out_sem) = scratch[:11]
    chain = Chain(size)
    one = Sum(chain, scratch[12:19], (scratch[11], 1), rows, width)
    two = Sum(chain, scratch[20:27], (scratch[19], 1), rows, width)
    plane = Plane(*plane_sizes)
    total = Total(plane, size, scratch[27:31], 8)
    share = width // plane.count
    units_wide, heads_wide, keys_wide = parts_v.shape[1], wq_v.shape[1], wk_v.shape[1]
    unit = min(256, keys_wide)
    parts_heads = parts_v.at[:, pl.ds(0, heads_wide)]
    scatter = Scatter(
        plane, scratch[31:],
        [
            (whole_v, parts_v, True, made[0], units_wide // unit, [(two_in, whole_v), (gate_in, parts_v)]),
            (whole_v, parts_v, True, made[1], units_wide // unit, [(up_in, parts_v)]),
            (whole_v, parts_v, False, made[2], units_wide // unit, [(first_in, whole_v), (hidden_in, parts_v)]),
            (whole_v, q_low, True, made[3], heads_wide // unit, [(normed_in, whole_v)]),
            (whole_v, k_low, True, made[4], keys_wide // unit, []),
            (whole_v, v_low, True, made[5], keys_wide // unit, []),
            (whole_v, parts_v, False, made[6], heads_wide // unit, [(low_in, whole_v), (mixed_in, parts_heads)]),
        ],
        share, unit,
    )
    span = one.block * GROUP
    loads = load_all(
        [(wq.at[depth], wq_v), (wk.at[depth], wk_v), (wv.at[depth], wv_v), (x_in, x_v),
         (grad_in, grad_v), (down_in, two.part)],
        load_sem,
    )
    chain.greet([*plane.partners(), *total.across])
    gain_one = attention_gain[depth : depth + 1, :]

    def out(k, g):
        at = rows_of(g, span)
        src, dst = ((one.spread, grad_o), (two.spread, result_o))[k]
        return pltpu.make_async_copy(src.at[at], dst.at[at], out_sem.at[k, g])

    def start(g):
        at = rows_of(g, span)
        fill(
            one.part,
            at,
            lambda col: back_product(q_low[at, :], wq_v[col, :])
            + back_product(k_low[at, :], wk_v[col, :])
            + back_product(v_low[at, :], wv_v[col, :])
            + back_product(l_low[at, :], gh[depth, col, :]),
        )
        one.offer(g)

    gain_v[...] = jnp.zeros_like(gain_v)

    def made_one(at, total_sum):
        pulled, terms = back_norm(x_v[at, :].astype(F32), gain_one, total_sum)
        gain_v[...] += fold(terms)
        return (grad_v[at, :] + pulled).astype(BF)

    def made_two(at, total_sum):
        return total_sum.astype(BF)

    first_step, first_total = 4, 2 * BLOCKS + 8

    def sums(i):
        @pl.when(i == 1)
        def _():
            wait_all(loads)
            loop(GROUPS, start)
            loop(GROUPS, two.offer)

        def one_step(k, sum_here, make, s):
            @pl.when((s >= 0) & (s < BLOCKS))
            def _():
                sum_here.relay(s)

            @pl.when((s >= 1) & (s <= BLOCKS))
            def _():
                sum_here.finish(s - 1, make)

                @pl.when(lax.rem(s, GROUP) == 0)
                def _():
                    group = lax.div(s, GROUP) - 1
                    sum_here.receive(group)
                    out(k, group).start()

        @pl.when((i >= first_step) & (lax.rem(i - first_step, 2) == 0))
        def _():
            one_step(0, one, made_one, lax.div(i - first_step, 2))

        @pl.when((i >= first_step + 9) & (lax.rem(i - first_step, 2) == 1))
        def _():
            one_step(1, two, made_two, lax.div(i - first_step - 9, 2))

    def totals(i):
        @pl.when(i == first_total)
        def _():
            total.value[0] = jnp.zeros(total_v.shape, F32)

            @pl.when(chain.first_mid)
            def _():
                total.value[0, pl.ds(0, 1)] = jnp.sum(gain_v[...], axis=0, keepdims=True)

            for k in range(3):
                total.value[0, pl.ds(k + 1, 1)] = jnp.sum(gain_rows[k], axis=0, keepdims=True)
            for k in range(4):
                total.value[0, pl.ds(4, 1), pl.ds(k * HD, HD)] = jnp.sum(
                    head_gains[k], axis=0, keepdims=True
                )
            for k in range(LAYERS):
                total.value[0, pl.ds(8 + 8 * k, 8)] = heads_below[k]

        for k in range(total.stages):

            @pl.when(i == first_total + 1 + k)
            def _(k=k):
                total.start(k)

    def step(i):
        scatter.tick(i)
        sums(i)
        totals(i)

    last_sum = first_step + 9 + 2 * BLOCKS + 1
    loop(max(scatter.steps, last_sum, first_total + 2 + total.stages), step)
    total.finish(total_v)
    total_out = pltpu.make_async_copy(total_v, total_o, out_sem.at[2, 0])
    total_out.start()
    one.close()
    two.close()
    scatter.close()

    def drain(g):
        out(0, g).wait()
        out(1, g).wait()

    loop(GROUPS, drain)
    total_out.wait()


def call(kernel, collective_id, in_specs, outs, scratch, flops, out_spec=ANY):
    return pl.pallas_call(
        kernel,
        out_shape=tuple(jax.ShapeDtypeStruct(shape, kind) for shape, kind in outs),
        in_specs=in_specs,
        out_specs=tuple(out_spec for _ in outs),
        scratch_shapes=scratch,
        cost_estimate=pl.CostEstimate(flops=flops, bytes_accessed=40_000_000, transcendentals=0),
        compiler_params=pltpu.CompilerParams(
            collective_id=collective_id, has_side_effects=True, vmem_limit_bytes=VMEM_LIMIT
        ),
    )


def dma(*shape):
    return pltpu.SemaphoreType.DMA(shape)


def shards(
    size,
    stream,
    cotangent,
    prefixes,
    attention_gain,
    query_weight,
    key_weight,
    value_weight,
    gate_heads,
    query_gain,
    key_gain,
    output_weight,
    feed_gain,
    gate_weight,
    up_weight,
    down_weight,
):
    seq_count, row_count, width = stream.shape
    rows = seq_count * row_count
    span = rows // GROUPS
    dp_size = lax.axis_size("dp")
    plane_sizes = (dp_size, lax.axis_size("ctx"))
    plane_count = plane_sizes[0] * plane_sizes[1]
    heads_wide = query_weight.shape[2]
    keys_wide = key_weight.shape[2]
    units = gate_weight.shape[2]
    gates = gate_heads.shape[2]
    share = width // plane_count
    unit = min(256, keys_wide)
    here = lax.axis_index("dp") * plane_sizes[1] + lax.axis_index("ctx")
    positions = lax.axis_index("ctx") * row_count + jnp.arange(row_count, dtype=jnp.int32)
    cos_table, sin_table = rotary_tables(positions, HD)
    cos = jnp.concatenate([cos_table, cos_table], axis=1)
    sin = jnp.concatenate([-sin_table, sin_table], axis=1)
    stream_flat = stream.reshape(rows, width)
    cot_flat = cotangent.reshape(rows, width)
    heads_padded = jnp.pad(gate_heads, ((0, 0), (0, 0), (0, LANES - gates)))
    sum_scratch = Sum.scratch(rows, width)
    landed = [pltpu.VMEM((2, rows, width), BF)]
    pair_scratch = [pltpu.VMEM((3, rows, width), BF)] + sum_scratch + sum_scratch

    key_heads = keys_wide // HD
    attend_outs = [
        ((rows, heads_wide), BF), ((rows, heads_wide), BF), ((2, key_heads, rows, HD), BF),
        ((2, key_heads, rows, HD), BF), ((heads_wide // HD, rows, 1), F32), ((rows, heads_wide), F32),
    ]
    smem = pl.BlockSpec(memory_space=pltpu.SMEM)

    def attention_back(depth, collective_id, mixed_grad, logits, saved, q_raw, k_raw, normed):
        mixed, q_rot, keys, values, norm, attended = saved
        return call(
            partial(attend_back_kernel, depth),
            collective_id,
            [smem] + [WHOLE] * 14,
            [
                ((rows, heads_wide), BF), ((rows, keys_wide), BF), ((rows, keys_wide), BF),
                ((rows, LANES), BF), ((8, width), F32), ((8, HD), F32), ((8, HD), F32),
            ],
            [
                pltpu.VMEM((rows, heads_wide), BF), pltpu.VMEM((heads_wide // HD, rows, 1), F32),
                pltpu.VMEM((rows, heads_wide), F32), pltpu.VMEM((key_heads, rows, HD), F32),
                pltpu.VMEM((key_heads, rows, HD), F32), pltpu.VMEM((key_heads, 2, rows, HD), BF),
                pltpu.VMEM((key_heads, 2, rows, HD), BF), dma(key_heads), dma(key_heads),
            ],
            3_000_000_000,
            WHOLE,
        )(
            prefixes, mixed_grad, logits, attended, q_rot, keys, values, norm, q_raw, k_raw,
            query_gain, key_gain, cos, sin, normed,
        )

    made_shapes = [
        ((share, units), BF), ((share, units), BF), ((units, share), BF),
        ((share, heads_wide), BF), ((share, keys_wide), BF), ((share, keys_wide), BF),
        ((heads_wide, share), BF),
    ]
    scatter_scratch = Scatter.scratch(plane_count, share, unit)

    *saved_zero, normed_zero, q_raw_zero, k_raw_zero, logits_zero = call(
        partial(first_kernel, 0),
        4,
        [smem, WHOLE, WHOLE, ANY, ANY, ANY] + [WHOLE] * 5,
        attend_outs
        + [
            ((rows, width), BF), ((rows, heads_wide), F32), ((rows, keys_wide), F32),
            ((rows, LANES), F32),
        ],
        [
            pltpu.VMEM((rows, keys_wide), BF), pltpu.VMEM((width, heads_wide), BF),
            pltpu.VMEM((width, keys_wide), BF), pltpu.VMEM((width, keys_wide), BF), dma(3),
        ]
        + attend_scratch(rows, heads_wide, keys_wide),
        3_500_000_000,
        WHOLE,
    )(
        prefixes, stream_flat, attention_gain, query_weight, key_weight, value_weight, heads_padded,
        query_gain, key_gain, cos, sin,
    )
    mixed_zero = saved_zero[0]
    middle_zero, two_zero, slope, silu, hidden_zero, x_one, normed_one, q_raw, k_raw, values, logits = call(
        partial(forward_kernel, size, 0, rows, width),
        0,
        [WHOLE, ANY, ANY, WHOLE, ANY, ANY, ANY, WHOLE, ANY, ANY, ANY, WHOLE],
        [
            ((rows, width), F32), ((rows, width), BF), ((rows, units), BF), ((rows, units), BF),
            ((rows, units), BF), ((rows, width), F32), ((rows, width), BF),
            ((rows, heads_wide), F32), ((rows, keys_wide), F32), ((rows, keys_wide), BF),
            ((rows, LANES), F32),
        ],
        [
            pltpu.VMEM((heads_wide, width), BF), pltpu.VMEM((width, units), BF),
            pltpu.VMEM((width, units), BF), pltpu.VMEM((units, width), BF),
            pltpu.VMEM((width, heads_wide), BF), pltpu.VMEM((width, keys_wide), BF),
            pltpu.VMEM((width, keys_wide), BF), pltpu.VMEM((rows, width), BF),
            pltpu.VMEM((rows, width), F32), pltpu.VMEM((rows, units), BF),
            pltpu.VMEM((rows, units), BF), pltpu.VMEM((rows, units), BF),
            pltpu.VMEM((rows, heads_wide), F32), pltpu.VMEM((rows, keys_wide), F32),
            pltpu.VMEM((rows, keys_wide), BF), pltpu.VMEM((rows, LANES), F32),
            dma(8), dma(11, GROUPS),
        ]
        + pair_scratch,
        13_000_000_000,
    )(
        mixed_zero, stream_flat, output_weight, feed_gain, gate_weight, up_weight, down_weight,
        attention_gain, query_weight, key_weight, value_weight, heads_padded,
    )
    saved_one = call(
        partial(attend_kernel, 1),
        5,
        [smem] + [WHOLE] * 8,
        attend_outs,
        attend_scratch(rows, heads_wide, keys_wide),
        1_000_000_000,
        WHOLE,
    )(prefixes, q_raw, k_raw, values, logits, query_gain, key_gain, cos, sin)
    mixed_one = saved_one[0]
    two_one, hidden_one, down_part, gate_low, up_low, grad, low, mixed_grad, feed_one = call(
        partial(turn_kernel, size, 1, rows, width),
        1,
        [WHOLE, ANY, ANY, ANY, WHOLE, ANY, ANY, ANY],
        [
            ((rows, width), BF), ((rows, units), BF), ((rows, width), BF), ((rows, units), BF),
            ((rows, units), BF), ((rows, width), F32), ((rows, width), BF),
            ((rows, heads_wide), F32), ((8, width), F32),
        ],
        [
            pltpu.VMEM((heads_wide, width), BF), pltpu.VMEM((width, units), BF),
            pltpu.VMEM((width, units), BF), pltpu.VMEM((units, width), BF),
            pltpu.VMEM((rows, width), F32), pltpu.VMEM((rows, width), BF),
            pltpu.VMEM((rows, units), BF), pltpu.VMEM((rows, units), BF),
            pltpu.VMEM((rows, units), BF), pltpu.VMEM((rows, heads_wide), F32),
            pltpu.VMEM((rows, width), BF), pltpu.VMEM((8, width), F32),
            dma(6), dma(9, GROUPS),
        ]
        + pair_scratch,
        24_000_000_000,
    )(mixed_one, x_one, cot_flat, output_weight, feed_gain, gate_weight, up_weight, down_weight)
    q_low, k_low, v_low, l_low, heads_one, q_gain_one, k_gain_one = attention_back(
        1, 6, mixed_grad, logits, saved_one, q_raw, k_raw, normed_one
    )
    gate_low, up_low, first_low, grad, low, mixed_grad, gain_one, feed_zero, *made_one = call(
        partial(back_kernel, size, plane_sizes, 1, rows, width),
        2,
        [WHOLE] * 4 + [ANY, ANY, ANY, WHOLE] + [ANY] * 9 + [WHOLE] + [ANY] * 9,
        [
            ((rows, units), BF), ((rows, units), BF), ((rows, width), BF), ((rows, width), F32),
            ((rows, width), BF), ((rows, heads_wide), F32), ((8, width), F32), ((8, width), F32),
            *made_shapes,
        ],
        [
            pltpu.VMEM((width, heads_wide), BF), pltpu.VMEM((width, keys_wide), BF),
            pltpu.VMEM((width, keys_wide), BF), pltpu.VMEM((units, width), BF),
            pltpu.VMEM((width, units), BF), pltpu.VMEM((width, units), BF),
            pltpu.VMEM((heads_wide, width), BF), pltpu.VMEM((span, width), F32),
            pltpu.VMEM((rows, width), F32), pltpu.VMEM((span, units), BF),
            pltpu.VMEM((span, units), BF), pltpu.VMEM((span, units), BF),
            pltpu.VMEM((span, units), BF), pltpu.VMEM((span, heads_wide), F32),
            pltpu.VMEM((8, width), F32), pltpu.VMEM((8, width), F32),
            pltpu.VMEM((rows, width), BF), pltpu.VMEM((rows, units), BF),
            pltpu.VMEM((width, LANES), BF),
            dma(9), dma(3), dma(2, PARTS - 1), dma(8, GROUPS),
        ]
        + pair_scratch + scatter_scratch,
        26_000_000_000,
    )(
        q_low, k_low, v_low, l_low, heads_padded, x_one, grad, attention_gain,
        query_weight, key_weight, value_weight, down_weight, gate_weight, up_weight, slope, silu,
        middle_zero, feed_gain, output_weight,
        two_one, gate_low, up_low, cot_flat, hidden_one, normed_one, low, mixed_one,
    )
    q_low, k_low, v_low, l_low, heads_zero, q_gain_zero, k_gain_zero = attention_back(
        0, 7, mixed_grad, logits_zero, saved_zero, q_raw_zero, k_raw_zero, normed_zero
    )
    gain_rows = jnp.stack([gain_one, feed_zero, feed_one])
    head_gains = jnp.stack([q_gain_zero, k_gain_zero, q_gain_one, k_gain_one])
    heads_below = jnp.stack([heads_zero, heads_one])
    below_rows = 8 * LAYERS
    stages = plane_count.bit_length() - 1 + size.bit_length() - 1
    stream_low, result, totals, *made_zero = call(
        partial(last_kernel, size, plane_sizes, 0, rows, width),
        3,
        [WHOLE] * 8 + [ANY, ANY, WHOLE] + [ANY] * 12,
        [
            ((rows, width), BF), ((rows, width), BF), ((8 + below_rows, width), F32), *made_shapes,
        ],
        [
            pltpu.VMEM((width, heads_wide), BF), pltpu.VMEM((width, keys_wide), BF),
            pltpu.VMEM((width, keys_wide), BF), pltpu.VMEM((rows, width), BF),
            pltpu.VMEM((rows, width), F32), pltpu.VMEM((8, width), F32),
            pltpu.VMEM((rows, width), BF), pltpu.VMEM((rows, units), BF),
            pltpu.VMEM((8 + below_rows, width), F32), dma(6), dma(3, GROUPS),
        ]
        + landed + sum_scratch + landed + sum_scratch + Total.scratch(8 + below_rows, width, stages) + scatter_scratch,
        16_000_000_000,
    )(
        q_low, k_low, v_low, l_low, heads_padded, gain_rows, head_gains, heads_below, stream_flat,
        grad, attention_gain, query_weight, key_weight, value_weight, down_part,
        two_zero, gate_low, up_low, first_low, hidden_zero, normed_zero, low, mixed_zero,
    )
    def own(array, wide_share):
        return lax.dynamic_slice_in_dim(array, here * wide_share, wide_share, array.ndim - 1)

    gains = own(totals[:4], share)
    head_gains = own(totals[4, : 4 * HD].reshape(2, 2, HD), HD // plane_count)
    heads = own(totals[8:].reshape(LAYERS, 8, width)[:, :gates], share)
    weights = [
        jnp.stack([made_zero[entry], made_one[entry]]).astype(F32) for entry in range(7)
    ]
    return (
        result.reshape(seq_count, row_count, width),
        stream_low.astype(F32).reshape(seq_count, row_count, width),
        gains[0:2],
        weights[3],
        weights[4],
        weights[5],
        heads.transpose(0, 2, 1),
        head_gains[:, 0],
        head_gains[:, 1],
        weights[6],
        gains[2:4],
        weights[0],
        weights[1],
        weights[2],
    )


def solution(mesh):
    return jax.shard_map(
        partial(shards, mesh.shape["tensor"]),
        mesh=mesh,
        in_specs=(
            P("dp", "ctx", None),
            P("dp", "ctx", None),
            P("dp"),
            P(),
            P(None, None, "tensor"),
            P(None, None, "tensor"),
            P(None, None, "tensor"),
            P(None, None, "tensor"),
            P(),
            P(),
            P(None, "tensor", None),
            P(),
            P(None, None, "tensor"),
            P(None, None, "tensor"),
            P(None, "tensor", None),
        ),
        out_specs=(
            P("dp", "ctx", None),
            P("dp", "ctx", None),
            P(None, ("dp", "ctx")),
            P(None, ("dp", "ctx"), "tensor"),
            P(None, ("dp", "ctx"), "tensor"),
            P(None, ("dp", "ctx"), "tensor"),
            P(None, ("dp", "ctx"), "tensor"),
            P(None, ("dp", "ctx")),
            P(None, ("dp", "ctx")),
            P(None, "tensor", ("dp", "ctx")),
            P(None, ("dp", "ctx")),
            P(None, ("dp", "ctx"), "tensor"),
            P(None, ("dp", "ctx"), "tensor"),
            P(None, "tensor", ("dp", "ctx")),
        ),
        check_vma=False,
    )
```

```python
from functools import partial

import jax
import jax.numpy as jnp
from jax import lax
from jax.experimental import pallas as pl
from jax.experimental.pallas import tpu as pltpu
from jax.sharding import PartitionSpec as P

HD = 128
LAYERS = 2
LANES = 128

epsilon = 1e-06
theta = 1000000.0
masked = -1000000000.0

BF = jnp.bfloat16
F32 = jnp.float32
ANY = pl.BlockSpec(memory_space=pl.ANY)
WHOLE = pl.BlockSpec(memory_space=pltpu.VMEM)
MESH = pl.DeviceIdType.MESH

BLOCKS = 8
PIECES = 2
GROUP = 4
STRIP = 16
VMEM_LIMIT = 63 * 1024 * 1024


def rms_scale(values, gain):
    return values * lax.rsqrt(jnp.mean(values * values, axis=-1, keepdims=True) + epsilon) * gain


def rotary_tables(positions, width):
    counter = jnp.arange(width // 2, dtype=jnp.float32)
    frequency = theta ** (-2.0 * counter / width)
    angles = positions.astype(jnp.float32)[:, None] * frequency[None, :]
    return (jnp.cos(angles), jnp.sin(angles))


def matmul(left, right):
    return jnp.dot(left, right, preferred_element_type=F32)


def weight_product(left, right):
    return lax.dot_general(left, right, (((0,), (0,)), ((), ())), preferred_element_type=F32)


def back_product(gradient, weight):
    return lax.dot_general(gradient, weight, (((1,), (1,)), ((), ())), preferred_element_type=F32)


def loop(count, body):
    def step(i, carry):
        body(i)
        return carry

    lax.fori_loop(0, count, step, 0)


def rows_of(r, block):
    return pl.ds(pl.multiple_of(r * block, block), block)


def columns(j, width):
    return pl.ds(pl.multiple_of(j * width, width), width)


def greet(targets, extra, has_extra):
    barrier = pltpu.get_barrier_semaphore()
    for target in targets:
        pl.semaphore_signal(barrier, inc=1, device_id=target, device_id_type=MESH)

    @pl.when(has_extra)
    def _():
        pl.semaphore_signal(barrier, inc=1, device_id=extra, device_id_type=MESH)
        pl.semaphore_wait(barrier, len(targets) + 1)

    @pl.when(jnp.logical_not(has_extra))
    def _():
        pl.semaphore_wait(barrier, len(targets))


class Chain:
    def __init__(self, size):
        self.size = size
        self.spot = lax.axis_index("tensor")
        half = size // 2
        on_left = self.spot < half
        self.end = (self.spot == 0) | (self.spot == size - 1)
        self.inner = jnp.logical_not(self.end)
        self.mid = (self.spot == half - 1) | (self.spot == half)
        self.outer = jnp.logical_not(self.mid)
        self.first_mid = self.spot == half - 1
        self.inward = {"tensor": jnp.where(on_left, self.spot + 1, self.spot - 1)}
        self.outward = {"tensor": jnp.where(on_left, self.spot - 1, self.spot + 1)}

    def greet(self, others=()):
        greet([self.inward, *others], self.outward, self.inner)


class Sum:
    def __init__(self, chain, refs, landed, rows, width):
        self.chain = chain
        self.part, self.spread, self.s_in, self.r_in, self.s_out, self.r_out, self.r_cross = refs
        self.landed, self.cross = landed
        self.block = rows // BLOCKS
        self.piece = width // PIECES

    @staticmethod
    def scratch(rows, width):
        return [
            pltpu.VMEM((rows, width), BF),
            pltpu.VMEM((rows, width), BF),
            pltpu.SemaphoreType.DMA((BLOCKS, PIECES)),
            pltpu.SemaphoreType.DMA((BLOCKS, PIECES)),
            pltpu.SemaphoreType.DMA((BLOCKS,)),
            pltpu.SemaphoreType.DMA((BLOCKS,)),
            pltpu.SemaphoreType.DMA((BLOCKS, PIECES)),
        ]

    def hop(self, r, p, across):
        where = (rows_of(r, self.block), columns(p, self.piece))
        return pltpu.make_async_remote_copy(
            src_ref=self.part.at[where],
            dst_ref=self.landed.at[(self.cross if across else 0,) + where],
            send_sem=self.s_in.at[r, p],
            recv_sem=(self.r_cross if across else self.r_in).at[r, p],
            device_id=self.chain.inward,
            device_id_type=MESH,
        )

    def out_hop(self, r):
        at = rows_of(r, self.block)
        return pltpu.make_async_remote_copy(
            src_ref=self.spread.at[at],
            dst_ref=self.spread.at[at],
            send_sem=self.s_out.at[r],
            recv_sem=self.r_out.at[r],
            device_id=self.chain.outward,
            device_id_type=MESH,
        )

    def offer(self, g):
        @pl.when(self.chain.end)
        def _():
            def one(k):
                for p in range(PIECES):
                    self.hop(g * GROUP + k, p, False).start()

            loop(GROUP, one)

    def relay(self, r):
        @pl.when(self.chain.inner)
        def _():
            for p in range(PIECES):
                self.hop(r, p, False).wait_recv()
                col = columns(p, self.piece)

                def strip(i, col=col):
                    at = pl.ds(pl.multiple_of(r * self.block + i * STRIP, STRIP), STRIP)
                    total = self.part[at, col].astype(F32) + self.landed[0, at, col].astype(F32)
                    self.part[at, col] = total.astype(BF)

                loop(self.block // STRIP, strip)

                @pl.when(self.chain.mid)
                def _(p=p):
                    self.hop(r, p, True).start()

                @pl.when(self.chain.outer)
                def _(p=p):
                    self.hop(r, p, False).start()

    def finish(self, r, make):
        @pl.when(self.chain.mid)
        def _():
            for p in range(PIECES):
                self.hop(r, p, True).wait_recv()

            def strip(i):
                at = pl.ds(pl.multiple_of(r * self.block + i * STRIP, STRIP), STRIP)
                total = self.part[at, :].astype(F32) + self.landed[self.cross, at, :].astype(F32)
                self.spread[at, :] = make(at, total)

            loop(self.block // STRIP, strip)
            self.out_hop(r).start()

    def receive(self, g):
        @pl.when(self.chain.outer)
        def _():
            def one(k):
                self.out_hop(g * GROUP + k).wait_recv()

                @pl.when(self.chain.inner)
                def _():
                    self.out_hop(g * GROUP + k).start()

            loop(GROUP, one)

    def close(self):
        def block(r):
            for p in range(PIECES):
                self.hop(r, p, False).wait_send()

            @pl.when(self.chain.inner)
            def _():
                self.out_hop(r).wait_send()

        loop(BLOCKS, block)


PARTS = GROUP
GROUPS = BLOCKS // GROUP
STEPS = 2 * BLOCKS + 1


def two_sums(s, first, second, made_one, between, ahead, made_two, after):
    @pl.when(s < BLOCKS)
    def _():
        first.relay(s)

    @pl.when((s >= 1) & (s <= BLOCKS))
    def _():
        first.finish(s - 1, made_one)

    @pl.when((s >= GROUP) & (s < BLOCKS + GROUP))
    def _():
        part = lax.rem(s - GROUP, PARTS)
        group = lax.div(s - GROUP, PARTS)

        @pl.when(part == 0)
        def _():
            first.receive(group)

        between(group, part)

    @pl.when((s >= BLOCKS) & (s < 2 * BLOCKS))
    def _():
        second.relay(s - BLOCKS)

    @pl.when((s >= BLOCKS + 1) & (s < STEPS))
    def _():
        @pl.when(lax.rem(s - BLOCKS - 1, GROUP) == 0)
        def _():
            ahead(lax.div(s - BLOCKS - 1, GROUP))

        second.finish(s - BLOCKS - 1, made_two)

        @pl.when(lax.rem(s - BLOCKS, GROUP) == 0)
        def _():
            group = lax.div(s - BLOCKS, GROUP) - 1
            second.receive(group)
            after(group)


def back_norm(value, gain, grad):
    spread = lax.rsqrt(jnp.mean(value * value, axis=-1, keepdims=True) + epsilon)
    scaled = grad * gain
    pulled = jnp.mean(scaled * value, axis=-1, keepdims=True)
    terms = grad * value * spread
    return spread * scaled - value * (spread * spread * spread * pulled), terms


def fold(terms):
    folded = terms[:8]
    for k in range(8, terms.shape[0], 8):
        folded = folded + terms[k : k + 8]
    return folded


def load_all(pairs, sems):
    copies = [pltpu.make_async_copy(src, dst, sems.at[k]) for k, (src, dst) in enumerate(pairs)]
    for copy in copies:
        copy.start()
    return copies


def wait_all(copies):
    for copy in copies:
        copy.wait()


def wide(width):
    return 512 if width % 512 == 0 else 256


def fill(target, at, make):
    width = target.shape[1]
    tile = wide(width)

    def one(p):
        col = columns(p, tile)
        target[at, col] = make(col).astype(target.dtype)

    loop(width // tile, one)


def flip(value, bit):
    return value + bit * (1 - 2 * lax.rem(lax.div(value, bit), 2))


class Plane:
    def __init__(self, dp_size, ctx_size):
        self.count = dp_size * ctx_size
        self.ctx_size = ctx_size
        self.me = lax.axis_index("dp") * ctx_size + lax.axis_index("ctx")
        bits = [1 << k for k in range(self.count.bit_length() - 1)]
        near = [bit for bit in bits if bit >= ctx_size][:1]
        rest = [bit for bit in bits if bit not in near]
        self.bits = bits
        self.orders = (near + rest, near + rest[1:] + rest[:1])

    def partner(self, bit):
        other = flip(self.me, bit)
        return {"dp": lax.div(other, self.ctx_size), "ctx": lax.rem(other, self.ctx_size)}

    def partners(self):
        return [self.partner(bit) for bit in self.bits]


class Scatter:
    SLOTS = (2, 4, 4, 4)
    KEPT = (2, 3, 3, 3)
    RESULTS = 2
    LAGS = (0, 1, 4, 7, 10, 13)

    def __init__(self, plane, refs, whole, parts, groups, share, tile):
        self.plane = plane
        self.whole, self.parts = whole, parts
        self.groups = groups
        self.share, self.tile = share, tile
        self.stages = len(plane.bits)
        self.units = sum(group[2] for group in groups)
        self.refs = [refs[6 * k : 6 * k + 6] for k in range(self.stages)]
        self.made, self.out_sem, self.load_sem = refs[6 * self.stages :]
        self.steps = self.units + self.LAGS[self.stages]

    @classmethod
    def scratch(cls, count, share, tile):
        found = []
        blocks = count // 2
        for k in range(count.bit_length() - 1):
            slots = cls.SLOTS[k]
            found += [
                pltpu.VMEM((depth, blocks, share, tile), BF) for depth in (slots, cls.KEPT[k], slots)
            ]
            found += [
                pltpu.SemaphoreType.DMA((slots,)),
                pltpu.SemaphoreType.DMA((slots,)),
                pltpu.SemaphoreType.REGULAR((slots,)),
            ]
            blocks //= 2
        return found + [
            pltpu.VMEM((cls.RESULTS, share, tile), BF),
            pltpu.SemaphoreType.DMA((cls.RESULTS,)),
            pltpu.SemaphoreType.DMA((4,)),
        ]

    def partner(self, stage, u):
        odd = lax.rem(u, 2) == 1
        even_one, odd_one = (self.plane.partner(order[stage]) for order in self.plane.orders)
        return {axis: jnp.where(odd, odd_one[axis], even_one[axis]) for axis in even_one}

    def copy(self, stage, u):
        send, unused, land, s_sem, r_sem, unused_credit = self.refs[stage]
        slot = lax.rem(u, self.SLOTS[stage])
        return pltpu.make_async_remote_copy(
            src_ref=send.at[slot],
            dst_ref=land.at[slot],
            send_sem=s_sem.at[slot],
            recv_sem=r_sem.at[slot],
            device_id=self.partner(stage, u),
            device_id_type=MESH,
        )

    def ready(self, stage, u):
        @pl.when(u >= self.SLOTS[stage])
        def _():
            self.copy(stage, u - self.SLOTS[stage]).wait_send()

    def push(self, stage, u):
        @pl.when(u >= self.SLOTS[stage])
        def _():
            pl.semaphore_wait(self.refs[stage][5].at[lax.rem(u, self.SLOTS[stage])], 1)

        self.copy(stage, u).start()

    def product(self, u):
        send, keep = self.refs[0][:2]
        slot, spot = lax.rem(u, self.SLOTS[0]), lax.rem(u, self.KEPT[0])
        odd = lax.rem(u, 2)
        orders = self.plane.orders
        first = 0
        place = u
        by_rows_here = u < 0
        for unused, by_rows, count, loads in self.groups:
            here = (u >= first) & (u < first + count)
            place = jnp.where(here, u - first, place)
            if by_rows:
                by_rows_here = by_rows_here | here

            @pl.when(u == first)
            def _(loads=loads):
                wait_all(load_all(loads, self.load_sem))

            first += count
        parts = self.parts[:, columns(place, self.tile)]

        def block(far, j):
            owner = flip(self.plane.me, orders[0][0]) if far else self.plane.me
            for bits in reversed(tuple(zip(*orders))[1:]):
                if j % 2:
                    owner = flip(owner, bits[0]) * (1 - odd) + flip(owner, bits[1]) * odd
                j //= 2
            return self.whole[:, columns(owner, self.share)]

        def all_blocks(make):
            for j in range(self.plane.count // 2):
                send[slot, j] = make(block(True, j)).astype(BF)
                keep[spot, j] = make(block(False, j)).astype(BF)

        @pl.when(by_rows_here)
        def _():
            all_blocks(lambda whole: weight_product(whole, parts))

        @pl.when(jnp.logical_not(by_rows_here))
        def _():
            all_blocks(lambda whole: weight_product(parts, whole))

    def merge(self, stage, u):
        unused, keep, land = self.refs[stage][:3]
        slots = self.SLOTS[stage]
        slot, spot = lax.rem(u, slots), lax.rem(u, self.KEPT[stage])
        self.copy(stage, u).wait_recv()
        half = (self.plane.count // 2) >> (stage + 1)
        last = stage == self.stages - 1
        if not last:
            self.ready(stage + 1, u)
            send_on, keep_on = self.refs[stage + 1][:2]
            slot_on = lax.rem(u, self.SLOTS[stage + 1])
            spot_on = lax.rem(u, self.KEPT[stage + 1])

            def one(j):
                far = keep[spot, half + j].astype(F32) + land[slot, half + j].astype(F32)
                send_on[slot_on, j] = far.astype(BF)
                near = keep[spot, j].astype(F32) + land[slot, j].astype(F32)
                keep_on[spot_on, j] = near.astype(BF)

            loop(half, one)
            self.push(stage + 1, u)
        else:
            place = lax.rem(u, self.RESULTS)

            @pl.when(u >= self.RESULTS)
            def _():
                self.results(u - self.RESULTS, lambda copy: copy.wait())

            total = keep[spot, 0].astype(F32) + land[slot, 0].astype(F32)
            self.made[place] = total.astype(BF)
            self.results(u, lambda copy: copy.start())

        @pl.when(u + slots < self.units)
        def _():
            pl.semaphore_signal(
                self.refs[stage][5].at[slot],
                inc=1,
                device_id=self.partner(stage, u),
                device_id_type=MESH,
            )

    def results(self, u, act):
        place = lax.rem(u, self.RESULTS)
        first = 0
        for out, by_rows, count, unused_loads in self.groups:

            @pl.when((u >= first) & (u < first + count))
            def _(by_rows=by_rows, out=out, first=first):
                if by_rows:
                    at = (slice(None), columns(u - first, self.tile))
                else:
                    at = (rows_of(u - first, self.tile), slice(None))
                act(pltpu.make_async_copy(self.made.at[place], out.at[at], self.out_sem.at[place]))

            first += count

    def tick(self, i):
        @pl.when(i < self.units)
        def _():
            self.ready(0, i)
            self.product(i)
            self.push(0, i)

        for stage in reversed(range(self.stages)):
            u = i - self.LAGS[stage + 1]

            @pl.when((u >= 0) & (u < self.units))
            def _(stage=stage, u=u):
                self.merge(stage, u)

    def close(self):
        for stage in range(self.stages):
            for k in range(max(0, self.units - self.SLOTS[stage]), self.units):
                self.copy(stage, jnp.int32(k)).wait_send()
        for k in range(max(0, self.units - self.RESULTS), self.units):
            self.results(jnp.int32(k), lambda copy: copy.wait())


class Total:
    def __init__(self, plane, size, refs, own):
        self.plane, self.own = plane, own
        self.value, self.land, self.s_sem, self.r_sem = refs
        spot = lax.axis_index("tensor")
        bits = [1 << k for k in range(size.bit_length() - 1)]
        self.targets = [plane.partner(bit) for bit in plane.bits]
        self.across = [{"tensor": flip(spot, bit)} for bit in bits]
        self.stages = len(self.targets) + len(bits)

    @staticmethod
    def scratch(rows, width, stages):
        return [
            pltpu.VMEM((stages, rows, width), F32),
            pltpu.VMEM((stages, rows, width), F32),
            pltpu.SemaphoreType.DMA((stages,)),
            pltpu.SemaphoreType.DMA((stages,)),
        ]

    def copy(self, k):
        count = len(self.targets)
        rows = slice(None) if k < count else pl.ds(0, self.own)
        return pltpu.make_async_remote_copy(
            src_ref=self.value.at[k, rows],
            dst_ref=self.land.at[k, rows],
            send_sem=self.s_sem.at[k],
            recv_sem=self.r_sem.at[k],
            device_id=(self.targets + self.across)[k],
            device_id_type=MESH,
        )

    def start(self, k):
        if k > 0:
            self.copy(k - 1).wait_recv()
            rows = slice(None) if k - 1 < len(self.targets) else pl.ds(0, self.own)
            if k - 1 >= len(self.targets):
                self.value[k] = self.value[k - 1]
            self.value[k, rows] = self.value[k - 1, rows] + self.land[k - 1, rows]
        self.copy(k).start()

    def finish(self, target):
        last = self.stages - 1
        self.copy(last).wait_recv()
        rows = pl.ds(0, self.own)
        target[...] = self.value[last]
        target[rows] = self.value[last, rows] + self.land[last, rows]
        for k in range(self.stages):
            self.copy(k).wait_send()


def turned(value):
    return pltpu.roll(value, HD // 2, 1)


def head_at(h):
    return pl.ds(h * HD, HD)


def head_norm(raw, gain, cos, sin):
    scaled = rms_scale(raw, gain)
    return scaled * cos + turned(scaled) * sin


def head_norm_back(raw, gain, cos, sin, grad):
    return back_norm(raw, gain, grad * cos - turned(grad) * sin)


def seen(rows, first_row, columns_wide, offset, prefix):
    query = first_row + lax.broadcasted_iota(jnp.int32, (rows, columns_wide), 0)
    key = lax.broadcasted_iota(jnp.int32, (rows, columns_wide), 1)
    return (key <= query) | (key + offset < prefix)


def attend(prefix, q_raw, k_raw, v, logits, query_gain, key_gain, cos, sin,
           mixed_o, q_o, keys_o, values_o, norm_o, attended_o, scratch, half):
    high, low, out, send_sem, land_sem = scratch
    rows = q_raw.shape[0]
    span = rows // GROUPS
    key_heads = k_raw.shape[1] // HD
    shared = q_raw.shape[1] // k_raw.shape[1]
    scale = HD ** (-0.5)

    def copy(j, which):
        ref = (keys_o, values_o)[which]
        return pltpu.make_async_remote_copy(
            src_ref=ref.at[0, j],
            dst_ref=ref.at[1, j],
            send_sem=send_sem.at[j, which],
            recv_sem=land_sem.at[j, which],
            device_id={"ctx": 1 - half},
            device_id_type=MESH,
        )

    for j in range(key_heads):

        def key_rows(g, j=j):
            at = rows_of(g, span)
            made = head_norm(k_raw[at, head_at(j)], key_gain, cos[at, :], sin[at, :])
            keys_o[0, j, at, :] = made.astype(BF)
            values_o[0, j, at, :] = v[at, head_at(j)]

        loop(GROUPS, key_rows)

        @pl.when(half == 0)
        def _(j=j):
            copy(j, 0).start()
            copy(j, 1).start()

    def own(g):
        at = rows_of(g, span)
        mask = seen(span, g * span, rows, half * rows, prefix)
        for h in range(key_heads * shared):
            j = h // shared
            query = head_norm(q_raw[at, head_at(h)], query_gain, cos[at, :], sin[at, :]).astype(BF)
            q_o[at, head_at(h)] = query
            scores = jnp.where(mask, back_product(query, keys_o[0, j]) * scale, masked)
            top = jnp.max(scores, axis=1, keepdims=True)
            weights = jnp.exp(scores - top)
            high[h, at, :] = top
            low[h, at, :] = jnp.sum(weights, axis=1, keepdims=True)
            out[at, head_at(h)] = matmul(weights.astype(BF), values_o[0, j])

    loop(GROUPS, own)

    @pl.when(half == 1)
    def _():
        for h in range(key_heads * shared):
            j = h // shared
            if h % shared == 0:
                copy(j, 0).wait_recv()
                copy(j, 1).wait_recv()

            def other(g, h=h, j=j):
                at = rows_of(g, span)
                scores = back_product(q_o[at, head_at(h)], keys_o[1, j]) * scale
                before = high[h, at, :]
                top = jnp.maximum(before, jnp.max(scores, axis=1, keepdims=True))
                weights = jnp.exp(scores - top)
                shrink = jnp.exp(before - top)
                high[h, at, :] = top
                low[h, at, :] = low[h, at, :] * shrink + jnp.sum(weights, axis=1, keepdims=True)
                out[at, head_at(h)] = out[at, head_at(h)] * shrink + matmul(
                    weights.astype(BF), values_o[1, j]
                )

            loop(GROUPS, other)

    def close(g):
        at = rows_of(g, span)
        open_gate = jax.nn.sigmoid(logits[at, :])
        for h in range(key_heads * shared):
            total = low[h, at, :]
            norm_o[h, at, :] = high[h, at, :] + jnp.log(total)
            attended = out[at, head_at(h)] * (1.0 / total)
            attended_o[at, head_at(h)] = attended
            mixed_o[at, head_at(h)] = (attended * open_gate[:, h : h + 1]).astype(BF)

    loop(GROUPS, close)

    @pl.when(half == 0)
    def _():
        for j in range(key_heads):
            copy(j, 0).wait_send()
            copy(j, 1).wait_send()


def attend_scratch(rows, heads_wide, keys_wide):
    return [
        pltpu.VMEM((heads_wide // HD, rows, 1), F32),
        pltpu.VMEM((heads_wide // HD, rows, 1), F32),
        pltpu.VMEM((rows, heads_wide), F32),
        pltpu.SemaphoreType.DMA((keys_wide // HD, 2)),
        pltpu.SemaphoreType.DMA((keys_wide // HD, 2)),
    ]


def greet_half(half):
    greet([{"ctx": 1 - half}], {"ctx": 1 - half}, half < 0)


def attend_kernel(
    depth, prefix, q_raw, k_raw, v, logits, query_gain, key_gain, cos, sin,
    mixed_o, q_o, keys_o, values_o, norm_o, attended_o, *scratch,
):
    half = lax.axis_index("ctx")
    greet_half(half)
    attend(prefix[0], q_raw, k_raw, v, logits, query_gain[depth : depth + 1, :],
           key_gain[depth : depth + 1, :], cos, sin,
           mixed_o, q_o, keys_o, values_o, norm_o, attended_o, scratch, half)


def first_kernel(
    depth, prefix, stream, gain, wq, wk, wv, gh, query_gain, key_gain, cos, sin,
    mixed_o, q_o, keys_o, values_o, norm_o, attended_o, normed_o, q_raw, k_raw, logits,
    v, wq_v, wk_v, wv_v, load_sem, *scratch,
):
    half = lax.axis_index("ctx")
    loads = load_all([(wk.at[depth], wk_v), (wv.at[depth], wv_v), (wq.at[depth], wq_v)], load_sem)
    greet_half(half)
    rows = stream.shape[0]
    span = rows // GROUPS

    def strip(i):
        at = rows_of(i, STRIP)
        value = stream[at, :].astype(F32)
        normed_o[at, :] = rms_scale(value, gain[depth : depth + 1, :]).astype(BF)

    loop(rows // STRIP, strip)
    wait_all(loads)

    def project(g):
        at = rows_of(g, span)
        k_raw[at, :] = matmul(normed_o[at, :], wk_v[...])
        v[at, :] = matmul(normed_o[at, :], wv_v[...]).astype(BF)
        q_raw[at, :] = matmul(normed_o[at, :], wq_v[...])
        logits[at, :] = matmul(normed_o[at, :], gh[depth])

    loop(GROUPS, project)
    attend(prefix[0], q_raw, k_raw, v, logits, query_gain[depth : depth + 1, :],
           key_gain[depth : depth + 1, :], cos, sin,
           mixed_o, q_o, keys_o, values_o, norm_o, attended_o, scratch, half)


def attend_back(
    half, depth, prefix, mixed_grad, logits, attended, q_rot, keys, values, norm, q_raw, k_raw,
    query_gain, key_gain, cos, sin, normed,
    q_o, k_o, v_o, l_o, heads_o, q_gain_o, k_gain_o,
    grad_low, inner, q_grad, k_grad, v_grad, given, landed, send_sem, land_sem,
):
    rows = q_raw.shape[0]
    span = rows // GROUPS
    key_heads = k_raw.shape[1] // HD
    shared = q_raw.shape[1] // k_raw.shape[1]
    heads = key_heads * shared
    scale = HD ** (-0.5)
    query_gain_here = query_gain[depth : depth + 1, :]
    key_gain_here = key_gain[depth : depth + 1, :]

    def copy(j):
        return pltpu.make_async_remote_copy(
            src_ref=given.at[j],
            dst_ref=landed.at[j],
            send_sem=send_sem.at[j],
            recv_sem=land_sem.at[j],
            device_id={"ctx": 1 - half},
            device_id_type=MESH,
        )

    def gate_back(g):
        at = rows_of(g, span)
        open_gate = jax.nn.sigmoid(logits[at, :])
        lane = lax.broadcasted_iota(jnp.int32, (span, LANES), 1)
        pulled = jnp.zeros((span, LANES), F32)
        for h in range(heads):
            grad = mixed_grad[at, head_at(h)]
            here = attended[at, head_at(h)]
            low_grad = (grad * open_gate[:, h : h + 1]).astype(BF)
            grad_low[at, head_at(h)] = low_grad
            inner[h, at, :] = jnp.sum(low_grad.astype(F32) * here, axis=1, keepdims=True)
            pulled = jnp.where(lane == h, jnp.sum(grad * here, axis=1, keepdims=True), pulled)
        l_o[at, :] = (pulled * (open_gate * (1.0 - open_gate))).astype(BF)

    def gates():
        loop(GROUPS, gate_back)
        heads_o[...] = weight_product(l_o[...], normed[...])[: heads_o.shape[0], :]

    def back(j, side, mask_of, first):
        k_grad[j] = jnp.zeros((rows, HD), F32)
        v_grad[j] = jnp.zeros((rows, HD), F32)

        def block(g):
            at = rows_of(g, span)
            for h in range(j * shared, (j + 1) * shared):
                query = q_rot[at, head_at(h)]
                pulled = grad_low[at, head_at(h)]
                scores = back_product(query, keys[side, j]) * scale
                if mask_of is not None:
                    scores = jnp.where(mask_of(g), scores, masked)
                weights = jnp.exp(scores - norm[h, at, :])
                slope = back_product(pulled, values[side, j])
                score_low = (weights * (slope - inner[h, at, :])).astype(BF)
                moved = matmul(score_low, keys[side, j])
                if first:
                    q_grad[at, head_at(h)] = moved
                else:
                    q_grad[at, head_at(h)] += moved
                k_grad[j] += weight_product(score_low, query)
                v_grad[j] += weight_product(weights.astype(BF), pulled)

        loop(GROUPS, block)

    def other(j):
        @pl.when(half == 1)
        def _():
            back(j, 1, None, True)
            given[j, 0] = (k_grad[j] * scale).astype(BF)
            given[j, 1] = v_grad[j].astype(BF)
            copy(j).start()

        @pl.when(half == 0)
        def _():
            wide_head = pl.ds(j * shared * HD, shared * HD)
            q_grad[:, wide_head] = jnp.zeros((rows, shared * HD), F32)

    def own(j):
        back(j, 0, lambda g: seen(span, g * span, rows, half * rows, prefix[0]), False)

    def query_rows(g):
        at = rows_of(g, span)
        for h in range(heads):
            pulled, terms = head_norm_back(
                q_raw[at, head_at(h)], query_gain_here, cos[at, :], sin[at, :],
                q_grad[at, head_at(h)] * scale,
            )
            q_o[at, head_at(h)] = pulled.astype(BF)
            q_gain_o[...] += jnp.sum(terms.reshape(span // 8, 8, HD), axis=0)

    def queries():
        q_gain_o[...] = jnp.zeros_like(q_gain_o)
        loop(GROUPS, query_rows)

    def keys_of(j):
        if j == 0:
            k_gain_o[...] = jnp.zeros_like(k_gain_o)

        @pl.when(half == 0)
        def _(j=j):
            copy(j).wait_recv()

        def key_rows(g, j=j):
            at = rows_of(g, span)
            k_total = k_grad[j, at, :] * scale
            v_total = v_grad[j, at, :]
            k_grad[j, at, :] = k_total
            v_o[at, head_at(j)] = v_total.astype(BF)

            @pl.when(half == 0)
            def _():
                k_grad[j, at, :] = k_total + landed[j, 0, at, :].astype(F32)
                v_o[at, head_at(j)] = (v_total + landed[j, 1, at, :].astype(F32)).astype(BF)

            pulled, terms = head_norm_back(
                k_raw[at, head_at(j)], key_gain_here, cos[at, :], sin[at, :], k_grad[j, at, :]
            )
            k_o[at, head_at(j)] = pulled.astype(BF)
            k_gain_o[...] += jnp.sum(terms.reshape(span // 8, 8, HD), axis=0)

        loop(GROUPS, key_rows)

    def close():
        @pl.when(half == 1)
        def _():
            for j in range(key_heads):
                copy(j).wait_send()

    heads_each = range(key_heads)
    return (
        [gates]
        + [partial(other, j) for j in heads_each]
        + [partial(own, j) for j in heads_each]
        + [queries]
        + [partial(keys_of, j) for j in heads_each],
        close,
    )


def attend_back_kernel(depth, *refs):
    half = lax.axis_index("ctx")
    greet_half(half)
    pieces, close = attend_back(half, depth, *refs)
    for piece in pieces:
        piece()
    close()


def forward_kernel(
    size, depth, rows, width,
    mixed, stream, wo, feed_gain, wg, wu, wd, next_gain, wq, wk, wv, gh,
    middle_o, two_o, slope_o, silu_o, hidden_o, x_o, normed_o, q_o, k_o, v_o, logit_o,
    *scratch,
):
    (wo_v, wg_v, wu_v, wd_v, wq_v, wk_v, wv_v, x_v, middle_v, slope_v, silu_v, hidden_v, q_v, k_v,
     v_v, logit_v, load_sem, out_sem) = scratch[:18]
    chain = Chain(size)
    landed = scratch[18]
    one = Sum(chain, scratch[19:26], (landed, 1), rows, width)
    two = Sum(chain, scratch[26:33], (landed, 2), rows, width)
    span = one.block * GROUP
    loads = load_all(
        [(wo.at[depth], wo_v), (stream, x_v), (wg.at[depth], wg_v), (wu.at[depth], wu_v),
         (wd.at[depth], wd_v), (wq.at[depth + 1], wq_v), (wk.at[depth + 1], wk_v),
         (wv.at[depth + 1], wv_v)],
        load_sem,
    )
    chain.greet()
    tile = wg_v.shape[1] // (PARTS - 1)
    gain_one = feed_gain[depth : depth + 1, :]
    gain_two = next_gain[depth + 1 : depth + 2, :]

    def out(k, g, src, dst):
        at = rows_of(g, span)
        return pltpu.make_async_copy(src.at[at], dst.at[at], out_sem.at[k, g])

    loads[0].wait()

    def start(g):
        at = rows_of(g, span)
        fill(one.part, at, lambda col: matmul(mixed[at, :], wo_v[:, col]))
        one.offer(g)

    loop(GROUPS, start)
    wait_all(loads[1:5])

    def made_one(at, total):
        value = x_v[at, :].astype(F32) + total
        middle_v[at, :] = value
        return rms_scale(value, gain_one).astype(BF)

    def between(g, part):
        at = rows_of(g, span)

        @pl.when(part == 0)
        def _():
            out(1, g, one.spread, two_o).start()

            @pl.when(chain.mid)
            def _():
                out(0, g, middle_v, middle_o).start()

        @pl.when(part < PARTS - 1)
        def _():
            col = columns(part, tile)
            gate = matmul(one.spread[at, :], wg_v[:, col])
            up = matmul(one.spread[at, :], wu_v[:, col])
            sig = jax.nn.sigmoid(gate)
            act = gate * sig
            hidden_v[at, col] = (act * up).astype(BF)
            silu_v[at, col] = act.astype(BF)
            slope_v[at, col] = (up * (sig * (1.0 + gate * (1.0 - sig)))).astype(BF)

        @pl.when(part == PARTS - 1)
        def _():
            fill(two.part, at, lambda col: matmul(hidden_v[at, :], wd_v[:, col]))
            two.offer(g)
            out(2, g, slope_v, slope_o).start()
            out(3, g, silu_v, silu_o).start()
            out(4, g, hidden_v, hidden_o).start()

    def ahead(g):
        @pl.when(g == 0)
        def _():
            wait_all(loads[5:])

        @pl.when(chain.mid)
        def _():
            out(0, g, middle_v, middle_o).wait()

    def made_two(at, total):
        value = middle_v[at, :] + total
        middle_v[at, :] = value
        return rms_scale(value, gain_two).astype(BF)

    def after(g):
        at = rows_of(g, span)

        @pl.when(chain.mid)
        def _():
            out(5, g, middle_v, x_o).start()

        q_v[at, :] = matmul(two.spread[at, :], wq_v[...])
        out(7, g, q_v, q_o).start()
        k_v[at, :] = matmul(two.spread[at, :], wk_v[...])
        out(8, g, k_v, k_o).start()
        v_v[at, :] = matmul(two.spread[at, :], wv_v[...]).astype(BF)
        out(9, g, v_v, v_o).start()
        logit_v[at, :] = matmul(two.spread[at, :], gh[depth + 1])
        out(10, g, logit_v, logit_o).start()
        out(6, g, two.spread, normed_o).start()

    loop(STEPS, lambda s: two_sums(s, one, two, made_one, between, ahead, made_two, after))
    one.close()
    two.close()

    def drain(g):
        @pl.when(chain.mid)
        def _():
            out(5, g, middle_v, x_o).wait()

        for k, src, dst in (
            (1, one.spread, two_o), (2, slope_v, slope_o), (3, silu_v, silu_o),
            (4, hidden_v, hidden_o), (6, two.spread, normed_o), (7, q_v, q_o),
            (8, k_v, k_o), (9, v_v, v_o), (10, logit_v, logit_o),
        ):
            out(k, g, src, dst).wait()

    loop(GROUPS, drain)


def turn_kernel(
    size, depth, rows, width,
    mixed, x_in, cot, wo, feed_gain, wg, wu, wd,
    two_o, hidden_o, down_o, gate_o, up_o, grad_o, low_o, mixed_o, gain_o,
    *scratch,
):
    (wo_v, wg_v, wu_v, wd_v, middle_v, cot_v, hidden_v, gate_v, up_v, mixed_v, down_v, gain_v,
     load_sem, out_sem) = scratch[:14]
    chain = Chain(size)
    landed = scratch[14]
    one = Sum(chain, scratch[15:22], (landed, 1), rows, width)
    two = Sum(chain, scratch[22:29], (landed, 2), rows, width)
    span = one.block * GROUP
    loads = load_all(
        [(wo.at[depth], wo_v), (x_in, middle_v), (cot, cot_v), (wg.at[depth], wg_v),
         (wu.at[depth], wu_v), (wd.at[depth], wd_v)],
        load_sem,
    )
    chain.greet()
    tile = wg_v.shape[1] // (PARTS - 1)
    gain_one = feed_gain[depth : depth + 1, :]

    def out(k, g, src, dst):
        at = rows_of(g, span)
        return pltpu.make_async_copy(src.at[at], dst.at[at], out_sem.at[k, g])

    loads[0].wait()

    def start(g):
        at = rows_of(g, span)
        fill(one.part, at, lambda col: matmul(mixed[at, :], wo_v[:, col]))
        one.offer(g)

    loop(GROUPS, start)
    gain_v[...] = jnp.zeros_like(gain_v)
    wait_all(loads[1:])

    def made_one(at, total):
        value = middle_v[at, :] + total
        middle_v[at, :] = value
        return rms_scale(value, gain_one).astype(BF)

    def between(g, part):
        at = rows_of(g, span)

        @pl.when(part == 0)
        def _():
            out(0, g, one.spread, two_o).start()

        @pl.when(part < PARTS - 1)
        def _():
            col = columns(part, tile)
            gate = matmul(one.spread[at, :], wg_v[:, col])
            sig = jax.nn.sigmoid(gate)
            act = gate * sig
            slope = sig * (1.0 + gate * (1.0 - sig))
            up = matmul(one.spread[at, :], wu_v[:, col])
            hidden_v[at, col] = (act * up).astype(BF)
            pulled = back_product(cot_v[at, :], wd_v[col, :])
            gate_v[at, col] = (pulled * up * slope).astype(BF)
            up_v[at, col] = (pulled * act).astype(BF)

        @pl.when(part == PARTS - 1)
        def _():
            fill(
                two.part,
                at,
                lambda col: back_product(gate_v[at, :], wg_v[col, :])
                + back_product(up_v[at, :], wu_v[col, :]),
            )
            two.offer(g)
            out(1, g, hidden_v, hidden_o).start()
            out(2, g, gate_v, gate_o).start()
            out(3, g, up_v, up_o).start()

    def ahead(g):
        at = rows_of(g, span)
        share = jnp.where(chain.first_mid, 1.0, 0.0)

        @pl.when(chain.first_mid)
        def _():
            fill(down_v, at, lambda col: matmul(hidden_v[at, :], wd_v[:, col]) + middle_v[at, col])

        @pl.when(jnp.logical_not(chain.first_mid))
        def _():
            fill(down_v, at, lambda col: matmul(hidden_v[at, :], wd_v[:, col]))

        out(4, g, down_v, down_o).start()

    def made_two(at, total):
        pulled, terms = back_norm(middle_v[at, :], gain_one, total)
        gain_v[...] += fold(terms)
        value = cot_v[at, :].astype(F32) + pulled
        middle_v[at, :] = value
        return value.astype(BF)

    def after(g):
        at = rows_of(g, span)

        @pl.when(chain.mid)
        def _():
            out(5, g, middle_v, grad_o).start()

        out(6, g, two.spread, low_o).start()
        mixed_v[at, :] = back_product(two.spread[at, :], wo_v[...])
        out(7, g, mixed_v, mixed_o).start()

    loop(STEPS, lambda s: two_sums(s, one, two, made_one, between, ahead, made_two, after))

    @pl.when(jnp.logical_not(chain.first_mid))
    def _():
        gain_v[...] = jnp.zeros_like(gain_v)

    gain_out = pltpu.make_async_copy(gain_v, gain_o, out_sem.at[8, 0])
    gain_out.start()
    one.close()
    two.close()

    def drain(g):
        @pl.when(chain.mid)
        def _():
            out(5, g, middle_v, grad_o).wait()

        for k, src, dst in (
            (0, one.spread, two_o), (1, hidden_v, hidden_o), (2, gate_v, gate_o),
            (3, up_v, up_o), (4, down_v, down_o), (6, two.spread, low_o), (7, mixed_v, mixed_o),
        ):
            out(k, g, src, dst).wait()

    loop(GROUPS, drain)
    gain_out.wait()


def back_kernel(
    size, plane_sizes, depth, rows, width,
    q_low, k_low, v_low, l_low, gh, x_in, grad_in, attention_gain, wq, wk, wv,
    wd, wg, wu, slope_in, silu_in, middle_in, feed_gain, wo,
    two_in, gate_in, up_in, cot_in, hidden_in, normed_in, low_in, mixed_in,
    gate_o, up_o, first_o, grad_o, low_o, mixed_o, gain_o, feed_gain_o,
    *rest,
):
    made, scratch = rest[:5], rest[5:]
    (wq_v, wk_v, wv_v, wd_v, wg_v, wu_v, wo_v, x_v, grad_v, slope_v, silu_v, gate_v, up_v, mixed_v,
     gain_v, feed_v, whole_v, parts_v, gh_v, load_sem, row_sem, tile_sem, out_sem) = scratch[:23]
    chain = Chain(size)
    landed = scratch[23]
    one = Sum(chain, scratch[24:31], (landed, 1), rows, width)
    two = Sum(chain, scratch[31:38], (landed, 2), rows, width)
    plane = Plane(*plane_sizes)
    share = width // plane.count
    unit = min(256, wk_v.shape[1])
    units_wide, heads_wide, keys_wide = wg_v.shape[1], wq_v.shape[1], wk_v.shape[1]
    parts_heads = parts_v.at[:, pl.ds(0, heads_wide)]
    heads_parts = [
        (q_low, parts_heads),
        (k_low, parts_v.at[:, pl.ds(heads_wide, keys_wide)]),
        (v_low, parts_v.at[:, pl.ds(heads_wide + keys_wide, keys_wide)]),
    ]
    scatter = Scatter(
        plane, scratch[38:], whole_v, parts_v,
        [
            (made[0], True, units_wide // unit, [(two_in, whole_v), (gate_in, parts_v)]),
            (made[1], True, units_wide // unit, [(up_in, parts_v)]),
            (made[2], False, units_wide // unit, [(cot_in, whole_v), (hidden_in, parts_v)]),
            (made[3], True, (heads_wide + 2 * keys_wide) // unit, [(normed_in, whole_v), *heads_parts]),
            (made[4], False, heads_wide // unit, [(low_in, whole_v), (mixed_in, parts_heads)]),
        ],
        share, unit,
    )
    span = one.block * GROUP
    below = depth - 1
    loads = load_all(
        [(wq.at[depth], wq_v), (wk.at[depth], wk_v), (wv.at[depth], wv_v), (gh.at[depth], gh_v),
         (grad_in, grad_v),
         (wd.at[below], wd_v), (wg.at[below], wg_v), (wu.at[below], wu_v), (wo.at[below], wo_v)],
        load_sem,
    )

    def row_load(src, g, k):
        return pltpu.make_async_copy(src.at[rows_of(g, span)], x_v, row_sem.at[k])

    tile = wg_v.shape[1] // (PARTS - 1)

    def tile_load(src, dst, g, part, k):
        col = columns(part, tile)
        return pltpu.make_async_copy(
            src.at[rows_of(g, span), col], dst.at[:, col], tile_sem.at[k, part]
        )

    row_load(x_in, 0, 0).start()

    def first_tiles(part):
        tile_load(slope_in, slope_v, 0, part, 0).start()
        tile_load(silu_in, silu_v, 0, part, 1).start()

    loop(PARTS - 1, first_tiles)
    chain.greet(plane.partners())
    wait_all(loads[:4])
    gain_one = attention_gain[depth : depth + 1, :]
    gain_two = feed_gain[below : below + 1, :]

    def out(k, g, src, dst, whole=True):
        at = rows_of(g, span)
        return pltpu.make_async_copy(src.at[at] if whole else src, dst.at[at], out_sem.at[k, g])

    def start(g):
        at = rows_of(g, span)
        fill(
            one.part,
            at,
            lambda col: back_product(q_low[at, :], wq_v[col, :])
            + back_product(k_low[at, :], wk_v[col, :])
            + back_product(v_low[at, :], wv_v[col, :])
            + back_product(l_low[at, :], gh_v[col, :]),
        )
        one.offer(g)

    loop(GROUPS, start)
    gain_v[...] = jnp.zeros_like(gain_v)
    feed_v[...] = jnp.zeros_like(feed_v)
    wait_all(loads[4:])
    row_load(x_in, 0, 0).wait()

    def local(at):
        return pl.ds(pl.multiple_of(lax.rem(at.start, span), STRIP), STRIP)

    def made_one(at, total):
        pulled, terms = back_norm(x_v[local(at), :], gain_one, total)
        gain_v[...] += fold(terms)
        value = grad_v[at, :] + pulled
        grad_v[at, :] = value
        return value.astype(BF)

    def between(g, part):
        at = rows_of(g, span)

        @pl.when(part == 0)
        def _():
            out(0, g, one.spread, first_o).start()

            @pl.when(g < GROUPS - 1)
            def _():
                copy = row_load(x_in, g + 1, 1)
                copy.start()
                copy.wait()

            @pl.when(g > 0)
            def _():
                out(1, g - 1, gate_v, gate_o, False).wait()
                out(2, g - 1, up_v, up_o, False).wait()

        @pl.when(part < PARTS - 1)
        def _():
            col = columns(part, tile)
            tile_load(slope_in, slope_v, g, part, 0).wait()
            tile_load(silu_in, silu_v, g, part, 1).wait()
            pulled = back_product(one.spread[at, :], wd_v[col, :])
            gate_v[:, col] = (pulled * slope_v[:, col].astype(F32)).astype(BF)
            up_v[:, col] = (pulled * silu_v[:, col].astype(F32)).astype(BF)

            @pl.when(g < GROUPS - 1)
            def _():
                tile_load(slope_in, slope_v, g + 1, part, 0).start()
                tile_load(silu_in, silu_v, g + 1, part, 1).start()

        @pl.when(part == PARTS - 1)
        def _():
            fill(
                two.part,
                at,
                lambda col: back_product(gate_v[...], wg_v[col, :])
                + back_product(up_v[...], wu_v[col, :]),
            )
            two.offer(g)
            out(1, g, gate_v, gate_o, False).start()
            out(2, g, up_v, up_o, False).start()

    def ahead(g):
        copy = row_load(middle_in, g, 2)
        copy.start()
        copy.wait()

    def made_two(at, total):
        pulled, terms = back_norm(x_v[local(at), :], gain_two, total)
        feed_v[...] += fold(terms)
        value = grad_v[at, :] + pulled
        grad_v[at, :] = value
        return value.astype(BF)

    def after(g):
        at = rows_of(g, span)

        @pl.when(chain.mid)
        def _():
            out(5, g, grad_v, grad_o).start()

        out(3, g, two.spread, low_o).start()

        @pl.when(g > 0)
        def _():
            out(4, g - 1, mixed_v, mixed_o, False).wait()

        mixed_v[...] = back_product(two.spread[at, :], wo_v[...])
        out(4, g, mixed_v, mixed_o, False).start()

    pace = 3

    def step(s):
        two_sums(s, one, two, made_one, between, ahead, made_two, after)
        begin = lax.div(s * pace, 2)
        stop = lax.div((s + 1) * pace, 2)
        lax.fori_loop(begin, stop, lambda i, carry: (scatter.tick(i), carry)[1], 0)

    loop(max(STEPS, (2 * scatter.steps + pace - 1) // pace), step)

    @pl.when(jnp.logical_not(chain.first_mid))
    def _():
        gain_v[...] = jnp.zeros_like(gain_v)
        feed_v[...] = jnp.zeros_like(feed_v)

    gain_out = pltpu.make_async_copy(gain_v, gain_o, out_sem.at[6, 0])
    feed_out = pltpu.make_async_copy(feed_v, feed_gain_o, out_sem.at[7, 0])
    gain_out.start()
    feed_out.start()
    one.close()
    two.close()
    scatter.close()

    def drain(g):
        out(0, g, one.spread, first_o).wait()
        out(3, g, two.spread, low_o).wait()

        @pl.when(chain.mid)
        def _():
            out(5, g, grad_v, grad_o).wait()

    loop(GROUPS, drain)
    out(1, GROUPS - 1, gate_v, gate_o, False).wait()
    out(2, GROUPS - 1, up_v, up_o, False).wait()
    out(4, GROUPS - 1, mixed_v, mixed_o, False).wait()
    gain_out.wait()
    feed_out.wait()


def last_kernel(
    size, plane_sizes, depth, rows, width,
    *refs,
):
    attend_in, refs = refs[:15], refs[15:]
    (gh, gain_one_in, feed_zero_in, feed_one_in, q_gain_one, k_gain_one, heads_one, x_in, grad_in,
     attention_gain, wq, wk, wv, down_in, two_in, gate_in, up_in, first_in, hidden_in, low_in, mixed_in,
     grad_o, result_o, total_o, *rest) = refs
    normed_in = attend_in[14]
    made, rest = rest[:5], rest[5:]
    attend_made, attend_scratch, scratch = rest[:7], rest[7:16], rest[16:]
    q_low, k_low, v_low, l_low, heads_zero, q_gain_zero, k_gain_zero = attend_made
    half = lax.axis_index("ctx")
    pieces, close_attend = attend_back(half, depth, *attend_in, *attend_made, *attend_scratch)
    (wq_v, wk_v, wv_v, x_v, grad_v, gain_v, whole_v, parts_v, total_v, load_sem, out_sem) = scratch[:11]
    chain = Chain(size)
    one = Sum(chain, scratch[12:19], (scratch[11], 1), rows, width)
    two = Sum(chain, scratch[20:27], (scratch[19], 1), rows, width)
    plane = Plane(*plane_sizes)
    total = Total(plane, size, scratch[27:31], 8)
    share = width // plane.count
    units_wide, heads_wide, keys_wide = parts_v.shape[1], wq_v.shape[1], wk_v.shape[1]
    unit = min(256, keys_wide)
    parts_heads = parts_v.at[:, pl.ds(0, heads_wide)]
    heads_parts = [
        (q_low, parts_heads),
        (k_low, parts_v.at[:, pl.ds(heads_wide, keys_wide)]),
        (v_low, parts_v.at[:, pl.ds(heads_wide + keys_wide, keys_wide)]),
    ]
    scatter = Scatter(
        plane, scratch[31:], whole_v, parts_v,
        [
            (made[0], True, units_wide // unit, [(two_in, whole_v), (gate_in, parts_v)]),
            (made[1], True, units_wide // unit, [(up_in, parts_v)]),
            (made[2], False, units_wide // unit, [(first_in, whole_v), (hidden_in, parts_v)]),
            (made[3], True, (heads_wide + 2 * keys_wide) // unit, [(normed_in, whole_v), *heads_parts]),
            (made[4], False, heads_wide // unit, [(low_in, whole_v), (mixed_in, parts_heads)]),
        ],
        share, unit,
    )
    span = one.block * GROUP
    loads = load_all(
        [(wq.at[depth], wq_v), (wk.at[depth], wk_v), (wv.at[depth], wv_v), (x_in, x_v),
         (grad_in, grad_v), (down_in, two.part)],
        load_sem,
    )
    chain.greet([*plane.partners(), *total.across, {"ctx": 1 - half}])
    gain_one = attention_gain[depth : depth + 1, :]

    def out(k, g):
        at = rows_of(g, span)
        src, dst = ((one.spread, grad_o), (two.spread, result_o))[k]
        return pltpu.make_async_copy(src.at[at], dst.at[at], out_sem.at[k, g])

    def start(g):
        at = rows_of(g, span)
        fill(
            one.part,
            at,
            lambda col: back_product(q_low[at, :], wq_v[col, :])
            + back_product(k_low[at, :], wk_v[col, :])
            + back_product(v_low[at, :], wv_v[col, :])
            + back_product(l_low[at, :], gh[depth, col, :]),
        )
        one.offer(g)

    gain_v[...] = jnp.zeros_like(gain_v)

    def made_one(at, total_sum):
        pulled, terms = back_norm(x_v[at, :].astype(F32), gain_one, total_sum)
        gain_v[...] += fold(terms)
        return (grad_v[at, :] + pulled).astype(BF)

    def made_two(at, total_sum):
        return total_sum.astype(BF)

    begin = len(pieces)
    first_two, first_one = 3, begin + 2
    sum_ticks = 4 * -(-(BLOCKS + 1) // 3)
    first_total = first_one + sum_ticks

    def sums(i):
        @pl.when(i == 0)
        def _():
            loads[5].wait()
            loop(GROUPS, two.offer)

        for place, piece in enumerate(pieces):
            pl.when(i == place)(piece)

        @pl.when(i == begin)
        def _():
            wait_all(loads[:5])
            loop(GROUPS, start)

        def one_step(k, sum_here, make, s):
            @pl.when((s >= 0) & (s < BLOCKS))
            def _():
                sum_here.relay(s)

            @pl.when((s >= 1) & (s <= BLOCKS))
            def _():
                sum_here.finish(s - 1, make)

                @pl.when(lax.rem(s, GROUP) == 0)
                def _():
                    group = lax.div(s, GROUP) - 1
                    sum_here.receive(group)
                    out(k, group).start()

        def paced(k, sum_here, make, first):
            since = i - first
            take = lax.rem(since, 4)

            @pl.when((since >= 0) & (take < 3))
            def _():
                one_step(k, sum_here, make, lax.div(since, 4) * 3 + take)

        paced(1, two, made_two, first_two)
        paced(0, one, made_one, first_one)

    def totals(i):
        @pl.when(i == first_total)
        def _():
            total.value[0] = jnp.zeros(total_v.shape, F32)

            @pl.when(chain.first_mid)
            def _():
                total.value[0, pl.ds(0, 1)] = jnp.sum(gain_v[...], axis=0, keepdims=True)

            for k, gains in enumerate((gain_one_in, feed_zero_in, feed_one_in)):
                total.value[0, pl.ds(k + 1, 1)] = jnp.sum(gains[...], axis=0, keepdims=True)
            for k, gains in enumerate((q_gain_zero, k_gain_zero, q_gain_one, k_gain_one)):
                total.value[0, pl.ds(4, 1), pl.ds(k * HD, HD)] = jnp.sum(
                    gains[...], axis=0, keepdims=True
                )
            for k, heads in enumerate((heads_zero, heads_one)):
                total.value[0, pl.ds(8 + 8 * k, 8)] = heads[...]

        for k in range(total.stages):

            @pl.when(i == first_total + 1 + k)
            def _(k=k):
                total.start(k)

    def step(i):
        scatter.tick(i)
        sums(i)
        totals(i)

    loop(max(scatter.steps, first_total + 1 + total.stages), step)
    close_attend()
    total.finish(total_v)
    total_out = pltpu.make_async_copy(total_v, total_o, out_sem.at[2, 0])
    total_out.start()
    one.close()
    two.close()
    scatter.close()

    def drain(g):
        out(0, g).wait()
        out(1, g).wait()

    loop(GROUPS, drain)
    total_out.wait()


def widen_kernel(heads_wide, keys_wide, low_in, *refs):
    below, above = refs[0:5], refs[5:10]
    stream_o, gate_o, up_o, down_o, q_o, k_o, v_o, out_o = refs[10:]
    stream_o[...] = low_in[...].astype(F32)
    for depth, made in enumerate((below, above)):
        gate_o[depth] = made[0][...].astype(F32)
        up_o[depth] = made[1][...].astype(F32)
        down_o[depth] = made[2][...].astype(F32)
        q_o[depth] = made[3][:, :heads_wide].astype(F32)
        k_o[depth] = made[3][:, heads_wide : heads_wide + keys_wide].astype(F32)
        v_o[depth] = made[3][:, heads_wide + keys_wide :].astype(F32)
        out_o[depth] = made[4][...].astype(F32)


def widen(stream_low, below, above, heads_wide, keys_wide):
    cuts = 4

    def cut(shape):
        return pl.BlockSpec((shape[0] // cuts, shape[1]), lambda i: (i, 0))

    def pair(shape):
        return pl.BlockSpec((2, shape[0] // cuts, shape[1]), lambda i: (0, i, 0))

    share = below[0].shape[0]
    shapes = [
        below[0].shape, below[1].shape, below[2].shape, (share, heads_wide), (share, keys_wide),
        (share, keys_wide), below[4].shape,
    ]
    inputs = [stream_low, *below, *above]
    return pl.pallas_call(
        partial(widen_kernel, heads_wide, keys_wide),
        grid=(cuts,),
        out_shape=(
            jax.ShapeDtypeStruct(stream_low.shape, F32),
            *(jax.ShapeDtypeStruct((2, *shape), F32) for shape in shapes),
        ),
        in_specs=[cut(array.shape) for array in inputs],
        out_specs=(cut(stream_low.shape), *(pair(shape) for shape in shapes)),
        compiler_params=pltpu.CompilerParams(vmem_limit_bytes=VMEM_LIMIT),
    )(*inputs)


def call(kernel, collective_id, in_specs, outs, scratch, flops, out_spec=ANY):
    return pl.pallas_call(
        kernel,
        out_shape=tuple(jax.ShapeDtypeStruct(shape, kind) for shape, kind in outs),
        in_specs=in_specs,
        out_specs=tuple(out_spec for _ in outs),
        scratch_shapes=scratch,
        cost_estimate=pl.CostEstimate(flops=flops, bytes_accessed=40_000_000, transcendentals=0),
        compiler_params=pltpu.CompilerParams(
            collective_id=collective_id, has_side_effects=True, vmem_limit_bytes=VMEM_LIMIT
        ),
    )


def dma(*shape):
    return pltpu.SemaphoreType.DMA(shape)


def shards(
    size,
    stream,
    cotangent,
    prefixes,
    attention_gain,
    query_weight,
    key_weight,
    value_weight,
    gate_heads,
    query_gain,
    key_gain,
    output_weight,
    feed_gain,
    gate_weight,
    up_weight,
    down_weight,
):
    seq_count, row_count, width = stream.shape
    rows = seq_count * row_count
    span = rows // GROUPS
    dp_size = lax.axis_size("dp")
    plane_sizes = (dp_size, lax.axis_size("ctx"))
    plane_count = plane_sizes[0] * plane_sizes[1]
    heads_wide = query_weight.shape[2]
    keys_wide = key_weight.shape[2]
    units = gate_weight.shape[2]
    gates = gate_heads.shape[2]
    share = width // plane_count
    unit = min(256, keys_wide)
    here = lax.axis_index("dp") * plane_sizes[1] + lax.axis_index("ctx")
    positions = lax.axis_index("ctx") * row_count + jnp.arange(row_count, dtype=jnp.int32)
    cos_table, sin_table = rotary_tables(positions, HD)
    cos = jnp.concatenate([cos_table, cos_table], axis=1)
    sin = jnp.concatenate([-sin_table, sin_table], axis=1)
    stream_flat = stream.reshape(rows, width)
    cot_flat = cotangent.reshape(rows, width)
    heads_padded = jnp.pad(gate_heads, ((0, 0), (0, 0), (0, LANES - gates)))
    sum_scratch = Sum.scratch(rows, width)
    landed = [pltpu.VMEM((2, rows, width), BF)]
    pair_scratch = [pltpu.VMEM((3, rows, width), BF)] + sum_scratch + sum_scratch

    key_heads = keys_wide // HD
    attend_outs = [
        ((rows, heads_wide), BF), ((rows, heads_wide), BF), ((2, key_heads, rows, HD), BF),
        ((2, key_heads, rows, HD), BF), ((heads_wide // HD, rows, 1), F32), ((rows, heads_wide), F32),
    ]
    smem = pl.BlockSpec(memory_space=pltpu.SMEM)

    attend_back_outs = [
        ((rows, heads_wide), BF), ((rows, keys_wide), BF), ((rows, keys_wide), BF),
        ((rows, LANES), BF), ((8, width), F32), ((8, HD), F32), ((8, HD), F32),
    ]
    attend_back_scratch = [
        pltpu.VMEM((rows, heads_wide), BF), pltpu.VMEM((heads_wide // HD, rows, 1), F32),
        pltpu.VMEM((rows, heads_wide), F32), pltpu.VMEM((key_heads, rows, HD), F32),
        pltpu.VMEM((key_heads, rows, HD), F32), pltpu.VMEM((key_heads, 2, rows, HD), BF),
        pltpu.VMEM((key_heads, 2, rows, HD), BF), dma(key_heads), dma(key_heads),
    ]

    def attend_back_in(mixed_grad, logits, saved, q_raw, k_raw, normed):
        mixed, q_rot, keys, values, norm, attended = saved
        return (
            prefixes, mixed_grad, logits, attended, q_rot, keys, values, norm, q_raw, k_raw,
            query_gain, key_gain, cos, sin, normed,
        )

    made_shapes = [
        ((share, units), BF), ((share, units), BF), ((units, share), BF),
        ((share, heads_wide + 2 * keys_wide), BF), ((heads_wide, share), BF),
    ]
    scatter_scratch = Scatter.scratch(plane_count, share, unit)

    *saved_zero, normed_zero, q_raw_zero, k_raw_zero, logits_zero = call(
        partial(first_kernel, 0),
        4,
        [smem, WHOLE, WHOLE, ANY, ANY, ANY] + [WHOLE] * 5,
        attend_outs
        + [
            ((rows, width), BF), ((rows, heads_wide), F32), ((rows, keys_wide), F32),
            ((rows, LANES), F32),
        ],
        [
            pltpu.VMEM((rows, keys_wide), BF), pltpu.VMEM((width, heads_wide), BF),
            pltpu.VMEM((width, keys_wide), BF), pltpu.VMEM((width, keys_wide), BF), dma(3),
        ]
        + attend_scratch(rows, heads_wide, keys_wide),
        3_500_000_000,
        WHOLE,
    )(
        prefixes, stream_flat, attention_gain, query_weight, key_weight, value_weight, heads_padded,
        query_gain, key_gain, cos, sin,
    )
    mixed_zero = saved_zero[0]
    middle_zero, two_zero, slope, silu, hidden_zero, x_one, normed_one, q_raw, k_raw, values, logits = call(
        partial(forward_kernel, size, 0, rows, width),
        0,
        [WHOLE, ANY, ANY, WHOLE, ANY, ANY, ANY, WHOLE, ANY, ANY, ANY, WHOLE],
        [
            ((rows, width), F32), ((rows, width), BF), ((rows, units), BF), ((rows, units), BF),
            ((rows, units), BF), ((rows, width), F32), ((rows, width), BF),
            ((rows, heads_wide), F32), ((rows, keys_wide), F32), ((rows, keys_wide), BF),
            ((rows, LANES), F32),
        ],
        [
            pltpu.VMEM((heads_wide, width), BF), pltpu.VMEM((width, units), BF),
            pltpu.VMEM((width, units), BF), pltpu.VMEM((units, width), BF),
            pltpu.VMEM((width, heads_wide), BF), pltpu.VMEM((width, keys_wide), BF),
            pltpu.VMEM((width, keys_wide), BF), pltpu.VMEM((rows, width), BF),
            pltpu.VMEM((rows, width), F32), pltpu.VMEM((rows, units), BF),
            pltpu.VMEM((rows, units), BF), pltpu.VMEM((rows, units), BF),
            pltpu.VMEM((rows, heads_wide), F32), pltpu.VMEM((rows, keys_wide), F32),
            pltpu.VMEM((rows, keys_wide), BF), pltpu.VMEM((rows, LANES), F32),
            dma(8), dma(11, GROUPS),
        ]
        + pair_scratch,
        13_000_000_000,
    )(
        mixed_zero, stream_flat, output_weight, feed_gain, gate_weight, up_weight, down_weight,
        attention_gain, query_weight, key_weight, value_weight, heads_padded,
    )
    saved_one = call(
        partial(attend_kernel, 1),
        5,
        [smem] + [WHOLE] * 8,
        attend_outs,
        attend_scratch(rows, heads_wide, keys_wide),
        1_000_000_000,
        WHOLE,
    )(prefixes, q_raw, k_raw, values, logits, query_gain, key_gain, cos, sin)
    mixed_one = saved_one[0]
    two_one, hidden_one, down_part, gate_low, up_low, grad, low, mixed_grad, feed_one = call(
        partial(turn_kernel, size, 1, rows, width),
        1,
        [WHOLE, ANY, ANY, ANY, WHOLE, ANY, ANY, ANY],
        [
            ((rows, width), BF), ((rows, units), BF), ((rows, width), BF), ((rows, units), BF),
            ((rows, units), BF), ((rows, width), F32), ((rows, width), BF),
            ((rows, heads_wide), F32), ((8, width), F32),
        ],
        [
            pltpu.VMEM((heads_wide, width), BF), pltpu.VMEM((width, units), BF),
            pltpu.VMEM((width, units), BF), pltpu.VMEM((units, width), BF),
            pltpu.VMEM((rows, width), F32), pltpu.VMEM((rows, width), BF),
            pltpu.VMEM((rows, units), BF), pltpu.VMEM((rows, units), BF),
            pltpu.VMEM((rows, units), BF), pltpu.VMEM((rows, heads_wide), F32),
            pltpu.VMEM((rows, width), BF), pltpu.VMEM((8, width), F32),
            dma(6), dma(9, GROUPS),
        ]
        + pair_scratch,
        24_000_000_000,
    )(mixed_one, x_one, cot_flat, output_weight, feed_gain, gate_weight, up_weight, down_weight)
    q_low, k_low, v_low, l_low, heads_one, q_gain_one, k_gain_one = call(
        partial(attend_back_kernel, 1),
        6,
        [smem] + [WHOLE] * 14,
        attend_back_outs,
        attend_back_scratch,
        3_000_000_000,
        WHOLE,
    )(*attend_back_in(mixed_grad, logits, saved_one, q_raw, k_raw, normed_one))
    gate_low, up_low, first_low, grad, low, mixed_grad, gain_one, feed_zero, *made_one = call(
        partial(back_kernel, size, plane_sizes, 1, rows, width),
        2,
        [WHOLE] * 4 + [ANY, ANY, ANY, WHOLE] + [ANY] * 9 + [WHOLE] + [ANY] * 9,
        [
            ((rows, units), BF), ((rows, units), BF), ((rows, width), BF), ((rows, width), F32),
            ((rows, width), BF), ((rows, heads_wide), F32), ((8, width), F32), ((8, width), F32),
            *made_shapes,
        ],
        [
            pltpu.VMEM((width, heads_wide), BF), pltpu.VMEM((width, keys_wide), BF),
            pltpu.VMEM((width, keys_wide), BF), pltpu.VMEM((units, width), BF),
            pltpu.VMEM((width, units), BF), pltpu.VMEM((width, units), BF),
            pltpu.VMEM((heads_wide, width), BF), pltpu.VMEM((span, width), F32),
            pltpu.VMEM((rows, width), F32), pltpu.VMEM((span, units), BF),
            pltpu.VMEM((span, units), BF), pltpu.VMEM((span, units), BF),
            pltpu.VMEM((span, units), BF), pltpu.VMEM((span, heads_wide), F32),
            pltpu.VMEM((8, width), F32), pltpu.VMEM((8, width), F32),
            pltpu.VMEM((rows, width), BF), pltpu.VMEM((rows, units), BF),
            pltpu.VMEM((width, LANES), BF),
            dma(9), dma(3), dma(2, PARTS - 1), dma(8, GROUPS),
        ]
        + pair_scratch + scatter_scratch,
        26_000_000_000,
    )(
        q_low, k_low, v_low, l_low, heads_padded, x_one, grad, attention_gain,
        query_weight, key_weight, value_weight, down_weight, gate_weight, up_weight, slope, silu,
        middle_zero, feed_gain, output_weight,
        two_one, gate_low, up_low, cot_flat, hidden_one, normed_one, low, mixed_one,
    )
    below_rows = 8 * LAYERS
    stages = plane_count.bit_length() - 1 + size.bit_length() - 1
    stream_low, result, totals, *made_zero = call(
        partial(last_kernel, size, plane_sizes, 0, rows, width),
        3,
        [smem] + [WHOLE] * 14 + [WHOLE] * 7 + [ANY, ANY, WHOLE] + [ANY] * 11,
        [
            ((rows, width), BF), ((rows, width), BF), ((8 + below_rows, width), F32), *made_shapes,
        ],
        [pltpu.VMEM(shape, kind) for shape, kind in attend_back_outs]
        + attend_back_scratch
        + [
            pltpu.VMEM((width, heads_wide), BF), pltpu.VMEM((width, keys_wide), BF),
            pltpu.VMEM((width, keys_wide), BF), pltpu.VMEM((rows, width), BF),
            pltpu.VMEM((rows, width), F32), pltpu.VMEM((8, width), F32),
            pltpu.VMEM((rows, width), BF), pltpu.VMEM((rows, units), BF),
            pltpu.VMEM((8 + below_rows, width), F32), dma(6), dma(3, GROUPS),
        ]
        + landed + sum_scratch + landed + sum_scratch
        + Total.scratch(8 + below_rows, width, stages) + scatter_scratch,
        19_000_000_000,
    )(
        *attend_back_in(mixed_grad, logits_zero, saved_zero, q_raw_zero, k_raw_zero, normed_zero),
        heads_padded, gain_one, feed_zero, feed_one, q_gain_one, k_gain_one, heads_one, stream_flat,
        grad, attention_gain, query_weight, key_weight, value_weight, down_part,
        two_zero, gate_low, up_low, first_low, hidden_zero, low, mixed_zero,
    )
    stream_grad, *weights = widen(stream_low, made_zero, made_one, heads_wide, keys_wide)

    def own(array, wide_share):
        return lax.dynamic_slice_in_dim(array, here * wide_share, wide_share, array.ndim - 1)

    gains = own(totals[:4], share)
    head_gains = own(totals[4, : 4 * HD].reshape(2, 2, HD), HD // plane_count)
    heads = own(totals[8:].reshape(LAYERS, 8, width)[:, :gates], share)
    return (
        result.reshape(seq_count, row_count, width),
        stream_grad.reshape(seq_count, row_count, width),
        gains[0:2],
        weights[3],
        weights[4],
        weights[5],
        heads.transpose(0, 2, 1),
        head_gains[:, 0],
        head_gains[:, 1],
        weights[6],
        gains[2:4],
        weights[0],
        weights[1],
        weights[2],
    )


def solution(mesh):
    return jax.shard_map(
        partial(shards, mesh.shape["tensor"]),
        mesh=mesh,
        in_specs=(
            P("dp", "ctx", None),
            P("dp", "ctx", None),
            P("dp"),
            P(),
            P(None, None, "tensor"),
            P(None, None, "tensor"),
            P(None, None, "tensor"),
            P(None, None, "tensor"),
            P(),
            P(),
            P(None, "tensor", None),
            P(),
            P(None, None, "tensor"),
            P(None, None, "tensor"),
            P(None, "tensor", None),
        ),
        out_specs=(
            P("dp", "ctx", None),
            P("dp", "ctx", None),
            P(None, ("dp", "ctx")),
            P(None, ("dp", "ctx"), "tensor"),
            P(None, ("dp", "ctx"), "tensor"),
            P(None, ("dp", "ctx"), "tensor"),
            P(None, ("dp", "ctx"), "tensor"),
            P(None, ("dp", "ctx")),
            P(None, ("dp", "ctx")),
            P(None, "tensor", ("dp", "ctx")),
            P(None, ("dp", "ctx")),
            P(None, ("dp", "ctx"), "tensor"),
            P(None, ("dp", "ctx"), "tensor"),
            P(None, "tensor", ("dp", "ctx")),
        ),
        check_vma=False,
    )
```

```python
from functools import partial

import jax
import jax.numpy as jnp
from jax import lax
from jax.experimental import pallas as pl
from jax.experimental.pallas import tpu as pltpu
from jax.sharding import PartitionSpec as P

HD = 128
LAYERS = 2
LANES = 128

epsilon = 1e-06
theta = 1000000.0
masked = -1000000000.0

BF = jnp.bfloat16
F32 = jnp.float32
ANY = pl.BlockSpec(memory_space=pl.ANY)
WHOLE = pl.BlockSpec(memory_space=pltpu.VMEM)
MESH = pl.DeviceIdType.MESH

BLOCKS = 8
PIECES = 2
GROUP = 4
STRIP = 16
UNROLL = 2
VMEM_LIMIT = 63 * 1024 * 1024


def rms_scale(values, gain):
    return values * lax.rsqrt(jnp.mean(values * values, axis=-1, keepdims=True) + epsilon) * gain


def rotary_tables(positions, width):
    counter = jnp.arange(width // 2, dtype=jnp.float32)
    frequency = theta ** (-2.0 * counter / width)
    angles = positions.astype(jnp.float32)[:, None] * frequency[None, :]
    return (jnp.cos(angles), jnp.sin(angles))


def matmul(left, right):
    return jnp.dot(left, right, preferred_element_type=F32)


def weight_product(left, right):
    return lax.dot_general(left, right, (((0,), (0,)), ((), ())), preferred_element_type=F32)


def back_product(gradient, weight):
    return lax.dot_general(gradient, weight, (((1,), (1,)), ((), ())), preferred_element_type=F32)


def loop(count, body, unroll=1):
    def step(i, carry):
        body(i)
        return carry

    lax.fori_loop(0, count, step, 0, unroll=unroll)


def rows_of(r, block):
    return pl.ds(pl.multiple_of(r * block, block), block)


def columns(j, width):
    return pl.ds(pl.multiple_of(j * width, width), width)


def greet(targets, extra, has_extra):
    barrier = pltpu.get_barrier_semaphore()
    for target in targets:
        pl.semaphore_signal(barrier, inc=1, device_id=target, device_id_type=MESH)

    @pl.when(has_extra)
    def _():
        pl.semaphore_signal(barrier, inc=1, device_id=extra, device_id_type=MESH)
        pl.semaphore_wait(barrier, len(targets) + 1)

    @pl.when(jnp.logical_not(has_extra))
    def _():
        pl.semaphore_wait(barrier, len(targets))


class Chain:
    def __init__(self, size):
        self.size = size
        self.spot = lax.axis_index("tensor")
        half = size // 2
        on_left = self.spot < half
        self.end = (self.spot == 0) | (self.spot == size - 1)
        self.inner = jnp.logical_not(self.end)
        self.mid = (self.spot == half - 1) | (self.spot == half)
        self.outer = jnp.logical_not(self.mid)
        self.first_mid = self.spot == half - 1
        self.inward = {"tensor": jnp.where(on_left, self.spot + 1, self.spot - 1)}
        self.outward = {"tensor": jnp.where(on_left, self.spot - 1, self.spot + 1)}

    def greet(self, others=()):
        greet([self.inward, *others], self.outward, self.inner)


class Sum:
    def __init__(self, chain, refs, landed, rows, width):
        self.chain = chain
        self.part, self.spread, self.s_in, self.r_in, self.s_out, self.r_out, self.r_cross = refs
        self.landed, self.cross = landed
        self.block = rows // BLOCKS
        self.piece = width // PIECES

    @staticmethod
    def scratch(rows, width):
        return [
            pltpu.VMEM((rows, width), BF),
            pltpu.VMEM((rows, width), BF),
            pltpu.SemaphoreType.DMA((BLOCKS, PIECES)),
            pltpu.SemaphoreType.DMA((BLOCKS, PIECES)),
            pltpu.SemaphoreType.DMA((BLOCKS,)),
            pltpu.SemaphoreType.DMA((BLOCKS,)),
            pltpu.SemaphoreType.DMA((BLOCKS, PIECES)),
        ]

    def hop(self, r, p, across):
        where = (rows_of(r, self.block), columns(p, self.piece))
        return pltpu.make_async_remote_copy(
            src_ref=self.part.at[where],
            dst_ref=self.landed.at[(self.cross if across else 0,) + where],
            send_sem=self.s_in.at[r, p],
            recv_sem=(self.r_cross if across else self.r_in).at[r, p],
            device_id=self.chain.inward,
            device_id_type=MESH,
        )

    def out_hop(self, r):
        at = rows_of(r, self.block)
        return pltpu.make_async_remote_copy(
            src_ref=self.spread.at[at],
            dst_ref=self.spread.at[at],
            send_sem=self.s_out.at[r],
            recv_sem=self.r_out.at[r],
            device_id=self.chain.outward,
            device_id_type=MESH,
        )

    def offer(self, g):
        @pl.when(self.chain.end)
        def _():
            def one(k):
                for p in range(PIECES):
                    self.hop(g * GROUP + k, p, False).start()

            loop(GROUP, one)

    def relay(self, r):
        @pl.when(self.chain.inner)
        def _():
            for p in range(PIECES):
                self.hop(r, p, False).wait_recv()
                col = columns(p, self.piece)

                def strip(i, col=col):
                    at = pl.ds(pl.multiple_of(r * self.block + i * STRIP, STRIP), STRIP)
                    self.part[at, col] = self.part[at, col] + self.landed[0, at, col]

                loop(self.block // STRIP, strip, True)

                @pl.when(self.chain.mid)
                def _(p=p):
                    self.hop(r, p, True).start()

                @pl.when(self.chain.outer)
                def _(p=p):
                    self.hop(r, p, False).start()

    def finish(self, r, make):
        @pl.when(self.chain.mid)
        def _():
            for p in range(PIECES):
                self.hop(r, p, True).wait_recv()

            def strip(i):
                at = pl.ds(pl.multiple_of(r * self.block + i * STRIP, STRIP), STRIP)
                total = self.part[at, :].astype(F32) + self.landed[self.cross, at, :].astype(F32)
                self.spread[at, :] = make(at, total)

            loop(self.block // STRIP, strip, UNROLL)
            self.out_hop(r).start()

    def receive(self, g):
        @pl.when(self.chain.outer)
        def _():
            def one(k):
                self.out_hop(g * GROUP + k).wait_recv()

                @pl.when(self.chain.inner)
                def _():
                    self.out_hop(g * GROUP + k).start()

            loop(GROUP, one)

    def close(self):
        def block(r):
            for p in range(PIECES):
                self.hop(r, p, False).wait_send()

            @pl.when(self.chain.inner)
            def _():
                self.out_hop(r).wait_send()

        loop(BLOCKS, block)


PARTS = 4
STRIDE = GROUP // PARTS
GROUPS = BLOCKS // GROUP
STEPS = 2 * BLOCKS + 1


def two_sums(s, first, second, made_one, between, ahead, made_two, after):
    @pl.when((s >= 0) & (s < BLOCKS))
    def _():
        first.relay(s)

    @pl.when((s >= 1) & (s <= BLOCKS))
    def _():
        first.finish(s - 1, made_one)

    @pl.when((s >= GROUP) & (s < BLOCKS + GROUP))
    def _():
        place = lax.rem(s - GROUP, GROUP)
        group = lax.div(s - GROUP, GROUP)

        @pl.when(place == 0)
        def _():
            first.receive(group)

        outer = first.chain.outer
        begin = jnp.where(outer, jnp.where(place == 0, 0, PARTS), lax.div(place + STRIDE - 1, STRIDE))
        stop = jnp.where(outer, PARTS, lax.div(place, STRIDE) + 1)
        lax.fori_loop(begin, stop, lambda part, carry: (between(group, part), carry)[1], 0)

    @pl.when((s >= BLOCKS) & (s < 2 * BLOCKS))
    def _():
        second.relay(s - BLOCKS)

    @pl.when((s >= BLOCKS + 1) & (s < STEPS))
    def _():
        @pl.when(lax.rem(s - BLOCKS - 1, GROUP) == 0)
        def _():
            ahead(lax.div(s - BLOCKS - 1, GROUP))

        second.finish(s - BLOCKS - 1, made_two)

        @pl.when(lax.rem(s - BLOCKS, GROUP) == 0)
        def _():
            group = lax.div(s - BLOCKS, GROUP) - 1
            second.receive(group)
            after(group)


def back_norm(value, gain, grad):
    spread = lax.rsqrt(jnp.mean(value * value, axis=-1, keepdims=True) + epsilon)
    scaled = grad * gain
    pulled = jnp.mean(scaled * value, axis=-1, keepdims=True)
    terms = grad * value * spread
    return spread * scaled - value * (spread * spread * spread * pulled), terms


def fold(terms):
    folded = terms[:8]
    for k in range(8, terms.shape[0], 8):
        folded = folded + terms[k : k + 8]
    return folded


def load_all(pairs, sems):
    copies = [pltpu.make_async_copy(src, dst, sems.at[k]) for k, (src, dst) in enumerate(pairs)]
    for copy in copies:
        copy.start()
    return copies


def wait_all(copies):
    for copy in copies:
        copy.wait()


def wide(width):
    return 512 if width % 512 == 0 else 256


def fill(target, at, make):
    width = target.shape[1]
    tile = wide(width)

    def one(p):
        col = columns(p, tile)
        target[at, col] = make(col).astype(target.dtype)

    loop(width // tile, one)


def flip(value, bit):
    return value + bit * (1 - 2 * lax.rem(lax.div(value, bit), 2))


class Plane:
    def __init__(self, dp_size, ctx_size):
        self.count = dp_size * ctx_size
        self.ctx_size = ctx_size
        self.me = lax.axis_index("dp") * ctx_size + lax.axis_index("ctx")
        bits = [1 << k for k in range(self.count.bit_length() - 1)]
        near = [bit for bit in bits if bit >= ctx_size][:1]
        rest = [bit for bit in bits if bit not in near]
        self.bits = bits
        self.orders = (near + rest, near + rest[1:] + rest[:1])

    def partner(self, bit):
        other = flip(self.me, bit)
        return {"dp": lax.div(other, self.ctx_size), "ctx": lax.rem(other, self.ctx_size)}

    def partners(self):
        return [self.partner(bit) for bit in self.bits]


BEFORE = 6
PACE = 11
ONE_AFTER = 3
EARLY = BLOCKS + GROUP - 1
TURN_PACE = 2
OUTER_AHEAD = 4


class Scatter:
    SLOTS = (2, 6, 6, 6)
    KEPT = (2, 4, 4, 4)
    RESULTS = 2
    LAGS = (0, 1, 5, 9, 13, 17)

    def __init__(self, plane, refs, whole, parts, groups, share, tile):
        self.plane = plane
        self.whole, self.parts = whole, parts
        self.groups = groups
        self.share, self.tile = share, tile
        self.stages = len(plane.bits)
        self.units = sum(group[2] for group in groups)
        self.refs = [refs[6 * k : 6 * k + 6] for k in range(self.stages)]
        self.made, self.out_sem, self.load_sem = refs[6 * self.stages :]
        self.steps = self.units + self.LAGS[self.stages]

    @classmethod
    def scratch(cls, count, share, tile):
        found = []
        blocks = count // 2
        for k in range(count.bit_length() - 1):
            slots = cls.SLOTS[k]
            found += [
                pltpu.VMEM((depth, blocks, share, tile), BF) for depth in (slots, cls.KEPT[k], slots)
            ]
            found += [
                pltpu.SemaphoreType.DMA((slots,)),
                pltpu.SemaphoreType.DMA((slots,)),
                pltpu.SemaphoreType.REGULAR((slots,)),
            ]
            blocks //= 2
        return found + [
            pltpu.VMEM((cls.RESULTS, share, tile), BF),
            pltpu.SemaphoreType.DMA((cls.RESULTS,)),
            pltpu.SemaphoreType.DMA((4,)),
        ]

    def partner(self, stage, u):
        odd = lax.rem(u, 2) == 1
        even_one, odd_one = (self.plane.partner(order[stage]) for order in self.plane.orders)
        return {axis: jnp.where(odd, odd_one[axis], even_one[axis]) for axis in even_one}

    def copy(self, stage, u):
        send, unused, land, s_sem, r_sem, unused_credit = self.refs[stage]
        slot = lax.rem(u, self.SLOTS[stage])
        return pltpu.make_async_remote_copy(
            src_ref=send.at[slot],
            dst_ref=land.at[slot],
            send_sem=s_sem.at[slot],
            recv_sem=r_sem.at[slot],
            device_id=self.partner(stage, u),
            device_id_type=MESH,
        )

    def ready(self, stage, u):
        @pl.when(u >= self.SLOTS[stage])
        def _():
            self.copy(stage, u - self.SLOTS[stage]).wait_send()

    def push(self, stage, u):
        @pl.when(u >= self.SLOTS[stage])
        def _():
            pl.semaphore_wait(self.refs[stage][5].at[lax.rem(u, self.SLOTS[stage])], 1)

        self.copy(stage, u).start()

    def product(self, u):
        send, keep = self.refs[0][:2]
        slot, spot = lax.rem(u, self.SLOTS[0]), lax.rem(u, self.KEPT[0])
        odd = lax.rem(u, 2)
        orders = self.plane.orders
        first = 0
        place = u
        by_rows_here = u < 0
        for unused, by_rows, count, loads in self.groups:
            here = (u >= first) & (u < first + count)
            place = jnp.where(here, u - first, place)
            if by_rows:
                by_rows_here = by_rows_here | here

            @pl.when(u == first)
            def _(loads=loads):
                wait_all(load_all(loads, self.load_sem))

            first += count
        parts = self.parts[:, columns(place, self.tile)]

        def block(far, j):
            owner = flip(self.plane.me, orders[0][0]) if far else self.plane.me
            for bits in reversed(tuple(zip(*orders))[1:]):
                if j % 2:
                    owner = flip(owner, bits[0]) * (1 - odd) + flip(owner, bits[1]) * odd
                j //= 2
            return self.whole[:, columns(owner, self.share)]

        def all_blocks(make):
            for j in range(self.plane.count // 2):
                send[slot, j] = make(block(True, j)).astype(BF)
                keep[spot, j] = make(block(False, j)).astype(BF)

        @pl.when(by_rows_here)
        def _():
            all_blocks(lambda whole: weight_product(whole, parts))

        @pl.when(jnp.logical_not(by_rows_here))
        def _():
            all_blocks(lambda whole: weight_product(parts, whole))

    def merge(self, stage, u):
        unused, keep, land = self.refs[stage][:3]
        slots = self.SLOTS[stage]
        slot, spot = lax.rem(u, slots), lax.rem(u, self.KEPT[stage])
        self.copy(stage, u).wait_recv()
        half = (self.plane.count // 2) >> (stage + 1)
        last = stage == self.stages - 1
        if not last:
            self.ready(stage + 1, u)
            send_on, keep_on = self.refs[stage + 1][:2]
            slot_on = lax.rem(u, self.SLOTS[stage + 1])
            spot_on = lax.rem(u, self.KEPT[stage + 1])

            def one(j):
                send_on[slot_on, j] = keep[spot, half + j] + land[slot, half + j]
                keep_on[spot_on, j] = keep[spot, j] + land[slot, j]

            loop(half, one)
            self.push(stage + 1, u)
        else:
            place = lax.rem(u, self.RESULTS)

            @pl.when(u >= self.RESULTS)
            def _():
                self.results(u - self.RESULTS, lambda copy: copy.wait())

            self.made[place] = keep[spot, 0] + land[slot, 0]
            self.results(u, lambda copy: copy.start())

        @pl.when(u + slots < self.units)
        def _():
            pl.semaphore_signal(
                self.refs[stage][5].at[slot],
                inc=1,
                device_id=self.partner(stage, u),
                device_id_type=MESH,
            )

    def results(self, u, act):
        place = lax.rem(u, self.RESULTS)
        first = 0
        for out, by_rows, count, unused_loads in self.groups:

            @pl.when((u >= first) & (u < first + count))
            def _(by_rows=by_rows, out=out, first=first):
                if by_rows:
                    at = (slice(None), columns(u - first, self.tile))
                else:
                    at = (rows_of(u - first, self.tile), slice(None))
                act(pltpu.make_async_copy(self.made.at[place], out.at[at], self.out_sem.at[place]))

            first += count

    def tick(self, i):
        @pl.when(i < self.units)
        def _():
            self.ready(0, i)
            self.product(i)
            self.push(0, i)

        for stage in reversed(range(self.stages)):
            u = i - self.LAGS[stage + 1]

            @pl.when((u >= 0) & (u < self.units))
            def _(stage=stage, u=u):
                self.merge(stage, u)

    def close(self):
        for stage in range(self.stages):
            for k in range(max(0, self.units - self.SLOTS[stage]), self.units):
                self.copy(stage, jnp.int32(k)).wait_send()
        for k in range(max(0, self.units - self.RESULTS), self.units):
            self.results(jnp.int32(k), lambda copy: copy.wait())


class Total:
    def __init__(self, plane, size, refs, own):
        self.value, self.land, self.s_sem, self.r_sem = refs
        spot = lax.axis_index("tensor")
        rows, first = pl.ds(0, self.value.shape[1]), pl.ds(0, own)
        near, *rest = plane.orders[0]
        across = [({"tensor": flip(spot, 1 << k)}, first) for k in range(size.bit_length() - 1)]
        self.across = [target for target, unused in across]
        self.stages = [(plane.partner(near), rows), *across]
        self.stages += [(plane.partner(bit), rows) for bit in rest]
        self.times = [0, 1]
        for unused in across:
            self.times.append(self.times[-1] + 2)
        for unused in rest:
            self.times.append(self.times[-1] + 3)

    @staticmethod
    def scratch(rows, width, stages):
        return [
            pltpu.VMEM((stages, rows, width), F32),
            pltpu.VMEM((stages, rows, width), F32),
            pltpu.SemaphoreType.DMA((stages,)),
            pltpu.SemaphoreType.DMA((stages,)),
        ]

    def copy(self, k):
        target, rows = self.stages[k]
        return pltpu.make_async_remote_copy(
            src_ref=self.value.at[k, rows],
            dst_ref=self.land.at[k, rows],
            send_sem=self.s_sem.at[k],
            recv_sem=self.r_sem.at[k],
            device_id=target,
            device_id_type=MESH,
        )

    def take(self, k, target):
        self.copy(k).wait_recv()
        rows = self.stages[k][1]
        target[...] = self.value[k]
        target[rows] = self.value[k, rows] + self.land[k, rows]

    def start(self, k):
        if k > 0:
            self.take(k - 1, self.value.at[k])
        self.copy(k).start()

    def finish(self, target):
        self.take(len(self.stages) - 1, target)
        for k in range(len(self.stages)):
            self.copy(k).wait_send()


def turned(value):
    return pltpu.roll(value, HD // 2, 1)


def head_at(h):
    return pl.ds(h * HD, HD)


def head_norm(raw, gain, cos, sin):
    scaled = rms_scale(raw, gain)
    return scaled * cos + turned(scaled) * sin


def head_norm_back(raw, gain, cos, sin, grad):
    return back_norm(raw, gain, grad * cos - turned(grad) * sin)


def seen(rows, first_row, columns_wide, offset, prefix):
    query = first_row + lax.broadcasted_iota(jnp.int32, (rows, columns_wide), 0)
    key = lax.broadcasted_iota(jnp.int32, (rows, columns_wide), 1)
    return (key <= query) | (key + offset < prefix)


def key_strip(raw, v, keys, values, gain, cos, sin, j, at):
    keys[j, at, :] = head_norm(raw[at, head_at(j)], gain, cos[at, :], sin[at, :]).astype(BF)
    values[j, at, :] = v[at, head_at(j)]


def attend(prefix, q_raw, logits, query_gain, cos, sin, keys, values,
           mixed_o, q_o, norm_o, attended_o, scratch, half, arrived):
    high, low, out = scratch
    rows = q_raw.shape[0]
    span = rows // GROUPS
    key_heads = keys.shape[1]
    shared = q_raw.shape[1] // HD // key_heads
    scale = HD ** (-0.5)

    def own(g):
        at = rows_of(g, span)
        mask = seen(span, g * span, rows, half * rows, prefix)
        for h in range(key_heads * shared):
            j = h // shared
            query = head_norm(q_raw[at, head_at(h)], query_gain, cos[at, :], sin[at, :]).astype(BF)
            q_o[at, head_at(h)] = query
            scores = jnp.where(mask, back_product(query, keys[0, j]) * scale, masked)
            top = jnp.max(scores, axis=1, keepdims=True)
            weights = jnp.exp(scores - top)
            high[h, at, :] = top
            low[h, at, :] = jnp.sum(weights, axis=1, keepdims=True)
            out[at, head_at(h)] = matmul(weights.astype(BF), values[0, j])

    loop(GROUPS, own)

    @pl.when(half == 1)
    def _():
        for h in range(key_heads * shared):
            j = h // shared
            if h % shared == 0:
                arrived(j)

            def other(g, h=h, j=j):
                at = rows_of(g, span)
                scores = back_product(q_o[at, head_at(h)], keys[1, j]) * scale
                before = high[h, at, :]
                top = jnp.maximum(before, jnp.max(scores, axis=1, keepdims=True))
                weights = jnp.exp(scores - top)
                shrink = jnp.exp(before - top)
                high[h, at, :] = top
                low[h, at, :] = low[h, at, :] * shrink + jnp.sum(weights, axis=1, keepdims=True)
                out[at, head_at(h)] = out[at, head_at(h)] * shrink + matmul(
                    weights.astype(BF), values[1, j]
                )

            loop(GROUPS, other)

    def close(g):
        at = rows_of(g, span)
        open_gate = jax.nn.sigmoid(logits[at, :])
        for h in range(key_heads * shared):
            total = low[h, at, :]
            norm_o[h, at, :] = high[h, at, :] + jnp.log(total)
            attended = out[at, head_at(h)] * (1.0 / total)
            attended_o[at, head_at(h)] = attended
            mixed_o[at, head_at(h)] = (attended * open_gate[:, h : h + 1]).astype(BF)

    loop(GROUPS, close)


def attend_scratch(rows, heads_wide):
    return [
        pltpu.VMEM((heads_wide // HD, rows, 1), F32),
        pltpu.VMEM((heads_wide // HD, rows, 1), F32),
        pltpu.VMEM((rows, heads_wide), F32),
    ]


def attend_kernel(
    depth, prefix, q_raw, logits, query_gain, cos, sin, keys, values,
    mixed_o, q_o, norm_o, attended_o, *scratch,
):
    half = lax.axis_index("ctx")
    attend(prefix[0], q_raw, logits, query_gain[depth : depth + 1, :], cos, sin, keys, values,
           mixed_o, q_o, norm_o, attended_o, scratch, half, lambda j: None)


def first_kernel(
    depth, prefix, stream, gain, wq, wk, wv, gh, query_gain, key_gain, cos, sin,
    mixed_o, q_o, norm_o, attended_o, keys_o, values_o, normed_o, q_raw, k_raw, logits,
    v, wq_v, wk_v, wv_v, load_sem, send_sem, land_sem, *scratch,
):
    half = lax.axis_index("ctx")
    loads = load_all([(wk.at[depth], wk_v), (wv.at[depth], wv_v), (wq.at[depth], wq_v)], load_sem)
    greet([{"ctx": 1 - half}], {"ctx": 1 - half}, half < 0)
    rows = stream.shape[0]
    span = rows // GROUPS
    key_heads = k_raw.shape[1] // HD

    def copy(j, which):
        ref = (keys_o, values_o)[which]
        return pltpu.make_async_remote_copy(
            src_ref=ref.at[0, j],
            dst_ref=ref.at[1, j],
            send_sem=send_sem.at[j, which],
            recv_sem=land_sem.at[j, which],
            device_id={"ctx": 1 - half},
            device_id_type=MESH,
        )

    def strip(i):
        at = rows_of(i, STRIP)
        value = stream[at, :].astype(F32)
        normed_o[at, :] = rms_scale(value, gain[depth : depth + 1, :]).astype(BF)

    loop(rows // STRIP, strip, UNROLL)
    wait_all(loads[:2])

    def project_keys(g):
        at = rows_of(g, span)
        k_raw[at, :] = matmul(normed_o[at, :], wk_v[...])
        v[at, :] = matmul(normed_o[at, :], wv_v[...]).astype(BF)
        for j in range(key_heads):
            key_strip(k_raw, v, keys_o.at[0], values_o.at[0], key_gain[depth : depth + 1, :], cos, sin, j, at)

    loop(GROUPS, project_keys)

    @pl.when(half == 0)
    def _():
        for j in range(key_heads):
            copy(j, 0).start()
            copy(j, 1).start()

    loads[2].wait()

    def project(g):
        at = rows_of(g, span)
        q_raw[at, :] = matmul(normed_o[at, :], wq_v[...])
        logits[at, :] = matmul(normed_o[at, :], gh[depth])

    loop(GROUPS, project)

    def arrived(j):
        copy(j, 0).wait_recv()
        copy(j, 1).wait_recv()

    attend(prefix[0], q_raw, logits, query_gain[depth : depth + 1, :], cos, sin, keys_o, values_o,
           mixed_o, q_o, norm_o, attended_o, scratch, half, arrived)

    @pl.when(half == 0)
    def _():
        for j in range(key_heads):
            copy(j, 0).wait_send()
            copy(j, 1).wait_send()


def attend_back(
    half, depth, prefix, mixed_grad, logits, attended, q_rot, keys, values, norm, q_raw, k_raw,
    query_gain, key_gain, cos, sin, normed,
    q_o, k_o, v_o, l_o, heads_o, q_gain_o, k_gain_o,
    grad_low, inner, q_grad, k_grad, v_grad, given, landed, send_sem, land_sem,
):
    rows = q_raw.shape[0]
    span = rows // GROUPS
    key_heads = k_raw.shape[1] // HD
    shared = q_raw.shape[1] // k_raw.shape[1]
    heads = key_heads * shared
    scale = HD ** (-0.5)
    query_gain_here = query_gain[depth : depth + 1, :]
    key_gain_here = key_gain[depth : depth + 1, :]

    def copy(j):
        return pltpu.make_async_remote_copy(
            src_ref=given.at[j],
            dst_ref=landed.at[j],
            send_sem=send_sem.at[j],
            recv_sem=land_sem.at[j],
            device_id={"ctx": 1 - half},
            device_id_type=MESH,
        )

    def gate_back(g):
        at = rows_of(g, span)
        open_gate = jax.nn.sigmoid(logits[at, :])
        lane = lax.broadcasted_iota(jnp.int32, (span, LANES), 1)
        pulled = jnp.zeros((span, LANES), F32)
        for h in range(heads):
            grad = mixed_grad[at, head_at(h)]
            here = attended[at, head_at(h)]
            low_grad = (grad * open_gate[:, h : h + 1]).astype(BF)
            grad_low[at, head_at(h)] = low_grad
            inner[h, at, :] = jnp.sum(low_grad.astype(F32) * here, axis=1, keepdims=True)
            pulled = jnp.where(lane == h, jnp.sum(grad * here, axis=1, keepdims=True), pulled)
        l_o[at, :] = (pulled * (open_gate * (1.0 - open_gate))).astype(BF)

    def gates():
        loop(GROUPS, gate_back)
        heads_o[...] = weight_product(l_o[...], normed[...])[: heads_o.shape[0], :]

    def back(j, side, mask_of, first):
        k_grad[j] = jnp.zeros((rows, HD), F32)
        v_grad[j] = jnp.zeros((rows, HD), F32)

        def block(g):
            at = rows_of(g, span)
            for h in range(j * shared, (j + 1) * shared):
                query = q_rot[at, head_at(h)]
                pulled = grad_low[at, head_at(h)]
                scores = back_product(query, keys[side, j]) * scale
                if mask_of is not None:
                    scores = jnp.where(mask_of(g), scores, masked)
                weights = jnp.exp(scores - norm[h, at, :])
                slope = back_product(pulled, values[side, j])
                score_low = (weights * (slope - inner[h, at, :])).astype(BF)
                moved = matmul(score_low, keys[side, j])
                if first:
                    q_grad[at, head_at(h)] = moved
                else:
                    q_grad[at, head_at(h)] += moved
                k_grad[j] += weight_product(score_low, query)
                v_grad[j] += weight_product(weights.astype(BF), pulled)

        loop(GROUPS, block)

    def other(j):
        @pl.when(half == 1)
        def _():
            back(j, 1, None, True)
            given[j, 0] = (k_grad[j] * scale).astype(BF)
            given[j, 1] = v_grad[j].astype(BF)
            copy(j).start()

        @pl.when(half == 0)
        def _():
            wide_head = pl.ds(j * shared * HD, shared * HD)
            q_grad[:, wide_head] = jnp.zeros((rows, shared * HD), F32)

    def own(j):
        back(j, 0, lambda g: seen(span, g * span, rows, half * rows, prefix[0]), False)

    def query_rows(g):
        at = rows_of(g, span)
        for h in range(heads):
            pulled, terms = head_norm_back(
                q_raw[at, head_at(h)], query_gain_here, cos[at, :], sin[at, :],
                q_grad[at, head_at(h)] * scale,
            )
            q_o[at, head_at(h)] = pulled.astype(BF)
            q_gain_o[...] += jnp.sum(terms.reshape(span // 8, 8, HD), axis=0)

    def queries():
        q_gain_o[...] = jnp.zeros_like(q_gain_o)
        loop(GROUPS, query_rows)

    def keys_of(j):
        if j == 0:
            k_gain_o[...] = jnp.zeros_like(k_gain_o)

        @pl.when(half == 0)
        def _(j=j):
            copy(j).wait_recv()

        def key_rows(g, j=j):
            at = rows_of(g, span)
            k_total = k_grad[j, at, :] * scale
            v_total = v_grad[j, at, :]
            k_grad[j, at, :] = k_total
            v_o[at, head_at(j)] = v_total.astype(BF)

            @pl.when(half == 0)
            def _():
                k_grad[j, at, :] = k_total + landed[j, 0, at, :].astype(F32)
                v_o[at, head_at(j)] = (v_total + landed[j, 1, at, :].astype(F32)).astype(BF)

            pulled, terms = head_norm_back(
                k_raw[at, head_at(j)], key_gain_here, cos[at, :], sin[at, :], k_grad[j, at, :]
            )
            k_o[at, head_at(j)] = pulled.astype(BF)
            k_gain_o[...] += jnp.sum(terms.reshape(span // 8, 8, HD), axis=0)

        loop(GROUPS, key_rows)

    def close():
        @pl.when(half == 1)
        def _():
            for j in range(key_heads):
                copy(j).wait_send()

    heads_each = range(key_heads)
    return (
        [gates]
        + [partial(other, j) for j in heads_each]
        + [partial(own, j) for j in heads_each]
        + [queries]
        + [partial(keys_of, j) for j in heads_each],
        close,
    )


def forward_kernel(
    size, depth, rows, width,
    mixed, stream, wo, feed_gain, wg, wu, wd, next_gain, wq, wk, wv, gh, key_gain, cos, sin,
    middle_o, two_o, slope_o, silu_o, hidden_o, x_o, normed_o, q_o, k_o, logit_o, keys_o, values_o,
    *scratch,
):
    (wo_v, wg_v, wu_v, wd_v, wq_v, wk_v, wv_v, x_v, middle_v, slope_v, silu_v, hidden_v, q_v, k_v,
     v_v, logit_v, load_sem, out_sem, keys_v, values_v, keep_sem, send_sem, land_sem) = scratch[:23]
    half = lax.axis_index("ctx")
    key_heads = keys_v.shape[0]
    chain = Chain(size)
    landed = scratch[23]
    one = Sum(chain, scratch[24:31], (landed, 1), rows, width)
    two = Sum(chain, scratch[31:38], (landed, 2), rows, width)
    span = one.block * GROUP
    loads = load_all(
        [(wo.at[depth], wo_v), (stream, x_v), (wg.at[depth], wg_v), (wu.at[depth], wu_v),
         (wd.at[depth], wd_v), (wq.at[depth + 1], wq_v), (wk.at[depth + 1], wk_v),
         (wv.at[depth + 1], wv_v)],
        load_sem,
    )
    chain.greet([{"ctx": 1 - half}])
    tile = wg_v.shape[1] // (PARTS - 1)
    gain_one = feed_gain[depth : depth + 1, :]
    gain_two = next_gain[depth + 1 : depth + 2, :]

    def out(k, g, src, dst):
        at = rows_of(g, span)
        return pltpu.make_async_copy(src.at[at], dst.at[at], out_sem.at[k, g])

    def keep_keys(g, which):
        at = rows_of(g, span)
        src, dst = ((keys_v, keys_o), (values_v, values_o))[which]
        return pltpu.make_async_copy(src.at[:, at], dst.at[0, :, at], keep_sem.at[which, g])

    def give_keys(g, which):
        at = rows_of(g, span)
        src, dst = ((keys_v, keys_o), (values_v, values_o))[which]
        return pltpu.make_async_remote_copy(
            src_ref=src.at[:, at],
            dst_ref=dst.at[1, :, at],
            send_sem=send_sem.at[which, g],
            recv_sem=land_sem.at[which, g],
            device_id={"ctx": 1 - half},
            device_id_type=MESH,
        )

    loads[0].wait()

    def start(g):
        at = rows_of(g, span)
        fill(one.part, at, lambda col: matmul(mixed[at, :], wo_v[:, col]))
        one.offer(g)

    loop(GROUPS, start)
    wait_all(loads[1:5])

    def made_one(at, total):
        value = x_v[at, :].astype(F32) + total
        middle_v[at, :] = value
        return rms_scale(value, gain_one).astype(BF)

    def between(g, part):
        at = rows_of(g, span)

        @pl.when(part == 0)
        def _():
            out(1, g, one.spread, two_o).start()

            @pl.when(chain.mid)
            def _():
                out(0, g, middle_v, middle_o).start()

        @pl.when(part < PARTS - 1)
        def _():
            col = columns(part, tile)
            gate = matmul(one.spread[at, :], wg_v[:, col])
            up = matmul(one.spread[at, :], wu_v[:, col])
            sig = jax.nn.sigmoid(gate)
            act = gate * sig
            hidden_v[at, col] = (act * up).astype(BF)
            silu_v[at, col] = act.astype(BF)
            slope_v[at, col] = (up * (sig * (1.0 + gate * (1.0 - sig)))).astype(BF)

        @pl.when(part == PARTS - 1)
        def _():
            fill(two.part, at, lambda col: matmul(hidden_v[at, :], wd_v[:, col]))
            two.offer(g)
            out(2, g, slope_v, slope_o).start()
            out(3, g, silu_v, silu_o).start()
            out(4, g, hidden_v, hidden_o).start()

    def ahead(g):
        @pl.when(g == 0)
        def _():
            wait_all(loads[5:])

        @pl.when(chain.mid)
        def _():
            out(0, g, middle_v, middle_o).wait()

    def made_two(at, total):
        value = middle_v[at, :] + total
        middle_v[at, :] = value
        return rms_scale(value, gain_two).astype(BF)

    def after(g):
        at = rows_of(g, span)

        @pl.when(chain.mid)
        def _():
            out(5, g, middle_v, x_o).start()

        k_v[at, :] = matmul(two.spread[at, :], wk_v[...])
        v_v[at, :] = matmul(two.spread[at, :], wv_v[...]).astype(BF)
        for j in range(key_heads):
            key_strip(k_v, v_v, keys_v, values_v, key_gain[depth + 1 : depth + 2, :], cos, sin, j, at)

        @pl.when(half == 0)
        def _():
            give_keys(g, 0).start()
            give_keys(g, 1).start()

        keep_keys(g, 0).start()
        keep_keys(g, 1).start()
        out(8, g, k_v, k_o).start()
        q_v[at, :] = matmul(two.spread[at, :], wq_v[...])
        out(7, g, q_v, q_o).start()
        logit_v[at, :] = matmul(two.spread[at, :], gh[depth + 1])
        out(10, g, logit_v, logit_o).start()
        out(6, g, two.spread, normed_o).start()

    loop(STEPS, lambda s: two_sums(s, one, two, made_one, between, ahead, made_two, after))
    one.close()
    two.close()

    def drain(g):
        @pl.when(chain.mid)
        def _():
            out(5, g, middle_v, x_o).wait()

        for k, src, dst in (
            (1, one.spread, two_o), (2, slope_v, slope_o), (3, silu_v, silu_o),
            (4, hidden_v, hidden_o), (6, two.spread, normed_o), (7, q_v, q_o),
            (8, k_v, k_o), (10, logit_v, logit_o),
        ):
            out(k, g, src, dst).wait()
        for which in range(2):
            keep_keys(g, which).wait()

            @pl.when(half == 0)
            def _(which=which):
                give_keys(g, which).wait_send()

            @pl.when(half == 1)
            def _(which=which):
                give_keys(g, which).wait_recv()

    loop(GROUPS, drain)


def turn_kernel(
    size, plane_sizes, depth, rows, width,
    mixed, x_in, cot, wo, feed_gain, wg, wu, wd,
    two_o, down_o, gate_o, up_o, grad_o, low_o, mixed_o, gain_o, made_o,
    *scratch,
):
    (wo_v, wg_v, wu_v, wd_v, middle_v, cot_v, hidden_v, gate_v, up_v, mixed_v, down_v, gain_v,
     load_sem, out_sem) = scratch[:14]
    chain = Chain(size)
    landed = scratch[14]
    one = Sum(chain, scratch[15:22], (landed, 1), rows, width)
    two = Sum(chain, scratch[22:29], (landed, 2), rows, width)
    plane = Plane(*plane_sizes)
    unit = made_o.shape[1] if made_o.shape[1] < 256 else 256
    scatter = Scatter(
        plane, scratch[29:], cot_v, hidden_v, [(made_o, False, hidden_v.shape[1] // unit, [])],
        width // plane.count, unit,
    )
    span = one.block * GROUP
    loads = load_all(
        [(wo.at[depth], wo_v), (x_in, middle_v), (cot, cot_v), (wg.at[depth], wg_v),
         (wu.at[depth], wu_v), (wd.at[depth], wd_v)],
        load_sem,
    )
    chain.greet(plane.partners())
    tile = wg_v.shape[1] // (PARTS - 1)
    gain_one = feed_gain[depth : depth + 1, :]

    def out(k, g, src, dst):
        at = rows_of(g, span)
        return pltpu.make_async_copy(src.at[at], dst.at[at], out_sem.at[k, g])

    loads[0].wait()

    def start(g):
        at = rows_of(g, span)
        fill(one.part, at, lambda col: matmul(mixed[at, :], wo_v[:, col]))
        one.offer(g)

    loop(GROUPS, start)
    gain_v[...] = jnp.zeros_like(gain_v)
    wait_all(loads[1:])

    def made_one(at, total):
        value = middle_v[at, :] + total
        middle_v[at, :] = value
        return rms_scale(value, gain_one).astype(BF)

    def between(g, part):
        at = rows_of(g, span)

        @pl.when(part == 0)
        def _():
            out(0, g, one.spread, two_o).start()

        @pl.when(part < PARTS - 1)
        def _():
            col = columns(part, tile)
            gate = matmul(one.spread[at, :], wg_v[:, col])
            sig = jax.nn.sigmoid(gate)
            act = gate * sig
            slope = sig * (1.0 + gate * (1.0 - sig))
            up = matmul(one.spread[at, :], wu_v[:, col])
            hidden_v[at, col] = (act * up).astype(BF)
            pulled = back_product(cot_v[at, :], wd_v[col, :])
            gate_v[at, col] = (pulled * up * slope).astype(BF)
            up_v[at, col] = (pulled * act).astype(BF)

        @pl.when(part == PARTS - 1)
        def _():
            fill(
                two.part,
                at,
                lambda col: back_product(gate_v[at, :], wg_v[col, :])
                + back_product(up_v[at, :], wu_v[col, :]),
            )
            two.offer(g)
            out(2, g, gate_v, gate_o).start()
            out(3, g, up_v, up_o).start()

    def ahead(g):
        at = rows_of(g, span)
        share = jnp.where(chain.first_mid, 1.0, 0.0)

        @pl.when(chain.first_mid)
        def _():
            fill(down_v, at, lambda col: matmul(hidden_v[at, :], wd_v[:, col]) + middle_v[at, col])

        @pl.when(jnp.logical_not(chain.first_mid))
        def _():
            fill(down_v, at, lambda col: matmul(hidden_v[at, :], wd_v[:, col]))

        out(4, g, down_v, down_o).start()

    def made_two(at, total):
        pulled, terms = back_norm(middle_v[at, :], gain_one, total)
        gain_v[...] += fold(terms)
        value = cot_v[at, :].astype(F32) + pulled
        middle_v[at, :] = value
        return value.astype(BF)

    def after(g):
        at = rows_of(g, span)

        @pl.when(chain.mid)
        def _():
            out(5, g, middle_v, grad_o).start()

        out(6, g, two.spread, low_o).start()
        mixed_v[at, :] = back_product(two.spread[at, :], wo_v[...])
        out(7, g, mixed_v, mixed_o).start()


    def step(s):
        two_sums(s, one, two, made_one, between, ahead, made_two, after)
        ahead_ticks = jnp.where(chain.outer, OUTER_AHEAD, 0)

        def ticks_before(s):
            return jnp.where(s > EARLY, (s - EARLY) * TURN_PACE + ahead_ticks, 0)

        lax.fori_loop(
            ticks_before(s), ticks_before(s + 1), lambda t, carry: (scatter.tick(t), carry)[1], 0
        )

    loop(max(STEPS, EARLY + -(-scatter.steps // TURN_PACE)), step)

    @pl.when(jnp.logical_not(chain.first_mid))
    def _():
        gain_v[...] = jnp.zeros_like(gain_v)

    gain_out = pltpu.make_async_copy(gain_v, gain_o, out_sem.at[8, 0])
    gain_out.start()
    one.close()
    two.close()
    scatter.close()

    def drain(g):
        @pl.when(chain.mid)
        def _():
            out(5, g, middle_v, grad_o).wait()

        for k, src, dst in (
            (0, one.spread, two_o), (2, gate_v, gate_o), (3, up_v, up_o), (4, down_v, down_o),
            (6, two.spread, low_o), (7, mixed_v, mixed_o),
        ):
            out(k, g, src, dst).wait()

    loop(GROUPS, drain)
    gain_out.wait()


def back_kernel(
    size, plane_sizes, depth, rows, width,
    *refs,
):
    (prefix, mixed_grad, logits, attended, q_rot, keys, values, norm, q_raw, k_raw, query_gain, key_gain,
     cos, sin, normed_in, gh, x_in, grad_in, attention_gain, wq, wk, wv,
     wd, wg, wu, slope_in, silu_in, middle_in, feed_gain, wo,
     two_in, gate_in, up_in, low_in, mixed_in,
     gate_o, up_o, first_o, grad_o, low_o, mixed_o, gain_o, feed_gain_o, heads_o, q_gain_o, k_gain_o,
     *rest) = refs
    made, scratch = rest[:4], rest[4:]
    attend_made, attend_scratch, scratch = scratch[:7], scratch[7:15], scratch[15:]
    q_low, k_low, v_low, l_low, heads_v, q_gain_v, k_gain_v = attend_made
    (wq_v, wk_v, wv_v, ring_v, wo_v, x_v, grad_v, slope_v, silu_v, gate_v, up_v, mixed_v,
     gain_v, feed_v, whole_v, parts_v, gh_v, load_sem, row_sem, tile_sem, out_sem, ring_sem, attend_sem,
     ) = scratch[:23]
    half = lax.axis_index("ctx")
    chain = Chain(size)
    landed = scratch[23]
    one = Sum(chain, scratch[24:31], (landed, 1), rows, width)
    two = Sum(chain, scratch[31:38], (landed, 2), rows, width)
    plane = Plane(*plane_sizes)
    share = width // plane.count
    unit = min(256, wk_v.shape[1])
    units_wide, heads_wide, keys_wide = gate_v.shape[1], wq_v.shape[1], wk_v.shape[1]
    mixed_grad_v, attended_v, q_raw_v, q_grad_v = (
        grad_v.at[:, pl.ds(quarter * heads_wide, heads_wide)] for quarter in range(4)
    )
    normed_v = two.part
    grad_low, inner, k_grad, v_grad, *given = attend_scratch
    pieces, close_attend = attend_back(
        half, depth, prefix, mixed_grad_v, logits, attended_v, q_rot, keys, values, norm, q_raw_v, k_raw,
        query_gain, key_gain, cos, sin, normed_v, *attend_made,
        grad_low, inner, q_grad_v, k_grad, v_grad, *given,
    )
    parts_heads = parts_v.at[:, pl.ds(0, heads_wide)]
    heads_parts = [
        (q_low, parts_heads),
        (k_low, parts_v.at[:, pl.ds(heads_wide, keys_wide)]),
        (v_low, parts_v.at[:, pl.ds(heads_wide + keys_wide, keys_wide)]),
    ]
    scatter = Scatter(
        plane, scratch[38:], whole_v, parts_v,
        [
            (made[0], True, units_wide // unit, [(two_in, whole_v), (gate_in, parts_v)]),
            (made[1], True, units_wide // unit, [(up_in, parts_v)]),
            (made[2], True, (heads_wide + 2 * keys_wide) // unit, [(normed_in, whole_v), *heads_parts]),
            (made[3], False, heads_wide // unit, [(low_in, whole_v), (mixed_in, parts_heads)]),
        ],
        share, unit,
    )
    span = one.block * GROUP
    below = depth - 1
    attend_loads = load_all(
        [(mixed_grad, mixed_grad_v), (attended, attended_v), (normed_in, normed_v), (q_raw, q_raw_v)],
        attend_sem,
    )
    loads = load_all(
        [(wq.at[depth], wq_v), (wk.at[depth], wk_v), (wv.at[depth], wv_v), (gh.at[depth], gh_v),
         (wo.at[below], wo_v)],
        load_sem,
    )
    grad_load = pltpu.make_async_copy(grad_in, grad_v, load_sem.at[5])

    def row_load(src, g, k):
        return pltpu.make_async_copy(src.at[rows_of(g, span)], x_v, row_sem.at[k])

    tile = units_wide // (PARTS - 1)
    strip_wide = wide(width)
    fetches = PARTS - 1 + 2 * (width // strip_wide)
    slots = ring_v.shape[0]

    def fetch(k, act):
        slot, place = lax.rem(k, slots), lax.rem(k, fetches)
        pair = jnp.maximum(place - (PARTS - 1), 0)

        @pl.when(place < PARTS - 1)
        def _():
            src = wd.at[below, rows_of(place, tile)]
            act(pltpu.make_async_copy(src, ring_v.at[slot, pl.ds(0, tile)], ring_sem.at[slot]))

        for which, weight in enumerate((wg, wu)):

            @pl.when((place >= PARTS - 1) & (lax.rem(pair, 2) == which))
            def _(weight=weight):
                src = weight.at[below, rows_of(lax.div(pair, 2), strip_wide)]
                dst = ring_v.at[slot, :, pl.ds(0, units_wide)]
                act(pltpu.make_async_copy(src, dst, ring_sem.at[slot]))

    def fetched(k):
        fetch(k, lambda copy: copy.wait())

    def used(k):
        @pl.when(k + slots < GROUPS * fetches)
        def _():
            fetch(k + slots, lambda copy: copy.start())

    for k in range(slots):
        fetch(jnp.int32(k), lambda copy: copy.start())

    def tile_load(src, dst, g, part, k):
        col = columns(part, tile)
        return pltpu.make_async_copy(
            src.at[rows_of(g, span), col], dst.at[:, col], tile_sem.at[k, part]
        )

    row_load(x_in, 0, 0).start()

    def first_tiles(part):
        tile_load(slope_in, slope_v, 0, part, 0).start()
        tile_load(silu_in, silu_v, 0, part, 1).start()

    loop(PARTS - 1, first_tiles)
    chain.greet([*plane.partners(), {"ctx": 1 - half}])
    wait_all(attend_loads)
    gain_one = attention_gain[depth : depth + 1, :]
    gain_two = feed_gain[below : below + 1, :]

    def out(k, g, src, dst, whole=True):
        at = rows_of(g, span)
        return pltpu.make_async_copy(src.at[at] if whole else src, dst.at[at], out_sem.at[k, g])

    def start(g):
        at = rows_of(g, span)
        fill(
            one.part,
            at,
            lambda col: back_product(q_low[at, :], wq_v[col, :])
            + back_product(k_low[at, :], wk_v[col, :])
            + back_product(v_low[at, :], wv_v[col, :])
            + back_product(l_low[at, :], gh_v[col, :]),
        )
        one.offer(g)

    gain_v[...] = jnp.zeros_like(gain_v)
    feed_v[...] = jnp.zeros_like(feed_v)

    def start_all():
        grad_load.start()
        wait_all(loads)
        loop(GROUPS, start)
        row_load(x_in, 0, 0).wait()
        grad_load.wait()

    def local(at):
        return pl.ds(pl.multiple_of(lax.rem(at.start, span), STRIP), STRIP)

    def made_one(at, total):
        pulled, terms = back_norm(x_v[local(at), :], gain_one, total)
        gain_v[...] += fold(terms)
        value = grad_v[at, :] + pulled
        grad_v[at, :] = value
        return value.astype(BF)

    def between(g, part):
        at = rows_of(g, span)

        @pl.when(part == 0)
        def _():
            out(0, g, one.spread, first_o).start()

            @pl.when(g < GROUPS - 1)
            def _():
                copy = row_load(x_in, g + 1, 1)
                copy.start()
                copy.wait()

            @pl.when(g > 0)
            def _():
                out(1, g - 1, gate_v, gate_o, False).wait()
                out(2, g - 1, up_v, up_o, False).wait()

        @pl.when(part < PARTS - 1)
        def _():
            col = columns(part, tile)
            tile_load(slope_in, slope_v, g, part, 0).wait()
            tile_load(silu_in, silu_v, g, part, 1).wait()
            k = g * fetches + part
            fetched(k)
            weight = ring_v[lax.rem(k, slots), pl.ds(0, tile), :]
            pulled = back_product(one.spread[at, :], weight)
            used(k)
            gate_v[:, col] = (pulled * slope_v[:, col].astype(F32)).astype(BF)
            up_v[:, col] = (pulled * silu_v[:, col].astype(F32)).astype(BF)

            @pl.when(g < GROUPS - 1)
            def _():
                tile_load(slope_in, slope_v, g + 1, part, 0).start()
                tile_load(silu_in, silu_v, g + 1, part, 1).start()

        @pl.when(part == PARTS - 1)
        def _():
            def pair(p):
                k = g * fetches + PARTS - 1 + 2 * p
                fetched(k)
                fetched(k + 1)
                here = pl.ds(0, units_wide)
                two.part[at, columns(p, strip_wide)] = (
                    back_product(gate_v[...], ring_v[lax.rem(k, slots), :, here])
                    + back_product(up_v[...], ring_v[lax.rem(k + 1, slots), :, here])
                ).astype(BF)
                used(k)
                used(k + 1)

            loop(width // strip_wide, pair)
            two.offer(g)
            out(1, g, gate_v, gate_o, False).start()
            out(2, g, up_v, up_o, False).start()

    def ahead(g):
        copy = row_load(middle_in, g, 2)
        copy.start()
        copy.wait()

    def made_two(at, total):
        pulled, terms = back_norm(x_v[local(at), :], gain_two, total)
        feed_v[...] += fold(terms)
        value = grad_v[at, :] + pulled
        grad_v[at, :] = value
        return value.astype(BF)

    def after(g):
        at = rows_of(g, span)

        @pl.when(chain.mid)
        def _():
            out(5, g, grad_v, grad_o).start()

        out(3, g, two.spread, low_o).start()

        @pl.when(g > 0)
        def _():
            out(4, g - 1, mixed_v, mixed_o, False).wait()

        mixed_v[...] = back_product(two.spread[at, :], wo_v[...])
        out(4, g, mixed_v, mixed_o, False).start()

    lead = len(pieces)

    def ticks_before(i):
        since = i - lead - 1
        return jnp.where(since < 0, lax.div(i + 1, 2), BEFORE + lax.div(since * PACE, 8))

    def step(i):
        for place, piece in enumerate(pieces):
            pl.when(i == place)(piece)
        pl.when(i == lead)(start_all)
        two_sums(i - lead - 1, one, two, made_one, between, ahead, made_two, after)
        lax.fori_loop(
            ticks_before(i), ticks_before(i + 1), lambda t, carry: (scatter.tick(t), carry)[1], 0
        )

    steps = lead + 1 + STEPS
    while BEFORE + (steps - lead - 1) * PACE // 8 < scatter.steps:
        steps += 1
    loop(steps, step)
    close_attend()

    @pl.when(jnp.logical_not(chain.first_mid))
    def _():
        gain_v[...] = jnp.zeros_like(gain_v)
        feed_v[...] = jnp.zeros_like(feed_v)

    gain_out = pltpu.make_async_copy(gain_v, gain_o, out_sem.at[6, 0])
    feed_out = pltpu.make_async_copy(feed_v, feed_gain_o, out_sem.at[7, 0])
    gain_out.start()
    feed_out.start()
    attend_outs = [
        pltpu.make_async_copy(src, dst, attend_sem.at[place])
        for place, (src, dst) in enumerate(
            ((heads_v, heads_o), (q_gain_v, q_gain_o), (k_gain_v, k_gain_o))
        )
    ]
    for copy in attend_outs:
        copy.start()
    one.close()
    two.close()
    scatter.close()

    def drain(g):
        out(0, g, one.spread, first_o).wait()
        out(3, g, two.spread, low_o).wait()

        @pl.when(chain.mid)
        def _():
            out(5, g, grad_v, grad_o).wait()

    loop(GROUPS, drain)
    out(1, GROUPS - 1, gate_v, gate_o, False).wait()
    out(2, GROUPS - 1, up_v, up_o, False).wait()
    out(4, GROUPS - 1, mixed_v, mixed_o, False).wait()
    gain_out.wait()
    feed_out.wait()
    wait_all(attend_outs)


def last_kernel(
    size, plane_sizes, depth, rows, width,
    *refs,
):
    attend_in, refs = refs[:15], refs[15:]
    (gh, gain_one_in, feed_zero_in, feed_one_in, q_gain_one, k_gain_one, heads_one, x_in, grad_in,
     attention_gain, wq, wk, wv, down_in, two_in, gate_in, up_in, first_in, hidden_in, low_in, mixed_in,
     grad_o, result_o, total_o, *rest) = refs
    normed_in = attend_in[14]
    made, rest = rest[:5], rest[5:]
    attend_made, attend_scratch, scratch = rest[:7], rest[7:16], rest[16:]
    q_low, k_low, v_low, l_low, heads_zero, q_gain_zero, k_gain_zero = attend_made
    half = lax.axis_index("ctx")
    pieces, close_attend = attend_back(half, depth, *attend_in, *attend_made, *attend_scratch)
    (wq_v, wk_v, wv_v, x_v, grad_v, gain_v, whole_v, parts_v, total_v, load_sem, out_sem) = scratch[:11]
    chain = Chain(size)
    one = Sum(chain, scratch[12:19], (scratch[11], 1), rows, width)
    two = Sum(chain, scratch[20:27], (scratch[19], 1), rows, width)
    plane = Plane(*plane_sizes)
    total = Total(plane, size, scratch[27:31], 8)
    share = width // plane.count
    units_wide, heads_wide, keys_wide = parts_v.shape[1], wq_v.shape[1], wk_v.shape[1]
    unit = min(256, keys_wide)
    parts_heads = parts_v.at[:, pl.ds(0, heads_wide)]
    heads_parts = [
        (q_low, parts_heads),
        (k_low, parts_v.at[:, pl.ds(heads_wide, keys_wide)]),
        (v_low, parts_v.at[:, pl.ds(heads_wide + keys_wide, keys_wide)]),
    ]
    scatter = Scatter(
        plane, scratch[31:], whole_v, parts_v,
        [
            (made[0], True, units_wide // unit, [(two_in, whole_v), (gate_in, parts_v)]),
            (made[1], True, units_wide // unit, [(up_in, parts_v)]),
            (made[2], False, units_wide // unit, [(first_in, whole_v), (hidden_in, parts_v)]),
            (made[3], True, (heads_wide + 2 * keys_wide) // unit, [(normed_in, whole_v), *heads_parts]),
            (made[4], False, heads_wide // unit, [(low_in, whole_v), (mixed_in, parts_heads)]),
        ],
        share, unit,
    )
    span = one.block * GROUP
    loads = load_all(
        [(wq.at[depth], wq_v), (wk.at[depth], wk_v), (wv.at[depth], wv_v), (x_in, x_v),
         (grad_in, grad_v), (down_in, two.part)],
        load_sem,
    )
    chain.greet([*plane.partners(), *total.across, {"ctx": 1 - half}])
    gain_one = attention_gain[depth : depth + 1, :]

    def out(k, g):
        at = rows_of(g, span)
        src, dst = ((one.spread, grad_o), (two.spread, result_o))[k]
        return pltpu.make_async_copy(src.at[at], dst.at[at], out_sem.at[k, g])

    def start(g):
        at = rows_of(g, span)
        fill(
            one.part,
            at,
            lambda col: back_product(q_low[at, :], wq_v[col, :])
            + back_product(k_low[at, :], wk_v[col, :])
            + back_product(v_low[at, :], wv_v[col, :])
            + back_product(l_low[at, :], gh[depth, col, :]),
        )
        one.offer(g)

    gain_v[...] = jnp.zeros_like(gain_v)

    def made_one(at, total_sum):
        pulled, terms = back_norm(x_v[at, :].astype(F32), gain_one, total_sum)
        gain_v[...] += fold(terms)
        return (grad_v[at, :] + pulled).astype(BF)

    def made_two(at, total_sum):
        return total_sum.astype(BF)

    begin = len(pieces)
    first_two, first_one = 3, begin + ONE_AFTER
    sum_ticks = 4 * -(-(BLOCKS + 1) // 3)
    first_total = first_one + sum_ticks - 1
    rest_two = first_one + 4 * -(-BLOCKS // 3) - 4

    def sums(i):
        @pl.when(i == 0)
        def _():
            loads[5].wait()
            two.offer(0)

        for place, piece in enumerate(pieces):
            pl.when(i == place)(piece)

        @pl.when(i == begin)
        def _():
            wait_all(loads[:5])
            loop(GROUPS, start)
            two.offer(1)

        def one_step(k, sum_here, make, s):
            @pl.when((s >= 0) & (s < BLOCKS))
            def _():
                sum_here.relay(s)

            @pl.when((s >= 1) & (s <= BLOCKS))
            def _():
                sum_here.finish(s - 1, make)

                @pl.when(lax.rem(s, GROUP) == 0)
                def _():
                    group = lax.div(s, GROUP) - 1
                    sum_here.receive(group)
                    out(k, group).start()

        def paced(k, sum_here, make, first, begin_step, end_step):
            since = i - first
            take = lax.rem(since, 4)
            s = lax.div(since, 4) * 3 + take + begin_step

            @pl.when((since >= 0) & (take < 3) & (s < end_step))
            def _():
                one_step(k, sum_here, make, s)

        paced(1, two, made_two, first_two, 0, GROUP)
        paced(0, one, made_one, first_one, 0, BLOCKS + 1)
        paced(1, two, made_two, rest_two, GROUP, BLOCKS + 1)

    def totals(i):
        @pl.when(i == first_total)
        def _():
            total.value[0] = jnp.zeros(total_v.shape, F32)

            @pl.when(chain.first_mid)
            def _():
                total.value[0, pl.ds(0, 1)] = jnp.sum(gain_v[...], axis=0, keepdims=True)

            for k, gains in enumerate((gain_one_in, feed_zero_in, feed_one_in)):
                total.value[0, pl.ds(k + 1, 1)] = jnp.sum(gains[...], axis=0, keepdims=True)
            for k, gains in enumerate((q_gain_zero, k_gain_zero, q_gain_one, k_gain_one)):
                total.value[0, pl.ds(4, 1), pl.ds(k * HD, HD)] = jnp.sum(
                    gains[...], axis=0, keepdims=True
                )
            for k, heads in enumerate((heads_zero, heads_one)):
                total.value[0, pl.ds(8 + 4 * k, 4)] = heads[pl.ds(0, 4), :]

        for k in range(len(total.stages)):

            @pl.when(i == first_total + total.times[k])
            def _(k=k):
                total.start(k)

    def step(i):
        scatter.tick(i)
        sums(i)
        totals(i)

    last_two = rest_two + 4 * -(-(BLOCKS + 1 - GROUP) // 3)
    loop(max(scatter.steps, last_two, first_total + total.times[-1]), step)
    close_attend()
    total.finish(total_v)
    total_out = pltpu.make_async_copy(total_v, total_o, out_sem.at[2, 0])
    total_out.start()
    one.close()
    two.close()
    scatter.close()

    def drain(g):
        out(0, g).wait()
        out(1, g).wait()

    loop(GROUPS, drain)
    total_out.wait()


def widen_kernel(heads_wide, keys_wide, low_in, *refs):
    below, above = refs[0:5], refs[5:10]
    stream_o, gate_o, up_o, down_o, q_o, k_o, v_o, out_o = refs[10:]
    stream_o[...] = low_in[...].astype(F32)
    for depth, made in enumerate((below, above)):
        gate_o[depth] = made[0][...].astype(F32)
        up_o[depth] = made[1][...].astype(F32)
        down_o[depth] = made[2][...].astype(F32)
        q_o[depth] = made[3][:, :heads_wide].astype(F32)
        k_o[depth] = made[3][:, heads_wide : heads_wide + keys_wide].astype(F32)
        v_o[depth] = made[3][:, heads_wide + keys_wide :].astype(F32)
        out_o[depth] = made[4][...].astype(F32)


def widen(stream_low, below, above, heads_wide, keys_wide):
    cuts = 4

    def cut(shape):
        return pl.BlockSpec((shape[0] // cuts, shape[1]), lambda i: (i, 0))

    def pair(shape):
        return pl.BlockSpec((2, shape[0] // cuts, shape[1]), lambda i: (0, i, 0))

    share = below[0].shape[0]
    shapes = [
        below[0].shape, below[1].shape, below[2].shape, (share, heads_wide), (share, keys_wide),
        (share, keys_wide), below[4].shape,
    ]
    inputs = [stream_low, *below, *above]
    return pl.pallas_call(
        partial(widen_kernel, heads_wide, keys_wide),
        grid=(cuts,),
        out_shape=(
            jax.ShapeDtypeStruct(stream_low.shape, F32),
            *(jax.ShapeDtypeStruct((2, *shape), F32) for shape in shapes),
        ),
        in_specs=[cut(array.shape) for array in inputs],
        out_specs=(cut(stream_low.shape), *(pair(shape) for shape in shapes)),
        compiler_params=pltpu.CompilerParams(vmem_limit_bytes=VMEM_LIMIT),
    )(*inputs)


def call(kernel, collective_id, in_specs, outs, scratch, flops, out_spec=ANY):
    return pl.pallas_call(
        kernel,
        out_shape=tuple(jax.ShapeDtypeStruct(shape, kind) for shape, kind in outs),
        in_specs=in_specs,
        out_specs=tuple(out_spec for _ in outs),
        scratch_shapes=scratch,
        cost_estimate=pl.CostEstimate(flops=flops, bytes_accessed=40_000_000, transcendentals=0),
        compiler_params=pltpu.CompilerParams(
            collective_id=collective_id,
            has_side_effects=collective_id is not None,
            vmem_limit_bytes=VMEM_LIMIT,
        ),
    )


def dma(*shape):
    return pltpu.SemaphoreType.DMA(shape)


def shards(
    size,
    stream,
    cotangent,
    prefixes,
    attention_gain,
    query_weight,
    key_weight,
    value_weight,
    gate_heads,
    query_gain,
    key_gain,
    output_weight,
    feed_gain,
    gate_weight,
    up_weight,
    down_weight,
):
    seq_count, row_count, width = stream.shape
    rows = seq_count * row_count
    span = rows // GROUPS
    dp_size = lax.axis_size("dp")
    plane_sizes = (dp_size, lax.axis_size("ctx"))
    plane_count = plane_sizes[0] * plane_sizes[1]
    heads_wide = query_weight.shape[2]
    keys_wide = key_weight.shape[2]
    units = gate_weight.shape[2]
    gates = gate_heads.shape[2]
    share = width // plane_count
    unit = min(256, keys_wide)
    here = lax.axis_index("dp") * plane_sizes[1] + lax.axis_index("ctx")
    positions = lax.axis_index("ctx") * row_count + jnp.arange(row_count, dtype=jnp.int32)
    cos_table, sin_table = rotary_tables(positions, HD)
    cos = jnp.concatenate([cos_table, cos_table], axis=1)
    sin = jnp.concatenate([-sin_table, sin_table], axis=1)
    stream_flat = stream.reshape(rows, width)
    cot_flat = cotangent.reshape(rows, width)
    heads_padded = jnp.pad(gate_heads, ((0, 0), (0, 0), (0, LANES - gates)))
    sum_scratch = Sum.scratch(rows, width)
    landed = [pltpu.VMEM((2, rows, width), BF)]
    pair_scratch = [pltpu.VMEM((3, rows, width), BF)] + sum_scratch + sum_scratch

    key_heads = keys_wide // HD
    attend_outs = [
        ((rows, heads_wide), BF), ((rows, heads_wide), BF), ((heads_wide // HD, rows, 1), F32),
        ((rows, heads_wide), F32),
    ]
    key_outs = [((2, key_heads, rows, HD), BF), ((2, key_heads, rows, HD), BF)]
    smem = pl.BlockSpec(memory_space=pltpu.SMEM)

    attend_back_outs = [
        ((rows, heads_wide), BF), ((rows, keys_wide), BF), ((rows, keys_wide), BF),
        ((rows, LANES), BF), ((8, width), F32), ((8, HD), F32), ((8, HD), F32),
    ]
    attend_back_scratch = [
        pltpu.VMEM((rows, heads_wide), BF), pltpu.VMEM((heads_wide // HD, rows, 1), F32),
        pltpu.VMEM((rows, heads_wide), F32), pltpu.VMEM((key_heads, rows, HD), F32),
        pltpu.VMEM((key_heads, rows, HD), F32), pltpu.VMEM((key_heads, 2, rows, HD), BF),
        pltpu.VMEM((key_heads, 2, rows, HD), BF), dma(key_heads), dma(key_heads),
    ]

    def attend_back_in(mixed_grad, logits, saved, q_raw, k_raw, normed):
        mixed, q_rot, norm, attended, keys, values = saved
        return (
            prefixes, mixed_grad, logits, attended, q_rot, keys, values, norm, q_raw, k_raw,
            query_gain, key_gain, cos, sin, normed,
        )

    made_shapes = [
        ((share, units), BF), ((share, units), BF), ((units, share), BF),
        ((share, heads_wide + 2 * keys_wide), BF), ((heads_wide, share), BF),
    ]
    scatter_scratch = Scatter.scratch(plane_count, share, unit)

    *saved_zero, normed_zero, q_raw_zero, k_raw_zero, logits_zero = call(
        partial(first_kernel, 0),
        4,
        [smem, WHOLE, WHOLE, ANY, ANY, ANY] + [WHOLE] * 5,
        attend_outs
        + key_outs
        + [
            ((rows, width), BF), ((rows, heads_wide), F32), ((rows, keys_wide), F32),
            ((rows, LANES), F32),
        ],
        [
            pltpu.VMEM((rows, keys_wide), BF), pltpu.VMEM((width, heads_wide), BF),
            pltpu.VMEM((width, keys_wide), BF), pltpu.VMEM((width, keys_wide), BF), dma(3),
            dma(key_heads, 2), dma(key_heads, 2),
        ]
        + attend_scratch(rows, heads_wide),
        3_500_000_000,
        WHOLE,
    )(
        prefixes, stream_flat, attention_gain, query_weight, key_weight, value_weight, heads_padded,
        query_gain, key_gain, cos, sin,
    )
    mixed_zero = saved_zero[0]
    middle_zero, two_zero, slope, silu, hidden_zero, x_one, normed_one, q_raw, k_raw, logits, *keys_one = call(
        partial(forward_kernel, size, 0, rows, width),
        0,
        [WHOLE, ANY, ANY, WHOLE, ANY, ANY, ANY, WHOLE, ANY, ANY, ANY] + [WHOLE] * 4,
        [
            ((rows, width), F32), ((rows, width), BF), ((rows, units), BF), ((rows, units), BF),
            ((rows, units), BF), ((rows, width), F32), ((rows, width), BF),
            ((rows, heads_wide), F32), ((rows, keys_wide), F32), ((rows, LANES), F32), *key_outs,
        ],
        [
            pltpu.VMEM((heads_wide, width), BF), pltpu.VMEM((width, units), BF),
            pltpu.VMEM((width, units), BF), pltpu.VMEM((units, width), BF),
            pltpu.VMEM((width, heads_wide), BF), pltpu.VMEM((width, keys_wide), BF),
            pltpu.VMEM((width, keys_wide), BF), pltpu.VMEM((rows, width), BF),
            pltpu.VMEM((rows, width), F32), pltpu.VMEM((rows, units), BF),
            pltpu.VMEM((rows, units), BF), pltpu.VMEM((rows, units), BF),
            pltpu.VMEM((rows, heads_wide), F32), pltpu.VMEM((rows, keys_wide), F32),
            pltpu.VMEM((rows, keys_wide), BF), pltpu.VMEM((rows, LANES), F32),
            dma(8), dma(11, GROUPS), pltpu.VMEM((key_heads, rows, HD), BF),
            pltpu.VMEM((key_heads, rows, HD), BF), dma(2, GROUPS), dma(2, GROUPS), dma(2, GROUPS),
        ]
        + pair_scratch,
        13_000_000_000,
    )(
        mixed_zero, stream_flat, output_weight, feed_gain, gate_weight, up_weight, down_weight,
        attention_gain, query_weight, key_weight, value_weight, heads_padded, key_gain, cos, sin,
    )
    attended_one = call(
        partial(attend_kernel, 1),
        None,
        [smem] + [WHOLE] * 7,
        attend_outs,
        attend_scratch(rows, heads_wide),
        1_000_000_000,
        WHOLE,
    )(prefixes, q_raw, logits, query_gain, cos, sin, *keys_one)
    saved_one = [*attended_one, *keys_one]
    mixed_one = saved_one[0]
    two_one, down_part, gate_low, up_low, grad, low, mixed_grad, feed_one, down_made = call(
        partial(turn_kernel, size, plane_sizes, 1, rows, width),
        1,
        [WHOLE, ANY, ANY, ANY, WHOLE, ANY, ANY, ANY],
        [
            ((rows, width), BF), ((rows, width), BF), ((rows, units), BF),
            ((rows, units), BF), ((rows, width), F32), ((rows, width), BF),
            ((rows, heads_wide), F32), ((8, width), F32), made_shapes[2],
        ],
        [
            pltpu.VMEM((heads_wide, width), BF), pltpu.VMEM((width, units), BF),
            pltpu.VMEM((width, units), BF), pltpu.VMEM((units, width), BF),
            pltpu.VMEM((rows, width), F32), pltpu.VMEM((rows, width), BF),
            pltpu.VMEM((rows, units), BF), pltpu.VMEM((rows, units), BF),
            pltpu.VMEM((rows, units), BF), pltpu.VMEM((rows, heads_wide), F32),
            pltpu.VMEM((rows, width), BF), pltpu.VMEM((8, width), F32),
            dma(6), dma(9, GROUPS),
        ]
        + pair_scratch + scatter_scratch,
        24_000_000_000,
    )(mixed_one, x_one, cot_flat, output_weight, feed_gain, gate_weight, up_weight, down_weight)
    (gate_low, up_low, first_low, grad, low, mixed_grad, gain_one, feed_zero, heads_one, q_gain_one,
     k_gain_one, *made_one) = call(
        partial(back_kernel, size, plane_sizes, 1, rows, width),
        2,
        [smem, ANY, WHOLE, ANY] + [WHOLE] * 4 + [ANY] + [WHOLE] * 5 + [ANY]
        + [ANY, ANY, ANY, WHOLE] + [ANY] * 9 + [WHOLE] + [ANY] * 6,
        [
            ((rows, units), BF), ((rows, units), BF), ((rows, width), BF), ((rows, width), F32),
            ((rows, width), BF), ((rows, heads_wide), F32), ((8, width), F32), ((8, width), F32),
            ((8, width), F32), ((8, HD), F32), ((8, HD), F32), *made_shapes[:2], *made_shapes[3:],
        ],
        [pltpu.VMEM(shape, kind) for shape, kind in attend_back_outs]
        + attend_back_scratch[:2] + attend_back_scratch[3:]
        + [
            pltpu.VMEM((width, heads_wide), BF), pltpu.VMEM((width, keys_wide), BF),
            pltpu.VMEM((width, keys_wide), BF), pltpu.VMEM((4, 512, width), BF),
            pltpu.VMEM((heads_wide, width), BF), pltpu.VMEM((span, width), F32),
            pltpu.VMEM((rows, width), F32), pltpu.VMEM((span, units), BF),
            pltpu.VMEM((span, units), BF), pltpu.VMEM((span, units), BF),
            pltpu.VMEM((span, units), BF), pltpu.VMEM((span, heads_wide), F32),
            pltpu.VMEM((8, width), F32), pltpu.VMEM((8, width), F32),
            pltpu.VMEM((rows, width), BF), pltpu.VMEM((rows, units), BF),
            pltpu.VMEM((width, LANES), BF),
            dma(6), dma(3), dma(2, PARTS - 1), dma(8, GROUPS), dma(4), dma(4),
        ]
        + pair_scratch + scatter_scratch,
        28_000_000_000,
    )(
        *attend_back_in(mixed_grad, logits, saved_one, q_raw, k_raw, normed_one),
        heads_padded, x_one, grad, attention_gain,
        query_weight, key_weight, value_weight, down_weight, gate_weight, up_weight, slope, silu,
        middle_zero, feed_gain, output_weight,
        two_one, gate_low, up_low, low, mixed_one,
    )
    made_one.insert(2, down_made)
    below_rows = 8
    stages = plane_count.bit_length() - 1 + size.bit_length() - 1
    stream_low, result, totals, *made_zero = call(
        partial(last_kernel, size, plane_sizes, 0, rows, width),
        3,
        [smem] + [WHOLE] * 14 + [WHOLE] * 7 + [ANY, ANY, WHOLE] + [ANY] * 11,
        [
            ((rows, width), BF), ((rows, width), BF), ((8 + below_rows, width), F32), *made_shapes,
        ],
        [pltpu.VMEM(shape, kind) for shape, kind in attend_back_outs]
        + attend_back_scratch
        + [
            pltpu.VMEM((width, heads_wide), BF), pltpu.VMEM((width, keys_wide), BF),
            pltpu.VMEM((width, keys_wide), BF), pltpu.VMEM((rows, width), BF),
            pltpu.VMEM((rows, width), F32), pltpu.VMEM((8, width), F32),
            pltpu.VMEM((rows, width), BF), pltpu.VMEM((rows, units), BF),
            pltpu.VMEM((8 + below_rows, width), F32), dma(6), dma(3, GROUPS),
        ]
        + landed + sum_scratch + landed + sum_scratch
        + Total.scratch(8 + below_rows, width, stages) + scatter_scratch,
        19_000_000_000,
    )(
        *attend_back_in(mixed_grad, logits_zero, saved_zero, q_raw_zero, k_raw_zero, normed_zero),
        heads_padded, gain_one, feed_zero, feed_one, q_gain_one, k_gain_one, heads_one, stream_flat,
        grad, attention_gain, query_weight, key_weight, value_weight, down_part,
        two_zero, gate_low, up_low, first_low, hidden_zero, low, mixed_zero,
    )
    stream_grad, *weights = widen(stream_low, made_zero, made_one, heads_wide, keys_wide)

    def own(array, wide_share):
        return lax.dynamic_slice_in_dim(array, here * wide_share, wide_share, array.ndim - 1)

    gains = own(totals[:4], share)
    head_gains = own(totals[4, : 4 * HD].reshape(2, 2, HD), HD // plane_count)
    heads = own(totals[8:].reshape(LAYERS, 4, width)[:, :gates], share)
    return (
        result.reshape(seq_count, row_count, width),
        stream_grad.reshape(seq_count, row_count, width),
        gains[0:2],
        weights[3],
        weights[4],
        weights[5],
        heads.transpose(0, 2, 1),
        head_gains[:, 0],
        head_gains[:, 1],
        weights[6],
        gains[2:4],
        weights[0],
        weights[1],
        weights[2],
    )


def solution(mesh):
    return jax.shard_map(
        partial(shards, mesh.shape["tensor"]),
        mesh=mesh,
        in_specs=(
            P("dp", "ctx", None),
            P("dp", "ctx", None),
            P("dp"),
            P(),
            P(None, None, "tensor"),
            P(None, None, "tensor"),
            P(None, None, "tensor"),
            P(None, None, "tensor"),
            P(),
            P(),
            P(None, "tensor", None),
            P(),
            P(None, None, "tensor"),
            P(None, None, "tensor"),
            P(None, "tensor", None),
        ),
        out_specs=(
            P("dp", "ctx", None),
            P("dp", "ctx", None),
            P(None, ("dp", "ctx")),
            P(None, ("dp", "ctx"), "tensor"),
            P(None, ("dp", "ctx"), "tensor"),
            P(None, ("dp", "ctx"), "tensor"),
            P(None, ("dp", "ctx"), "tensor"),
            P(None, ("dp", "ctx")),
            P(None, ("dp", "ctx")),
            P(None, "tensor", ("dp", "ctx")),
            P(None, ("dp", "ctx")),
            P(None, ("dp", "ctx"), "tensor"),
            P(None, ("dp", "ctx"), "tensor"),
            P(None, "tensor", ("dp", "ctx")),
        ),
        check_vma=False,
    )
```

```python
from functools import partial

import jax
import jax.numpy as jnp
import numpy as np
from jax import lax
from jax.experimental import pallas as pl
from jax.experimental.pallas import tpu as pltpu
from jax.sharding import PartitionSpec as P

HD = 128
LAYERS = 2
LANES = 128

epsilon = 1e-06
theta = 1000000.0
masked = -1000000000.0

BF = jnp.bfloat16
F32 = jnp.float32
ANY = pl.BlockSpec(memory_space=pl.ANY)
WHOLE = pl.BlockSpec(memory_space=pltpu.VMEM)
MESH = pl.DeviceIdType.MESH

BLOCKS = 8
PIECES = 2
GROUP = 4
STRIP = 16
UNROLL = 2
VMEM_LIMIT = 63 * 1024 * 1024


def rms_scale(values, gain):
    return values * lax.rsqrt(jnp.mean(values * values, axis=-1, keepdims=True) + epsilon) * gain


def rotary_tables(length):
    counter = np.arange(HD // 2, dtype=np.float32)
    frequency = np.power(np.float32(theta), np.float32(-2.0) * counter / np.float32(HD))
    angles = np.arange(length, dtype=np.float32)[:, None] * frequency[None, :].astype(np.float32)
    cos, sin = np.cos(angles), np.sin(angles)
    return (
        np.concatenate([cos, cos], axis=1).astype(np.float32),
        np.concatenate([-sin, sin], axis=1).astype(np.float32),
    )


def matmul(left, right):
    return jnp.dot(left, right, preferred_element_type=F32)


def weight_product(left, right):
    return lax.dot_general(left, right, (((0,), (0,)), ((), ())), preferred_element_type=F32)


def back_product(gradient, weight):
    return lax.dot_general(gradient, weight, (((1,), (1,)), ((), ())), preferred_element_type=F32)


def loop(count, body, unroll=1):
    def step(i, carry):
        body(i)
        return carry

    lax.fori_loop(0, count, step, 0, unroll=unroll)


def rows_of(r, block):
    return pl.ds(pl.multiple_of(r * block, block), block)


def columns(j, width):
    return pl.ds(pl.multiple_of(j * width, width), width)


def greet(targets, extra, has_extra):
    barrier = pltpu.get_barrier_semaphore()
    for target in targets:
        pl.semaphore_signal(barrier, inc=1, device_id=target, device_id_type=MESH)

    @pl.when(has_extra)
    def _():
        pl.semaphore_signal(barrier, inc=1, device_id=extra, device_id_type=MESH)
        pl.semaphore_wait(barrier, len(targets) + 1)

    @pl.when(jnp.logical_not(has_extra))
    def _():
        pl.semaphore_wait(barrier, len(targets))


class Chain:
    def __init__(self, size):
        self.size = size
        self.spot = lax.axis_index("tensor")
        half = size // 2
        on_left = self.spot < half
        self.end = (self.spot == 0) | (self.spot == size - 1)
        self.inner = jnp.logical_not(self.end)
        self.mid = (self.spot == half - 1) | (self.spot == half)
        self.outer = jnp.logical_not(self.mid)
        self.first_mid = self.spot == half - 1
        self.inward = {"tensor": jnp.where(on_left, self.spot + 1, self.spot - 1)}
        self.outward = {"tensor": jnp.where(on_left, self.spot - 1, self.spot + 1)}

    def greet(self, others=()):
        greet([self.inward, *others], self.outward, self.inner)


class Sum:
    def __init__(self, chain, refs, landed, rows, width):
        self.chain = chain
        self.part, self.spread, self.s_in, self.r_in, self.s_out, self.r_out, self.r_cross = refs
        self.landed, self.cross = landed
        self.block = rows // BLOCKS
        self.piece = width // PIECES

    @staticmethod
    def scratch(rows, width):
        return [
            pltpu.VMEM((rows, width), BF),
            pltpu.VMEM((rows, width), BF),
            pltpu.SemaphoreType.DMA((BLOCKS, PIECES)),
            pltpu.SemaphoreType.DMA((BLOCKS, PIECES)),
            pltpu.SemaphoreType.DMA((BLOCKS,)),
            pltpu.SemaphoreType.DMA((BLOCKS,)),
            pltpu.SemaphoreType.DMA((BLOCKS, PIECES)),
        ]

    def hop(self, r, p, across):
        where = (rows_of(r, self.block), columns(p, self.piece))
        return pltpu.make_async_remote_copy(
            src_ref=self.part.at[where],
            dst_ref=self.landed.at[(self.cross if across else 0,) + where],
            send_sem=self.s_in.at[r, p],
            recv_sem=(self.r_cross if across else self.r_in).at[r, p],
            device_id=self.chain.inward,
            device_id_type=MESH,
        )

    def out_hop(self, r):
        at = rows_of(r, self.block)
        return pltpu.make_async_remote_copy(
            src_ref=self.spread.at[at],
            dst_ref=self.spread.at[at],
            send_sem=self.s_out.at[r],
            recv_sem=self.r_out.at[r],
            device_id=self.chain.outward,
            device_id_type=MESH,
        )

    def offer(self, g):
        @pl.when(self.chain.end)
        def _():
            def one(k):
                for p in range(PIECES):
                    self.hop(g * GROUP + k, p, False).start()

            loop(GROUP, one)

    def relay(self, r):
        @pl.when(self.chain.inner)
        def _():
            for p in range(PIECES):
                self.hop(r, p, False).wait_recv()
                col = columns(p, self.piece)

                def strip(i, col=col):
                    at = pl.ds(pl.multiple_of(r * self.block + i * STRIP, STRIP), STRIP)
                    self.part[at, col] = self.part[at, col] + self.landed[0, at, col]

                loop(self.block // STRIP, strip, True)

                @pl.when(self.chain.mid)
                def _(p=p):
                    self.hop(r, p, True).start()

                @pl.when(self.chain.outer)
                def _(p=p):
                    self.hop(r, p, False).start()

    def finish(self, r, make):
        @pl.when(self.chain.mid)
        def _():
            for p in range(PIECES):
                self.hop(r, p, True).wait_recv()

            def strip(i):
                at = pl.ds(pl.multiple_of(r * self.block + i * STRIP, STRIP), STRIP)
                total = self.part[at, :].astype(F32) + self.landed[self.cross, at, :].astype(F32)
                self.spread[at, :] = make(at, total)

            loop(self.block // STRIP, strip, UNROLL)
            self.out_hop(r).start()

    def receive(self, g):
        @pl.when(self.chain.outer)
        def _():
            def one(k):
                self.out_hop(g * GROUP + k).wait_recv()

                @pl.when(self.chain.inner)
                def _():
                    self.out_hop(g * GROUP + k).start()

            loop(GROUP, one)

    def close(self):
        def block(r):
            for p in range(PIECES):
                self.hop(r, p, False).wait_send()

            @pl.when(self.chain.inner)
            def _():
                self.out_hop(r).wait_send()

        loop(BLOCKS, block)


PARTS = 4
STRIDE = GROUP // PARTS
GROUPS = BLOCKS // GROUP
STEPS = 2 * BLOCKS + 1


def two_sums(s, first, second, made_one, between, ahead, made_two, after):
    @pl.when((s >= 0) & (s < BLOCKS))
    def _():
        first.relay(s)

    @pl.when((s >= 1) & (s <= BLOCKS))
    def _():
        first.finish(s - 1, made_one)

    @pl.when((s >= GROUP) & (s < BLOCKS + GROUP))
    def _():
        place = lax.rem(s - GROUP, GROUP)
        group = lax.div(s - GROUP, GROUP)

        @pl.when(place == 0)
        def _():
            first.receive(group)

        outer = first.chain.outer
        begin = jnp.where(outer, jnp.where(place == 0, 0, PARTS), lax.div(place + STRIDE - 1, STRIDE))
        stop = jnp.where(outer, PARTS, lax.div(place, STRIDE) + 1)
        lax.fori_loop(begin, stop, lambda part, carry: (between(group, part), carry)[1], 0)

    @pl.when((s >= BLOCKS) & (s < 2 * BLOCKS))
    def _():
        second.relay(s - BLOCKS)

    @pl.when((s >= BLOCKS + 1) & (s < STEPS))
    def _():
        @pl.when(lax.rem(s - BLOCKS - 1, GROUP) == 0)
        def _():
            ahead(lax.div(s - BLOCKS - 1, GROUP))

        second.finish(s - BLOCKS - 1, made_two)

        @pl.when(lax.rem(s - BLOCKS, GROUP) == 0)
        def _():
            group = lax.div(s - BLOCKS, GROUP) - 1
            second.receive(group)
            after(group)


def back_norm(value, gain, grad):
    spread = lax.rsqrt(jnp.mean(value * value, axis=-1, keepdims=True) + epsilon)
    scaled = grad * gain
    pulled = jnp.mean(scaled * value, axis=-1, keepdims=True)
    terms = grad * value * spread
    return spread * scaled - value * (spread * spread * spread * pulled), terms


def fold(terms):
    folded = terms[:8]
    for k in range(8, terms.shape[0], 8):
        folded = folded + terms[k : k + 8]
    return folded


def load_all(pairs, sems):
    copies = [pltpu.make_async_copy(src, dst, sems.at[k]) for k, (src, dst) in enumerate(pairs)]
    for copy in copies:
        copy.start()
    return copies


def wait_all(copies):
    for copy in copies:
        copy.wait()


def wide(width):
    return 512 if width % 512 == 0 else 256


def fill(target, at, make):
    width = target.shape[1]
    tile = wide(width)

    def one(p):
        col = columns(p, tile)
        target[at, col] = make(col).astype(target.dtype)

    loop(width // tile, one)


def flip(value, bit):
    return value + bit * (1 - 2 * lax.rem(lax.div(value, bit), 2))


class Plane:
    def __init__(self, dp_size, ctx_size):
        self.count = dp_size * ctx_size
        self.ctx_size = ctx_size
        self.me = lax.axis_index("dp") * ctx_size + lax.axis_index("ctx")
        bits = [1 << k for k in range(self.count.bit_length() - 1)]
        near = [bit for bit in bits if bit >= ctx_size][:1]
        rest = [bit for bit in bits if bit not in near]
        self.bits = bits
        self.orders = (near + rest, near + rest[1:] + rest[:1])

    def partner(self, bit):
        other = flip(self.me, bit)
        return {"dp": lax.div(other, self.ctx_size), "ctx": lax.rem(other, self.ctx_size)}

    def partners(self):
        return [self.partner(bit) for bit in self.bits]


BEFORE = 8
OUTER_MORE = 0
PACE = 12
ONE_PACE = 8
PER_TICK = 1
ONE_AFTER = 3
EARLY = BLOCKS + GROUP - 1
TURN_PACE = 2
OUTER_AHEAD = 4


class Scatter:
    SLOTS = (2, 6, 6, 6)
    KEPT = (2, 4, 4, 4)
    RESULTS = 2
    LAGS = (0, 1, 5, 9, 13, 17)

    def __init__(self, plane, refs, whole, parts, groups, share, tile):
        self.plane = plane
        self.whole, self.parts = whole, parts
        self.groups = groups
        self.share, self.tile = share, tile
        self.stages = len(plane.bits)
        self.units = sum(group[2] for group in groups)
        self.refs = [refs[6 * k : 6 * k + 6] for k in range(self.stages)]
        self.made, self.out_sem, self.load_sem = refs[6 * self.stages :]
        self.steps = self.units + self.LAGS[self.stages]

    @classmethod
    def scratch(cls, count, share, tile):
        found = []
        blocks = count // 2
        for k in range(count.bit_length() - 1):
            slots = cls.SLOTS[k]
            found += [
                pltpu.VMEM((depth, blocks, share, tile), BF) for depth in (slots, cls.KEPT[k], slots)
            ]
            found += [
                pltpu.SemaphoreType.DMA((slots,)),
                pltpu.SemaphoreType.DMA((slots,)),
                pltpu.SemaphoreType.REGULAR((slots,)),
            ]
            blocks //= 2
        return found + [
            pltpu.VMEM((cls.RESULTS, share, tile), BF),
            pltpu.SemaphoreType.DMA((cls.RESULTS,)),
            pltpu.SemaphoreType.DMA((4,)),
        ]

    def partner(self, stage, u):
        odd = lax.rem(u, 2) == 1
        even_one, odd_one = (self.plane.partner(order[stage]) for order in self.plane.orders)
        return {axis: jnp.where(odd, odd_one[axis], even_one[axis]) for axis in even_one}

    def copy(self, stage, u):
        send, unused, land, s_sem, r_sem, unused_credit = self.refs[stage]
        slot = lax.rem(u, self.SLOTS[stage])
        return pltpu.make_async_remote_copy(
            src_ref=send.at[slot],
            dst_ref=land.at[slot],
            send_sem=s_sem.at[slot],
            recv_sem=r_sem.at[slot],
            device_id=self.partner(stage, u),
            device_id_type=MESH,
        )

    def ready(self, stage, u):
        @pl.when(u >= self.SLOTS[stage])
        def _():
            self.copy(stage, u - self.SLOTS[stage]).wait_send()

    def push(self, stage, u):
        @pl.when(u >= self.SLOTS[stage])
        def _():
            pl.semaphore_wait(self.refs[stage][5].at[lax.rem(u, self.SLOTS[stage])], 1)

        self.copy(stage, u).start()

    def product(self, u):
        send, keep = self.refs[0][:2]
        slot, spot = lax.rem(u, self.SLOTS[0]), lax.rem(u, self.KEPT[0])
        odd = lax.rem(u, 2)
        orders = self.plane.orders
        first = 0
        place = u
        by_rows_here = u < 0
        for unused, by_rows, count, loads in self.groups:
            here = (u >= first) & (u < first + count)
            place = jnp.where(here, u - first, place)
            if by_rows:
                by_rows_here = by_rows_here | here

            @pl.when(u == first)
            def _(loads=loads):
                wait_all(load_all(loads, self.load_sem))

            first += count
        parts = self.parts[:, columns(place, self.tile)]

        def block(far, j):
            owner = flip(self.plane.me, orders[0][0]) if far else self.plane.me
            for bits in reversed(tuple(zip(*orders))[1:]):
                if j % 2:
                    owner = flip(owner, bits[0]) * (1 - odd) + flip(owner, bits[1]) * odd
                j //= 2
            return self.whole[:, columns(owner, self.share)]

        def all_blocks(make):
            for j in range(self.plane.count // 2):
                send[slot, j] = make(block(True, j)).astype(BF)
                keep[spot, j] = make(block(False, j)).astype(BF)

        @pl.when(by_rows_here)
        def _():
            all_blocks(lambda whole: weight_product(whole, parts))

        @pl.when(jnp.logical_not(by_rows_here))
        def _():
            all_blocks(lambda whole: weight_product(parts, whole))

    def merge(self, stage, u):
        unused, keep, land = self.refs[stage][:3]
        slots = self.SLOTS[stage]
        slot, spot = lax.rem(u, slots), lax.rem(u, self.KEPT[stage])
        self.copy(stage, u).wait_recv()
        half = (self.plane.count // 2) >> (stage + 1)
        last = stage == self.stages - 1
        if not last:
            self.ready(stage + 1, u)
            send_on, keep_on = self.refs[stage + 1][:2]
            slot_on = lax.rem(u, self.SLOTS[stage + 1])
            spot_on = lax.rem(u, self.KEPT[stage + 1])

            def one(j):
                send_on[slot_on, j] = keep[spot, half + j] + land[slot, half + j]
                keep_on[spot_on, j] = keep[spot, j] + land[slot, j]

            loop(half, one)
            self.push(stage + 1, u)
        else:
            place = lax.rem(u, self.RESULTS)

            @pl.when(u >= self.RESULTS)
            def _():
                self.results(u - self.RESULTS, lambda copy: copy.wait())

            self.made[place] = keep[spot, 0] + land[slot, 0]
            self.results(u, lambda copy: copy.start())

        @pl.when(u + slots < self.units)
        def _():
            pl.semaphore_signal(
                self.refs[stage][5].at[slot],
                inc=1,
                device_id=self.partner(stage, u),
                device_id_type=MESH,
            )

    def results(self, u, act):
        place = lax.rem(u, self.RESULTS)
        first = 0
        for out, by_rows, count, unused_loads in self.groups:

            @pl.when((u >= first) & (u < first + count))
            def _(by_rows=by_rows, out=out, first=first):
                if by_rows:
                    at = (slice(None), columns(u - first, self.tile))
                else:
                    at = (rows_of(u - first, self.tile), slice(None))
                act(pltpu.make_async_copy(self.made.at[place], out.at[at], self.out_sem.at[place]))

            first += count

    def tick(self, i):
        @pl.when(i < self.units)
        def _():
            self.ready(0, i)
            self.product(i)
            self.push(0, i)

        for stage in reversed(range(self.stages)):
            u = i - self.LAGS[stage + 1]

            @pl.when((u >= 0) & (u < self.units))
            def _(stage=stage, u=u):
                self.merge(stage, u)

    def close(self):
        for stage in range(self.stages):
            for k in range(max(0, self.units - self.SLOTS[stage]), self.units):
                self.copy(stage, jnp.int32(k)).wait_send()
        for k in range(max(0, self.units - self.RESULTS), self.units):
            self.results(jnp.int32(k), lambda copy: copy.wait())


Z_APART = 1
PLANE_APART = 3


class Total:
    def __init__(self, plane, size, refs, own):
        self.value, self.land, self.s_sem, self.r_sem = refs
        spot = lax.axis_index("tensor")
        rows, first = pl.ds(0, self.value.shape[1]), pl.ds(0, own)
        near, *rest = plane.orders[0]
        across = [({"tensor": flip(spot, 1 << k)}, first) for k in range(size.bit_length() - 1)]
        self.across = [target for target, unused in across]
        self.stages = [(plane.partner(near), rows), *across]
        self.stages += [(plane.partner(bit), rows) for bit in rest]
        self.times = [0, 1]
        for unused in across:
            self.times.append(self.times[-1] + Z_APART)
        for unused in rest:
            self.times.append(self.times[-1] + PLANE_APART)

    @staticmethod
    def scratch(rows, width, stages):
        return [
            pltpu.VMEM((stages, rows, width), F32),
            pltpu.VMEM((stages, rows, width), F32),
            pltpu.SemaphoreType.DMA((stages,)),
            pltpu.SemaphoreType.DMA((stages,)),
        ]

    def copy(self, k):
        target, rows = self.stages[k]
        return pltpu.make_async_remote_copy(
            src_ref=self.value.at[k, rows],
            dst_ref=self.land.at[k, rows],
            send_sem=self.s_sem.at[k],
            recv_sem=self.r_sem.at[k],
            device_id=target,
            device_id_type=MESH,
        )

    def take(self, k, target):
        self.copy(k).wait_recv()
        rows = self.stages[k][1]
        target[...] = self.value[k]
        target[rows] = self.value[k, rows] + self.land[k, rows]

    def start(self, k):
        if k > 0:
            self.take(k - 1, self.value.at[k])
        self.copy(k).start()

    def finish(self, target):
        self.take(len(self.stages) - 1, target)
        for k in range(len(self.stages)):
            self.copy(k).wait_send()


def turned(value):
    return pltpu.roll(value, HD // 2, 1)


def head_at(h):
    return pl.ds(h * HD, HD)


def head_norm(raw, gain, cos, sin):
    scaled = rms_scale(raw, gain)
    return scaled * cos + turned(scaled) * sin


def head_norm_back(raw, gain, cos, sin, grad):
    return back_norm(raw, gain, grad * cos - turned(grad) * sin)


def seen(rows, first_row, columns_wide, offset, prefix):
    query = first_row + lax.broadcasted_iota(jnp.int32, (rows, columns_wide), 0)
    key = lax.broadcasted_iota(jnp.int32, (rows, columns_wide), 1)
    return (key <= query) | (key + offset < prefix)


def key_strip(raw, v, keys, values, gain, cos, sin, j, at):
    keys[j, at, :] = head_norm(raw[at, head_at(j)], gain, cos[at, :], sin[at, :]).astype(BF)
    values[j, at, :] = v[at, head_at(j)]


def attend(prefix, q_raw, logits, query_gain, cos, sin, keys, values,
           mixed_o, q_o, norm_o, attended_o, scratch, half, arrived):
    high, low, out = scratch
    rows = q_raw.shape[0]
    span = rows // GROUPS
    key_heads = keys.shape[1]
    shared = q_raw.shape[1] // HD // key_heads
    scale = HD ** (-0.5)

    def own(g):
        at = rows_of(g, span)
        mask = seen(span, g * span, rows, half * rows, prefix)
        for h in range(key_heads * shared):
            j = h // shared
            query = head_norm(q_raw[at, head_at(h)], query_gain, cos[at, :], sin[at, :]).astype(BF)
            q_o[at, head_at(h)] = query
            scores = jnp.where(mask, back_product(query, keys[0, j]) * scale, masked)
            top = jnp.max(scores, axis=1, keepdims=True)
            weights = jnp.exp(scores - top)
            high[h, at, :] = top
            low[h, at, :] = jnp.sum(weights, axis=1, keepdims=True)
            out[at, head_at(h)] = matmul(weights.astype(BF), values[0, j])

    loop(GROUPS, own)

    @pl.when(half == 1)
    def _():
        for h in range(key_heads * shared):
            j = h // shared
            if h % shared == 0:
                arrived(j)

            def other(g, h=h, j=j):
                at = rows_of(g, span)
                scores = back_product(q_o[at, head_at(h)], keys[1, j]) * scale
                before = high[h, at, :]
                top = jnp.maximum(before, jnp.max(scores, axis=1, keepdims=True))
                weights = jnp.exp(scores - top)
                shrink = jnp.exp(before - top)
                high[h, at, :] = top
                low[h, at, :] = low[h, at, :] * shrink + jnp.sum(weights, axis=1, keepdims=True)
                out[at, head_at(h)] = out[at, head_at(h)] * shrink + matmul(
                    weights.astype(BF), values[1, j]
                )

            loop(GROUPS, other)

    def close(g):
        at = rows_of(g, span)
        open_gate = jax.nn.sigmoid(logits[at, :])
        for h in range(key_heads * shared):
            total = low[h, at, :]
            norm_o[h, at, :] = high[h, at, :] + jnp.log(total)
            attended = out[at, head_at(h)] * (1.0 / total)
            attended_o[at, head_at(h)] = attended
            mixed_o[at, head_at(h)] = (attended * open_gate[:, h : h + 1]).astype(BF)

    loop(GROUPS, close)


def attend_scratch(rows, heads_wide):
    return [
        pltpu.VMEM((heads_wide // HD, rows, 1), F32),
        pltpu.VMEM((heads_wide // HD, rows, 1), F32),
        pltpu.VMEM((rows, heads_wide), F32),
    ]


def attend_kernel(
    depth, prefix, q_raw, logits, query_gain, cos, sin, keys, values,
    mixed_o, q_o, norm_o, attended_o, *scratch,
):
    half = lax.axis_index("ctx")
    attend(prefix[0], q_raw, logits, query_gain[depth : depth + 1, :], cos, sin, keys, values,
           mixed_o, q_o, norm_o, attended_o, scratch, half, lambda j: None)


def first_kernel(
    depth, prefix, stream, gain, wq, wk, wv, gh, query_gain, key_gain, cos, sin,
    mixed_o, q_o, norm_o, attended_o, keys_o, values_o, normed_o, q_raw, k_raw, logits,
    v, wq_v, wk_v, wv_v, load_sem, send_sem, land_sem, *scratch,
):
    half = lax.axis_index("ctx")
    loads = load_all([(wk.at[depth], wk_v), (wv.at[depth], wv_v), (wq.at[depth], wq_v)], load_sem)
    greet([{"ctx": 1 - half}], {"ctx": 1 - half}, half < 0)
    rows = stream.shape[0]
    span = rows // GROUPS
    key_heads = k_raw.shape[1] // HD

    def copy(j, which):
        ref = (keys_o, values_o)[which]
        return pltpu.make_async_remote_copy(
            src_ref=ref.at[0, j],
            dst_ref=ref.at[1, j],
            send_sem=send_sem.at[j, which],
            recv_sem=land_sem.at[j, which],
            device_id={"ctx": 1 - half},
            device_id_type=MESH,
        )

    def strip(i):
        at = rows_of(i, STRIP)
        value = stream[at, :].astype(F32)
        normed_o[at, :] = rms_scale(value, gain[depth : depth + 1, :]).astype(BF)

    loop(rows // STRIP, strip, UNROLL)
    wait_all(loads[:2])

    def project_keys(g):
        at = rows_of(g, span)
        k_raw[at, :] = matmul(normed_o[at, :], wk_v[...])
        v[at, :] = matmul(normed_o[at, :], wv_v[...]).astype(BF)
        for j in range(key_heads):
            key_strip(k_raw, v, keys_o.at[0], values_o.at[0], key_gain[depth : depth + 1, :], cos, sin, j, at)

    loop(GROUPS, project_keys)

    @pl.when(half == 0)
    def _():
        for j in range(key_heads):
            copy(j, 0).start()
            copy(j, 1).start()

    loads[2].wait()

    def project(g):
        at = rows_of(g, span)
        q_raw[at, :] = matmul(normed_o[at, :], wq_v[...])
        logits[at, :] = matmul(normed_o[at, :], gh[depth])

    loop(GROUPS, project)

    def arrived(j):
        copy(j, 0).wait_recv()
        copy(j, 1).wait_recv()

    attend(prefix[0], q_raw, logits, query_gain[depth : depth + 1, :], cos, sin, keys_o, values_o,
           mixed_o, q_o, norm_o, attended_o, scratch, half, arrived)

    @pl.when(half == 0)
    def _():
        for j in range(key_heads):
            copy(j, 0).wait_send()
            copy(j, 1).wait_send()


def attend_back(
    half, depth, prefix, mixed_grad, logits, attended, q_rot, keys, values, norm, q_raw, k_raw,
    query_gain, key_gain, cos, sin, normed,
    q_o, k_o, v_o, l_o, heads_o, q_gain_o, k_gain_o,
    grad_low, inner, q_grad, k_grad, v_grad, given, landed, send_sem, land_sem,
):
    rows = q_raw.shape[0]
    span = rows // GROUPS
    key_heads = k_raw.shape[1] // HD
    shared = q_raw.shape[1] // k_raw.shape[1]
    heads = key_heads * shared
    scale = HD ** (-0.5)
    query_gain_here = query_gain[depth : depth + 1, :]
    key_gain_here = key_gain[depth : depth + 1, :]

    def copy(j):
        return pltpu.make_async_remote_copy(
            src_ref=given.at[j],
            dst_ref=landed.at[j],
            send_sem=send_sem.at[j],
            recv_sem=land_sem.at[j],
            device_id={"ctx": 1 - half},
            device_id_type=MESH,
        )

    def gate_back(g):
        at = rows_of(g, span)
        open_gate = jax.nn.sigmoid(logits[at, :])
        lane = lax.broadcasted_iota(jnp.int32, (span, LANES), 1)
        pulled = jnp.zeros((span, LANES), F32)
        for h in range(heads):
            grad = mixed_grad[at, head_at(h)]
            here = attended[at, head_at(h)]
            low_grad = (grad * open_gate[:, h : h + 1]).astype(BF)
            grad_low[at, head_at(h)] = low_grad
            inner[h, at, :] = jnp.sum(low_grad.astype(F32) * here, axis=1, keepdims=True)
            pulled = jnp.where(lane == h, jnp.sum(grad * here, axis=1, keepdims=True), pulled)
        l_o[at, :] = (pulled * (open_gate * (1.0 - open_gate))).astype(BF)

    def gates():
        loop(GROUPS, gate_back)
        heads_o[...] = weight_product(l_o[...], normed[...])[: heads_o.shape[0], :]

    def back(j, side, mask_of, first):
        k_grad[j] = jnp.zeros((rows, HD), F32)
        v_grad[j] = jnp.zeros((rows, HD), F32)

        def block(g):
            at = rows_of(g, span)
            for h in range(j * shared, (j + 1) * shared):
                query = q_rot[at, head_at(h)]
                pulled = grad_low[at, head_at(h)]
                scores = back_product(query, keys[side, j]) * scale
                if mask_of is not None:
                    scores = jnp.where(mask_of(g), scores, masked)
                weights = jnp.exp(scores - norm[h, at, :])
                slope = back_product(pulled, values[side, j])
                score_low = (weights * (slope - inner[h, at, :])).astype(BF)
                moved = matmul(score_low, keys[side, j])
                if first:
                    q_grad[at, head_at(h)] = moved
                else:
                    q_grad[at, head_at(h)] += moved
                k_grad[j] += weight_product(score_low, query)
                v_grad[j] += weight_product(weights.astype(BF), pulled)

        loop(GROUPS, block)

    def other(j):
        @pl.when(half == 1)
        def _():
            back(j, 1, None, True)
            given[j, 0] = (k_grad[j] * scale).astype(BF)
            given[j, 1] = v_grad[j].astype(BF)
            copy(j).start()

        @pl.when(half == 0)
        def _():
            wide_head = pl.ds(j * shared * HD, shared * HD)
            q_grad[:, wide_head] = jnp.zeros((rows, shared * HD), F32)

    def own(j):
        back(j, 0, lambda g: seen(span, g * span, rows, half * rows, prefix[0]), False)

    def query_rows(g):
        at = rows_of(g, span)
        for h in range(heads):
            pulled, terms = head_norm_back(
                q_raw[at, head_at(h)], query_gain_here, cos[at, :], sin[at, :],
                q_grad[at, head_at(h)] * scale,
            )
            q_o[at, head_at(h)] = pulled.astype(BF)
            q_gain_o[...] += jnp.sum(terms.reshape(span // 8, 8, HD), axis=0)

    def queries():
        q_gain_o[...] = jnp.zeros_like(q_gain_o)
        loop(GROUPS, query_rows)

    def keys_of(j):
        if j == 0:
            k_gain_o[...] = jnp.zeros_like(k_gain_o)

        @pl.when(half == 0)
        def _(j=j):
            copy(j).wait_recv()

        def key_rows(g, j=j):
            at = rows_of(g, span)
            k_total = k_grad[j, at, :] * scale
            v_total = v_grad[j, at, :]
            k_grad[j, at, :] = k_total
            v_o[at, head_at(j)] = v_total.astype(BF)

            @pl.when(half == 0)
            def _():
                k_grad[j, at, :] = k_total + landed[j, 0, at, :].astype(F32)
                v_o[at, head_at(j)] = (v_total + landed[j, 1, at, :].astype(F32)).astype(BF)

            pulled, terms = head_norm_back(
                k_raw[at, head_at(j)], key_gain_here, cos[at, :], sin[at, :], k_grad[j, at, :]
            )
            k_o[at, head_at(j)] = pulled.astype(BF)
            k_gain_o[...] += jnp.sum(terms.reshape(span // 8, 8, HD), axis=0)

        loop(GROUPS, key_rows)

    def close():
        @pl.when(half == 1)
        def _():
            for j in range(key_heads):
                copy(j).wait_send()

    heads_each = range(key_heads)
    return (
        [gates]
        + [partial(other, j) for j in heads_each]
        + [partial(own, j) for j in heads_each]
        + [queries]
        + [partial(keys_of, j) for j in heads_each],
        close,
    )


def forward_kernel(
    size, depth, rows, width,
    mixed, stream, wo, feed_gain, wg, wu, wd, next_gain, wq, wk, wv, gh, key_gain, cos, sin,
    middle_o, two_o, slope_o, silu_o, hidden_o, x_o, normed_o, q_o, k_o, logit_o, keys_o, values_o,
    *scratch,
):
    (wo_v, wg_v, wu_v, wd_v, wq_v, wk_v, wv_v, x_v, middle_v, slope_v, silu_v, hidden_v, q_v, k_v,
     v_v, logit_v, load_sem, out_sem, keys_v, values_v, keep_sem, send_sem, land_sem) = scratch[:23]
    half = lax.axis_index("ctx")
    key_heads = keys_v.shape[0]
    chain = Chain(size)
    landed = scratch[23]
    one = Sum(chain, scratch[24:31], (landed, 1), rows, width)
    two = Sum(chain, scratch[31:38], (landed, 2), rows, width)
    span = one.block * GROUP
    loads = load_all(
        [(wo.at[depth], wo_v), (stream, x_v), (wg.at[depth], wg_v), (wu.at[depth], wu_v),
         (wd.at[depth], wd_v), (wq.at[depth + 1], wq_v), (wk.at[depth + 1], wk_v),
         (wv.at[depth + 1], wv_v)],
        load_sem,
    )
    chain.greet([{"ctx": 1 - half}])
    tile = wg_v.shape[1] // (PARTS - 1)
    gain_one = feed_gain[depth : depth + 1, :]
    gain_two = next_gain[depth + 1 : depth + 2, :]

    def out(k, g, src, dst):
        at = rows_of(g, span)
        return pltpu.make_async_copy(src.at[at], dst.at[at], out_sem.at[k, g])

    def keep_keys(g, which):
        at = rows_of(g, span)
        src, dst = ((keys_v, keys_o), (values_v, values_o))[which]
        return pltpu.make_async_copy(src.at[:, at], dst.at[0, :, at], keep_sem.at[which, g])

    def give_keys(g, which):
        at = rows_of(g, span)
        src, dst = ((keys_v, keys_o), (values_v, values_o))[which]
        return pltpu.make_async_remote_copy(
            src_ref=src.at[:, at],
            dst_ref=dst.at[1, :, at],
            send_sem=send_sem.at[which, g],
            recv_sem=land_sem.at[which, g],
            device_id={"ctx": 1 - half},
            device_id_type=MESH,
        )

    loads[0].wait()

    def start(g):
        at = rows_of(g, span)
        fill(one.part, at, lambda col: matmul(mixed[at, :], wo_v[:, col]))
        one.offer(g)

    loop(GROUPS, start)
    wait_all(loads[1:5])

    def made_one(at, total):
        value = x_v[at, :].astype(F32) + total
        middle_v[at, :] = value
        return rms_scale(value, gain_one).astype(BF)

    def between(g, part):
        at = rows_of(g, span)

        @pl.when(part == 0)
        def _():
            out(1, g, one.spread, two_o).start()

            @pl.when(chain.mid)
            def _():
                out(0, g, middle_v, middle_o).start()

        @pl.when(part < PARTS - 1)
        def _():
            col = columns(part, tile)
            gate = matmul(one.spread[at, :], wg_v[:, col])
            up = matmul(one.spread[at, :], wu_v[:, col])
            sig = jax.nn.sigmoid(gate)
            act = gate * sig
            hidden_v[at, col] = (act * up).astype(BF)
            silu_v[at, col] = act.astype(BF)
            slope_v[at, col] = (up * (sig * (1.0 + gate * (1.0 - sig)))).astype(BF)

        @pl.when(part == PARTS - 1)
        def _():
            fill(two.part, at, lambda col: matmul(hidden_v[at, :], wd_v[:, col]))
            two.offer(g)
            out(2, g, slope_v, slope_o).start()
            out(3, g, silu_v, silu_o).start()
            out(4, g, hidden_v, hidden_o).start()

    def ahead(g):
        @pl.when(g == 0)
        def _():
            wait_all(loads[5:])

        @pl.when(chain.mid)
        def _():
            out(0, g, middle_v, middle_o).wait()

    def made_two(at, total):
        value = middle_v[at, :] + total
        middle_v[at, :] = value
        return rms_scale(value, gain_two).astype(BF)

    def after(g):
        at = rows_of(g, span)

        @pl.when(chain.mid)
        def _():
            out(5, g, middle_v, x_o).start()

        k_v[at, :] = matmul(two.spread[at, :], wk_v[...])
        v_v[at, :] = matmul(two.spread[at, :], wv_v[...]).astype(BF)
        for j in range(key_heads):
            key_strip(k_v, v_v, keys_v, values_v, key_gain[depth + 1 : depth + 2, :], cos, sin, j, at)

        @pl.when(half == 0)
        def _():
            give_keys(g, 0).start()
            give_keys(g, 1).start()

        keep_keys(g, 0).start()
        keep_keys(g, 1).start()
        out(8, g, k_v, k_o).start()
        q_v[at, :] = matmul(two.spread[at, :], wq_v[...])
        out(7, g, q_v, q_o).start()
        logit_v[at, :] = matmul(two.spread[at, :], gh[depth + 1])
        out(10, g, logit_v, logit_o).start()
        out(6, g, two.spread, normed_o).start()

    loop(STEPS, lambda s: two_sums(s, one, two, made_one, between, ahead, made_two, after))
    one.close()
    two.close()

    def drain(g):
        @pl.when(chain.mid)
        def _():
            out(5, g, middle_v, x_o).wait()

        for k, src, dst in (
            (1, one.spread, two_o), (2, slope_v, slope_o), (3, silu_v, silu_o),
            (4, hidden_v, hidden_o), (6, two.spread, normed_o), (7, q_v, q_o),
            (8, k_v, k_o), (10, logit_v, logit_o),
        ):
            out(k, g, src, dst).wait()
        for which in range(2):
            keep_keys(g, which).wait()

            @pl.when(half == 0)
            def _(which=which):
                give_keys(g, which).wait_send()

            @pl.when(half == 1)
            def _(which=which):
                give_keys(g, which).wait_recv()

    loop(GROUPS, drain)


def turn_kernel(
    size, plane_sizes, depth, rows, width,
    mixed, x_in, cot, wo, feed_gain, wg, wu, wd,
    two_o, down_o, gate_o, up_o, grad_o, low_o, mixed_o, gain_o, made_o,
    *scratch,
):
    (wo_v, wg_v, wu_v, wd_v, middle_v, cot_v, hidden_v, gate_v, up_v, mixed_v, down_v, gain_v,
     load_sem, out_sem) = scratch[:14]
    chain = Chain(size)
    landed = scratch[14]
    one = Sum(chain, scratch[15:22], (landed, 1), rows, width)
    two = Sum(chain, scratch[22:29], (landed, 2), rows, width)
    plane = Plane(*plane_sizes)
    unit = made_o.shape[1] if made_o.shape[1] < 256 else 256
    scatter = Scatter(
        plane, scratch[29:], cot_v, hidden_v, [(made_o, False, hidden_v.shape[1] // unit, [])],
        width // plane.count, unit,
    )
    span = one.block * GROUP
    loads = load_all(
        [(wo.at[depth], wo_v), (x_in, middle_v), (cot, cot_v), (wg.at[depth], wg_v),
         (wu.at[depth], wu_v), (wd.at[depth], wd_v)],
        load_sem,
    )
    chain.greet(plane.partners())
    tile = wg_v.shape[1] // (PARTS - 1)
    gain_one = feed_gain[depth : depth + 1, :]

    def out(k, g, src, dst):
        at = rows_of(g, span)
        return pltpu.make_async_copy(src.at[at], dst.at[at], out_sem.at[k, g])

    loads[0].wait()

    def start(g):
        at = rows_of(g, span)
        fill(one.part, at, lambda col: matmul(mixed[at, :], wo_v[:, col]))
        one.offer(g)

    loop(GROUPS, start)
    gain_v[...] = jnp.zeros_like(gain_v)
    wait_all(loads[1:])

    def made_one(at, total):
        value = middle_v[at, :] + total
        middle_v[at, :] = value
        return rms_scale(value, gain_one).astype(BF)

    def between(g, part):
        at = rows_of(g, span)

        @pl.when(part == 0)
        def _():
            out(0, g, one.spread, two_o).start()

        @pl.when(part < PARTS - 1)
        def _():
            col = columns(part, tile)
            gate = matmul(one.spread[at, :], wg_v[:, col])
            sig = jax.nn.sigmoid(gate)
            act = gate * sig
            slope = sig * (1.0 + gate * (1.0 - sig))
            up = matmul(one.spread[at, :], wu_v[:, col])
            hidden_v[at, col] = (act * up).astype(BF)
            pulled = back_product(cot_v[at, :], wd_v[col, :])
            gate_v[at, col] = (pulled * up * slope).astype(BF)
            up_v[at, col] = (pulled * act).astype(BF)

        @pl.when(part == PARTS - 1)
        def _():
            fill(
                two.part,
                at,
                lambda col: back_product(gate_v[at, :], wg_v[col, :])
                + back_product(up_v[at, :], wu_v[col, :]),
            )
            two.offer(g)
            out(2, g, gate_v, gate_o).start()
            out(3, g, up_v, up_o).start()

    def ahead(g):
        at = rows_of(g, span)
        share = jnp.where(chain.first_mid, 1.0, 0.0)

        @pl.when(chain.first_mid)
        def _():
            fill(down_v, at, lambda col: matmul(hidden_v[at, :], wd_v[:, col]) + middle_v[at, col])

        @pl.when(jnp.logical_not(chain.first_mid))
        def _():
            fill(down_v, at, lambda col: matmul(hidden_v[at, :], wd_v[:, col]))

        out(4, g, down_v, down_o).start()

    def made_two(at, total):
        pulled, terms = back_norm(middle_v[at, :], gain_one, total)
        gain_v[...] += fold(terms)
        value = cot_v[at, :].astype(F32) + pulled
        middle_v[at, :] = value
        return value.astype(BF)

    def after(g):
        at = rows_of(g, span)

        @pl.when(chain.mid)
        def _():
            out(5, g, middle_v, grad_o).start()

        out(6, g, two.spread, low_o).start()
        mixed_v[at, :] = back_product(two.spread[at, :], wo_v[...])
        out(7, g, mixed_v, mixed_o).start()


    def step(s):
        two_sums(s, one, two, made_one, between, ahead, made_two, after)
        ahead_ticks = jnp.where(chain.outer, OUTER_AHEAD, 0)

        def ticks_before(s):
            return jnp.where(s > EARLY, (s - EARLY) * TURN_PACE + ahead_ticks, 0)

        lax.fori_loop(
            ticks_before(s), ticks_before(s + 1), lambda t, carry: (scatter.tick(t), carry)[1], 0
        )

    loop(max(STEPS, EARLY + -(-scatter.steps // TURN_PACE)), step)

    @pl.when(jnp.logical_not(chain.first_mid))
    def _():
        gain_v[...] = jnp.zeros_like(gain_v)

    gain_out = pltpu.make_async_copy(gain_v, gain_o, out_sem.at[8, 0])
    gain_out.start()
    one.close()
    two.close()
    scatter.close()

    def drain(g):
        @pl.when(chain.mid)
        def _():
            out(5, g, middle_v, grad_o).wait()

        for k, src, dst in (
            (0, one.spread, two_o), (2, gate_v, gate_o), (3, up_v, up_o), (4, down_v, down_o),
            (6, two.spread, low_o), (7, mixed_v, mixed_o),
        ):
            out(k, g, src, dst).wait()

    loop(GROUPS, drain)
    gain_out.wait()


def back_kernel(
    size, plane_sizes, depth, rows, width,
    *refs,
):
    (prefix, mixed_grad, logits, attended, q_rot, keys, values, norm, q_raw, k_raw, query_gain, key_gain,
     cos, sin, normed_in, gh, x_in, grad_in, attention_gain, wq, wk, wv,
     wd, wg, wu, slope_in, silu_in, middle_in, feed_gain, wo,
     two_in, gate_in, up_in, low_in, mixed_in,
     gate_o, up_o, first_o, grad_o, low_o, mixed_o, gain_o, feed_gain_o, heads_o, q_gain_o, k_gain_o,
     *rest) = refs
    made, scratch = rest[:4], rest[4:]
    attend_made, attend_scratch, scratch = scratch[:7], scratch[7:15], scratch[15:]
    q_low, k_low, v_low, l_low, heads_v, q_gain_v, k_gain_v = attend_made
    (wq_v, wk_v, wv_v, ring_v, wo_v, x_v, grad_v, slope_v, silu_v, gate_v, up_v, mixed_v,
     gain_v, feed_v, whole_v, parts_v, gh_v, load_sem, row_sem, tile_sem, out_sem, ring_sem, attend_sem,
     ) = scratch[:23]
    half = lax.axis_index("ctx")
    chain = Chain(size)
    landed = scratch[23]
    one = Sum(chain, scratch[24:31], (landed, 1), rows, width)
    two = Sum(chain, scratch[31:38], (landed, 2), rows, width)
    plane = Plane(*plane_sizes)
    share = width // plane.count
    unit = min(256, wk_v.shape[1])
    units_wide, heads_wide, keys_wide = gate_v.shape[1], wq_v.shape[1], wk_v.shape[1]
    mixed_grad_v, attended_v, q_raw_v, q_grad_v = (
        grad_v.at[:, pl.ds(quarter * heads_wide, heads_wide)] for quarter in range(4)
    )
    normed_v = two.part
    grad_low, inner, k_grad, v_grad, *given = attend_scratch
    pieces, close_attend = attend_back(
        half, depth, prefix, mixed_grad_v, logits, attended_v, q_rot, keys, values, norm, q_raw_v, k_raw,
        query_gain, key_gain, cos, sin, normed_v, *attend_made,
        grad_low, inner, q_grad_v, k_grad, v_grad, *given,
    )
    parts_heads = parts_v.at[:, pl.ds(0, heads_wide)]
    heads_parts = [
        (q_low, parts_heads),
        (k_low, parts_v.at[:, pl.ds(heads_wide, keys_wide)]),
        (v_low, parts_v.at[:, pl.ds(heads_wide + keys_wide, keys_wide)]),
    ]
    scatter = Scatter(
        plane, scratch[38:], whole_v, parts_v,
        [
            (made[0], True, units_wide // unit, [(two_in, whole_v), (gate_in, parts_v)]),
            (made[1], True, units_wide // unit, [(up_in, parts_v)]),
            (made[2], True, (heads_wide + 2 * keys_wide) // unit, [(normed_in, whole_v), *heads_parts]),
            (made[3], False, heads_wide // unit, [(low_in, whole_v), (mixed_in, parts_heads)]),
        ],
        share, unit,
    )
    span = one.block * GROUP
    below = depth - 1
    attend_loads = load_all(
        [(mixed_grad, mixed_grad_v), (attended, attended_v), (normed_in, normed_v), (q_raw, q_raw_v)],
        attend_sem,
    )
    loads = load_all(
        [(wq.at[depth], wq_v), (wk.at[depth], wk_v), (wv.at[depth], wv_v), (gh.at[depth], gh_v),
         (wo.at[below], wo_v)],
        load_sem,
    )
    grad_load = pltpu.make_async_copy(grad_in, grad_v, load_sem.at[5])

    def row_load(src, g, k):
        return pltpu.make_async_copy(src.at[rows_of(g, span)], x_v, row_sem.at[k])

    tile = units_wide // (PARTS - 1)
    strip_wide = wide(width)
    fetches = PARTS - 1 + 2 * (width // strip_wide)
    slots = ring_v.shape[0]

    def fetch(k, act):
        slot, place = lax.rem(k, slots), lax.rem(k, fetches)
        pair = jnp.maximum(place - (PARTS - 1), 0)

        @pl.when(place < PARTS - 1)
        def _():
            src = wd.at[below, rows_of(place, tile)]
            act(pltpu.make_async_copy(src, ring_v.at[slot, pl.ds(0, tile)], ring_sem.at[slot]))

        for which, weight in enumerate((wg, wu)):

            @pl.when((place >= PARTS - 1) & (lax.rem(pair, 2) == which))
            def _(weight=weight):
                src = weight.at[below, rows_of(lax.div(pair, 2), strip_wide)]
                dst = ring_v.at[slot, :, pl.ds(0, units_wide)]
                act(pltpu.make_async_copy(src, dst, ring_sem.at[slot]))

    def fetched(k):
        fetch(k, lambda copy: copy.wait())

    def used(k):
        @pl.when(k + slots < GROUPS * fetches)
        def _():
            fetch(k + slots, lambda copy: copy.start())

    for k in range(slots):
        fetch(jnp.int32(k), lambda copy: copy.start())

    def tile_load(src, dst, g, part, k):
        col = columns(part, tile)
        return pltpu.make_async_copy(
            src.at[rows_of(g, span), col], dst.at[:, col], tile_sem.at[k, part]
        )

    row_load(x_in, 0, 0).start()

    def first_tiles(part):
        tile_load(slope_in, slope_v, 0, part, 0).start()
        tile_load(silu_in, silu_v, 0, part, 1).start()

    loop(PARTS - 1, first_tiles)
    chain.greet([*plane.partners(), {"ctx": 1 - half}])
    wait_all(attend_loads)
    gain_one = attention_gain[depth : depth + 1, :]
    gain_two = feed_gain[below : below + 1, :]

    def out(k, g, src, dst, whole=True):
        at = rows_of(g, span)
        return pltpu.make_async_copy(src.at[at] if whole else src, dst.at[at], out_sem.at[k, g])

    def start(g):
        at = rows_of(g, span)
        fill(
            one.part,
            at,
            lambda col: back_product(q_low[at, :], wq_v[col, :])
            + back_product(k_low[at, :], wk_v[col, :])
            + back_product(v_low[at, :], wv_v[col, :])
            + back_product(l_low[at, :], gh_v[col, :]),
        )
        one.offer(g)

    gain_v[...] = jnp.zeros_like(gain_v)
    feed_v[...] = jnp.zeros_like(feed_v)

    def start_all():
        grad_load.start()
        wait_all(loads)
        loop(GROUPS, start)
        row_load(x_in, 0, 0).wait()
        grad_load.wait()

    def local(at):
        return pl.ds(pl.multiple_of(lax.rem(at.start, span), STRIP), STRIP)

    def made_one(at, total):
        pulled, terms = back_norm(x_v[local(at), :], gain_one, total)
        gain_v[...] += fold(terms)
        value = grad_v[at, :] + pulled
        grad_v[at, :] = value
        return value.astype(BF)

    def between(g, part):
        at = rows_of(g, span)

        @pl.when(part == 0)
        def _():
            out(0, g, one.spread, first_o).start()

            @pl.when(g < GROUPS - 1)
            def _():
                copy = row_load(x_in, g + 1, 1)
                copy.start()
                copy.wait()

            @pl.when(g > 0)
            def _():
                out(1, g - 1, gate_v, gate_o, False).wait()
                out(2, g - 1, up_v, up_o, False).wait()

        @pl.when(part < PARTS - 1)
        def _():
            col = columns(part, tile)
            tile_load(slope_in, slope_v, g, part, 0).wait()
            tile_load(silu_in, silu_v, g, part, 1).wait()
            k = g * fetches + part
            fetched(k)
            weight = ring_v[lax.rem(k, slots), pl.ds(0, tile), :]
            pulled = back_product(one.spread[at, :], weight)
            used(k)
            gate_v[:, col] = (pulled * slope_v[:, col].astype(F32)).astype(BF)
            up_v[:, col] = (pulled * silu_v[:, col].astype(F32)).astype(BF)

            @pl.when(g < GROUPS - 1)
            def _():
                tile_load(slope_in, slope_v, g + 1, part, 0).start()
                tile_load(silu_in, silu_v, g + 1, part, 1).start()

        @pl.when(part == PARTS - 1)
        def _():
            def pair(p):
                k = g * fetches + PARTS - 1 + 2 * p
                fetched(k)
                fetched(k + 1)
                here = pl.ds(0, units_wide)
                two.part[at, columns(p, strip_wide)] = (
                    back_product(gate_v[...], ring_v[lax.rem(k, slots), :, here])
                    + back_product(up_v[...], ring_v[lax.rem(k + 1, slots), :, here])
                ).astype(BF)
                used(k)
                used(k + 1)

            loop(width // strip_wide, pair)
            two.offer(g)
            out(1, g, gate_v, gate_o, False).start()
            out(2, g, up_v, up_o, False).start()

    def ahead(g):
        copy = row_load(middle_in, g, 2)
        copy.start()
        copy.wait()

    def made_two(at, total):
        pulled, terms = back_norm(x_v[local(at), :], gain_two, total)
        feed_v[...] += fold(terms)
        value = grad_v[at, :] + pulled
        grad_v[at, :] = value
        return value.astype(BF)

    def after(g):
        at = rows_of(g, span)

        @pl.when(chain.mid)
        def _():
            out(5, g, grad_v, grad_o).start()

        out(3, g, two.spread, low_o).start()

        @pl.when(g > 0)
        def _():
            out(4, g - 1, mixed_v, mixed_o, False).wait()

        mixed_v[...] = back_product(two.spread[at, :], wo_v[...])
        out(4, g, mixed_v, mixed_o, False).start()

    lead = len(pieces)

    def ticks_before(i):
        since = i - lead - 1
        more = jnp.where(chain.outer & (since >= GROUP), OUTER_MORE, 0)
        return jnp.where(since < 0, lax.div(i + 1, 2), BEFORE + lax.div(since * PACE, 8) + more)

    def step(i):
        for place, piece in enumerate(pieces):
            pl.when(i == place)(piece)
        pl.when(i == lead)(start_all)
        two_sums(i - lead - 1, one, two, made_one, between, ahead, made_two, after)
        lax.fori_loop(
            ticks_before(i), ticks_before(i + 1), lambda t, carry: (scatter.tick(t), carry)[1], 0
        )

    steps = lead + 1 + STEPS
    while BEFORE + (steps - lead - 1) * PACE // 8 < scatter.steps:
        steps += 1
    loop(steps, step)
    close_attend()

    @pl.when(jnp.logical_not(chain.first_mid))
    def _():
        gain_v[...] = jnp.zeros_like(gain_v)
        feed_v[...] = jnp.zeros_like(feed_v)

    gain_out = pltpu.make_async_copy(gain_v, gain_o, out_sem.at[6, 0])
    feed_out = pltpu.make_async_copy(feed_v, feed_gain_o, out_sem.at[7, 0])
    gain_out.start()
    feed_out.start()
    attend_outs = [
        pltpu.make_async_copy(src, dst, attend_sem.at[place])
        for place, (src, dst) in enumerate(
            ((heads_v, heads_o), (q_gain_v, q_gain_o), (k_gain_v, k_gain_o))
        )
    ]
    for copy in attend_outs:
        copy.start()
    one.close()
    two.close()
    scatter.close()

    def drain(g):
        out(0, g, one.spread, first_o).wait()
        out(3, g, two.spread, low_o).wait()

        @pl.when(chain.mid)
        def _():
            out(5, g, grad_v, grad_o).wait()

    loop(GROUPS, drain)
    out(1, GROUPS - 1, gate_v, gate_o, False).wait()
    out(2, GROUPS - 1, up_v, up_o, False).wait()
    out(4, GROUPS - 1, mixed_v, mixed_o, False).wait()
    gain_out.wait()
    feed_out.wait()
    wait_all(attend_outs)


def last_kernel(
    size, plane_sizes, depth, rows, width,
    *refs,
):
    attend_in, refs = refs[:15], refs[15:]
    (gh, gain_one_in, feed_zero_in, feed_one_in, q_gain_one, k_gain_one, heads_one, x_in, grad_in,
     attention_gain, wq, wk, wv, down_in, two_in, gate_in, up_in, first_in, hidden_in, low_in, mixed_in,
     grad_o, result_o, total_o, *rest) = refs
    normed_in = attend_in[14]
    made, rest = rest[:5], rest[5:]
    attend_made, attend_scratch, scratch = rest[:7], rest[7:16], rest[16:]
    q_low, k_low, v_low, l_low, heads_zero, q_gain_zero, k_gain_zero = attend_made
    half = lax.axis_index("ctx")
    pieces, close_attend = attend_back(half, depth, *attend_in, *attend_made, *attend_scratch)
    (wq_v, wk_v, wv_v, x_v, grad_v, gain_v, whole_v, parts_v, total_v, load_sem, out_sem) = scratch[:11]
    chain = Chain(size)
    one = Sum(chain, scratch[12:19], (scratch[11], 1), rows, width)
    two = Sum(chain, scratch[20:27], (scratch[19], 1), rows, width)
    plane = Plane(*plane_sizes)
    total = Total(plane, size, scratch[27:31], 8)
    share = width // plane.count
    units_wide, heads_wide, keys_wide = parts_v.shape[1], wq_v.shape[1], wk_v.shape[1]
    unit = min(256, keys_wide)
    parts_heads = parts_v.at[:, pl.ds(0, heads_wide)]
    heads_parts = [
        (q_low, parts_heads),
        (k_low, parts_v.at[:, pl.ds(heads_wide, keys_wide)]),
        (v_low, parts_v.at[:, pl.ds(heads_wide + keys_wide, keys_wide)]),
    ]
    scatter = Scatter(
        plane, scratch[31:], whole_v, parts_v,
        [
            (made[0], True, units_wide // unit, [(two_in, whole_v), (gate_in, parts_v)]),
            (made[1], True, units_wide // unit, [(up_in, parts_v)]),
            (made[2], False, units_wide // unit, [(first_in, whole_v), (hidden_in, parts_v)]),
            (made[3], True, (heads_wide + 2 * keys_wide) // unit, [(normed_in, whole_v), *heads_parts]),
            (made[4], False, heads_wide // unit, [(low_in, whole_v), (mixed_in, parts_heads)]),
        ],
        share, unit,
    )
    span = one.block * GROUP
    loads = load_all(
        [(wq.at[depth], wq_v), (wk.at[depth], wk_v), (wv.at[depth], wv_v), (x_in, x_v),
         (grad_in, grad_v), (down_in, two.part)],
        load_sem,
    )
    chain.greet([*plane.partners(), *total.across, {"ctx": 1 - half}])
    gain_one = attention_gain[depth : depth + 1, :]

    def out(k, g):
        at = rows_of(g, span)
        src, dst = ((one.spread, grad_o), (two.spread, result_o))[k]
        return pltpu.make_async_copy(src.at[at], dst.at[at], out_sem.at[k, g])

    def start(g):
        at = rows_of(g, span)
        fill(
            one.part,
            at,
            lambda col: back_product(q_low[at, :], wq_v[col, :])
            + back_product(k_low[at, :], wk_v[col, :])
            + back_product(v_low[at, :], wv_v[col, :])
            + back_product(l_low[at, :], gh[depth, col, :]),
        )
        one.offer(g)

    gain_v[...] = jnp.zeros_like(gain_v)

    def made_one(at, total_sum):
        pulled, terms = back_norm(x_v[at, :].astype(F32), gain_one, total_sum)
        gain_v[...] += fold(terms)
        return (grad_v[at, :] + pulled).astype(BF)

    def made_two(at, total_sum):
        return total_sum.astype(BF)

    begin = -(-len(pieces) // PER_TICK)
    first_two, first_one = 3, begin + ONE_AFTER
    sum_ticks = BLOCKS + BLOCKS // ONE_PACE + 1
    first_total = first_one + sum_ticks
    rest_two = first_one + sum_ticks - 1

    def sums(i):
        @pl.when(i == 0)
        def _():
            loads[5].wait()
            two.offer(0)

        for place, piece in enumerate(pieces):
            pl.when(i == place // PER_TICK)(piece)

        @pl.when(i == begin)
        def _():
            wait_all(loads[:5])
            loop(GROUPS, start)
            two.offer(1)

        def one_step(k, sum_here, make, s):
            @pl.when((s >= 0) & (s < BLOCKS))
            def _():
                sum_here.relay(s)

            @pl.when((s >= 1) & (s <= BLOCKS))
            def _():
                sum_here.finish(s - 1, make)

                @pl.when((lax.rem(s, GROUP) == 0) & chain.mid)
                def _():
                    out(k, lax.div(s, GROUP) - 1).start()

        def paced(k, sum_here, make, first, begin_step, end_step, pace):
            since = i - first
            take = lax.rem(since, pace + 1)
            s = lax.div(since, pace + 1) * pace + take + begin_step

            @pl.when((since >= 0) & (take < pace) & (s < end_step))
            def _():
                one_step(k, sum_here, make, s)

        paced(1, two, made_two, first_two, 0, GROUP, 3)
        paced(0, one, made_one, first_one, 0, BLOCKS + 1, ONE_PACE)
        paced(1, two, made_two, rest_two, GROUP, BLOCKS + 1, 3)

    def totals(i):
        @pl.when(i == first_total)
        def _():
            total.value[0] = jnp.zeros(total_v.shape, F32)

            @pl.when(chain.first_mid)
            def _():
                total.value[0, pl.ds(0, 1)] = jnp.sum(gain_v[...], axis=0, keepdims=True)

            for k, gains in enumerate((gain_one_in, feed_zero_in, feed_one_in)):
                total.value[0, pl.ds(k + 1, 1)] = jnp.sum(gains[...], axis=0, keepdims=True)
            for k, gains in enumerate((q_gain_zero, k_gain_zero, q_gain_one, k_gain_one)):
                total.value[0, pl.ds(4, 1), pl.ds(k * HD, HD)] = jnp.sum(
                    gains[...], axis=0, keepdims=True
                )
            for k, heads in enumerate((heads_zero, heads_one)):
                total.value[0, pl.ds(8 + 4 * k, 4)] = heads[pl.ds(0, 4), :]

        for k in range(len(total.stages)):

            @pl.when(i == first_total + total.times[k])
            def _(k=k):
                total.start(k)

    def step(i):
        scatter.tick(i)
        sums(i)
        totals(i)

    last_two = rest_two + 4 * -(-(BLOCKS + 1 - GROUP) // 3)
    loop(max(scatter.steps, last_two, first_total + total.times[-1]), step)
    close_attend()

    def receive(g):
        one.receive(g)
        two.receive(g)

        @pl.when(chain.outer)
        def _():
            out(0, g).start()
            out(1, g).start()

    loop(GROUPS, receive)
    total.finish(total_v)
    total_out = pltpu.make_async_copy(total_v, total_o, out_sem.at[2, 0])
    total_out.start()
    one.close()
    two.close()
    scatter.close()

    def drain(g):
        out(0, g).wait()
        out(1, g).wait()

    loop(GROUPS, drain)
    total_out.wait()


def widen_kernel(heads_wide, keys_wide, low_in, result_in, *refs):
    below, above = refs[0:5], refs[5:10]
    stream_o, result_o, gate_o, up_o, down_o, q_o, k_o, v_o, out_o = refs[10:]
    result_o[...] = result_in[...]
    stream_o[...] = low_in[...].astype(F32)
    for depth, made in enumerate((below, above)):
        gate_o[depth] = made[0][...].astype(F32)
        up_o[depth] = made[1][...].astype(F32)
        down_o[depth] = made[2][...].astype(F32)
        q_o[depth] = made[3][:, :heads_wide].astype(F32)
        k_o[depth] = made[3][:, heads_wide : heads_wide + keys_wide].astype(F32)
        v_o[depth] = made[3][:, heads_wide + keys_wide :].astype(F32)
        out_o[depth] = made[4][...].astype(F32)


def widen(stream_low, result, below, above, heads_wide, keys_wide):
    cuts = 4

    def cut(shape):
        return pl.BlockSpec((shape[0] // cuts, shape[1]), lambda i: (i, 0))

    def pair(shape):
        return pl.BlockSpec((2, shape[0] // cuts, shape[1]), lambda i: (0, i, 0))

    share = below[0].shape[0]
    shapes = [
        below[0].shape, below[1].shape, below[2].shape, (share, heads_wide), (share, keys_wide),
        (share, keys_wide), below[4].shape,
    ]
    inputs = [stream_low, result, *below, *above]
    return pl.pallas_call(
        partial(widen_kernel, heads_wide, keys_wide),
        grid=(cuts,),
        out_shape=(
            jax.ShapeDtypeStruct(stream_low.shape, F32),
            jax.ShapeDtypeStruct(result.shape, BF),
            *(jax.ShapeDtypeStruct((2, *shape), F32) for shape in shapes),
        ),
        in_specs=[cut(array.shape) for array in inputs],
        out_specs=(cut(stream_low.shape), cut(result.shape), *(pair(shape) for shape in shapes)),
        compiler_params=pltpu.CompilerParams(vmem_limit_bytes=VMEM_LIMIT),
    )(*inputs)


def call(kernel, collective_id, in_specs, outs, scratch, flops, out_spec=ANY):
    return pl.pallas_call(
        kernel,
        out_shape=tuple(jax.ShapeDtypeStruct(shape, kind) for shape, kind in outs),
        in_specs=in_specs,
        out_specs=tuple(out_spec for _ in outs),
        scratch_shapes=scratch,
        cost_estimate=pl.CostEstimate(flops=flops, bytes_accessed=40_000_000, transcendentals=0),
        compiler_params=pltpu.CompilerParams(
            collective_id=collective_id,
            has_side_effects=collective_id is not None,
            vmem_limit_bytes=VMEM_LIMIT,
        ),
    )


def dma(*shape):
    return pltpu.SemaphoreType.DMA(shape)


def shards(
    size,
    stream,
    cotangent,
    prefixes,
    attention_gain,
    query_weight,
    key_weight,
    value_weight,
    gate_heads,
    query_gain,
    key_gain,
    output_weight,
    feed_gain,
    gate_weight,
    up_weight,
    down_weight,
):
    seq_count, row_count, width = stream.shape
    rows = seq_count * row_count
    span = rows // GROUPS
    dp_size = lax.axis_size("dp")
    plane_sizes = (dp_size, lax.axis_size("ctx"))
    plane_count = plane_sizes[0] * plane_sizes[1]
    heads_wide = query_weight.shape[2]
    keys_wide = key_weight.shape[2]
    units = gate_weight.shape[2]
    gates = gate_heads.shape[2]
    share = width // plane_count
    unit = min(256, keys_wide)
    here = lax.axis_index("dp") * plane_sizes[1] + lax.axis_index("ctx")
    first_row = lax.axis_index("ctx") * row_count
    cos, sin = (
        lax.dynamic_slice_in_dim(jnp.asarray(table), first_row, row_count)
        for table in rotary_tables(row_count * plane_sizes[1])
    )
    stream_flat = stream.reshape(rows, width)
    cot_flat = cotangent.reshape(rows, width)
    heads_padded = jnp.pad(gate_heads, ((0, 0), (0, 0), (0, LANES - gates)))
    sum_scratch = Sum.scratch(rows, width)
    landed = [pltpu.VMEM((2, rows, width), BF)]
    pair_scratch = [pltpu.VMEM((3, rows, width), BF)] + sum_scratch + sum_scratch

    key_heads = keys_wide // HD
    attend_outs = [
        ((rows, heads_wide), BF), ((rows, heads_wide), BF), ((heads_wide // HD, rows, 1), F32),
        ((rows, heads_wide), F32),
    ]
    key_outs = [((2, key_heads, rows, HD), BF), ((2, key_heads, rows, HD), BF)]
    smem = pl.BlockSpec(memory_space=pltpu.SMEM)

    attend_back_outs = [
        ((rows, heads_wide), BF), ((rows, keys_wide), BF), ((rows, keys_wide), BF),
        ((rows, LANES), BF), ((8, width), F32), ((8, HD), F32), ((8, HD), F32),
    ]
    attend_back_scratch = [
        pltpu.VMEM((rows, heads_wide), BF), pltpu.VMEM((heads_wide // HD, rows, 1), F32),
        pltpu.VMEM((rows, heads_wide), F32), pltpu.VMEM((key_heads, rows, HD), F32),
        pltpu.VMEM((key_heads, rows, HD), F32), pltpu.VMEM((key_heads, 2, rows, HD), BF),
        pltpu.VMEM((key_heads, 2, rows, HD), BF), dma(key_heads), dma(key_heads),
    ]

    def attend_back_in(mixed_grad, logits, saved, q_raw, k_raw, normed):
        mixed, q_rot, norm, attended, keys, values = saved
        return (
            prefixes, mixed_grad, logits, attended, q_rot, keys, values, norm, q_raw, k_raw,
            query_gain, key_gain, cos, sin, normed,
        )

    made_shapes = [
        ((share, units), BF), ((share, units), BF), ((units, share), BF),
        ((share, heads_wide + 2 * keys_wide), BF), ((heads_wide, share), BF),
    ]
    scatter_scratch = Scatter.scratch(plane_count, share, unit)

    *saved_zero, normed_zero, q_raw_zero, k_raw_zero, logits_zero = call(
        partial(first_kernel, 0),
        4,
        [smem, WHOLE, WHOLE, ANY, ANY, ANY] + [WHOLE] * 5,
        attend_outs
        + key_outs
        + [
            ((rows, width), BF), ((rows, heads_wide), F32), ((rows, keys_wide), F32),
            ((rows, LANES), F32),
        ],
        [
            pltpu.VMEM((rows, keys_wide), BF), pltpu.VMEM((width, heads_wide), BF),
            pltpu.VMEM((width, keys_wide), BF), pltpu.VMEM((width, keys_wide), BF), dma(3),
            dma(key_heads, 2), dma(key_heads, 2),
        ]
        + attend_scratch(rows, heads_wide),
        3_500_000_000,
        WHOLE,
    )(
        prefixes, stream_flat, attention_gain, query_weight, key_weight, value_weight, heads_padded,
        query_gain, key_gain, cos, sin,
    )
    mixed_zero = saved_zero[0]
    middle_zero, two_zero, slope, silu, hidden_zero, x_one, normed_one, q_raw, k_raw, logits, *keys_one = call(
        partial(forward_kernel, size, 0, rows, width),
        0,
        [WHOLE, ANY, ANY, WHOLE, ANY, ANY, ANY, WHOLE, ANY, ANY, ANY] + [WHOLE] * 4,
        [
            ((rows, width), F32), ((rows, width), BF), ((rows, units), BF), ((rows, units), BF),
            ((rows, units), BF), ((rows, width), F32), ((rows, width), BF),
            ((rows, heads_wide), F32), ((rows, keys_wide), F32), ((rows, LANES), F32), *key_outs,
        ],
        [
            pltpu.VMEM((heads_wide, width), BF), pltpu.VMEM((width, units), BF),
            pltpu.VMEM((width, units), BF), pltpu.VMEM((units, width), BF),
            pltpu.VMEM((width, heads_wide), BF), pltpu.VMEM((width, keys_wide), BF),
            pltpu.VMEM((width, keys_wide), BF), pltpu.VMEM((rows, width), BF),
            pltpu.VMEM((rows, width), F32), pltpu.VMEM((rows, units), BF),
            pltpu.VMEM((rows, units), BF), pltpu.VMEM((rows, units), BF),
            pltpu.VMEM((rows, heads_wide), F32), pltpu.VMEM((rows, keys_wide), F32),
            pltpu.VMEM((rows, keys_wide), BF), pltpu.VMEM((rows, LANES), F32),
            dma(8), dma(11, GROUPS), pltpu.VMEM((key_heads, rows, HD), BF),
            pltpu.VMEM((key_heads, rows, HD), BF), dma(2, GROUPS), dma(2, GROUPS), dma(2, GROUPS),
        ]
        + pair_scratch,
        13_000_000_000,
    )(
        mixed_zero, stream_flat, output_weight, feed_gain, gate_weight, up_weight, down_weight,
        attention_gain, query_weight, key_weight, value_weight, heads_padded, key_gain, cos, sin,
    )
    attended_one = call(
        partial(attend_kernel, 1),
        None,
        [smem] + [WHOLE] * 7,
        attend_outs,
        attend_scratch(rows, heads_wide),
        1_000_000_000,
        WHOLE,
    )(prefixes, q_raw, logits, query_gain, cos, sin, *keys_one)
    saved_one = [*attended_one, *keys_one]
    mixed_one = saved_one[0]
    two_one, down_part, gate_low, up_low, grad, low, mixed_grad, feed_one, down_made = call(
        partial(turn_kernel, size, plane_sizes, 1, rows, width),
        1,
        [WHOLE, ANY, ANY, ANY, WHOLE, ANY, ANY, ANY],
        [
            ((rows, width), BF), ((rows, width), BF), ((rows, units), BF),
            ((rows, units), BF), ((rows, width), F32), ((rows, width), BF),
            ((rows, heads_wide), F32), ((8, width), F32), made_shapes[2],
        ],
        [
            pltpu.VMEM((heads_wide, width), BF), pltpu.VMEM((width, units), BF),
            pltpu.VMEM((width, units), BF), pltpu.VMEM((units, width), BF),
            pltpu.VMEM((rows, width), F32), pltpu.VMEM((rows, width), BF),
            pltpu.VMEM((rows, units), BF), pltpu.VMEM((rows, units), BF),
            pltpu.VMEM((rows, units), BF), pltpu.VMEM((rows, heads_wide), F32),
            pltpu.VMEM((rows, width), BF), pltpu.VMEM((8, width), F32),
            dma(6), dma(9, GROUPS),
        ]
        + pair_scratch + scatter_scratch,
        24_000_000_000,
    )(mixed_one, x_one, cot_flat, output_weight, feed_gain, gate_weight, up_weight, down_weight)
    (gate_low, up_low, first_low, grad, low, mixed_grad, gain_one, feed_zero, heads_one, q_gain_one,
     k_gain_one, *made_one) = call(
        partial(back_kernel, size, plane_sizes, 1, rows, width),
        2,
        [smem, ANY, WHOLE, ANY] + [WHOLE] * 4 + [ANY] + [WHOLE] * 5 + [ANY]
        + [ANY, ANY, ANY, WHOLE] + [ANY] * 9 + [WHOLE] + [ANY] * 6,
        [
            ((rows, units), BF), ((rows, units), BF), ((rows, width), BF), ((rows, width), F32),
            ((rows, width), BF), ((rows, heads_wide), F32), ((8, width), F32), ((8, width), F32),
            ((8, width), F32), ((8, HD), F32), ((8, HD), F32), *made_shapes[:2], *made_shapes[3:],
        ],
        [pltpu.VMEM(shape, kind) for shape, kind in attend_back_outs]
        + attend_back_scratch[:2] + attend_back_scratch[3:]
        + [
            pltpu.VMEM((width, heads_wide), BF), pltpu.VMEM((width, keys_wide), BF),
            pltpu.VMEM((width, keys_wide), BF), pltpu.VMEM((4, 512, width), BF),
            pltpu.VMEM((heads_wide, width), BF), pltpu.VMEM((span, width), F32),
            pltpu.VMEM((rows, width), F32), pltpu.VMEM((span, units), BF),
            pltpu.VMEM((span, units), BF), pltpu.VMEM((span, units), BF),
            pltpu.VMEM((span, units), BF), pltpu.VMEM((span, heads_wide), F32),
            pltpu.VMEM((8, width), F32), pltpu.VMEM((8, width), F32),
            pltpu.VMEM((rows, width), BF), pltpu.VMEM((rows, units), BF),
            pltpu.VMEM((width, LANES), BF),
            dma(6), dma(3), dma(2, PARTS - 1), dma(8, GROUPS), dma(4), dma(4),
        ]
        + pair_scratch + scatter_scratch,
        28_000_000_000,
    )(
        *attend_back_in(mixed_grad, logits, saved_one, q_raw, k_raw, normed_one),
        heads_padded, x_one, grad, attention_gain,
        query_weight, key_weight, value_weight, down_weight, gate_weight, up_weight, slope, silu,
        middle_zero, feed_gain, output_weight,
        two_one, gate_low, up_low, low, mixed_one,
    )
    made_one.insert(2, down_made)
    below_rows = 8
    stages = plane_count.bit_length() - 1 + size.bit_length() - 1
    stream_low, result, totals, *made_zero = call(
        partial(last_kernel, size, plane_sizes, 0, rows, width),
        3,
        [smem] + [WHOLE] * 14 + [WHOLE] * 7 + [ANY, ANY, WHOLE] + [ANY] * 11,
        [
            ((rows, width), BF), ((rows, width), BF), ((8 + below_rows, width), F32), *made_shapes,
        ],
        [pltpu.VMEM(shape, kind) for shape, kind in attend_back_outs]
        + attend_back_scratch
        + [
            pltpu.VMEM((width, heads_wide), BF), pltpu.VMEM((width, keys_wide), BF),
            pltpu.VMEM((width, keys_wide), BF), pltpu.VMEM((rows, width), BF),
            pltpu.VMEM((rows, width), F32), pltpu.VMEM((8, width), F32),
            pltpu.VMEM((rows, width), BF), pltpu.VMEM((rows, units), BF),
            pltpu.VMEM((8 + below_rows, width), F32), dma(6), dma(3, GROUPS),
        ]
        + landed + sum_scratch + landed + sum_scratch
        + Total.scratch(8 + below_rows, width, stages) + scatter_scratch,
        19_000_000_000,
    )(
        *attend_back_in(mixed_grad, logits_zero, saved_zero, q_raw_zero, k_raw_zero, normed_zero),
        heads_padded, gain_one, feed_zero, feed_one, q_gain_one, k_gain_one, heads_one, stream_flat,
        grad, attention_gain, query_weight, key_weight, value_weight, down_part,
        two_zero, gate_low, up_low, first_low, hidden_zero, low, mixed_zero,
    )
    stream_grad, result, *weights = widen(stream_low, result, made_zero, made_one, heads_wide, keys_wide)

    def own(array, wide_share):
        return lax.dynamic_slice_in_dim(array, here * wide_share, wide_share, array.ndim - 1)

    gains = own(totals[:4], share)
    head_gains = own(totals[4, : 4 * HD].reshape(2, 2, HD), HD // plane_count)
    heads = own(totals[8:].reshape(LAYERS, 4, width)[:, :gates], share)
    return (
        result.reshape(seq_count, row_count, width),
        stream_grad.reshape(seq_count, row_count, width),
        gains[0:2],
        weights[3],
        weights[4],
        weights[5],
        heads.transpose(0, 2, 1),
        head_gains[:, 0],
        head_gains[:, 1],
        weights[6],
        gains[2:4],
        weights[0],
        weights[1],
        weights[2],
    )


def solution(mesh):
    return jax.shard_map(
        partial(shards, mesh.shape["tensor"]),
        mesh=mesh,
        in_specs=(
            P("dp", "ctx", None),
            P("dp", "ctx", None),
            P("dp"),
            P(),
            P(None, None, "tensor"),
            P(None, None, "tensor"),
            P(None, None, "tensor"),
            P(None, None, "tensor"),
            P(),
            P(),
            P(None, "tensor", None),
            P(),
            P(None, None, "tensor"),
            P(None, None, "tensor"),
            P(None, "tensor", None),
        ),
        out_specs=(
            P("dp", "ctx", None),
            P("dp", "ctx", None),
            P(None, ("dp", "ctx")),
            P(None, ("dp", "ctx"), "tensor"),
            P(None, ("dp", "ctx"), "tensor"),
            P(None, ("dp", "ctx"), "tensor"),
            P(None, ("dp", "ctx"), "tensor"),
            P(None, ("dp", "ctx")),
            P(None, ("dp", "ctx")),
            P(None, "tensor", ("dp", "ctx")),
            P(None, ("dp", "ctx")),
            P(None, ("dp", "ctx"), "tensor"),
            P(None, ("dp", "ctx"), "tensor"),
            P(None, "tensor", ("dp", "ctx")),
        ),
        check_vma=False,
    )
```

```python
from functools import partial

import jax
import jax.numpy as jnp
import numpy as np
from jax import lax
from jax.experimental import pallas as pl
from jax.experimental.pallas import tpu as pltpu
from jax.sharding import PartitionSpec as P

HD = 128
LAYERS = 2
LANES = 128

epsilon = 1e-06
theta = 1000000.0
masked = -1000000000.0

BF = jnp.bfloat16
F32 = jnp.float32
ANY = pl.BlockSpec(memory_space=pl.ANY)
WHOLE = pl.BlockSpec(memory_space=pltpu.VMEM)
MESH = pl.DeviceIdType.MESH

BLOCKS = 8
PIECES = 2
GROUP = 4
STRIP = 16
UNROLL = 2
VMEM_LIMIT = 63 * 1024 * 1024


def rms_scale(values, gain):
    return values * lax.rsqrt(jnp.mean(values * values, axis=-1, keepdims=True) + epsilon) * gain


def rotary_tables(length):
    counter = np.arange(HD // 2, dtype=np.float32)
    frequency = np.power(np.float32(theta), np.float32(-2.0) * counter / np.float32(HD))
    angles = np.arange(length, dtype=np.float32)[:, None] * frequency[None, :].astype(np.float32)
    cos, sin = np.cos(angles), np.sin(angles)
    return (
        np.concatenate([cos, cos], axis=1).astype(np.float32),
        np.concatenate([-sin, sin], axis=1).astype(np.float32),
    )


def matmul(left, right):
    return jnp.dot(left, right, preferred_element_type=F32)


def weight_product(left, right):
    return lax.dot_general(left, right, (((0,), (0,)), ((), ())), preferred_element_type=F32)


def back_product(gradient, weight):
    return lax.dot_general(gradient, weight, (((1,), (1,)), ((), ())), preferred_element_type=F32)


def loop(count, body, unroll=1):
    def step(i, carry):
        body(i)
        return carry

    lax.fori_loop(0, count, step, 0, unroll=unroll)


def rows_of(r, block):
    return pl.ds(pl.multiple_of(r * block, block), block)


def columns(j, width):
    return pl.ds(pl.multiple_of(j * width, width), width)


def greet(targets, extra, has_extra):
    barrier = pltpu.get_barrier_semaphore()
    for target in targets:
        pl.semaphore_signal(barrier, inc=1, device_id=target, device_id_type=MESH)

    @pl.when(has_extra)
    def _():
        pl.semaphore_signal(barrier, inc=1, device_id=extra, device_id_type=MESH)
        pl.semaphore_wait(barrier, len(targets) + 1)

    @pl.when(jnp.logical_not(has_extra))
    def _():
        pl.semaphore_wait(barrier, len(targets))


class Chain:
    def __init__(self, size):
        self.size = size
        self.spot = lax.axis_index("tensor")
        half = size // 2
        on_left = self.spot < half
        self.end = (self.spot == 0) | (self.spot == size - 1)
        self.inner = jnp.logical_not(self.end)
        self.mid = (self.spot == half - 1) | (self.spot == half)
        self.outer = jnp.logical_not(self.mid)
        self.first_mid = self.spot == half - 1
        self.inward = {"tensor": jnp.where(on_left, self.spot + 1, self.spot - 1)}
        self.outward = {"tensor": jnp.where(on_left, self.spot - 1, self.spot + 1)}

    def greet(self, others=()):
        greet([self.inward, *others], self.outward, self.inner)


class Sum:
    def __init__(self, chain, refs, landed, rows, width):
        self.chain = chain
        self.part, self.spread, self.s_in, self.r_in, self.s_out, self.r_out, self.r_cross = refs
        self.landed, self.cross = landed
        self.block = rows // BLOCKS
        self.piece = width // PIECES

    @staticmethod
    def scratch(rows, width):
        return [
            pltpu.VMEM((rows, width), BF),
            pltpu.VMEM((rows, width), BF),
            pltpu.SemaphoreType.DMA((BLOCKS, PIECES)),
            pltpu.SemaphoreType.DMA((BLOCKS, PIECES)),
            pltpu.SemaphoreType.DMA((BLOCKS,)),
            pltpu.SemaphoreType.DMA((BLOCKS,)),
            pltpu.SemaphoreType.DMA((BLOCKS, PIECES)),
        ]

    def hop(self, r, p, across):
        where = (rows_of(r, self.block), columns(p, self.piece))
        return pltpu.make_async_remote_copy(
            src_ref=self.part.at[where],
            dst_ref=self.landed.at[(self.cross if across else 0,) + where],
            send_sem=self.s_in.at[r, p],
            recv_sem=(self.r_cross if across else self.r_in).at[r, p],
            device_id=self.chain.inward,
            device_id_type=MESH,
        )

    def out_hop(self, r):
        at = rows_of(r, self.block)
        return pltpu.make_async_remote_copy(
            src_ref=self.spread.at[at],
            dst_ref=self.spread.at[at],
            send_sem=self.s_out.at[r],
            recv_sem=self.r_out.at[r],
            device_id=self.chain.outward,
            device_id_type=MESH,
        )

    def offer(self, g):
        @pl.when(self.chain.end)
        def _():
            def one(k):
                for p in range(PIECES):
                    self.hop(g * GROUP + k, p, False).start()

            loop(GROUP, one)

    def relay(self, r):
        @pl.when(self.chain.inner)
        def _():
            for p in range(PIECES):
                self.hop(r, p, False).wait_recv()
                col = columns(p, self.piece)

                def strip(i, col=col):
                    at = pl.ds(pl.multiple_of(r * self.block + i * STRIP, STRIP), STRIP)
                    self.part[at, col] = self.part[at, col] + self.landed[0, at, col]

                loop(self.block // STRIP, strip, True)

                @pl.when(self.chain.mid)
                def _(p=p):
                    self.hop(r, p, True).start()

                @pl.when(self.chain.outer)
                def _(p=p):
                    self.hop(r, p, False).start()

    def finish(self, r, make):
        @pl.when(self.chain.mid)
        def _():
            for p in range(PIECES):
                self.hop(r, p, True).wait_recv()

            def strip(i):
                at = pl.ds(pl.multiple_of(r * self.block + i * STRIP, STRIP), STRIP)
                total = self.part[at, :].astype(F32) + self.landed[self.cross, at, :].astype(F32)
                self.spread[at, :] = make(at, total)

            loop(self.block // STRIP, strip, UNROLL)
            self.out_hop(r).start()

    def receive(self, g):
        @pl.when(self.chain.outer)
        def _():
            def one(k):
                self.out_hop(g * GROUP + k).wait_recv()

                @pl.when(self.chain.inner)
                def _():
                    self.out_hop(g * GROUP + k).start()

            loop(GROUP, one)

    def close(self):
        def block(r):
            for p in range(PIECES):
                self.hop(r, p, False).wait_send()

            @pl.when(self.chain.inner)
            def _():
                self.out_hop(r).wait_send()

        loop(BLOCKS, block)


PARTS = 4
STRIDE = GROUP // PARTS
GROUPS = BLOCKS // GROUP
STEPS = 2 * BLOCKS + 1


def two_sums(s, first, second, made_one, between, ahead, made_two, after):
    @pl.when((s >= 0) & (s < BLOCKS))
    def _():
        first.relay(s)

    @pl.when((s >= 1) & (s <= BLOCKS))
    def _():
        first.finish(s - 1, made_one)

    @pl.when((s >= GROUP) & (s < BLOCKS + GROUP))
    def _():
        place = lax.rem(s - GROUP, GROUP)
        group = lax.div(s - GROUP, GROUP)

        @pl.when(place == 0)
        def _():
            first.receive(group)

        outer = first.chain.outer
        begin = jnp.where(outer, jnp.where(place == 0, 0, PARTS), lax.div(place + STRIDE - 1, STRIDE))
        stop = jnp.where(outer, PARTS, lax.div(place, STRIDE) + 1)
        lax.fori_loop(begin, stop, lambda part, carry: (between(group, part), carry)[1], 0)

    @pl.when((s >= BLOCKS) & (s < 2 * BLOCKS))
    def _():
        second.relay(s - BLOCKS)

    @pl.when((s >= BLOCKS + 1) & (s < STEPS))
    def _():
        @pl.when(lax.rem(s - BLOCKS - 1, GROUP) == 0)
        def _():
            ahead(lax.div(s - BLOCKS - 1, GROUP))

        second.finish(s - BLOCKS - 1, made_two)

        @pl.when(lax.rem(s - BLOCKS, GROUP) == 0)
        def _():
            group = lax.div(s - BLOCKS, GROUP) - 1
            second.receive(group)
            after(group)


def back_norm(value, gain, grad):
    spread = lax.rsqrt(jnp.mean(value * value, axis=-1, keepdims=True) + epsilon)
    scaled = grad * gain
    pulled = jnp.mean(scaled * value, axis=-1, keepdims=True)
    terms = grad * value * spread
    return spread * scaled - value * (spread * spread * spread * pulled), terms


def fold(terms):
    folded = terms[:8]
    for k in range(8, terms.shape[0], 8):
        folded = folded + terms[k : k + 8]
    return folded


def load_all(pairs, sems):
    copies = [pltpu.make_async_copy(src, dst, sems.at[k]) for k, (src, dst) in enumerate(pairs)]
    for copy in copies:
        copy.start()
    return copies


def start_all(copies):
    for copy in copies:
        copy.start()


def wait_all(copies):
    for copy in copies:
        copy.wait()


def wide(width):
    return 512 if width % 512 == 0 else 256


def fill(target, at, make):
    width = target.shape[1]
    tile = wide(width)

    def one(p):
        col = columns(p, tile)
        target[at, col] = make(col).astype(target.dtype)

    loop(width // tile, one)


def flip(value, bit):
    return value + bit * (1 - 2 * lax.rem(lax.div(value, bit), 2))


class Plane:
    def __init__(self, dp_size, ctx_size):
        self.count = dp_size * ctx_size
        self.ctx_size = ctx_size
        self.me = lax.axis_index("dp") * ctx_size + lax.axis_index("ctx")
        bits = [1 << k for k in range(self.count.bit_length() - 1)]
        near = [bit for bit in bits if bit >= ctx_size][:1]
        rest = [bit for bit in bits if bit not in near]
        self.bits = bits
        self.orders = (near + rest, near + rest[1:] + rest[:1])

    def partner(self, bit):
        other = flip(self.me, bit)
        return {"dp": lax.div(other, self.ctx_size), "ctx": lax.rem(other, self.ctx_size)}

    def partners(self):
        return [self.partner(bit) for bit in self.bits]


LEAD = 4
LAST_LEAD = 8
LAST_PACE = 9
BEFORE = 8
OUTER_MORE = 0
PACE = 12
ONE_PACE = 8
PER_TICK = 1
ONE_AFTER = 3
EARLY = BLOCKS + GROUP - 1
TURN_PACE = 2
OUTER_AHEAD = 4


class Scatter:
    SLOTS = (2, 6, 6, 6)
    KEPT = (2, 4, 4, 4)
    RESULTS = 2
    LAGS = (0, 1, 5, 9, 13, 17)

    def __init__(self, plane, refs, whole, parts, groups, share, tile):
        self.plane = plane
        self.whole, self.parts = whole, parts
        self.groups = groups
        self.share, self.tile = share, tile
        self.stages = len(plane.bits)
        self.units = sum(group[2] for group in groups)
        self.refs = [refs[6 * k : 6 * k + 6] for k in range(self.stages)]
        self.made, self.out_sem, self.load_sem = refs[6 * self.stages :]
        self.steps = self.units + self.LAGS[self.stages]

    @classmethod
    def scratch(cls, count, share, tile):
        found = []
        blocks = count // 2
        for k in range(count.bit_length() - 1):
            slots = cls.SLOTS[k]
            found += [
                pltpu.VMEM((depth, blocks, share, tile), BF) for depth in (slots, cls.KEPT[k], slots)
            ]
            found += [
                pltpu.SemaphoreType.DMA((slots,)),
                pltpu.SemaphoreType.DMA((slots,)),
                pltpu.SemaphoreType.REGULAR((slots,)),
            ]
            blocks //= 2
        return found + [
            pltpu.VMEM((cls.RESULTS, share, tile), BF),
            pltpu.SemaphoreType.DMA((cls.RESULTS,)),
            pltpu.SemaphoreType.DMA((4,)),
        ]

    def partner(self, stage, u):
        odd = lax.rem(u, 2) == 1
        even_one, odd_one = (self.plane.partner(order[stage]) for order in self.plane.orders)
        return {axis: jnp.where(odd, odd_one[axis], even_one[axis]) for axis in even_one}

    def copy(self, stage, u):
        send, unused, land, s_sem, r_sem, unused_credit = self.refs[stage]
        slot = lax.rem(u, self.SLOTS[stage])
        return pltpu.make_async_remote_copy(
            src_ref=send.at[slot],
            dst_ref=land.at[slot],
            send_sem=s_sem.at[slot],
            recv_sem=r_sem.at[slot],
            device_id=self.partner(stage, u),
            device_id_type=MESH,
        )

    def ready(self, stage, u):
        @pl.when(u >= self.SLOTS[stage])
        def _():
            self.copy(stage, u - self.SLOTS[stage]).wait_send()

    def push(self, stage, u):
        @pl.when(u >= self.SLOTS[stage])
        def _():
            pl.semaphore_wait(self.refs[stage][5].at[lax.rem(u, self.SLOTS[stage])], 1)

        self.copy(stage, u).start()

    def loads(self, pairs):
        return [
            pltpu.make_async_copy(src, dst, self.load_sem.at[k]) for k, (src, dst) in enumerate(pairs)
        ]

    def prefetch(self):
        start_all(self.loads(self.groups[0][3]))

    def product(self, u):
        send, keep = self.refs[0][:2]
        slot, spot = lax.rem(u, self.SLOTS[0]), lax.rem(u, self.KEPT[0])
        odd = lax.rem(u, 2)
        orders = self.plane.orders
        first = 0
        place = u
        by_rows_here = u < 0
        for index, (unused, by_rows, count, loads) in enumerate(self.groups):
            here = (u >= first) & (u < first + count)
            place = jnp.where(here, u - first, place)
            if by_rows:
                by_rows_here = by_rows_here | here

            @pl.when(u == first)
            def _(loads=loads, index=index):
                copies = self.loads(loads)
                if index:
                    start_all(copies)
                wait_all(copies)

            first += count
        parts = self.parts[:, columns(place, self.tile)]

        def block(far, j):
            owner = flip(self.plane.me, orders[0][0]) if far else self.plane.me
            for bits in reversed(tuple(zip(*orders))[1:]):
                if j % 2:
                    owner = flip(owner, bits[0]) * (1 - odd) + flip(owner, bits[1]) * odd
                j //= 2
            return self.whole[:, columns(owner, self.share)]

        def all_blocks(make):
            for j in range(self.plane.count // 2):
                send[slot, j] = make(block(True, j)).astype(BF)
                keep[spot, j] = make(block(False, j)).astype(BF)

        @pl.when(by_rows_here)
        def _():
            all_blocks(lambda whole: weight_product(whole, parts))

        @pl.when(jnp.logical_not(by_rows_here))
        def _():
            all_blocks(lambda whole: weight_product(parts, whole))

    def merge(self, stage, u):
        unused, keep, land = self.refs[stage][:3]
        slots = self.SLOTS[stage]
        slot, spot = lax.rem(u, slots), lax.rem(u, self.KEPT[stage])
        self.copy(stage, u).wait_recv()
        half = (self.plane.count // 2) >> (stage + 1)
        last = stage == self.stages - 1
        if not last:
            self.ready(stage + 1, u)
            send_on, keep_on = self.refs[stage + 1][:2]
            slot_on = lax.rem(u, self.SLOTS[stage + 1])
            spot_on = lax.rem(u, self.KEPT[stage + 1])

            def one(j):
                send_on[slot_on, j] = keep[spot, half + j] + land[slot, half + j]
                keep_on[spot_on, j] = keep[spot, j] + land[slot, j]

            loop(half, one)
            self.push(stage + 1, u)
        else:
            place = lax.rem(u, self.RESULTS)

            @pl.when(u >= self.RESULTS)
            def _():
                self.results(u - self.RESULTS, lambda copy: copy.wait())

            self.made[place] = keep[spot, 0] + land[slot, 0]
            self.results(u, lambda copy: copy.start())

        @pl.when(u + slots < self.units)
        def _():
            pl.semaphore_signal(
                self.refs[stage][5].at[slot],
                inc=1,
                device_id=self.partner(stage, u),
                device_id_type=MESH,
            )

    def results(self, u, act):
        place = lax.rem(u, self.RESULTS)
        first = 0
        for out, by_rows, count, unused_loads in self.groups:

            @pl.when((u >= first) & (u < first + count))
            def _(by_rows=by_rows, out=out, first=first):
                if by_rows:
                    at = (slice(None), columns(u - first, self.tile))
                else:
                    at = (rows_of(u - first, self.tile), slice(None))
                act(pltpu.make_async_copy(self.made.at[place], out.at[at], self.out_sem.at[place]))

            first += count

    def tick(self, i):
        @pl.when(i < self.units)
        def _():
            self.ready(0, i)
            self.product(i)
            self.push(0, i)

        for stage in reversed(range(self.stages)):
            u = i - self.LAGS[stage + 1]

            @pl.when((u >= 0) & (u < self.units))
            def _(stage=stage, u=u):
                self.merge(stage, u)

    def close(self):
        for stage in range(self.stages):
            for k in range(max(0, self.units - self.SLOTS[stage]), self.units):
                self.copy(stage, jnp.int32(k)).wait_send()
        for k in range(max(0, self.units - self.RESULTS), self.units):
            self.results(jnp.int32(k), lambda copy: copy.wait())


Z_APART = 1
PLANE_APART = 3


class Total:
    def __init__(self, plane, size, refs, own):
        self.value, self.land, self.s_sem, self.r_sem = refs
        spot = lax.axis_index("tensor")
        rows, first = pl.ds(0, self.value.shape[1]), pl.ds(0, own)
        near, *rest = plane.orders[0]
        across = [({"tensor": flip(spot, 1 << k)}, first) for k in range(size.bit_length() - 1)]
        self.across = [target for target, unused in across]
        self.stages = [(plane.partner(near), rows), *across]
        self.stages += [(plane.partner(bit), rows) for bit in rest]
        self.times = [0, 1]
        for unused in across:
            self.times.append(self.times[-1] + Z_APART)
        for unused in rest:
            self.times.append(self.times[-1] + PLANE_APART)

    @staticmethod
    def scratch(rows, width, stages):
        return [
            pltpu.VMEM((stages, rows, width), F32),
            pltpu.VMEM((stages, rows, width), F32),
            pltpu.SemaphoreType.DMA((stages,)),
            pltpu.SemaphoreType.DMA((stages,)),
        ]

    def copy(self, k):
        target, rows = self.stages[k]
        return pltpu.make_async_remote_copy(
            src_ref=self.value.at[k, rows],
            dst_ref=self.land.at[k, rows],
            send_sem=self.s_sem.at[k],
            recv_sem=self.r_sem.at[k],
            device_id=target,
            device_id_type=MESH,
        )

    def take(self, k, target):
        self.copy(k).wait_recv()
        rows = self.stages[k][1]
        target[...] = self.value[k]
        target[rows] = self.value[k, rows] + self.land[k, rows]

    def start(self, k):
        if k > 0:
            self.take(k - 1, self.value.at[k])
        self.copy(k).start()

    def finish(self, target):
        self.take(len(self.stages) - 1, target)
        for k in range(len(self.stages)):
            self.copy(k).wait_send()


def turned(value):
    return pltpu.roll(value, HD // 2, 1)


def head_at(h):
    return pl.ds(h * HD, HD)


def head_norm(raw, gain, cos, sin):
    scaled = rms_scale(raw, gain)
    return scaled * cos + turned(scaled) * sin


def head_norm_back(raw, gain, cos, sin, grad):
    return back_norm(raw, gain, grad * cos - turned(grad) * sin)


def seen(rows, first_row, columns_wide, offset, prefix):
    query = first_row + lax.broadcasted_iota(jnp.int32, (rows, columns_wide), 0)
    key = lax.broadcasted_iota(jnp.int32, (rows, columns_wide), 1)
    return (key <= query) | (key + offset < prefix)


def key_strip(raw, v, keys, values, gain, cos, sin, j, at):
    keys[j, at, :] = head_norm(raw[at, head_at(j)], gain, cos[at, :], sin[at, :]).astype(BF)
    values[j, at, :] = v[at, head_at(j)]


def attend(prefix, q_raw, logits, query_gain, cos, sin, keys, values,
           mixed_o, q_o, norm_o, attended_o, scratch, half, arrived):
    high, low, out = scratch
    rows = q_raw.shape[0]
    span = rows // GROUPS
    key_heads = keys.shape[1]
    shared = q_raw.shape[1] // HD // key_heads
    scale = HD ** (-0.5)

    def own(g):
        at = rows_of(g, span)
        mask = seen(span, g * span, rows, half * rows, prefix)
        for h in range(key_heads * shared):
            j = h // shared
            query = head_norm(q_raw[at, head_at(h)], query_gain, cos[at, :], sin[at, :]).astype(BF)
            q_o[at, head_at(h)] = query
            scores = jnp.where(mask, back_product(query, keys[0, j]) * scale, masked)
            top = jnp.max(scores, axis=1, keepdims=True)
            weights = jnp.exp(scores - top)
            high[h, at, :] = top
            low[h, at, :] = jnp.sum(weights, axis=1, keepdims=True)
            out[at, head_at(h)] = matmul(weights.astype(BF), values[0, j])

    loop(GROUPS, own)

    @pl.when(half == 1)
    def _():
        for h in range(key_heads * shared):
            j = h // shared
            if h % shared == 0:
                arrived(j)

            def other(g, h=h, j=j):
                at = rows_of(g, span)
                scores = back_product(q_o[at, head_at(h)], keys[1, j]) * scale
                before = high[h, at, :]
                top = jnp.maximum(before, jnp.max(scores, axis=1, keepdims=True))
                weights = jnp.exp(scores - top)
                shrink = jnp.exp(before - top)
                high[h, at, :] = top
                low[h, at, :] = low[h, at, :] * shrink + jnp.sum(weights, axis=1, keepdims=True)
                out[at, head_at(h)] = out[at, head_at(h)] * shrink + matmul(
                    weights.astype(BF), values[1, j]
                )

            loop(GROUPS, other)

    def close(g):
        at = rows_of(g, span)
        open_gate = jax.nn.sigmoid(logits[at, :])
        for h in range(key_heads * shared):
            total = low[h, at, :]
            norm_o[h, at, :] = high[h, at, :] + jnp.log(total)
            attended = out[at, head_at(h)] * (1.0 / total)
            attended_o[at, head_at(h)] = attended
            mixed_o[at, head_at(h)] = (attended * open_gate[:, h : h + 1]).astype(BF)

    loop(GROUPS, close)


def attend_scratch(rows, heads_wide):
    return [
        pltpu.VMEM((heads_wide // HD, rows, 1), F32),
        pltpu.VMEM((heads_wide // HD, rows, 1), F32),
        pltpu.VMEM((rows, heads_wide), F32),
    ]


def attend_kernel(
    depth, prefix, q_raw, logits, query_gain, cos, sin, keys_in, values_in,
    mixed_o, q_o, norm_o, attended_o, keys_o, values_o, load_sem, send_sem, land_sem, *scratch,
):
    half = lax.axis_index("ctx")
    rows = q_raw.shape[0]
    span = rows // GROUPS
    early, late = pl.ds(0, rows - span), pl.ds(rows - span, span)
    pairs = ((keys_in, keys_o), (values_in, values_o))
    own = [pltpu.make_async_copy(src.at[0], dst.at[0], load_sem.at[0, k]) for k, (src, dst) in enumerate(pairs)]
    other = [
        pltpu.make_async_copy(src.at[1, :, early], dst.at[1, :, early], load_sem.at[1, k])
        for k, (src, dst) in enumerate(pairs)
    ]
    travel = [
        pltpu.make_async_remote_copy(
            src_ref=src.at[0, :, late],
            dst_ref=dst.at[1, :, late],
            send_sem=send_sem.at[k],
            recv_sem=land_sem.at[k],
            device_id={"ctx": 1 - half},
            device_id_type=MESH,
        )
        for k, (src, dst) in enumerate(pairs)
    ]
    start_all(own)
    greet([{"ctx": 1 - half}], {"ctx": 1 - half}, half < 0)

    @pl.when(half == 0)
    def _():
        start_all(travel)

    @pl.when(half == 1)
    def _():
        start_all(other)

    wait_all(own)

    def arrived(j):
        if j == 0:
            wait_all(other)
            for copy in travel:
                copy.wait_recv()

    attend(prefix[0], q_raw, logits, query_gain[depth : depth + 1, :], cos, sin, keys_o, values_o,
           mixed_o, q_o, norm_o, attended_o, scratch, half, arrived)

    @pl.when(half == 0)
    def _():
        for copy in travel:
            copy.wait_send()


def first_kernel(
    depth, prefix, stream, gain, wq, wk, wv, gh, query_gain, key_gain, cos, sin,
    mixed_o, q_o, norm_o, attended_o, keys_o, values_o, normed_o, q_raw, k_raw, logits,
    v, wq_v, wk_v, wv_v, load_sem, send_sem, land_sem, *scratch,
):
    half = lax.axis_index("ctx")
    loads = load_all([(wk.at[depth], wk_v), (wv.at[depth], wv_v), (wq.at[depth], wq_v)], load_sem)
    greet([{"ctx": 1 - half}], {"ctx": 1 - half}, half < 0)
    rows = stream.shape[0]
    span = rows // GROUPS
    key_heads = k_raw.shape[1] // HD

    def copy(j, which):
        ref = (keys_o, values_o)[which]
        return pltpu.make_async_remote_copy(
            src_ref=ref.at[0, j],
            dst_ref=ref.at[1, j],
            send_sem=send_sem.at[j, which],
            recv_sem=land_sem.at[j, which],
            device_id={"ctx": 1 - half},
            device_id_type=MESH,
        )

    def strip(i):
        at = rows_of(i, STRIP)
        value = stream[at, :].astype(F32)
        normed_o[at, :] = rms_scale(value, gain[depth : depth + 1, :]).astype(BF)

    loop(rows // STRIP, strip, UNROLL)
    wait_all(loads[:2])

    def project_keys(g):
        at = rows_of(g, span)
        k_raw[at, :] = matmul(normed_o[at, :], wk_v[...])
        v[at, :] = matmul(normed_o[at, :], wv_v[...]).astype(BF)
        for j in range(key_heads):
            key_strip(k_raw, v, keys_o.at[0], values_o.at[0], key_gain[depth : depth + 1, :], cos, sin, j, at)

    loop(GROUPS, project_keys)

    @pl.when(half == 0)
    def _():
        for j in range(key_heads):
            copy(j, 0).start()
            copy(j, 1).start()

    loads[2].wait()

    def project(g):
        at = rows_of(g, span)
        q_raw[at, :] = matmul(normed_o[at, :], wq_v[...])
        logits[at, :] = matmul(normed_o[at, :], gh[depth])

    loop(GROUPS, project)

    def arrived(j):
        copy(j, 0).wait_recv()
        copy(j, 1).wait_recv()

    attend(prefix[0], q_raw, logits, query_gain[depth : depth + 1, :], cos, sin, keys_o, values_o,
           mixed_o, q_o, norm_o, attended_o, scratch, half, arrived)

    @pl.when(half == 0)
    def _():
        for j in range(key_heads):
            copy(j, 0).wait_send()
            copy(j, 1).wait_send()


def attend_back(
    half, depth, prefix, mixed_grad, logits, attended, q_rot, keys, values, norm, q_raw, k_raw,
    query_gain, key_gain, cos, sin, normed,
    q_o, k_o, v_o, l_o, heads_o, q_gain_o, k_gain_o,
    grad_low, inner, q_grad, k_grad, v_grad, given, landed, send_sem, land_sem,
):
    rows = q_raw.shape[0]
    span = rows // GROUPS
    key_heads = k_raw.shape[1] // HD
    shared = q_raw.shape[1] // k_raw.shape[1]
    heads = key_heads * shared
    scale = HD ** (-0.5)
    query_gain_here = query_gain[depth : depth + 1, :]
    key_gain_here = key_gain[depth : depth + 1, :]

    def copy(j):
        return pltpu.make_async_remote_copy(
            src_ref=given.at[j],
            dst_ref=landed.at[j],
            send_sem=send_sem.at[j],
            recv_sem=land_sem.at[j],
            device_id={"ctx": 1 - half},
            device_id_type=MESH,
        )

    def gate_back(g):
        at = rows_of(g, span)
        open_gate = jax.nn.sigmoid(logits[at, :])
        lane = lax.broadcasted_iota(jnp.int32, (span, LANES), 1)
        pulled = jnp.zeros((span, LANES), F32)
        for h in range(heads):
            grad = mixed_grad[at, head_at(h)]
            here = attended[at, head_at(h)]
            low_grad = (grad * open_gate[:, h : h + 1]).astype(BF)
            grad_low[at, head_at(h)] = low_grad
            inner[h, at, :] = jnp.sum(low_grad.astype(F32) * here, axis=1, keepdims=True)
            pulled = jnp.where(lane == h, jnp.sum(grad * here, axis=1, keepdims=True), pulled)
        l_o[at, :] = (pulled * (open_gate * (1.0 - open_gate))).astype(BF)

    def gates():
        loop(GROUPS, gate_back)
        heads_o[...] = weight_product(l_o[...], normed[...])[: heads_o.shape[0], :]

    def back(j, side, mask_of, first):
        k_grad[j] = jnp.zeros((rows, HD), F32)
        v_grad[j] = jnp.zeros((rows, HD), F32)

        def block(g):
            at = rows_of(g, span)
            for h in range(j * shared, (j + 1) * shared):
                query = q_rot[at, head_at(h)]
                pulled = grad_low[at, head_at(h)]
                scores = back_product(query, keys[side, j]) * scale
                if mask_of is not None:
                    scores = jnp.where(mask_of(g), scores, masked)
                weights = jnp.exp(scores - norm[h, at, :])
                slope = back_product(pulled, values[side, j])
                score_low = (weights * (slope - inner[h, at, :])).astype(BF)
                moved = matmul(score_low, keys[side, j])
                if first:
                    q_grad[at, head_at(h)] = moved
                else:
                    q_grad[at, head_at(h)] += moved
                k_grad[j] += weight_product(score_low, query)
                v_grad[j] += weight_product(weights.astype(BF), pulled)

        loop(GROUPS, block)

    def other(j):
        @pl.when(half == 1)
        def _():
            back(j, 1, None, True)
            given[j, 0] = (k_grad[j] * scale).astype(BF)
            given[j, 1] = v_grad[j].astype(BF)
            copy(j).start()

        @pl.when(half == 0)
        def _():
            wide_head = pl.ds(j * shared * HD, shared * HD)
            q_grad[:, wide_head] = jnp.zeros((rows, shared * HD), F32)

    def own(j):
        back(j, 0, lambda g: seen(span, g * span, rows, half * rows, prefix[0]), False)

    def query_rows(g):
        at = rows_of(g, span)
        for h in range(heads):
            pulled, terms = head_norm_back(
                q_raw[at, head_at(h)], query_gain_here, cos[at, :], sin[at, :],
                q_grad[at, head_at(h)] * scale,
            )
            q_o[at, head_at(h)] = pulled.astype(BF)
            q_gain_o[...] += jnp.sum(terms.reshape(span // 8, 8, HD), axis=0)

    def queries():
        q_gain_o[...] = jnp.zeros_like(q_gain_o)
        loop(GROUPS, query_rows)

    def keys_of(j):
        if j == 0:
            k_gain_o[...] = jnp.zeros_like(k_gain_o)

        @pl.when(half == 0)
        def _(j=j):
            copy(j).wait_recv()

        def key_rows(g, j=j):
            at = rows_of(g, span)
            k_total = k_grad[j, at, :] * scale
            v_total = v_grad[j, at, :]
            k_grad[j, at, :] = k_total
            v_o[at, head_at(j)] = v_total.astype(BF)

            @pl.when(half == 0)
            def _():
                k_grad[j, at, :] = k_total + landed[j, 0, at, :].astype(F32)
                v_o[at, head_at(j)] = (v_total + landed[j, 1, at, :].astype(F32)).astype(BF)

            pulled, terms = head_norm_back(
                k_raw[at, head_at(j)], key_gain_here, cos[at, :], sin[at, :], k_grad[j, at, :]
            )
            k_o[at, head_at(j)] = pulled.astype(BF)
            k_gain_o[...] += jnp.sum(terms.reshape(span // 8, 8, HD), axis=0)

        loop(GROUPS, key_rows)

    def close():
        @pl.when(half == 1)
        def _():
            for j in range(key_heads):
                copy(j).wait_send()

    heads_each = range(key_heads)
    return (
        [gates]
        + [partial(other, j) for j in heads_each]
        + [partial(own, j) for j in heads_each]
        + [queries]
        + [partial(keys_of, j) for j in heads_each],
        close,
    )


def forward_kernel(
    size, depth, rows, width,
    mixed, stream, wo, feed_gain, wg, wu, wd, next_gain, wq, wk, wv, gh, key_gain, cos, sin,
    middle_o, two_o, slope_o, silu_o, hidden_o, x_o, normed_o, q_o, k_o, logit_o, keys_o, values_o,
    *scratch,
):
    (wo_v, wg_v, wu_v, wd_v, wq_v, wk_v, wv_v, x_v, middle_v, slope_v, silu_v, hidden_v, q_v, k_v,
     v_v, logit_v, load_sem, out_sem, keys_v, values_v, keep_sem, send_sem, land_sem) = scratch[:23]
    half = lax.axis_index("ctx")
    key_heads = keys_v.shape[0]
    chain = Chain(size)
    landed = scratch[23]
    one = Sum(chain, scratch[24:31], (landed, 1), rows, width)
    two = Sum(chain, scratch[31:38], (landed, 2), rows, width)
    span = one.block * GROUP
    loads = load_all(
        [(wo.at[depth], wo_v), (stream, x_v), (wg.at[depth], wg_v), (wu.at[depth], wu_v),
         (wd.at[depth], wd_v), (wq.at[depth + 1], wq_v), (wk.at[depth + 1], wk_v),
         (wv.at[depth + 1], wv_v)],
        load_sem,
    )
    chain.greet([{"ctx": 1 - half}])
    tile = wg_v.shape[1] // (PARTS - 1)
    gain_one = feed_gain[depth : depth + 1, :]
    gain_two = next_gain[depth + 1 : depth + 2, :]

    def out(k, g, src, dst):
        at = rows_of(g, span)
        return pltpu.make_async_copy(src.at[at], dst.at[at], out_sem.at[k, g])

    def keep_keys(g, which):
        at = rows_of(g, span)
        src, dst = ((keys_v, keys_o), (values_v, values_o))[which]
        return pltpu.make_async_copy(src.at[:, at], dst.at[0, :, at], keep_sem.at[which, g])

    def give_keys(g, which):
        at = rows_of(g, span)
        src, dst = ((keys_v, keys_o), (values_v, values_o))[which]
        return pltpu.make_async_remote_copy(
            src_ref=src.at[:, at],
            dst_ref=dst.at[1, :, at],
            send_sem=send_sem.at[which, g],
            recv_sem=land_sem.at[which, g],
            device_id={"ctx": 1 - half},
            device_id_type=MESH,
        )

    loads[0].wait()

    def start(g):
        at = rows_of(g, span)
        fill(one.part, at, lambda col: matmul(mixed[at, :], wo_v[:, col]))
        one.offer(g)

    loop(GROUPS, start)
    wait_all(loads[1:5])

    def made_one(at, total):
        value = x_v[at, :].astype(F32) + total
        middle_v[at, :] = value
        return rms_scale(value, gain_one).astype(BF)

    def between(g, part):
        at = rows_of(g, span)

        @pl.when(part == 0)
        def _():
            out(1, g, one.spread, two_o).start()

            @pl.when(chain.mid)
            def _():
                out(0, g, middle_v, middle_o).start()

        @pl.when(part < PARTS - 1)
        def _():
            col = columns(part, tile)
            gate = matmul(one.spread[at, :], wg_v[:, col])
            up = matmul(one.spread[at, :], wu_v[:, col])
            sig = jax.nn.sigmoid(gate)
            act = gate * sig
            hidden_v[at, col] = (act * up).astype(BF)
            silu_v[at, col] = act.astype(BF)
            slope_v[at, col] = (up * (sig * (1.0 + gate * (1.0 - sig)))).astype(BF)

        @pl.when(part == PARTS - 1)
        def _():
            fill(two.part, at, lambda col: matmul(hidden_v[at, :], wd_v[:, col]))
            two.offer(g)
            out(2, g, slope_v, slope_o).start()
            out(3, g, silu_v, silu_o).start()
            out(4, g, hidden_v, hidden_o).start()

    def ahead(g):
        @pl.when(g == 0)
        def _():
            wait_all(loads[5:])

        @pl.when(chain.mid)
        def _():
            out(0, g, middle_v, middle_o).wait()

    def made_two(at, total):
        value = middle_v[at, :] + total
        middle_v[at, :] = value
        return rms_scale(value, gain_two).astype(BF)

    def after(g):
        at = rows_of(g, span)

        @pl.when(chain.mid)
        def _():
            out(5, g, middle_v, x_o).start()

        k_v[at, :] = matmul(two.spread[at, :], wk_v[...])
        v_v[at, :] = matmul(two.spread[at, :], wv_v[...]).astype(BF)
        for j in range(key_heads):
            key_strip(k_v, v_v, keys_v, values_v, key_gain[depth + 1 : depth + 2, :], cos, sin, j, at)

        @pl.when((half == 0) & (g < GROUPS - 1))
        def _():
            give_keys(g, 0).start()
            give_keys(g, 1).start()

        keep_keys(g, 0).start()
        keep_keys(g, 1).start()
        out(8, g, k_v, k_o).start()
        q_v[at, :] = matmul(two.spread[at, :], wq_v[...])
        out(7, g, q_v, q_o).start()
        logit_v[at, :] = matmul(two.spread[at, :], gh[depth + 1])
        out(10, g, logit_v, logit_o).start()
        out(6, g, two.spread, normed_o).start()

    loop(STEPS, lambda s: two_sums(s, one, two, made_one, between, ahead, made_two, after))
    one.close()
    two.close()

    def drain(g):
        @pl.when(chain.mid)
        def _():
            out(5, g, middle_v, x_o).wait()

        for k, src, dst in (
            (1, one.spread, two_o), (2, slope_v, slope_o), (3, silu_v, silu_o),
            (4, hidden_v, hidden_o), (6, two.spread, normed_o), (7, q_v, q_o),
            (8, k_v, k_o), (10, logit_v, logit_o),
        ):
            out(k, g, src, dst).wait()
        for which in range(2):
            keep_keys(g, which).wait()

            @pl.when((half == 0) & (g < GROUPS - 1))
            def _(which=which):
                give_keys(g, which).wait_send()

            @pl.when((half == 1) & (g < GROUPS - 1))
            def _(which=which):
                give_keys(g, which).wait_recv()

    loop(GROUPS, drain)


def turn_kernel(
    size, plane_sizes, depth, rows, width,
    mixed, x_in, cot, wo, feed_gain, wg, wu, wd,
    two_o, down_o, gate_o, up_o, grad_o, low_o, mixed_o, gain_o, made_o,
    *scratch,
):
    (wo_v, wg_v, wu_v, wd_v, middle_v, cot_v, hidden_v, gate_v, up_v, mixed_v, down_v, gain_v,
     load_sem, out_sem) = scratch[:14]
    chain = Chain(size)
    landed = scratch[14]
    one = Sum(chain, scratch[15:22], (landed, 1), rows, width)
    two = Sum(chain, scratch[22:29], (landed, 2), rows, width)
    plane = Plane(*plane_sizes)
    unit = made_o.shape[1] if made_o.shape[1] < 256 else 256
    scatter = Scatter(
        plane, scratch[29:], cot_v, hidden_v, [(made_o, False, hidden_v.shape[1] // unit, [])],
        width // plane.count, unit,
    )
    span = one.block * GROUP
    loads = load_all(
        [(wo.at[depth], wo_v), (x_in, middle_v), (cot, cot_v), (wg.at[depth], wg_v),
         (wu.at[depth], wu_v), (wd.at[depth], wd_v)],
        load_sem,
    )
    chain.greet(plane.partners())
    tile = wg_v.shape[1] // (PARTS - 1)
    gain_one = feed_gain[depth : depth + 1, :]

    def out(k, g, src, dst):
        at = rows_of(g, span)
        return pltpu.make_async_copy(src.at[at], dst.at[at], out_sem.at[k, g])

    loads[0].wait()

    def start(g):
        at = rows_of(g, span)
        fill(one.part, at, lambda col: matmul(mixed[at, :], wo_v[:, col]))
        one.offer(g)

    loop(GROUPS, start)
    gain_v[...] = jnp.zeros_like(gain_v)
    wait_all(loads[1:])

    def made_one(at, total):
        value = middle_v[at, :] + total
        middle_v[at, :] = value
        return rms_scale(value, gain_one).astype(BF)

    def between(g, part):
        at = rows_of(g, span)

        @pl.when(part == 0)
        def _():
            out(0, g, one.spread, two_o).start()

        @pl.when(part < PARTS - 1)
        def _():
            col = columns(part, tile)
            gate = matmul(one.spread[at, :], wg_v[:, col])
            sig = jax.nn.sigmoid(gate)
            act = gate * sig
            slope = sig * (1.0 + gate * (1.0 - sig))
            up = matmul(one.spread[at, :], wu_v[:, col])
            hidden_v[at, col] = (act * up).astype(BF)
            pulled = back_product(cot_v[at, :], wd_v[col, :])
            gate_v[at, col] = (pulled * up * slope).astype(BF)
            up_v[at, col] = (pulled * act).astype(BF)

        @pl.when(part == PARTS - 1)
        def _():
            fill(
                two.part,
                at,
                lambda col: back_product(gate_v[at, :], wg_v[col, :])
                + back_product(up_v[at, :], wu_v[col, :]),
            )
            two.offer(g)
            out(2, g, gate_v, gate_o).start()
            out(3, g, up_v, up_o).start()

    def ahead(g):
        at = rows_of(g, span)
        share = jnp.where(chain.first_mid, 1.0, 0.0)

        @pl.when(chain.first_mid)
        def _():
            fill(down_v, at, lambda col: matmul(hidden_v[at, :], wd_v[:, col]) + middle_v[at, col])

        @pl.when(jnp.logical_not(chain.first_mid))
        def _():
            fill(down_v, at, lambda col: matmul(hidden_v[at, :], wd_v[:, col]))

        out(4, g, down_v, down_o).start()

    def made_two(at, total):
        pulled, terms = back_norm(middle_v[at, :], gain_one, total)
        gain_v[...] += fold(terms)
        value = cot_v[at, :].astype(F32) + pulled
        middle_v[at, :] = value
        return value.astype(BF)

    def after(g):
        at = rows_of(g, span)

        @pl.when(chain.mid)
        def _():
            out(5, g, middle_v, grad_o).start()

        out(6, g, two.spread, low_o).start()
        mixed_v[at, :] = back_product(two.spread[at, :], wo_v[...])
        out(7, g, mixed_v, mixed_o).start()


    def step(s):
        two_sums(s, one, two, made_one, between, ahead, made_two, after)
        ahead_ticks = jnp.where(chain.outer, OUTER_AHEAD, 0)

        def ticks_before(s):
            return jnp.where(s > EARLY, (s - EARLY) * TURN_PACE + ahead_ticks, 0)

        lax.fori_loop(
            ticks_before(s), ticks_before(s + 1), lambda t, carry: (scatter.tick(t), carry)[1], 0
        )

    loop(max(STEPS, EARLY + -(-scatter.steps // TURN_PACE)), step)

    @pl.when(jnp.logical_not(chain.first_mid))
    def _():
        gain_v[...] = jnp.zeros_like(gain_v)

    gain_out = pltpu.make_async_copy(gain_v, gain_o, out_sem.at[8, 0])
    gain_out.start()
    one.close()
    two.close()
    scatter.close()

    def drain(g):
        @pl.when(chain.mid)
        def _():
            out(5, g, middle_v, grad_o).wait()

        for k, src, dst in (
            (0, one.spread, two_o), (2, gate_v, gate_o), (3, up_v, up_o), (4, down_v, down_o),
            (6, two.spread, low_o), (7, mixed_v, mixed_o),
        ):
            out(k, g, src, dst).wait()

    loop(GROUPS, drain)
    gain_out.wait()


def back_kernel(
    size, plane_sizes, depth, rows, width,
    *refs,
):
    (prefix, mixed_grad, logits, attended, q_rot, keys, values, norm, q_raw, k_raw, query_gain, key_gain,
     cos, sin, normed_in, gh, x_in, grad_in, attention_gain, wq, wk, wv,
     wd, wg, wu, slope_in, silu_in, middle_in, feed_gain, wo,
     two_in, gate_in, up_in, low_in, mixed_in,
     gate_o, up_o, first_o, grad_o, low_o, mixed_o, gain_o, feed_gain_o, heads_o, q_gain_o, k_gain_o,
     *rest) = refs
    made, scratch = rest[:4], rest[4:]
    attend_made, attend_scratch, scratch = scratch[:7], scratch[7:15], scratch[15:]
    q_low, k_low, v_low, l_low, heads_v, q_gain_v, k_gain_v = attend_made
    (wq_v, wk_v, wv_v, ring_v, wo_v, x_v, grad_v, slope_v, silu_v, gate_v, up_v, mixed_v,
     gain_v, feed_v, whole_v, parts_v, gh_v, load_sem, row_sem, tile_sem, out_sem, ring_sem, attend_sem,
     ) = scratch[:23]
    half = lax.axis_index("ctx")
    chain = Chain(size)
    landed = scratch[23]
    one = Sum(chain, scratch[24:31], (landed, 1), rows, width)
    two = Sum(chain, scratch[31:38], (landed, 2), rows, width)
    plane = Plane(*plane_sizes)
    share = width // plane.count
    unit = min(256, wk_v.shape[1])
    units_wide, heads_wide, keys_wide = gate_v.shape[1], wq_v.shape[1], wk_v.shape[1]
    mixed_grad_v, attended_v, q_raw_v, q_grad_v = (
        grad_v.at[:, pl.ds(quarter * heads_wide, heads_wide)] for quarter in range(4)
    )
    normed_v = two.part
    grad_low, inner, k_grad, v_grad, *given = attend_scratch
    pieces, close_attend = attend_back(
        half, depth, prefix, mixed_grad_v, logits, attended_v, q_rot, keys, values, norm, q_raw_v, k_raw,
        query_gain, key_gain, cos, sin, normed_v, *attend_made,
        grad_low, inner, q_grad_v, k_grad, v_grad, *given,
    )
    parts_heads = parts_v.at[:, pl.ds(0, heads_wide)]
    heads_parts = [
        (q_low, parts_heads),
        (k_low, parts_v.at[:, pl.ds(heads_wide, keys_wide)]),
        (v_low, parts_v.at[:, pl.ds(heads_wide + keys_wide, keys_wide)]),
    ]
    scatter = Scatter(
        plane, scratch[38:], whole_v, parts_v,
        [
            (made[0], True, units_wide // unit, [(two_in, whole_v), (gate_in, parts_v)]),
            (made[1], True, units_wide // unit, [(up_in, parts_v)]),
            (made[2], True, (heads_wide + 2 * keys_wide) // unit, [(normed_in, whole_v), *heads_parts]),
            (made[3], False, heads_wide // unit, [(low_in, whole_v), (mixed_in, parts_heads)]),
        ],
        share, unit,
    )
    span = one.block * GROUP
    below = depth - 1
    attend_loads = load_all(
        [(mixed_grad, mixed_grad_v), (attended, attended_v), (normed_in, normed_v), (q_raw, q_raw_v)],
        attend_sem,
    )
    loads = load_all(
        [(wq.at[depth], wq_v), (wk.at[depth], wk_v), (wv.at[depth], wv_v), (gh.at[depth], gh_v),
         (wo.at[below], wo_v)],
        load_sem,
    )
    grad_load = pltpu.make_async_copy(grad_in, grad_v, load_sem.at[5])

    def row_load(src, g, k):
        return pltpu.make_async_copy(src.at[rows_of(g, span)], x_v, row_sem.at[k])

    tile = units_wide // (PARTS - 1)
    strip_wide = wide(width)
    fetches = PARTS - 1 + 2 * (width // strip_wide)
    slots = ring_v.shape[0]

    def fetch(k, act):
        slot, place = lax.rem(k, slots), lax.rem(k, fetches)
        pair = jnp.maximum(place - (PARTS - 1), 0)

        @pl.when(place < PARTS - 1)
        def _():
            src = wd.at[below, rows_of(place, tile)]
            act(pltpu.make_async_copy(src, ring_v.at[slot, pl.ds(0, tile)], ring_sem.at[slot]))

        for which, weight in enumerate((wg, wu)):

            @pl.when((place >= PARTS - 1) & (lax.rem(pair, 2) == which))
            def _(weight=weight):
                src = weight.at[below, rows_of(lax.div(pair, 2), strip_wide)]
                dst = ring_v.at[slot, :, pl.ds(0, units_wide)]
                act(pltpu.make_async_copy(src, dst, ring_sem.at[slot]))

    def fetched(k):
        fetch(k, lambda copy: copy.wait())

    def used(k):
        @pl.when(k + slots < GROUPS * fetches)
        def _():
            fetch(k + slots, lambda copy: copy.start())

    for k in range(slots):
        fetch(jnp.int32(k), lambda copy: copy.start())
    scatter.prefetch()

    def tile_load(src, dst, g, part, k):
        col = columns(part, tile)
        return pltpu.make_async_copy(
            src.at[rows_of(g, span), col], dst.at[:, col], tile_sem.at[k, part]
        )

    row_load(x_in, 0, 0).start()

    def first_tiles(part):
        tile_load(slope_in, slope_v, 0, part, 0).start()
        tile_load(silu_in, silu_v, 0, part, 1).start()

    loop(PARTS - 1, first_tiles)
    chain.greet([*plane.partners(), {"ctx": 1 - half}])
    wait_all(attend_loads)
    gain_one = attention_gain[depth : depth + 1, :]
    gain_two = feed_gain[below : below + 1, :]

    def out(k, g, src, dst, whole=True):
        at = rows_of(g, span)
        return pltpu.make_async_copy(src.at[at] if whole else src, dst.at[at], out_sem.at[k, g])

    def start(g):
        at = rows_of(g, span)
        fill(
            one.part,
            at,
            lambda col: back_product(q_low[at, :], wq_v[col, :])
            + back_product(k_low[at, :], wk_v[col, :])
            + back_product(v_low[at, :], wv_v[col, :])
            + back_product(l_low[at, :], gh_v[col, :]),
        )
        one.offer(g)

    gain_v[...] = jnp.zeros_like(gain_v)
    feed_v[...] = jnp.zeros_like(feed_v)

    def begin_sums():
        grad_load.start()
        wait_all(loads)
        loop(GROUPS, start)
        row_load(x_in, 0, 0).wait()
        grad_load.wait()

    def local(at):
        return pl.ds(pl.multiple_of(lax.rem(at.start, span), STRIP), STRIP)

    def made_one(at, total):
        pulled, terms = back_norm(x_v[local(at), :], gain_one, total)
        gain_v[...] += fold(terms)
        value = grad_v[at, :] + pulled
        grad_v[at, :] = value
        return value.astype(BF)

    def between(g, part):
        at = rows_of(g, span)

        @pl.when(part == 0)
        def _():
            out(0, g, one.spread, first_o).start()

            @pl.when(g < GROUPS - 1)
            def _():
                copy = row_load(x_in, g + 1, 1)
                copy.start()
                copy.wait()

            @pl.when(g > 0)
            def _():
                out(1, g - 1, gate_v, gate_o, False).wait()
                out(2, g - 1, up_v, up_o, False).wait()

        @pl.when(part < PARTS - 1)
        def _():
            col = columns(part, tile)
            tile_load(slope_in, slope_v, g, part, 0).wait()
            tile_load(silu_in, silu_v, g, part, 1).wait()
            k = g * fetches + part
            fetched(k)
            weight = ring_v[lax.rem(k, slots), pl.ds(0, tile), :]
            pulled = back_product(one.spread[at, :], weight)
            used(k)
            gate_v[:, col] = (pulled * slope_v[:, col].astype(F32)).astype(BF)
            up_v[:, col] = (pulled * silu_v[:, col].astype(F32)).astype(BF)

            @pl.when(g < GROUPS - 1)
            def _():
                tile_load(slope_in, slope_v, g + 1, part, 0).start()
                tile_load(silu_in, silu_v, g + 1, part, 1).start()

        @pl.when(part == PARTS - 1)
        def _():
            def pair(p):
                k = g * fetches + PARTS - 1 + 2 * p
                fetched(k)
                fetched(k + 1)
                here = pl.ds(0, units_wide)
                two.part[at, columns(p, strip_wide)] = (
                    back_product(gate_v[...], ring_v[lax.rem(k, slots), :, here])
                    + back_product(up_v[...], ring_v[lax.rem(k + 1, slots), :, here])
                ).astype(BF)
                used(k)
                used(k + 1)

            loop(width // strip_wide, pair)
            two.offer(g)
            out(1, g, gate_v, gate_o, False).start()
            out(2, g, up_v, up_o, False).start()

    def ahead(g):
        copy = row_load(middle_in, g, 2)
        copy.start()
        copy.wait()

    def made_two(at, total):
        pulled, terms = back_norm(x_v[local(at), :], gain_two, total)
        feed_v[...] += fold(terms)
        value = grad_v[at, :] + pulled
        grad_v[at, :] = value
        return value.astype(BF)

    def after(g):
        at = rows_of(g, span)

        @pl.when(chain.mid)
        def _():
            out(5, g, grad_v, grad_o).start()

        out(3, g, two.spread, low_o).start()

        @pl.when(g > 0)
        def _():
            out(4, g - 1, mixed_v, mixed_o, False).wait()

        mixed_v[...] = back_product(two.spread[at, :], wo_v[...])
        out(4, g, mixed_v, mixed_o, False).start()

    lead = len(pieces)

    def ticks_before(i):
        since = i - lead - 1
        more = jnp.where(chain.outer & (since >= GROUP), OUTER_MORE, 0)
        return jnp.where(since < 0, lax.div(i * LEAD + 4, 8), BEFORE + lax.div(since * PACE, 8) + more)

    def step(i):
        for place, piece in enumerate(pieces):
            pl.when(i == place)(piece)
        pl.when(i == lead)(begin_sums)
        two_sums(i - lead - 1, one, two, made_one, between, ahead, made_two, after)
        lax.fori_loop(
            ticks_before(i), ticks_before(i + 1), lambda t, carry: (scatter.tick(t), carry)[1], 0
        )

    steps = lead + 1 + STEPS
    while BEFORE + (steps - lead - 1) * PACE // 8 < scatter.steps:
        steps += 1
    loop(steps, step)
    close_attend()

    @pl.when(jnp.logical_not(chain.first_mid))
    def _():
        gain_v[...] = jnp.zeros_like(gain_v)
        feed_v[...] = jnp.zeros_like(feed_v)

    gain_out = pltpu.make_async_copy(gain_v, gain_o, out_sem.at[6, 0])
    feed_out = pltpu.make_async_copy(feed_v, feed_gain_o, out_sem.at[7, 0])
    gain_out.start()
    feed_out.start()
    attend_outs = [
        pltpu.make_async_copy(src, dst, attend_sem.at[place])
        for place, (src, dst) in enumerate(
            ((heads_v, heads_o), (q_gain_v, q_gain_o), (k_gain_v, k_gain_o))
        )
    ]
    for copy in attend_outs:
        copy.start()
    one.close()
    two.close()
    scatter.close()

    def drain(g):
        out(0, g, one.spread, first_o).wait()
        out(3, g, two.spread, low_o).wait()

        @pl.when(chain.mid)
        def _():
            out(5, g, grad_v, grad_o).wait()

    loop(GROUPS, drain)
    out(1, GROUPS - 1, gate_v, gate_o, False).wait()
    out(2, GROUPS - 1, up_v, up_o, False).wait()
    out(4, GROUPS - 1, mixed_v, mixed_o, False).wait()
    gain_out.wait()
    feed_out.wait()
    wait_all(attend_outs)


def last_kernel(
    size, plane_sizes, depth, rows, width,
    *refs,
):
    attend_in, refs = refs[:15], refs[15:]
    (gh, gain_one_in, feed_zero_in, feed_one_in, q_gain_one, k_gain_one, heads_one, x_in, grad_in,
     attention_gain, wq, wk, wv, down_in, two_in, gate_in, up_in, first_in, hidden_in, low_in, mixed_in,
     grad_o, result_o, total_o, *rest) = refs
    normed_in = attend_in[14]
    made, rest = rest[:5], rest[5:]
    attend_made, attend_scratch, scratch = rest[:7], rest[7:16], rest[16:]
    q_low, k_low, v_low, l_low, heads_zero, q_gain_zero, k_gain_zero = attend_made
    half = lax.axis_index("ctx")
    pieces, close_attend = attend_back(half, depth, *attend_in, *attend_made, *attend_scratch)
    (wq_v, wk_v, wv_v, x_v, grad_v, gain_v, whole_v, parts_v, total_v, load_sem, out_sem) = scratch[:11]
    chain = Chain(size)
    one = Sum(chain, scratch[12:19], (scratch[11], 1), rows, width)
    two = Sum(chain, scratch[20:27], (scratch[19], 1), rows, width)
    plane = Plane(*plane_sizes)
    total = Total(plane, size, scratch[27:31], 8)
    share = width // plane.count
    units_wide, heads_wide, keys_wide = parts_v.shape[1], wq_v.shape[1], wk_v.shape[1]
    unit = min(256, keys_wide)
    parts_heads = parts_v.at[:, pl.ds(0, heads_wide)]
    heads_parts = [
        (q_low, parts_heads),
        (k_low, parts_v.at[:, pl.ds(heads_wide, keys_wide)]),
        (v_low, parts_v.at[:, pl.ds(heads_wide + keys_wide, keys_wide)]),
    ]
    scatter = Scatter(
        plane, scratch[31:], whole_v, parts_v,
        [
            (made[0], True, units_wide // unit, [(two_in, whole_v), (gate_in, parts_v)]),
            (made[1], True, units_wide // unit, [(up_in, parts_v)]),
            (made[2], False, units_wide // unit, [(first_in, whole_v), (hidden_in, parts_v)]),
            (made[3], True, (heads_wide + 2 * keys_wide) // unit, [(normed_in, whole_v), *heads_parts]),
            (made[4], False, heads_wide // unit, [(low_in, whole_v), (mixed_in, parts_heads)]),
        ],
        share, unit,
    )
    span = one.block * GROUP
    loads = load_all(
        [(wq.at[depth], wq_v), (wk.at[depth], wk_v), (wv.at[depth], wv_v), (x_in, x_v),
         (grad_in, grad_v), (down_in, two.part)],
        load_sem,
    )
    scatter.prefetch()
    chain.greet([*plane.partners(), *total.across, {"ctx": 1 - half}])
    gain_one = attention_gain[depth : depth + 1, :]

    def out(k, g):
        at = rows_of(g, span)
        src, dst = ((one.spread, grad_o), (two.spread, result_o))[k]
        return pltpu.make_async_copy(src.at[at], dst.at[at], out_sem.at[k, g])

    def start(g):
        at = rows_of(g, span)
        fill(
            one.part,
            at,
            lambda col: back_product(q_low[at, :], wq_v[col, :])
            + back_product(k_low[at, :], wk_v[col, :])
            + back_product(v_low[at, :], wv_v[col, :])
            + back_product(l_low[at, :], gh[depth, col, :]),
        )
        one.offer(g)

    gain_v[...] = jnp.zeros_like(gain_v)

    def made_one(at, total_sum):
        pulled, terms = back_norm(x_v[at, :].astype(F32), gain_one, total_sum)
        gain_v[...] += fold(terms)
        return (grad_v[at, :] + pulled).astype(BF)

    def made_two(at, total_sum):
        return total_sum.astype(BF)

    begin = -(-len(pieces) // PER_TICK)
    first_two, first_one = 3, begin + ONE_AFTER
    sum_ticks = BLOCKS + BLOCKS // ONE_PACE + 1
    first_total = first_one + sum_ticks
    rest_two = first_one + sum_ticks - 1

    def sums(i):
        @pl.when(i == 0)
        def _():
            loads[5].wait()
            two.offer(0)

        for place, piece in enumerate(pieces):
            pl.when(i == place // PER_TICK)(piece)

        @pl.when(i == begin)
        def _():
            wait_all(loads[:5])
            loop(GROUPS, start)
            two.offer(1)

        def one_step(k, sum_here, make, s):
            @pl.when((s >= 0) & (s < BLOCKS))
            def _():
                sum_here.relay(s)

            @pl.when((s >= 1) & (s <= BLOCKS))
            def _():
                sum_here.finish(s - 1, make)

                @pl.when((lax.rem(s, GROUP) == 0) & chain.mid)
                def _():
                    out(k, lax.div(s, GROUP) - 1).start()

        def paced(k, sum_here, make, first, begin_step, end_step, pace):
            since = i - first
            take = lax.rem(since, pace + 1)
            s = lax.div(since, pace + 1) * pace + take + begin_step

            @pl.when((since >= 0) & (take < pace) & (s < end_step))
            def _():
                one_step(k, sum_here, make, s)

        paced(1, two, made_two, first_two, 0, GROUP, 3)
        paced(0, one, made_one, first_one, 0, BLOCKS + 1, ONE_PACE)
        paced(1, two, made_two, rest_two, GROUP, BLOCKS + 1, 3)

    def totals(i):
        @pl.when(i == first_total)
        def _():
            total.value[0] = jnp.zeros(total_v.shape, F32)

            @pl.when(chain.first_mid)
            def _():
                total.value[0, pl.ds(0, 1)] = jnp.sum(gain_v[...], axis=0, keepdims=True)

            for k, gains in enumerate((gain_one_in, feed_zero_in, feed_one_in)):
                total.value[0, pl.ds(k + 1, 1)] = jnp.sum(gains[...], axis=0, keepdims=True)
            for k, gains in enumerate((q_gain_zero, k_gain_zero, q_gain_one, k_gain_one)):
                total.value[0, pl.ds(4, 1), pl.ds(k * HD, HD)] = jnp.sum(
                    gains[...], axis=0, keepdims=True
                )
            for k, heads in enumerate((heads_zero, heads_one)):
                total.value[0, pl.ds(8 + 4 * k, 4)] = heads[pl.ds(0, 4), :]

        for k in range(len(total.stages)):

            @pl.when(i == first_total + total.times[k])
            def _(k=k):
                total.start(k)

    def ticks_before(i):
        return jnp.where(i < begin, lax.div(i * LAST_LEAD, 8), lead_ticks + lax.div((i - begin) * LAST_PACE, 8))

    def step(i):
        lax.fori_loop(
            ticks_before(i), ticks_before(i + 1), lambda t, carry: (scatter.tick(t), carry)[1], 0
        )
        sums(i)
        totals(i)

    last_two = rest_two + 4 * -(-(BLOCKS + 1 - GROUP) // 3)
    lead_ticks = begin * LAST_LEAD // 8
    scatter_steps = begin + -(-(scatter.steps - lead_ticks) * 8 // LAST_PACE)
    loop(max(scatter_steps, last_two, first_total + total.times[-1]), step)
    close_attend()

    def receive(g):
        one.receive(g)
        two.receive(g)

        @pl.when(chain.outer)
        def _():
            out(0, g).start()
            out(1, g).start()

    loop(GROUPS, receive)
    total.finish(total_v)
    total_out = pltpu.make_async_copy(total_v, total_o, out_sem.at[2, 0])
    total_out.start()
    one.close()
    two.close()
    scatter.close()

    def drain(g):
        out(0, g).wait()
        out(1, g).wait()

    loop(GROUPS, drain)
    total_out.wait()


def widen_kernel(heads_wide, keys_wide, low_in, result_in, *refs):
    below, above = refs[0:5], refs[5:10]
    stream_o, result_o, gate_o, up_o, down_o, q_o, k_o, v_o, out_o = refs[10:]
    result_o[...] = result_in[...]
    stream_o[...] = low_in[...].astype(F32)
    for depth, made in enumerate((below, above)):
        gate_o[depth] = made[0][...].astype(F32)
        up_o[depth] = made[1][...].astype(F32)
        down_o[depth] = made[2][...].astype(F32)
        q_o[depth] = made[3][:, :heads_wide].astype(F32)
        k_o[depth] = made[3][:, heads_wide : heads_wide + keys_wide].astype(F32)
        v_o[depth] = made[3][:, heads_wide + keys_wide :].astype(F32)
        out_o[depth] = made[4][...].astype(F32)


def widen(stream_low, result, below, above, heads_wide, keys_wide):
    cuts = 4

    def cut(shape):
        return pl.BlockSpec((shape[0] // cuts, shape[1]), lambda i: (i, 0))

    def pair(shape):
        return pl.BlockSpec((2, shape[0] // cuts, shape[1]), lambda i: (0, i, 0))

    share = below[0].shape[0]
    shapes = [
        below[0].shape, below[1].shape, below[2].shape, (share, heads_wide), (share, keys_wide),
        (share, keys_wide), below[4].shape,
    ]
    inputs = [stream_low, result, *below, *above]
    return pl.pallas_call(
        partial(widen_kernel, heads_wide, keys_wide),
        grid=(cuts,),
        out_shape=(
            jax.ShapeDtypeStruct(stream_low.shape, F32),
            jax.ShapeDtypeStruct(result.shape, BF),
            *(jax.ShapeDtypeStruct((2, *shape), F32) for shape in shapes),
        ),
        in_specs=[cut(array.shape) for array in inputs],
        out_specs=(cut(stream_low.shape), cut(result.shape), *(pair(shape) for shape in shapes)),
        compiler_params=pltpu.CompilerParams(vmem_limit_bytes=VMEM_LIMIT),
    )(*inputs)


def call(kernel, collective_id, in_specs, outs, scratch, flops, out_spec=ANY):
    return pl.pallas_call(
        kernel,
        out_shape=tuple(jax.ShapeDtypeStruct(shape, kind) for shape, kind in outs),
        in_specs=in_specs,
        out_specs=tuple(out_spec for _ in outs),
        scratch_shapes=scratch,
        cost_estimate=pl.CostEstimate(flops=flops, bytes_accessed=40_000_000, transcendentals=0),
        compiler_params=pltpu.CompilerParams(
            collective_id=collective_id, has_side_effects=True, vmem_limit_bytes=VMEM_LIMIT
        ),
    )


def dma(*shape):
    return pltpu.SemaphoreType.DMA(shape)


def shards(
    size,
    stream,
    cotangent,
    prefixes,
    attention_gain,
    query_weight,
    key_weight,
    value_weight,
    gate_heads,
    query_gain,
    key_gain,
    output_weight,
    feed_gain,
    gate_weight,
    up_weight,
    down_weight,
):
    seq_count, row_count, width = stream.shape
    rows = seq_count * row_count
    span = rows // GROUPS
    dp_size = lax.axis_size("dp")
    plane_sizes = (dp_size, lax.axis_size("ctx"))
    plane_count = plane_sizes[0] * plane_sizes[1]
    heads_wide = query_weight.shape[2]
    keys_wide = key_weight.shape[2]
    units = gate_weight.shape[2]
    gates = gate_heads.shape[2]
    share = width // plane_count
    unit = min(256, keys_wide)
    here = lax.axis_index("dp") * plane_sizes[1] + lax.axis_index("ctx")
    first_row = lax.axis_index("ctx") * row_count
    cos, sin = (
        lax.dynamic_slice_in_dim(jnp.asarray(table), first_row, row_count)
        for table in rotary_tables(row_count * plane_sizes[1])
    )
    stream_flat = stream.reshape(rows, width)
    cot_flat = cotangent.reshape(rows, width)
    heads_padded = jnp.dot(gate_heads, jnp.eye(gates, LANES, dtype=BF), preferred_element_type=F32).astype(BF)
    sum_scratch = Sum.scratch(rows, width)
    landed = [pltpu.VMEM((2, rows, width), BF)]
    pair_scratch = [pltpu.VMEM((3, rows, width), BF)] + sum_scratch + sum_scratch

    key_heads = keys_wide // HD
    attend_outs = [
        ((rows, heads_wide), BF), ((rows, heads_wide), BF), ((heads_wide // HD, rows, 1), F32),
        ((rows, heads_wide), F32),
    ]
    key_outs = [((2, key_heads, rows, HD), BF), ((2, key_heads, rows, HD), BF)]
    smem = pl.BlockSpec(memory_space=pltpu.SMEM)

    attend_back_outs = [
        ((rows, heads_wide), BF), ((rows, keys_wide), BF), ((rows, keys_wide), BF),
        ((rows, LANES), BF), ((8, width), F32), ((8, HD), F32), ((8, HD), F32),
    ]
    attend_back_scratch = [
        pltpu.VMEM((rows, heads_wide), BF), pltpu.VMEM((heads_wide // HD, rows, 1), F32),
        pltpu.VMEM((rows, heads_wide), F32), pltpu.VMEM((key_heads, rows, HD), F32),
        pltpu.VMEM((key_heads, rows, HD), F32), pltpu.VMEM((key_heads, 2, rows, HD), BF),
        pltpu.VMEM((key_heads, 2, rows, HD), BF), dma(key_heads), dma(key_heads),
    ]

    def attend_back_in(mixed_grad, logits, saved, q_raw, k_raw, normed):
        mixed, q_rot, norm, attended, keys, values = saved
        return (
            prefixes, mixed_grad, logits, attended, q_rot, keys, values, norm, q_raw, k_raw,
            query_gain, key_gain, cos, sin, normed,
        )

    made_shapes = [
        ((share, units), BF), ((share, units), BF), ((units, share), BF),
        ((share, heads_wide + 2 * keys_wide), BF), ((heads_wide, share), BF),
    ]
    scatter_scratch = Scatter.scratch(plane_count, share, unit)

    *saved_zero, normed_zero, q_raw_zero, k_raw_zero, logits_zero = call(
        partial(first_kernel, 0),
        4,
        [smem, WHOLE, WHOLE, ANY, ANY, ANY] + [WHOLE] * 5,
        attend_outs
        + key_outs
        + [
            ((rows, width), BF), ((rows, heads_wide), F32), ((rows, keys_wide), F32),
            ((rows, LANES), F32),
        ],
        [
            pltpu.VMEM((rows, keys_wide), BF), pltpu.VMEM((width, heads_wide), BF),
            pltpu.VMEM((width, keys_wide), BF), pltpu.VMEM((width, keys_wide), BF), dma(3),
            dma(key_heads, 2), dma(key_heads, 2),
        ]
        + attend_scratch(rows, heads_wide),
        3_500_000_000,
        WHOLE,
    )(
        prefixes, stream_flat, attention_gain, query_weight, key_weight, value_weight, heads_padded,
        query_gain, key_gain, cos, sin,
    )
    mixed_zero = saved_zero[0]
    middle_zero, two_zero, slope, silu, hidden_zero, x_one, normed_one, q_raw, k_raw, logits, *keys_one = call(
        partial(forward_kernel, size, 0, rows, width),
        0,
        [WHOLE, ANY, ANY, WHOLE, ANY, ANY, ANY, WHOLE, ANY, ANY, ANY] + [WHOLE] * 4,
        [
            ((rows, width), F32), ((rows, width), BF), ((rows, units), BF), ((rows, units), BF),
            ((rows, units), BF), ((rows, width), F32), ((rows, width), BF),
            ((rows, heads_wide), F32), ((rows, keys_wide), F32), ((rows, LANES), F32), *key_outs,
        ],
        [
            pltpu.VMEM((heads_wide, width), BF), pltpu.VMEM((width, units), BF),
            pltpu.VMEM((width, units), BF), pltpu.VMEM((units, width), BF),
            pltpu.VMEM((width, heads_wide), BF), pltpu.VMEM((width, keys_wide), BF),
            pltpu.VMEM((width, keys_wide), BF), pltpu.VMEM((rows, width), BF),
            pltpu.VMEM((rows, width), F32), pltpu.VMEM((rows, units), BF),
            pltpu.VMEM((rows, units), BF), pltpu.VMEM((rows, units), BF),
            pltpu.VMEM((rows, heads_wide), F32), pltpu.VMEM((rows, keys_wide), F32),
            pltpu.VMEM((rows, keys_wide), BF), pltpu.VMEM((rows, LANES), F32),
            dma(8), dma(11, GROUPS), pltpu.VMEM((key_heads, rows, HD), BF),
            pltpu.VMEM((key_heads, rows, HD), BF), dma(2, GROUPS), dma(2, GROUPS), dma(2, GROUPS),
        ]
        + pair_scratch,
        13_000_000_000,
    )(
        mixed_zero, stream_flat, output_weight, feed_gain, gate_weight, up_weight, down_weight,
        attention_gain, query_weight, key_weight, value_weight, heads_padded, key_gain, cos, sin,
    )
    saved_one = call(
        partial(attend_kernel, 1),
        5,
        [smem] + [WHOLE] * 5 + [ANY] * 2,
        attend_outs + key_outs,
        [dma(2, 2), dma(2), dma(2)] + attend_scratch(rows, heads_wide),
        1_000_000_000,
        WHOLE,
    )(prefixes, q_raw, logits, query_gain, cos, sin, *keys_one)
    mixed_one = saved_one[0]
    two_one, down_part, gate_low, up_low, grad, low, mixed_grad, feed_one, down_made = call(
        partial(turn_kernel, size, plane_sizes, 1, rows, width),
        1,
        [WHOLE, ANY, ANY, ANY, WHOLE, ANY, ANY, ANY],
        [
            ((rows, width), BF), ((rows, width), BF), ((rows, units), BF),
            ((rows, units), BF), ((rows, width), F32), ((rows, width), BF),
            ((rows, heads_wide), F32), ((8, width), F32), made_shapes[2],
        ],
        [
            pltpu.VMEM((heads_wide, width), BF), pltpu.VMEM((width, units), BF),
            pltpu.VMEM((width, units), BF), pltpu.VMEM((units, width), BF),
            pltpu.VMEM((rows, width), F32), pltpu.VMEM((rows, width), BF),
            pltpu.VMEM((rows, units), BF), pltpu.VMEM((rows, units), BF),
            pltpu.VMEM((rows, units), BF), pltpu.VMEM((rows, heads_wide), F32),
            pltpu.VMEM((rows, width), BF), pltpu.VMEM((8, width), F32),
            dma(6), dma(9, GROUPS),
        ]
        + pair_scratch + scatter_scratch,
        24_000_000_000,
    )(mixed_one, x_one, cot_flat, output_weight, feed_gain, gate_weight, up_weight, down_weight)
    (gate_low, up_low, first_low, grad, low, mixed_grad, gain_one, feed_zero, heads_one, q_gain_one,
     k_gain_one, *made_one) = call(
        partial(back_kernel, size, plane_sizes, 1, rows, width),
        2,
        [smem, ANY, WHOLE, ANY] + [WHOLE] * 4 + [ANY] + [WHOLE] * 5 + [ANY]
        + [ANY, ANY, ANY, WHOLE] + [ANY] * 9 + [WHOLE] + [ANY] * 6,
        [
            ((rows, units), BF), ((rows, units), BF), ((rows, width), BF), ((rows, width), F32),
            ((rows, width), BF), ((rows, heads_wide), F32), ((8, width), F32), ((8, width), F32),
            ((8, width), F32), ((8, HD), F32), ((8, HD), F32), *made_shapes[:2], *made_shapes[3:],
        ],
        [pltpu.VMEM(shape, kind) for shape, kind in attend_back_outs]
        + attend_back_scratch[:2] + attend_back_scratch[3:]
        + [
            pltpu.VMEM((width, heads_wide), BF), pltpu.VMEM((width, keys_wide), BF),
            pltpu.VMEM((width, keys_wide), BF), pltpu.VMEM((4, 512, width), BF),
            pltpu.VMEM((heads_wide, width), BF), pltpu.VMEM((span, width), F32),
            pltpu.VMEM((rows, width), F32), pltpu.VMEM((span, units), BF),
            pltpu.VMEM((span, units), BF), pltpu.VMEM((span, units), BF),
            pltpu.VMEM((span, units), BF), pltpu.VMEM((span, heads_wide), F32),
            pltpu.VMEM((8, width), F32), pltpu.VMEM((8, width), F32),
            pltpu.VMEM((rows, width), BF), pltpu.VMEM((rows, units), BF),
            pltpu.VMEM((width, LANES), BF),
            dma(6), dma(3), dma(2, PARTS - 1), dma(8, GROUPS), dma(4), dma(4),
        ]
        + pair_scratch + scatter_scratch,
        28_000_000_000,
    )(
        *attend_back_in(mixed_grad, logits, saved_one, q_raw, k_raw, normed_one),
        heads_padded, x_one, grad, attention_gain,
        query_weight, key_weight, value_weight, down_weight, gate_weight, up_weight, slope, silu,
        middle_zero, feed_gain, output_weight,
        two_one, gate_low, up_low, low, mixed_one,
    )
    made_one.insert(2, down_made)
    below_rows = 8
    stages = plane_count.bit_length() - 1 + size.bit_length() - 1
    stream_low, result, totals, *made_zero = call(
        partial(last_kernel, size, plane_sizes, 0, rows, width),
        3,
        [smem] + [WHOLE] * 14 + [WHOLE] * 7 + [ANY, ANY, WHOLE] + [ANY] * 11,
        [
            ((rows, width), BF), ((rows, width), BF), ((8 + below_rows, width), F32), *made_shapes,
        ],
        [pltpu.VMEM(shape, kind) for shape, kind in attend_back_outs]
        + attend_back_scratch
        + [
            pltpu.VMEM((width, heads_wide), BF), pltpu.VMEM((width, keys_wide), BF),
            pltpu.VMEM((width, keys_wide), BF), pltpu.VMEM((rows, width), BF),
            pltpu.VMEM((rows, width), F32), pltpu.VMEM((8, width), F32),
            pltpu.VMEM((rows, width), BF), pltpu.VMEM((rows, units), BF),
            pltpu.VMEM((8 + below_rows, width), F32), dma(6), dma(3, GROUPS),
        ]
        + landed + sum_scratch + landed + sum_scratch
        + Total.scratch(8 + below_rows, width, stages) + scatter_scratch,
        19_000_000_000,
    )(
        *attend_back_in(mixed_grad, logits_zero, saved_zero, q_raw_zero, k_raw_zero, normed_zero),
        heads_padded, gain_one, feed_zero, feed_one, q_gain_one, k_gain_one, heads_one, stream_flat,
        grad, attention_gain, query_weight, key_weight, value_weight, down_part,
        two_zero, gate_low, up_low, first_low, hidden_zero, low, mixed_zero,
    )
    stream_grad, result, *weights = widen(stream_low, result, made_zero, made_one, heads_wide, keys_wide)

    def own(array, wide_share):
        return lax.dynamic_slice_in_dim(array, here * wide_share, wide_share, array.ndim - 1)

    gains = own(totals[:4], share)
    head_gains = own(totals[4, : 4 * HD].reshape(2, 2, HD), HD // plane_count)
    heads = own(totals[8:].reshape(LAYERS, 4, width)[:, :gates], share)
    return (
        result.reshape(seq_count, row_count, width),
        stream_grad.reshape(seq_count, row_count, width),
        gains[0:2],
        weights[3],
        weights[4],
        weights[5],
        heads.transpose(0, 2, 1),
        head_gains[:, 0],
        head_gains[:, 1],
        weights[6],
        gains[2:4],
        weights[0],
        weights[1],
        weights[2],
    )


def solution(mesh):
    return jax.shard_map(
        partial(shards, mesh.shape["tensor"]),
        mesh=mesh,
        in_specs=(
            P("dp", "ctx", None),
            P("dp", "ctx", None),
            P("dp"),
            P(),
            P(None, None, "tensor"),
            P(None, None, "tensor"),
            P(None, None, "tensor"),
            P(None, None, "tensor"),
            P(),
            P(),
            P(None, "tensor", None),
            P(),
            P(None, None, "tensor"),
            P(None, None, "tensor"),
            P(None, "tensor", None),
        ),
        out_specs=(
            P("dp", "ctx", None),
            P("dp", "ctx", None),
            P(None, ("dp", "ctx")),
            P(None, ("dp", "ctx"), "tensor"),
            P(None, ("dp", "ctx"), "tensor"),
            P(None, ("dp", "ctx"), "tensor"),
            P(None, ("dp", "ctx"), "tensor"),
            P(None, ("dp", "ctx")),
            P(None, ("dp", "ctx")),
            P(None, "tensor", ("dp", "ctx")),
            P(None, ("dp", "ctx")),
            P(None, ("dp", "ctx"), "tensor"),
            P(None, ("dp", "ctx"), "tensor"),
            P(None, "tensor", ("dp", "ctx")),
        ),
        check_vma=False,
    )
```

```python
from functools import partial

import jax
import jax.numpy as jnp
import numpy as np
from jax import lax
from jax.experimental import pallas as pl
from jax.experimental.pallas import tpu as pltpu
from jax.sharding import PartitionSpec as P

HD = 128
LAYERS = 2
LANES = 128

epsilon = 1e-06
theta = 1000000.0
masked = -1000000000.0

BF = jnp.bfloat16
F32 = jnp.float32
ANY = pl.BlockSpec(memory_space=pl.ANY)
WHOLE = pl.BlockSpec(memory_space=pltpu.VMEM)
MESH = pl.DeviceIdType.MESH

BLOCKS = 8
PIECES = 2
GROUP = 4
STRIP = 16
UNROLL = 2
VMEM_LIMIT = 63 * 1024 * 1024


def rms_scale(values, gain):
    return values * lax.rsqrt(jnp.mean(values * values, axis=-1, keepdims=True) + epsilon) * gain


def rotary_tables(length):
    counter = np.arange(HD // 2, dtype=np.float32)
    frequency = np.power(np.float32(theta), np.float32(-2.0) * counter / np.float32(HD))
    angles = np.arange(length, dtype=np.float32)[:, None] * frequency[None, :].astype(np.float32)
    cos, sin = np.cos(angles), np.sin(angles)
    return (
        np.concatenate([cos, cos], axis=1).astype(np.float32),
        np.concatenate([-sin, sin], axis=1).astype(np.float32),
    )


def matmul(left, right):
    return jnp.dot(left, right, preferred_element_type=F32)


def weight_product(left, right):
    return lax.dot_general(left, right, (((0,), (0,)), ((), ())), preferred_element_type=F32)


def back_product(gradient, weight):
    return lax.dot_general(gradient, weight, (((1,), (1,)), ((), ())), preferred_element_type=F32)


def loop(count, body, unroll=1):
    def step(i, carry):
        body(i)
        return carry

    lax.fori_loop(0, count, step, 0, unroll=unroll)


def rows_of(r, block):
    return pl.ds(pl.multiple_of(r * block, block), block)


def columns(j, width):
    return pl.ds(pl.multiple_of(j * width, width), width)


def greet(targets, extra, has_extra):
    barrier = pltpu.get_barrier_semaphore()
    for target in targets:
        pl.semaphore_signal(barrier, inc=1, device_id=target, device_id_type=MESH)

    @pl.when(has_extra)
    def _():
        pl.semaphore_signal(barrier, inc=1, device_id=extra, device_id_type=MESH)
        pl.semaphore_wait(barrier, len(targets) + 1)

    @pl.when(jnp.logical_not(has_extra))
    def _():
        pl.semaphore_wait(barrier, len(targets))


class Chain:
    def __init__(self, size):
        self.size = size
        self.spot = lax.axis_index("tensor")
        half = size // 2
        on_left = self.spot < half
        self.end = (self.spot == 0) | (self.spot == size - 1)
        self.inner = jnp.logical_not(self.end)
        self.mid = (self.spot == half - 1) | (self.spot == half)
        self.outer = jnp.logical_not(self.mid)
        self.first_mid = self.spot == half - 1
        self.inward = {"tensor": jnp.where(on_left, self.spot + 1, self.spot - 1)}
        self.outward = {"tensor": jnp.where(on_left, self.spot - 1, self.spot + 1)}

    def greet(self, others=()):
        greet([self.inward, *others], self.outward, self.inner)


class Sum:
    def __init__(self, chain, refs, landed, rows, width):
        self.chain = chain
        self.part, self.spread, self.s_in, self.r_in, self.s_out, self.r_out, self.r_cross = refs
        self.landed, self.cross = landed
        self.block = rows // BLOCKS
        self.piece = width // PIECES

    @staticmethod
    def scratch(rows, width):
        return [
            pltpu.VMEM((rows, width), BF),
            pltpu.VMEM((rows, width), BF),
            pltpu.SemaphoreType.DMA((BLOCKS, PIECES)),
            pltpu.SemaphoreType.DMA((BLOCKS, PIECES)),
            pltpu.SemaphoreType.DMA((BLOCKS,)),
            pltpu.SemaphoreType.DMA((BLOCKS,)),
            pltpu.SemaphoreType.DMA((BLOCKS, PIECES)),
        ]

    def hop(self, r, p, across):
        where = (rows_of(r, self.block), columns(p, self.piece))
        return pltpu.make_async_remote_copy(
            src_ref=self.part.at[where],
            dst_ref=self.landed.at[(self.cross if across else 0,) + where],
            send_sem=self.s_in.at[r, p],
            recv_sem=(self.r_cross if across else self.r_in).at[r, p],
            device_id=self.chain.inward,
            device_id_type=MESH,
        )

    def out_hop(self, r):
        at = rows_of(r, self.block)
        return pltpu.make_async_remote_copy(
            src_ref=self.spread.at[at],
            dst_ref=self.spread.at[at],
            send_sem=self.s_out.at[r],
            recv_sem=self.r_out.at[r],
            device_id=self.chain.outward,
            device_id_type=MESH,
        )

    def offer(self, g):
        @pl.when(self.chain.end)
        def _():
            def one(k):
                for p in range(PIECES):
                    self.hop(g * GROUP + k, p, False).start()

            loop(GROUP, one)

    def relay(self, r):
        @pl.when(self.chain.inner)
        def _():
            for p in range(PIECES):
                self.hop(r, p, False).wait_recv()
                col = columns(p, self.piece)

                def strip(i, col=col):
                    at = pl.ds(pl.multiple_of(r * self.block + i * STRIP, STRIP), STRIP)
                    self.part[at, col] = self.part[at, col] + self.landed[0, at, col]

                loop(self.block // STRIP, strip, True)

                @pl.when(self.chain.mid)
                def _(p=p):
                    self.hop(r, p, True).start()

                @pl.when(self.chain.outer)
                def _(p=p):
                    self.hop(r, p, False).start()

    def finish(self, r, make):
        @pl.when(self.chain.mid)
        def _():
            for p in range(PIECES):
                self.hop(r, p, True).wait_recv()

            def strip(i):
                at = pl.ds(pl.multiple_of(r * self.block + i * STRIP, STRIP), STRIP)
                total = self.part[at, :].astype(F32) + self.landed[self.cross, at, :].astype(F32)
                self.spread[at, :] = make(at, total)

            loop(self.block // STRIP, strip, UNROLL)
            self.out_hop(r).start()

    def receive(self, g):
        @pl.when(self.chain.outer)
        def _():
            def one(k):
                self.out_hop(g * GROUP + k).wait_recv()

                @pl.when(self.chain.inner)
                def _():
                    self.out_hop(g * GROUP + k).start()

            loop(GROUP, one)

    def close(self):
        def block(r):
            for p in range(PIECES):
                self.hop(r, p, False).wait_send()

            @pl.when(self.chain.inner)
            def _():
                self.out_hop(r).wait_send()

        loop(BLOCKS, block)


PARTS = 4
STRIDE = GROUP // PARTS
GROUPS = BLOCKS // GROUP
STEPS = 2 * BLOCKS + 1


def two_sums(s, first, second, made_one, between, ahead, made_two, after, late=False):
    @pl.when((s >= 0) & (s < BLOCKS))
    def _():
        first.relay(s)

    @pl.when((s >= 1) & (s <= BLOCKS))
    def _():
        first.finish(s - 1, made_one)

    @pl.when((s >= GROUP) & (s < BLOCKS + GROUP))
    def _():
        place = lax.rem(s - GROUP, GROUP)
        group = lax.div(s - GROUP, GROUP)

        @pl.when(place == 0)
        def _():
            first.receive(group)

        outer = first.chain.outer
        begin = jnp.where(outer, jnp.where(place == 0, 0, PARTS), lax.div(place + STRIDE - 1, STRIDE))
        stop = jnp.where(outer, PARTS, lax.div(place, STRIDE) + 1)
        lax.fori_loop(begin, stop, lambda part, carry: (between(group, part), carry)[1], 0)

    @pl.when((s >= BLOCKS) & (s < 2 * BLOCKS))
    def _():
        second.relay(s - BLOCKS)

    @pl.when((s >= BLOCKS + 1) & (s < STEPS))
    def _():
        @pl.when(lax.rem(s - BLOCKS - 1, GROUP) == 0)
        def _():
            ahead(lax.div(s - BLOCKS - 1, GROUP))

        second.finish(s - BLOCKS - 1, made_two)

        @pl.when(lax.rem(s - BLOCKS, GROUP) == 0)
        def _():
            group = lax.div(s - BLOCKS, GROUP) - 1
            begin, stop = group, group + 1
            if late:
                outer = second.chain.outer
                begin = jnp.where(outer, jnp.where(s == 2 * BLOCKS, 0, GROUPS), begin)
                stop = jnp.where(outer, GROUPS, stop)

            def one(g, carry):
                second.receive(g)
                after(g)
                return carry

            lax.fori_loop(begin, stop, one, 0)


def back_norm(value, gain, grad):
    spread = lax.rsqrt(jnp.mean(value * value, axis=-1, keepdims=True) + epsilon)
    scaled = grad * gain
    pulled = jnp.mean(scaled * value, axis=-1, keepdims=True)
    terms = grad * value * spread
    return spread * scaled - value * (spread * spread * spread * pulled), terms


def fold(terms):
    folded = terms[:8]
    for k in range(8, terms.shape[0], 8):
        folded = folded + terms[k : k + 8]
    return folded


def load_all(pairs, sems):
    copies = [pltpu.make_async_copy(src, dst, sems.at[k]) for k, (src, dst) in enumerate(pairs)]
    for copy in copies:
        copy.start()
    return copies


def start_all(copies):
    for copy in copies:
        copy.start()


def wait_all(copies):
    for copy in copies:
        copy.wait()


def wide(width):
    return 512 if width % 512 == 0 else 256


def fill(target, at, make):
    width = target.shape[1]
    tile = wide(width)

    def one(p):
        col = columns(p, tile)
        target[at, col] = make(col).astype(target.dtype)

    loop(width // tile, one)


def flip(value, bit):
    return value + bit * (1 - 2 * lax.rem(lax.div(value, bit), 2))


class Plane:
    def __init__(self, dp_size, ctx_size):
        self.count = dp_size * ctx_size
        self.ctx_size = ctx_size
        self.me = lax.axis_index("dp") * ctx_size + lax.axis_index("ctx")
        bits = [1 << k for k in range(self.count.bit_length() - 1)]
        near = [bit for bit in bits if bit >= ctx_size][:1]
        rest = [bit for bit in bits if bit not in near]
        self.bits = bits
        self.orders = (near + rest, near + rest[1:] + rest[:1])

    def partner(self, bit):
        other = flip(self.me, bit)
        return {"dp": lax.div(other, self.ctx_size), "ctx": lax.rem(other, self.ctx_size)}

    def partners(self):
        return [self.partner(bit) for bit in self.bits]


LEAD = 4
LAST_LEAD = 8
LAST_PACE = 9
BEFORE = 8
OUTER_MORE = 0
PACE = 12
ONE_PACE = 8
PER_TICK = 1
ONE_AFTER = 3
EARLY = BLOCKS + GROUP - 1
TURN_PACE = 2
OUTER_AHEAD = 4


class Scatter:
    SLOTS = (2, 6, 6, 6)
    KEPT = (2, 4, 4, 4)
    RESULTS = 2
    LAGS = (0, 1, 5, 9, 13, 17)

    def __init__(self, plane, refs, whole, parts, groups, share, tile):
        self.plane = plane
        self.whole, self.parts = whole, parts
        self.groups = groups
        self.share, self.tile = share, tile
        self.stages = len(plane.bits)
        self.units = sum(group[2] for group in groups)
        self.refs = [refs[6 * k : 6 * k + 6] for k in range(self.stages)]
        self.made, self.out_sem, self.load_sem = refs[6 * self.stages :]
        self.steps = self.units + self.LAGS[self.stages]

    @classmethod
    def scratch(cls, count, share, tile):
        found = []
        blocks = count // 2
        for k in range(count.bit_length() - 1):
            slots = cls.SLOTS[k]
            found += [
                pltpu.VMEM((depth, blocks, share, tile), BF) for depth in (slots, cls.KEPT[k], slots)
            ]
            found += [
                pltpu.SemaphoreType.DMA((slots,)),
                pltpu.SemaphoreType.DMA((slots,)),
                pltpu.SemaphoreType.REGULAR((slots,)),
            ]
            blocks //= 2
        return found + [
            pltpu.VMEM((cls.RESULTS, share, tile), BF),
            pltpu.SemaphoreType.DMA((cls.RESULTS,)),
            pltpu.SemaphoreType.DMA((4,)),
        ]

    def partner(self, stage, u):
        odd = lax.rem(u, 2) == 1
        even_one, odd_one = (self.plane.partner(order[stage]) for order in self.plane.orders)
        return {axis: jnp.where(odd, odd_one[axis], even_one[axis]) for axis in even_one}

    def copy(self, stage, u):
        send, unused, land, s_sem, r_sem, unused_credit = self.refs[stage]
        slot = lax.rem(u, self.SLOTS[stage])
        return pltpu.make_async_remote_copy(
            src_ref=send.at[slot],
            dst_ref=land.at[slot],
            send_sem=s_sem.at[slot],
            recv_sem=r_sem.at[slot],
            device_id=self.partner(stage, u),
            device_id_type=MESH,
        )

    def ready(self, stage, u):
        @pl.when(u >= self.SLOTS[stage])
        def _():
            self.copy(stage, u - self.SLOTS[stage]).wait_send()

    def push(self, stage, u):
        @pl.when(u >= self.SLOTS[stage])
        def _():
            pl.semaphore_wait(self.refs[stage][5].at[lax.rem(u, self.SLOTS[stage])], 1)

        self.copy(stage, u).start()

    def loads(self, pairs):
        return [
            pltpu.make_async_copy(src, dst, self.load_sem.at[k]) for k, (src, dst) in enumerate(pairs)
        ]

    def prefetch(self):
        start_all(self.loads(self.groups[0][3]))

    def product(self, u):
        send, keep = self.refs[0][:2]
        slot, spot = lax.rem(u, self.SLOTS[0]), lax.rem(u, self.KEPT[0])
        odd = lax.rem(u, 2)
        orders = self.plane.orders
        first = 0
        place = u
        by_rows_here = u < 0
        for index, (unused, by_rows, count, loads) in enumerate(self.groups):
            here = (u >= first) & (u < first + count)
            place = jnp.where(here, u - first, place)
            if by_rows:
                by_rows_here = by_rows_here | here

            @pl.when(u == first)
            def _(loads=loads, index=index):
                copies = self.loads(loads)
                if index:
                    start_all(copies)
                wait_all(copies)

            first += count
        parts = self.parts[:, columns(place, self.tile)]

        def block(far, j):
            owner = flip(self.plane.me, orders[0][0]) if far else self.plane.me
            for bits in reversed(tuple(zip(*orders))[1:]):
                if j % 2:
                    owner = flip(owner, bits[0]) * (1 - odd) + flip(owner, bits[1]) * odd
                j //= 2
            return self.whole[:, columns(owner, self.share)]

        def all_blocks(make):
            for j in range(self.plane.count // 2):
                send[slot, j] = make(block(True, j)).astype(BF)
                keep[spot, j] = make(block(False, j)).astype(BF)

        @pl.when(by_rows_here)
        def _():
            all_blocks(lambda whole: weight_product(whole, parts))

        @pl.when(jnp.logical_not(by_rows_here))
        def _():
            all_blocks(lambda whole: weight_product(parts, whole))

    def merge(self, stage, u):
        unused, keep, land = self.refs[stage][:3]
        slots = self.SLOTS[stage]
        slot, spot = lax.rem(u, slots), lax.rem(u, self.KEPT[stage])
        self.copy(stage, u).wait_recv()
        half = (self.plane.count // 2) >> (stage + 1)
        last = stage == self.stages - 1
        if not last:
            self.ready(stage + 1, u)
            send_on, keep_on = self.refs[stage + 1][:2]
            slot_on = lax.rem(u, self.SLOTS[stage + 1])
            spot_on = lax.rem(u, self.KEPT[stage + 1])

            def one(j):
                send_on[slot_on, j] = keep[spot, half + j] + land[slot, half + j]
                keep_on[spot_on, j] = keep[spot, j] + land[slot, j]

            loop(half, one)
            self.push(stage + 1, u)
        else:
            place = lax.rem(u, self.RESULTS)

            @pl.when(u >= self.RESULTS)
            def _():
                self.results(u - self.RESULTS, lambda copy: copy.wait())

            self.made[place] = keep[spot, 0] + land[slot, 0]
            self.results(u, lambda copy: copy.start())

        @pl.when(u + slots < self.units)
        def _():
            pl.semaphore_signal(
                self.refs[stage][5].at[slot],
                inc=1,
                device_id=self.partner(stage, u),
                device_id_type=MESH,
            )

    def results(self, u, act):
        place = lax.rem(u, self.RESULTS)
        first = 0
        for out, by_rows, count, unused_loads in self.groups:

            @pl.when((u >= first) & (u < first + count))
            def _(by_rows=by_rows, out=out, first=first):
                if by_rows:
                    at = (slice(None), columns(u - first, self.tile))
                else:
                    at = (rows_of(u - first, self.tile), slice(None))
                act(pltpu.make_async_copy(self.made.at[place], out.at[at], self.out_sem.at[place]))

            first += count

    def tick(self, i):
        @pl.when(i < self.units)
        def _():
            self.ready(0, i)
            self.product(i)
            self.push(0, i)

        for stage in reversed(range(self.stages)):
            u = i - self.LAGS[stage + 1]

            @pl.when((u >= 0) & (u < self.units))
            def _(stage=stage, u=u):
                self.merge(stage, u)

    def close(self):
        for stage in range(self.stages):
            for k in range(max(0, self.units - self.SLOTS[stage]), self.units):
                self.copy(stage, jnp.int32(k)).wait_send()
        for k in range(max(0, self.units - self.RESULTS), self.units):
            self.results(jnp.int32(k), lambda copy: copy.wait())


Z_APART = 1
PLANE_APART = 3


class Total:
    def __init__(self, plane, size, refs, own):
        self.value, self.land, self.s_sem, self.r_sem = refs
        spot = lax.axis_index("tensor")
        rows, first = pl.ds(0, self.value.shape[1]), pl.ds(0, own)
        near, *rest = plane.orders[0]
        across = [({"tensor": flip(spot, 1 << k)}, first) for k in range(size.bit_length() - 1)]
        self.across = [target for target, unused in across]
        self.stages = [(plane.partner(near), rows), *across]
        self.stages += [(plane.partner(bit), rows) for bit in rest]
        self.times = [0, 1]
        for unused in across:
            self.times.append(self.times[-1] + Z_APART)
        for unused in rest:
            self.times.append(self.times[-1] + PLANE_APART)

    @staticmethod
    def scratch(rows, width, stages):
        return [
            pltpu.VMEM((stages, rows, width), F32),
            pltpu.VMEM((stages, rows, width), F32),
            pltpu.SemaphoreType.DMA((stages,)),
            pltpu.SemaphoreType.DMA((stages,)),
        ]

    def copy(self, k):
        target, rows = self.stages[k]
        return pltpu.make_async_remote_copy(
            src_ref=self.value.at[k, rows],
            dst_ref=self.land.at[k, rows],
            send_sem=self.s_sem.at[k],
            recv_sem=self.r_sem.at[k],
            device_id=target,
            device_id_type=MESH,
        )

    def take(self, k, target):
        self.copy(k).wait_recv()
        rows = self.stages[k][1]
        target[...] = self.value[k]
        target[rows] = self.value[k, rows] + self.land[k, rows]

    def start(self, k):
        if k > 0:
            self.take(k - 1, self.value.at[k])
        self.copy(k).start()

    def finish(self, target):
        self.take(len(self.stages) - 1, target)
        for k in range(len(self.stages)):
            self.copy(k).wait_send()


def turned(value):
    return pltpu.roll(value, HD // 2, 1)


def head_at(h):
    return pl.ds(h * HD, HD)


def head_norm(raw, gain, cos, sin):
    scaled = rms_scale(raw, gain)
    return scaled * cos + turned(scaled) * sin


def head_norm_back(raw, gain, cos, sin, grad):
    return back_norm(raw, gain, grad * cos - turned(grad) * sin)


def seen(rows, first_row, columns_wide, offset, prefix):
    query = first_row + lax.broadcasted_iota(jnp.int32, (rows, columns_wide), 0)
    key = lax.broadcasted_iota(jnp.int32, (rows, columns_wide), 1)
    return (key <= query) | (key + offset < prefix)


def key_strip(raw, v, keys, values, gain, cos, sin, j, at):
    keys[j, at, :] = head_norm(raw[at, head_at(j)], gain, cos[at, :], sin[at, :]).astype(BF)
    values[j, at, :] = v[at, head_at(j)]


def attend(prefix, q_raw, logits, query_gain, cos, sin, keys, values,
           mixed_o, q_o, norm_o, attended_o, scratch, half, arrived):
    high, low, out = scratch
    rows = q_raw.shape[0]
    span = rows // GROUPS
    key_heads = keys.shape[1]
    shared = q_raw.shape[1] // HD // key_heads
    scale = HD ** (-0.5)

    def own(g):
        at = rows_of(g, span)
        mask = seen(span, g * span, rows, half * rows, prefix)
        for h in range(key_heads * shared):
            j = h // shared
            query = head_norm(q_raw[at, head_at(h)], query_gain, cos[at, :], sin[at, :]).astype(BF)
            q_o[at, head_at(h)] = query
            scores = jnp.where(mask, back_product(query, keys[0, j]) * scale, masked)
            top = jnp.max(scores, axis=1, keepdims=True)
            weights = jnp.exp(scores - top)
            high[h, at, :] = top
            low[h, at, :] = jnp.sum(weights, axis=1, keepdims=True)
            out[at, head_at(h)] = matmul(weights.astype(BF), values[0, j])

    loop(GROUPS, own)

    @pl.when(half == 1)
    def _():
        for h in range(key_heads * shared):
            j = h // shared
            if h % shared == 0:
                arrived(j)

            def other(g, h=h, j=j):
                at = rows_of(g, span)
                scores = back_product(q_o[at, head_at(h)], keys[1, j]) * scale
                before = high[h, at, :]
                top = jnp.maximum(before, jnp.max(scores, axis=1, keepdims=True))
                weights = jnp.exp(scores - top)
                shrink = jnp.exp(before - top)
                high[h, at, :] = top
                low[h, at, :] = low[h, at, :] * shrink + jnp.sum(weights, axis=1, keepdims=True)
                out[at, head_at(h)] = out[at, head_at(h)] * shrink + matmul(
                    weights.astype(BF), values[1, j]
                )

            loop(GROUPS, other)

    def close(g):
        at = rows_of(g, span)
        open_gate = jax.nn.sigmoid(logits[at, :])
        for h in range(key_heads * shared):
            total = low[h, at, :]
            norm_o[h, at, :] = high[h, at, :] + jnp.log(total)
            attended = out[at, head_at(h)] * (1.0 / total)
            attended_o[at, head_at(h)] = attended
            mixed_o[at, head_at(h)] = (attended * open_gate[:, h : h + 1]).astype(BF)

    loop(GROUPS, close)


def attend_scratch(rows, heads_wide):
    return [
        pltpu.VMEM((heads_wide // HD, rows, 1), F32),
        pltpu.VMEM((heads_wide // HD, rows, 1), F32),
        pltpu.VMEM((rows, heads_wide), F32),
    ]


def attend_kernel(
    depth, prefix, q_raw, logits, query_gain, cos, sin, keys_in, values_in,
    mixed_o, q_o, norm_o, attended_o, keys_o, values_o, load_sem, send_sem, land_sem, *scratch,
):
    half = lax.axis_index("ctx")
    rows = q_raw.shape[0]
    span = rows // GROUPS
    early, late = pl.ds(0, rows - span), pl.ds(rows - span, span)
    pairs = ((keys_in, keys_o), (values_in, values_o))
    own = [pltpu.make_async_copy(src.at[0], dst.at[0], load_sem.at[0, k]) for k, (src, dst) in enumerate(pairs)]
    other = [
        pltpu.make_async_copy(src.at[1, :, early], dst.at[1, :, early], load_sem.at[1, k])
        for k, (src, dst) in enumerate(pairs)
    ]
    travel = [
        pltpu.make_async_remote_copy(
            src_ref=src.at[0, :, late],
            dst_ref=dst.at[1, :, late],
            send_sem=send_sem.at[k],
            recv_sem=land_sem.at[k],
            device_id={"ctx": 1 - half},
            device_id_type=MESH,
        )
        for k, (src, dst) in enumerate(pairs)
    ]
    start_all(own)
    greet([{"ctx": 1 - half}], {"ctx": 1 - half}, half < 0)

    @pl.when(half == 0)
    def _():
        start_all(travel)

    @pl.when(half == 1)
    def _():
        start_all(other)

    wait_all(own)

    def arrived(j):
        if j == 0:
            wait_all(other)
            for copy in travel:
                copy.wait_recv()

    attend(prefix[0], q_raw, logits, query_gain[depth : depth + 1, :], cos, sin, keys_o, values_o,
           mixed_o, q_o, norm_o, attended_o, scratch, half, arrived)

    @pl.when(half == 0)
    def _():
        for copy in travel:
            copy.wait_send()


def first_kernel(
    depth, prefix, stream, gain, wq, wk, wv, gh, query_gain, key_gain, cos, sin,
    mixed_o, q_o, norm_o, attended_o, keys_o, values_o, normed_o, q_raw, k_raw, logits,
    v, wq_v, wk_v, wv_v, load_sem, send_sem, land_sem, *scratch,
):
    half = lax.axis_index("ctx")
    loads = load_all([(wk.at[depth], wk_v), (wv.at[depth], wv_v), (wq.at[depth], wq_v)], load_sem)
    greet([{"ctx": 1 - half}], {"ctx": 1 - half}, half < 0)
    rows = stream.shape[0]
    span = rows // GROUPS
    key_heads = k_raw.shape[1] // HD

    def copy(j, which):
        ref = (keys_o, values_o)[which]
        return pltpu.make_async_remote_copy(
            src_ref=ref.at[0, j],
            dst_ref=ref.at[1, j],
            send_sem=send_sem.at[j, which],
            recv_sem=land_sem.at[j, which],
            device_id={"ctx": 1 - half},
            device_id_type=MESH,
        )

    def strip(i):
        at = rows_of(i, STRIP)
        value = stream[at, :].astype(F32)
        normed_o[at, :] = rms_scale(value, gain[depth : depth + 1, :]).astype(BF)

    loop(rows // STRIP, strip, UNROLL)
    wait_all(loads[:2])

    def project_keys(g):
        at = rows_of(g, span)
        k_raw[at, :] = matmul(normed_o[at, :], wk_v[...])
        v[at, :] = matmul(normed_o[at, :], wv_v[...]).astype(BF)
        for j in range(key_heads):
            key_strip(k_raw, v, keys_o.at[0], values_o.at[0], key_gain[depth : depth + 1, :], cos, sin, j, at)

    loop(GROUPS, project_keys)

    @pl.when(half == 0)
    def _():
        for j in range(key_heads):
            copy(j, 0).start()
            copy(j, 1).start()

    loads[2].wait()

    def project(g):
        at = rows_of(g, span)
        q_raw[at, :] = matmul(normed_o[at, :], wq_v[...])
        logits[at, :] = matmul(normed_o[at, :], gh[depth])

    loop(GROUPS, project)

    def arrived(j):
        copy(j, 0).wait_recv()
        copy(j, 1).wait_recv()

    attend(prefix[0], q_raw, logits, query_gain[depth : depth + 1, :], cos, sin, keys_o, values_o,
           mixed_o, q_o, norm_o, attended_o, scratch, half, arrived)

    @pl.when(half == 0)
    def _():
        for j in range(key_heads):
            copy(j, 0).wait_send()
            copy(j, 1).wait_send()


def attend_back(
    half, depth, prefix, mixed_grad, logits, attended, q_rot, keys, values, norm, q_raw, k_raw,
    query_gain, key_gain, cos, sin, normed,
    q_o, k_o, v_o, l_o, heads_o, q_gain_o, k_gain_o,
    grad_low, inner, q_grad, k_grad, v_grad, given, landed, send_sem, land_sem,
):
    rows = q_raw.shape[0]
    span = rows // GROUPS
    key_heads = k_raw.shape[1] // HD
    shared = q_raw.shape[1] // k_raw.shape[1]
    heads = key_heads * shared
    scale = HD ** (-0.5)
    query_gain_here = query_gain[depth : depth + 1, :]
    key_gain_here = key_gain[depth : depth + 1, :]

    def copy(j):
        return pltpu.make_async_remote_copy(
            src_ref=given.at[j],
            dst_ref=landed.at[j],
            send_sem=send_sem.at[j],
            recv_sem=land_sem.at[j],
            device_id={"ctx": 1 - half},
            device_id_type=MESH,
        )

    def gate_back(g):
        at = rows_of(g, span)
        open_gate = jax.nn.sigmoid(logits[at, :])
        lane = lax.broadcasted_iota(jnp.int32, (span, LANES), 1)
        pulled = jnp.zeros((span, LANES), F32)
        for h in range(heads):
            grad = mixed_grad[at, head_at(h)]
            here = attended[at, head_at(h)]
            low_grad = (grad * open_gate[:, h : h + 1]).astype(BF)
            grad_low[at, head_at(h)] = low_grad
            inner[h, at, :] = jnp.sum(low_grad.astype(F32) * here, axis=1, keepdims=True)
            pulled = jnp.where(lane == h, jnp.sum(grad * here, axis=1, keepdims=True), pulled)
        l_o[at, :] = (pulled * (open_gate * (1.0 - open_gate))).astype(BF)

    def gates():
        loop(GROUPS, gate_back)
        heads_o[...] = weight_product(l_o[...], normed[...])[: heads_o.shape[0], :]

    def back(j, side, mask_of, first):
        k_grad[j] = jnp.zeros((rows, HD), F32)
        v_grad[j] = jnp.zeros((rows, HD), F32)

        def block(g):
            at = rows_of(g, span)
            for h in range(j * shared, (j + 1) * shared):
                query = q_rot[at, head_at(h)]
                pulled = grad_low[at, head_at(h)]
                scores = back_product(query, keys[side, j]) * scale
                if mask_of is not None:
                    scores = jnp.where(mask_of(g), scores, masked)
                weights = jnp.exp(scores - norm[h, at, :])
                slope = back_product(pulled, values[side, j])
                score_low = (weights * (slope - inner[h, at, :])).astype(BF)
                moved = matmul(score_low, keys[side, j])
                if first:
                    q_grad[at, head_at(h)] = moved
                else:
                    q_grad[at, head_at(h)] += moved
                k_grad[j] += weight_product(score_low, query)
                v_grad[j] += weight_product(weights.astype(BF), pulled)

        loop(GROUPS, block)

    def other(j):
        @pl.when(half == 1)
        def _():
            back(j, 1, None, True)
            given[j, 0] = (k_grad[j] * scale).astype(BF)
            given[j, 1] = v_grad[j].astype(BF)
            copy(j).start()

        @pl.when(half == 0)
        def _():
            wide_head = pl.ds(j * shared * HD, shared * HD)
            q_grad[:, wide_head] = jnp.zeros((rows, shared * HD), F32)

    def own(j):
        back(j, 0, lambda g: seen(span, g * span, rows, half * rows, prefix[0]), False)

    def query_rows(g):
        at = rows_of(g, span)
        for h in range(heads):
            pulled, terms = head_norm_back(
                q_raw[at, head_at(h)], query_gain_here, cos[at, :], sin[at, :],
                q_grad[at, head_at(h)] * scale,
            )
            q_o[at, head_at(h)] = pulled.astype(BF)
            q_gain_o[...] += jnp.sum(terms.reshape(span // 8, 8, HD), axis=0)

    def queries():
        q_gain_o[...] = jnp.zeros_like(q_gain_o)
        loop(GROUPS, query_rows)

    def keys_of(j):
        if j == 0:
            k_gain_o[...] = jnp.zeros_like(k_gain_o)

        @pl.when(half == 0)
        def _(j=j):
            copy(j).wait_recv()

        def key_rows(g, j=j):
            at = rows_of(g, span)
            k_total = k_grad[j, at, :] * scale
            v_total = v_grad[j, at, :]
            k_grad[j, at, :] = k_total
            v_o[at, head_at(j)] = v_total.astype(BF)

            @pl.when(half == 0)
            def _():
                k_grad[j, at, :] = k_total + landed[j, 0, at, :].astype(F32)
                v_o[at, head_at(j)] = (v_total + landed[j, 1, at, :].astype(F32)).astype(BF)

            pulled, terms = head_norm_back(
                k_raw[at, head_at(j)], key_gain_here, cos[at, :], sin[at, :], k_grad[j, at, :]
            )
            k_o[at, head_at(j)] = pulled.astype(BF)
            k_gain_o[...] += jnp.sum(terms.reshape(span // 8, 8, HD), axis=0)

        loop(GROUPS, key_rows)

    def close():
        @pl.when(half == 1)
        def _():
            for j in range(key_heads):
                copy(j).wait_send()

    heads_each = range(key_heads)
    return (
        [gates]
        + [partial(other, j) for j in heads_each]
        + [partial(own, j) for j in heads_each]
        + [queries]
        + [partial(keys_of, j) for j in heads_each],
        close,
    )


def forward_kernel(
    size, depth, rows, width,
    mixed, stream, wo, feed_gain, wg, wu, wd, next_gain, wq, wk, wv, gh, key_gain, cos, sin,
    middle_o, two_o, slope_o, silu_o, hidden_o, x_o, normed_o, q_o, k_o, logit_o, keys_o, values_o,
    *scratch,
):
    (wo_v, wg_v, wu_v, wd_v, wq_v, wk_v, wv_v, x_v, middle_v, slope_v, silu_v, hidden_v, q_v, k_v,
     v_v, logit_v, load_sem, out_sem, keys_v, values_v, keep_sem, send_sem, land_sem) = scratch[:23]
    half = lax.axis_index("ctx")
    key_heads = keys_v.shape[0]
    chain = Chain(size)
    landed = scratch[23]
    one = Sum(chain, scratch[24:31], (landed, 1), rows, width)
    two = Sum(chain, scratch[31:38], (landed, 2), rows, width)
    span = one.block * GROUP
    loads = load_all(
        [(wo.at[depth], wo_v), (stream, x_v), (wg.at[depth], wg_v), (wu.at[depth], wu_v),
         (wd.at[depth], wd_v), (wq.at[depth + 1], wq_v), (wk.at[depth + 1], wk_v),
         (wv.at[depth + 1], wv_v)],
        load_sem,
    )
    chain.greet([{"ctx": 1 - half}])
    tile = wg_v.shape[1] // (PARTS - 1)
    gain_one = feed_gain[depth : depth + 1, :]
    gain_two = next_gain[depth + 1 : depth + 2, :]

    def out(k, g, src, dst):
        at = rows_of(g, span)
        return pltpu.make_async_copy(src.at[at], dst.at[at], out_sem.at[k, g])

    def keep_keys(g, which):
        at = rows_of(g, span)
        src, dst = ((keys_v, keys_o), (values_v, values_o))[which]
        return pltpu.make_async_copy(src.at[:, at], dst.at[0, :, at], keep_sem.at[which, g])

    def give_keys(g, which):
        at = rows_of(g, span)
        src, dst = ((keys_v, keys_o), (values_v, values_o))[which]
        return pltpu.make_async_remote_copy(
            src_ref=src.at[:, at],
            dst_ref=dst.at[1, :, at],
            send_sem=send_sem.at[which, g],
            recv_sem=land_sem.at[which, g],
            device_id={"ctx": 1 - half},
            device_id_type=MESH,
        )

    loads[0].wait()

    def start(g):
        at = rows_of(g, span)
        fill(one.part, at, lambda col: matmul(mixed[at, :], wo_v[:, col]))
        one.offer(g)

    loop(GROUPS, start)
    wait_all(loads[1:5])

    def made_one(at, total):
        value = x_v[at, :].astype(F32) + total
        middle_v[at, :] = value
        return rms_scale(value, gain_one).astype(BF)

    def between(g, part):
        at = rows_of(g, span)

        @pl.when(part == 0)
        def _():
            out(1, g, one.spread, two_o).start()

            @pl.when(chain.mid)
            def _():
                out(0, g, middle_v, middle_o).start()

        @pl.when(part < PARTS - 1)
        def _():
            col = columns(part, tile)
            gate = matmul(one.spread[at, :], wg_v[:, col])
            up = matmul(one.spread[at, :], wu_v[:, col])
            sig = jax.nn.sigmoid(gate)
            act = gate * sig
            hidden_v[at, col] = (act * up).astype(BF)
            silu_v[at, col] = act.astype(BF)
            slope_v[at, col] = (up * (sig * (1.0 + gate * (1.0 - sig)))).astype(BF)

        @pl.when(part == PARTS - 1)
        def _():
            fill(two.part, at, lambda col: matmul(hidden_v[at, :], wd_v[:, col]))
            two.offer(g)
            out(2, g, slope_v, slope_o).start()
            out(3, g, silu_v, silu_o).start()
            out(4, g, hidden_v, hidden_o).start()

    def ahead(g):
        @pl.when(g == 0)
        def _():
            wait_all(loads[5:])

        @pl.when(chain.mid)
        def _():
            out(0, g, middle_v, middle_o).wait()

    def made_two(at, total):
        value = middle_v[at, :] + total
        middle_v[at, :] = value
        return rms_scale(value, gain_two).astype(BF)

    def after(g):
        at = rows_of(g, span)

        @pl.when(chain.mid)
        def _():
            out(5, g, middle_v, x_o).start()

        k_v[at, :] = matmul(two.spread[at, :], wk_v[...])
        v_v[at, :] = matmul(two.spread[at, :], wv_v[...]).astype(BF)
        for j in range(key_heads):
            key_strip(k_v, v_v, keys_v, values_v, key_gain[depth + 1 : depth + 2, :], cos, sin, j, at)

        @pl.when((half == 0) & (g < GROUPS - 1))
        def _():
            give_keys(g, 0).start()
            give_keys(g, 1).start()

        keep_keys(g, 0).start()
        keep_keys(g, 1).start()
        out(8, g, k_v, k_o).start()
        q_v[at, :] = matmul(two.spread[at, :], wq_v[...])
        out(7, g, q_v, q_o).start()
        logit_v[at, :] = matmul(two.spread[at, :], gh[depth + 1])
        out(10, g, logit_v, logit_o).start()
        out(6, g, two.spread, normed_o).start()

    loop(STEPS, lambda s: two_sums(s, one, two, made_one, between, ahead, made_two, after))
    one.close()
    two.close()

    def drain(g):
        @pl.when(chain.mid)
        def _():
            out(5, g, middle_v, x_o).wait()

        for k, src, dst in (
            (1, one.spread, two_o), (2, slope_v, slope_o), (3, silu_v, silu_o),
            (4, hidden_v, hidden_o), (6, two.spread, normed_o), (7, q_v, q_o),
            (8, k_v, k_o), (10, logit_v, logit_o),
        ):
            out(k, g, src, dst).wait()
        for which in range(2):
            keep_keys(g, which).wait()

            @pl.when((half == 0) & (g < GROUPS - 1))
            def _(which=which):
                give_keys(g, which).wait_send()

            @pl.when((half == 1) & (g < GROUPS - 1))
            def _(which=which):
                give_keys(g, which).wait_recv()

    loop(GROUPS, drain)


def turn_kernel(
    size, plane_sizes, depth, rows, width,
    mixed, x_in, cot, wo, feed_gain, wg, wu, wd,
    two_o, down_o, gate_o, up_o, grad_o, low_o, mixed_o, gain_o, made_o,
    *scratch,
):
    (wo_v, wg_v, wu_v, wd_v, middle_v, cot_v, hidden_v, gate_v, up_v, mixed_v, down_v, gain_v,
     load_sem, out_sem) = scratch[:14]
    chain = Chain(size)
    landed = scratch[14]
    one = Sum(chain, scratch[15:22], (landed, 1), rows, width)
    two = Sum(chain, scratch[22:29], (landed, 2), rows, width)
    plane = Plane(*plane_sizes)
    unit = made_o.shape[1] if made_o.shape[1] < 256 else 256
    scatter = Scatter(
        plane, scratch[29:], cot_v, hidden_v, [(made_o, False, hidden_v.shape[1] // unit, [])],
        width // plane.count, unit,
    )
    span = one.block * GROUP
    loads = load_all(
        [(wo.at[depth], wo_v), (x_in, middle_v), (cot, cot_v), (wg.at[depth], wg_v),
         (wu.at[depth], wu_v), (wd.at[depth], wd_v)],
        load_sem,
    )
    chain.greet(plane.partners())
    tile = wg_v.shape[1] // (PARTS - 1)
    gain_one = feed_gain[depth : depth + 1, :]

    def out(k, g, src, dst):
        at = rows_of(g, span)
        return pltpu.make_async_copy(src.at[at], dst.at[at], out_sem.at[k, g])

    loads[0].wait()

    def start(g):
        at = rows_of(g, span)
        fill(one.part, at, lambda col: matmul(mixed[at, :], wo_v[:, col]))
        one.offer(g)

    loop(GROUPS, start)
    gain_v[...] = jnp.zeros_like(gain_v)
    wait_all(loads[1:])

    def made_one(at, total):
        value = middle_v[at, :] + total
        middle_v[at, :] = value
        return rms_scale(value, gain_one).astype(BF)

    def between(g, part):
        at = rows_of(g, span)

        @pl.when(part == 0)
        def _():
            out(0, g, one.spread, two_o).start()

        @pl.when(part < PARTS - 1)
        def _():
            col = columns(part, tile)
            gate = matmul(one.spread[at, :], wg_v[:, col])
            sig = jax.nn.sigmoid(gate)
            act = gate * sig
            slope = sig * (1.0 + gate * (1.0 - sig))
            up = matmul(one.spread[at, :], wu_v[:, col])
            hidden_v[at, col] = (act * up).astype(BF)
            pulled = back_product(cot_v[at, :], wd_v[col, :])
            gate_v[at, col] = (pulled * up * slope).astype(BF)
            up_v[at, col] = (pulled * act).astype(BF)

        @pl.when(part == PARTS - 1)
        def _():
            fill(
                two.part,
                at,
                lambda col: back_product(gate_v[at, :], wg_v[col, :])
                + back_product(up_v[at, :], wu_v[col, :]),
            )
            two.offer(g)
            out(2, g, gate_v, gate_o).start()
            out(3, g, up_v, up_o).start()

    def ahead(g):
        at = rows_of(g, span)
        share = jnp.where(chain.first_mid, 1.0, 0.0)

        @pl.when(chain.first_mid)
        def _():
            fill(down_v, at, lambda col: matmul(hidden_v[at, :], wd_v[:, col]) + middle_v[at, col])

        @pl.when(jnp.logical_not(chain.first_mid))
        def _():
            fill(down_v, at, lambda col: matmul(hidden_v[at, :], wd_v[:, col]))

        out(4, g, down_v, down_o).start()

    def made_two(at, total):
        pulled, terms = back_norm(middle_v[at, :], gain_one, total)
        gain_v[...] += fold(terms)
        value = cot_v[at, :].astype(F32) + pulled
        middle_v[at, :] = value
        return value.astype(BF)

    def after(g):
        at = rows_of(g, span)

        @pl.when(chain.mid)
        def _():
            out(5, g, middle_v, grad_o).start()

        out(6, g, two.spread, low_o).start()
        mixed_v[at, :] = back_product(two.spread[at, :], wo_v[...])
        out(7, g, mixed_v, mixed_o).start()


    def step(s):
        two_sums(s, one, two, made_one, between, ahead, made_two, after, True)
        ahead_ticks = jnp.where(chain.outer, OUTER_AHEAD, 0)

        def ticks_before(s):
            return jnp.where(s > EARLY, (s - EARLY) * TURN_PACE + ahead_ticks, 0)

        lax.fori_loop(
            ticks_before(s), ticks_before(s + 1), lambda t, carry: (scatter.tick(t), carry)[1], 0
        )

    loop(max(STEPS, EARLY + -(-scatter.steps // TURN_PACE)), step)

    @pl.when(jnp.logical_not(chain.first_mid))
    def _():
        gain_v[...] = jnp.zeros_like(gain_v)

    gain_out = pltpu.make_async_copy(gain_v, gain_o, out_sem.at[8, 0])
    gain_out.start()
    one.close()
    two.close()
    scatter.close()

    def drain(g):
        @pl.when(chain.mid)
        def _():
            out(5, g, middle_v, grad_o).wait()

        for k, src, dst in (
            (0, one.spread, two_o), (2, gate_v, gate_o), (3, up_v, up_o), (4, down_v, down_o),
            (6, two.spread, low_o), (7, mixed_v, mixed_o),
        ):
            out(k, g, src, dst).wait()

    loop(GROUPS, drain)
    gain_out.wait()


def back_kernel(
    size, plane_sizes, depth, rows, width,
    *refs,
):
    (prefix, mixed_grad, logits, attended, q_rot, keys, values, norm, q_raw, k_raw, query_gain, key_gain,
     cos, sin, normed_in, gh, x_in, grad_in, attention_gain, wq, wk, wv,
     wd, wg, wu, slope_in, silu_in, middle_in, feed_gain, wo,
     two_in, gate_in, up_in, low_in, mixed_in,
     gate_o, up_o, first_o, grad_o, low_o, mixed_o, gain_o, feed_gain_o, heads_o, q_gain_o, k_gain_o,
     *rest) = refs
    made, scratch = rest[:4], rest[4:]
    attend_made, attend_scratch, scratch = scratch[:7], scratch[7:15], scratch[15:]
    q_low, k_low, v_low, l_low, heads_v, q_gain_v, k_gain_v = attend_made
    (wq_v, wk_v, wv_v, ring_v, wo_v, x_v, grad_v, slope_v, silu_v, gate_v, up_v, mixed_v,
     gain_v, feed_v, whole_v, parts_v, gh_v, load_sem, row_sem, tile_sem, out_sem, ring_sem, attend_sem,
     ) = scratch[:23]
    half = lax.axis_index("ctx")
    chain = Chain(size)
    landed = scratch[23]
    one = Sum(chain, scratch[24:31], (landed, 1), rows, width)
    two = Sum(chain, scratch[31:38], (landed, 2), rows, width)
    plane = Plane(*plane_sizes)
    share = width // plane.count
    unit = min(256, wk_v.shape[1])
    units_wide, heads_wide, keys_wide = gate_v.shape[1], wq_v.shape[1], wk_v.shape[1]
    mixed_grad_v, attended_v, q_raw_v, q_grad_v = (
        grad_v.at[:, pl.ds(quarter * heads_wide, heads_wide)] for quarter in range(4)
    )
    normed_v = two.part
    grad_low, inner, k_grad, v_grad, *given = attend_scratch
    pieces, close_attend = attend_back(
        half, depth, prefix, mixed_grad_v, logits, attended_v, q_rot, keys, values, norm, q_raw_v, k_raw,
        query_gain, key_gain, cos, sin, normed_v, *attend_made,
        grad_low, inner, q_grad_v, k_grad, v_grad, *given,
    )
    parts_heads = parts_v.at[:, pl.ds(0, heads_wide)]
    heads_parts = [
        (q_low, parts_heads),
        (k_low, parts_v.at[:, pl.ds(heads_wide, keys_wide)]),
        (v_low, parts_v.at[:, pl.ds(heads_wide + keys_wide, keys_wide)]),
    ]
    scatter = Scatter(
        plane, scratch[38:], whole_v, parts_v,
        [
            (made[0], True, units_wide // unit, [(two_in, whole_v), (gate_in, parts_v)]),
            (made[1], True, units_wide // unit, [(up_in, parts_v)]),
            (made[2], True, (heads_wide + 2 * keys_wide) // unit, [(normed_in, whole_v), *heads_parts]),
            (made[3], False, heads_wide // unit, [(low_in, whole_v), (mixed_in, parts_heads)]),
        ],
        share, unit,
    )
    span = one.block * GROUP
    below = depth - 1
    attend_loads = load_all(
        [(mixed_grad, mixed_grad_v), (attended, attended_v), (normed_in, normed_v), (q_raw, q_raw_v)],
        attend_sem,
    )
    loads = load_all(
        [(wq.at[depth], wq_v), (wk.at[depth], wk_v), (wv.at[depth], wv_v), (gh.at[depth], gh_v),
         (wo.at[below], wo_v)],
        load_sem,
    )
    grad_load = pltpu.make_async_copy(grad_in, grad_v, load_sem.at[5])

    def row_load(src, g, k):
        return pltpu.make_async_copy(src.at[rows_of(g, span)], x_v, row_sem.at[k])

    tile = units_wide // (PARTS - 1)
    strip_wide = wide(width)
    fetches = PARTS - 1 + 2 * (width // strip_wide)
    slots = ring_v.shape[0]

    def fetch(k, act):
        slot, place = lax.rem(k, slots), lax.rem(k, fetches)
        pair = jnp.maximum(place - (PARTS - 1), 0)

        @pl.when(place < PARTS - 1)
        def _():
            src = wd.at[below, rows_of(place, tile)]
            act(pltpu.make_async_copy(src, ring_v.at[slot, pl.ds(0, tile)], ring_sem.at[slot]))

        for which, weight in enumerate((wg, wu)):

            @pl.when((place >= PARTS - 1) & (lax.rem(pair, 2) == which))
            def _(weight=weight):
                src = weight.at[below, rows_of(lax.div(pair, 2), strip_wide)]
                dst = ring_v.at[slot, :, pl.ds(0, units_wide)]
                act(pltpu.make_async_copy(src, dst, ring_sem.at[slot]))

    def fetched(k):
        fetch(k, lambda copy: copy.wait())

    def used(k):
        @pl.when(k + slots < GROUPS * fetches)
        def _():
            fetch(k + slots, lambda copy: copy.start())

    for k in range(slots):
        fetch(jnp.int32(k), lambda copy: copy.start())
    scatter.prefetch()

    def tile_load(src, dst, g, part, k):
        col = columns(part, tile)
        return pltpu.make_async_copy(
            src.at[rows_of(g, span), col], dst.at[:, col], tile_sem.at[k, part]
        )

    row_load(x_in, 0, 0).start()

    def first_tiles(part):
        tile_load(slope_in, slope_v, 0, part, 0).start()
        tile_load(silu_in, silu_v, 0, part, 1).start()

    loop(PARTS - 1, first_tiles)
    chain.greet([*plane.partners(), {"ctx": 1 - half}])
    wait_all(attend_loads)
    gain_one = attention_gain[depth : depth + 1, :]
    gain_two = feed_gain[below : below + 1, :]

    def out(k, g, src, dst, whole=True):
        at = rows_of(g, span)
        return pltpu.make_async_copy(src.at[at] if whole else src, dst.at[at], out_sem.at[k, g])

    def start(g):
        at = rows_of(g, span)
        fill(
            one.part,
            at,
            lambda col: back_product(q_low[at, :], wq_v[col, :])
            + back_product(k_low[at, :], wk_v[col, :])
            + back_product(v_low[at, :], wv_v[col, :])
            + back_product(l_low[at, :], gh_v[col, :]),
        )
        one.offer(g)

    gain_v[...] = jnp.zeros_like(gain_v)
    feed_v[...] = jnp.zeros_like(feed_v)

    def begin_sums():
        grad_load.start()
        wait_all(loads)
        loop(GROUPS, start)
        row_load(x_in, 0, 0).wait()
        grad_load.wait()

    def local(at):
        return pl.ds(pl.multiple_of(lax.rem(at.start, span), STRIP), STRIP)

    def made_one(at, total):
        pulled, terms = back_norm(x_v[local(at), :], gain_one, total)
        gain_v[...] += fold(terms)
        value = grad_v[at, :] + pulled
        grad_v[at, :] = value
        return value.astype(BF)

    def between(g, part):
        at = rows_of(g, span)

        @pl.when(part == 0)
        def _():
            out(0, g, one.spread, first_o).start()

            @pl.when(g < GROUPS - 1)
            def _():
                copy = row_load(x_in, g + 1, 1)
                copy.start()
                copy.wait()

            @pl.when(g > 0)
            def _():
                out(1, g - 1, gate_v, gate_o, False).wait()
                out(2, g - 1, up_v, up_o, False).wait()

        @pl.when(part < PARTS - 1)
        def _():
            col = columns(part, tile)
            tile_load(slope_in, slope_v, g, part, 0).wait()
            tile_load(silu_in, silu_v, g, part, 1).wait()
            k = g * fetches + part
            fetched(k)
            weight = ring_v[lax.rem(k, slots), pl.ds(0, tile), :]
            pulled = back_product(one.spread[at, :], weight)
            used(k)
            gate_v[:, col] = (pulled * slope_v[:, col].astype(F32)).astype(BF)
            up_v[:, col] = (pulled * silu_v[:, col].astype(F32)).astype(BF)

            @pl.when(g < GROUPS - 1)
            def _():
                tile_load(slope_in, slope_v, g + 1, part, 0).start()
                tile_load(silu_in, silu_v, g + 1, part, 1).start()

        @pl.when(part == PARTS - 1)
        def _():
            def pair(p):
                k = g * fetches + PARTS - 1 + 2 * p
                fetched(k)
                fetched(k + 1)
                here = pl.ds(0, units_wide)
                two.part[at, columns(p, strip_wide)] = (
                    back_product(gate_v[...], ring_v[lax.rem(k, slots), :, here])
                    + back_product(up_v[...], ring_v[lax.rem(k + 1, slots), :, here])
                ).astype(BF)
                used(k)
                used(k + 1)

            loop(width // strip_wide, pair)
            two.offer(g)
            out(1, g, gate_v, gate_o, False).start()
            out(2, g, up_v, up_o, False).start()

    def ahead(g):
        copy = row_load(middle_in, g, 2)
        copy.start()
        copy.wait()

    def made_two(at, total):
        pulled, terms = back_norm(x_v[local(at), :], gain_two, total)
        feed_v[...] += fold(terms)
        value = grad_v[at, :] + pulled
        grad_v[at, :] = value
        return value.astype(BF)

    def after(g):
        at = rows_of(g, span)

        @pl.when(chain.mid)
        def _():
            out(5, g, grad_v, grad_o).start()

        out(3, g, two.spread, low_o).start()

        @pl.when(g > 0)
        def _():
            out(4, g - 1, mixed_v, mixed_o, False).wait()

        mixed_v[...] = back_product(two.spread[at, :], wo_v[...])
        out(4, g, mixed_v, mixed_o, False).start()

    lead = len(pieces)

    def ticks_before(i):
        since = i - lead - 1
        more = jnp.where(chain.outer & (since >= GROUP), OUTER_MORE, 0)
        return jnp.where(since < 0, lax.div(i * LEAD + 4, 8), BEFORE + lax.div(since * PACE, 8) + more)

    def step(i):
        for place, piece in enumerate(pieces):
            pl.when(i == place)(piece)
        pl.when(i == lead)(begin_sums)
        two_sums(i - lead - 1, one, two, made_one, between, ahead, made_two, after, True)
        lax.fori_loop(
            ticks_before(i), ticks_before(i + 1), lambda t, carry: (scatter.tick(t), carry)[1], 0
        )

    steps = lead + 1 + STEPS
    while BEFORE + (steps - lead - 1) * PACE // 8 < scatter.steps:
        steps += 1
    loop(steps, step)
    close_attend()

    @pl.when(jnp.logical_not(chain.first_mid))
    def _():
        gain_v[...] = jnp.zeros_like(gain_v)
        feed_v[...] = jnp.zeros_like(feed_v)

    gain_out = pltpu.make_async_copy(gain_v, gain_o, out_sem.at[6, 0])
    feed_out = pltpu.make_async_copy(feed_v, feed_gain_o, out_sem.at[7, 0])
    gain_out.start()
    feed_out.start()
    attend_outs = [
        pltpu.make_async_copy(src, dst, attend_sem.at[place])
        for place, (src, dst) in enumerate(
            ((heads_v, heads_o), (q_gain_v, q_gain_o), (k_gain_v, k_gain_o))
        )
    ]
    for copy in attend_outs:
        copy.start()
    one.close()
    two.close()
    scatter.close()

    def drain(g):
        out(0, g, one.spread, first_o).wait()
        out(3, g, two.spread, low_o).wait()

        @pl.when(chain.mid)
        def _():
            out(5, g, grad_v, grad_o).wait()

    loop(GROUPS, drain)
    out(1, GROUPS - 1, gate_v, gate_o, False).wait()
    out(2, GROUPS - 1, up_v, up_o, False).wait()
    out(4, GROUPS - 1, mixed_v, mixed_o, False).wait()
    gain_out.wait()
    feed_out.wait()
    wait_all(attend_outs)


def last_kernel(
    size, plane_sizes, depth, rows, width,
    *refs,
):
    attend_in, refs = refs[:15], refs[15:]
    (gh, gain_one_in, feed_zero_in, feed_one_in, q_gain_one, k_gain_one, heads_one, x_in, grad_in,
     attention_gain, wq, wk, wv, down_in, two_in, gate_in, up_in, first_in, hidden_in, low_in, mixed_in,
     grad_o, result_o, total_o, *rest) = refs
    normed_in = attend_in[14]
    made, rest = rest[:5], rest[5:]
    attend_made, attend_scratch, scratch = rest[:7], rest[7:16], rest[16:]
    q_low, k_low, v_low, l_low, heads_zero, q_gain_zero, k_gain_zero = attend_made
    half = lax.axis_index("ctx")
    pieces, close_attend = attend_back(half, depth, *attend_in, *attend_made, *attend_scratch)
    (wq_v, wk_v, wv_v, x_v, grad_v, gain_v, whole_v, parts_v, total_v, load_sem, out_sem) = scratch[:11]
    chain = Chain(size)
    one = Sum(chain, scratch[12:19], (scratch[11], 1), rows, width)
    two = Sum(chain, scratch[20:27], (scratch[19], 1), rows, width)
    plane = Plane(*plane_sizes)
    total = Total(plane, size, scratch[27:31], 8)
    share = width // plane.count
    units_wide, heads_wide, keys_wide = parts_v.shape[1], wq_v.shape[1], wk_v.shape[1]
    unit = min(256, keys_wide)
    parts_heads = parts_v.at[:, pl.ds(0, heads_wide)]
    heads_parts = [
        (q_low, parts_heads),
        (k_low, parts_v.at[:, pl.ds(heads_wide, keys_wide)]),
        (v_low, parts_v.at[:, pl.ds(heads_wide + keys_wide, keys_wide)]),
    ]
    scatter = Scatter(
        plane, scratch[31:], whole_v, parts_v,
        [
            (made[0], True, units_wide // unit, [(two_in, whole_v), (gate_in, parts_v)]),
            (made[1], True, units_wide // unit, [(up_in, parts_v)]),
            (made[2], False, units_wide // unit, [(first_in, whole_v), (hidden_in, parts_v)]),
            (made[3], True, (heads_wide + 2 * keys_wide) // unit, [(normed_in, whole_v), *heads_parts]),
            (made[4], False, heads_wide // unit, [(low_in, whole_v), (mixed_in, parts_heads)]),
        ],
        share, unit,
    )
    span = one.block * GROUP
    loads = load_all(
        [(wq.at[depth], wq_v), (wk.at[depth], wk_v), (wv.at[depth], wv_v), (x_in, x_v),
         (grad_in, grad_v), (down_in, two.part)],
        load_sem,
    )
    scatter.prefetch()
    chain.greet([*plane.partners(), *total.across, {"ctx": 1 - half}])
    gain_one = attention_gain[depth : depth + 1, :]

    def out(k, g):
        at = rows_of(g, span)
        src, dst = ((one.spread, grad_o), (two.spread, result_o))[k]
        return pltpu.make_async_copy(src.at[at], dst.at[at], out_sem.at[k, g])

    def start(g):
        at = rows_of(g, span)
        fill(
            one.part,
            at,
            lambda col: back_product(q_low[at, :], wq_v[col, :])
            + back_product(k_low[at, :], wk_v[col, :])
            + back_product(v_low[at, :], wv_v[col, :])
            + back_product(l_low[at, :], gh[depth, col, :]),
        )
        one.offer(g)

    gain_v[...] = jnp.zeros_like(gain_v)

    def made_one(at, total_sum):
        pulled, terms = back_norm(x_v[at, :].astype(F32), gain_one, total_sum)
        gain_v[...] += fold(terms)
        return (grad_v[at, :] + pulled).astype(BF)

    def made_two(at, total_sum):
        return total_sum.astype(BF)

    begin = -(-len(pieces) // PER_TICK)
    first_two, first_one = 3, begin + ONE_AFTER
    sum_ticks = BLOCKS + BLOCKS // ONE_PACE + 1
    first_total = first_one + sum_ticks
    rest_two = first_one + sum_ticks - 1

    def sums(i):
        @pl.when(i == 0)
        def _():
            loads[5].wait()
            two.offer(0)

        for place, piece in enumerate(pieces):
            pl.when(i == place // PER_TICK)(piece)

        @pl.when(i == begin)
        def _():
            wait_all(loads[:5])
            loop(GROUPS, start)
            two.offer(1)

        def one_step(k, sum_here, make, s):
            @pl.when((s >= 0) & (s < BLOCKS))
            def _():
                sum_here.relay(s)

            @pl.when((s >= 1) & (s <= BLOCKS))
            def _():
                sum_here.finish(s - 1, make)

                @pl.when((lax.rem(s, GROUP) == 0) & chain.mid)
                def _():
                    out(k, lax.div(s, GROUP) - 1).start()

        def paced(k, sum_here, make, first, begin_step, end_step, pace):
            since = i - first
            take = lax.rem(since, pace + 1)
            s = lax.div(since, pace + 1) * pace + take + begin_step

            @pl.when((since >= 0) & (take < pace) & (s < end_step))
            def _():
                one_step(k, sum_here, make, s)

        paced(1, two, made_two, first_two, 0, GROUP, 3)
        paced(0, one, made_one, first_one, 0, BLOCKS + 1, ONE_PACE)
        paced(1, two, made_two, rest_two, GROUP, BLOCKS + 1, 3)

    def totals(i):
        @pl.when(i == first_total)
        def _():
            total.value[0] = jnp.zeros(total_v.shape, F32)

            @pl.when(chain.first_mid)
            def _():
                total.value[0, pl.ds(0, 1)] = jnp.sum(gain_v[...], axis=0, keepdims=True)

            for k, gains in enumerate((gain_one_in, feed_zero_in, feed_one_in)):
                total.value[0, pl.ds(k + 1, 1)] = jnp.sum(gains[...], axis=0, keepdims=True)
            for k, gains in enumerate((q_gain_zero, k_gain_zero, q_gain_one, k_gain_one)):
                total.value[0, pl.ds(4, 1), pl.ds(k * HD, HD)] = jnp.sum(
                    gains[...], axis=0, keepdims=True
                )
            for k, heads in enumerate((heads_zero, heads_one)):
                total.value[0, pl.ds(8 + 4 * k, 4)] = heads[pl.ds(0, 4), :]

        for k in range(len(total.stages)):

            @pl.when(i == first_total + total.times[k])
            def _(k=k):
                total.start(k)

    def ticks_before(i):
        return jnp.where(i < begin, lax.div(i * LAST_LEAD, 8), lead_ticks + lax.div((i - begin) * LAST_PACE, 8))

    def step(i):
        lax.fori_loop(
            ticks_before(i), ticks_before(i + 1), lambda t, carry: (scatter.tick(t), carry)[1], 0
        )
        sums(i)
        totals(i)

    last_two = rest_two + 4 * -(-(BLOCKS + 1 - GROUP) // 3)
    lead_ticks = begin * LAST_LEAD // 8
    scatter_steps = begin + -(-(scatter.steps - lead_ticks) * 8 // LAST_PACE)
    loop(max(scatter_steps, last_two, first_total + total.times[-1]), step)
    close_attend()

    def receive(g):
        one.receive(g)
        two.receive(g)

        @pl.when(chain.outer)
        def _():
            out(0, g).start()
            out(1, g).start()

    loop(GROUPS, receive)
    total.finish(total_v)
    total_out = pltpu.make_async_copy(total_v, total_o, out_sem.at[2, 0])
    total_out.start()
    one.close()
    two.close()
    scatter.close()

    def drain(g):
        out(0, g).wait()
        out(1, g).wait()

    loop(GROUPS, drain)
    total_out.wait()


def widen_kernel(heads_wide, keys_wide, halves, totals, low_in, result_in, *refs):
    below, above = refs[0:5], refs[5:10]
    attention_o, feed_o, stream_o, result_o, gate_o, up_o, down_o, q_o, k_o, v_o, out_o = refs[10:]
    here = lax.axis_index("dp") * halves + lax.axis_index("ctx")
    gains = totals[pl.ds(0, 8), columns(here, attention_o.shape[1])]
    attention_o[...] = gains[0:2]
    feed_o[...] = gains[2:4]
    result_o[...] = result_in[...]
    stream_o[...] = low_in[...].astype(F32)
    for depth, made in enumerate((below, above)):
        gate_o[depth] = made[0][...].astype(F32)
        up_o[depth] = made[1][...].astype(F32)
        down_o[depth] = made[2][...].astype(F32)
        q_o[depth] = made[3][:, :heads_wide].astype(F32)
        k_o[depth] = made[3][:, heads_wide : heads_wide + keys_wide].astype(F32)
        v_o[depth] = made[3][:, heads_wide + keys_wide :].astype(F32)
        out_o[depth] = made[4][...].astype(F32)


def widen(totals, halves, stream_low, result, below, above, heads_wide, keys_wide):
    cuts = 4

    def cut(shape):
        return pl.BlockSpec((shape[0] // cuts, shape[1]), lambda i: (i, 0))

    def fixed(shape):
        return pl.BlockSpec(shape, lambda i: (0, 0))

    def pair(shape):
        return pl.BlockSpec((2, shape[0] // cuts, shape[1]), lambda i: (0, i, 0))

    share = below[0].shape[0]
    shapes = [
        below[0].shape, below[1].shape, below[2].shape, (share, heads_wide), (share, keys_wide),
        (share, keys_wide), below[4].shape,
    ]
    inputs = [stream_low, result, *below, *above]
    return pl.pallas_call(
        partial(widen_kernel, heads_wide, keys_wide, halves),
        grid=(cuts,),
        out_shape=(
            jax.ShapeDtypeStruct((LAYERS, share), F32),
            jax.ShapeDtypeStruct((LAYERS, share), F32),
            jax.ShapeDtypeStruct(stream_low.shape, F32),
            jax.ShapeDtypeStruct(result.shape, BF),
            *(jax.ShapeDtypeStruct((2, *shape), F32) for shape in shapes),
        ),
        in_specs=[fixed(totals.shape)] + [cut(array.shape) for array in inputs],
        out_specs=(fixed((LAYERS, share)), fixed((LAYERS, share)), cut(stream_low.shape), cut(result.shape), *(pair(shape) for shape in shapes)),
        compiler_params=pltpu.CompilerParams(vmem_limit_bytes=VMEM_LIMIT),
    )(totals, *inputs)


def call(kernel, collective_id, in_specs, outs, scratch, flops, out_spec=ANY):
    return pl.pallas_call(
        kernel,
        out_shape=tuple(jax.ShapeDtypeStruct(shape, kind) for shape, kind in outs),
        in_specs=in_specs,
        out_specs=tuple(out_spec for _ in outs),
        scratch_shapes=scratch,
        cost_estimate=pl.CostEstimate(flops=flops, bytes_accessed=40_000_000, transcendentals=0),
        compiler_params=pltpu.CompilerParams(
            collective_id=collective_id, has_side_effects=True, vmem_limit_bytes=VMEM_LIMIT
        ),
    )


def dma(*shape):
    return pltpu.SemaphoreType.DMA(shape)


def shards(
    size,
    stream,
    cotangent,
    prefixes,
    attention_gain,
    query_weight,
    key_weight,
    value_weight,
    gate_heads,
    query_gain,
    key_gain,
    output_weight,
    feed_gain,
    gate_weight,
    up_weight,
    down_weight,
):
    seq_count, row_count, width = stream.shape
    rows = seq_count * row_count
    span = rows // GROUPS
    dp_size = lax.axis_size("dp")
    plane_sizes = (dp_size, lax.axis_size("ctx"))
    plane_count = plane_sizes[0] * plane_sizes[1]
    heads_wide = query_weight.shape[2]
    keys_wide = key_weight.shape[2]
    units = gate_weight.shape[2]
    gates = gate_heads.shape[2]
    share = width // plane_count
    unit = min(256, keys_wide)
    here = lax.axis_index("dp") * plane_sizes[1] + lax.axis_index("ctx")
    first_row = lax.axis_index("ctx") * row_count
    cos, sin = (
        lax.dynamic_slice_in_dim(jnp.asarray(table), first_row, row_count)
        for table in rotary_tables(row_count * plane_sizes[1])
    )
    stream_flat = stream.reshape(rows, width)
    cot_flat = cotangent.reshape(rows, width)
    heads_padded = jnp.dot(gate_heads, jnp.eye(gates, LANES, dtype=BF), preferred_element_type=F32).astype(BF)
    sum_scratch = Sum.scratch(rows, width)
    landed = [pltpu.VMEM((2, rows, width), BF)]
    pair_scratch = [pltpu.VMEM((3, rows, width), BF)] + sum_scratch + sum_scratch

    key_heads = keys_wide // HD
    attend_outs = [
        ((rows, heads_wide), BF), ((rows, heads_wide), BF), ((heads_wide // HD, rows, 1), F32),
        ((rows, heads_wide), F32),
    ]
    key_outs = [((2, key_heads, rows, HD), BF), ((2, key_heads, rows, HD), BF)]
    smem = pl.BlockSpec(memory_space=pltpu.SMEM)

    attend_back_outs = [
        ((rows, heads_wide), BF), ((rows, keys_wide), BF), ((rows, keys_wide), BF),
        ((rows, LANES), BF), ((8, width), F32), ((8, HD), F32), ((8, HD), F32),
    ]
    attend_back_scratch = [
        pltpu.VMEM((rows, heads_wide), BF), pltpu.VMEM((heads_wide // HD, rows, 1), F32),
        pltpu.VMEM((rows, heads_wide), F32), pltpu.VMEM((key_heads, rows, HD), F32),
        pltpu.VMEM((key_heads, rows, HD), F32), pltpu.VMEM((key_heads, 2, rows, HD), BF),
        pltpu.VMEM((key_heads, 2, rows, HD), BF), dma(key_heads), dma(key_heads),
    ]

    def attend_back_in(mixed_grad, logits, saved, q_raw, k_raw, normed):
        mixed, q_rot, norm, attended, keys, values = saved
        return (
            prefixes, mixed_grad, logits, attended, q_rot, keys, values, norm, q_raw, k_raw,
            query_gain, key_gain, cos, sin, normed,
        )

    made_shapes = [
        ((share, units), BF), ((share, units), BF), ((units, share), BF),
        ((share, heads_wide + 2 * keys_wide), BF), ((heads_wide, share), BF),
    ]
    scatter_scratch = Scatter.scratch(plane_count, share, unit)

    *saved_zero, normed_zero, q_raw_zero, k_raw_zero, logits_zero = call(
        partial(first_kernel, 0),
        4,
        [smem, WHOLE, WHOLE, ANY, ANY, ANY] + [WHOLE] * 5,
        attend_outs
        + key_outs
        + [
            ((rows, width), BF), ((rows, heads_wide), F32), ((rows, keys_wide), F32),
            ((rows, LANES), F32),
        ],
        [
            pltpu.VMEM((rows, keys_wide), BF), pltpu.VMEM((width, heads_wide), BF),
            pltpu.VMEM((width, keys_wide), BF), pltpu.VMEM((width, keys_wide), BF), dma(3),
            dma(key_heads, 2), dma(key_heads, 2),
        ]
        + attend_scratch(rows, heads_wide),
        3_500_000_000,
        WHOLE,
    )(
        prefixes, stream_flat, attention_gain, query_weight, key_weight, value_weight, heads_padded,
        query_gain, key_gain, cos, sin,
    )
    mixed_zero = saved_zero[0]
    middle_zero, two_zero, slope, silu, hidden_zero, x_one, normed_one, q_raw, k_raw, logits, *keys_one = call(
        partial(forward_kernel, size, 0, rows, width),
        0,
        [WHOLE, ANY, ANY, WHOLE, ANY, ANY, ANY, WHOLE, ANY, ANY, ANY] + [WHOLE] * 4,
        [
            ((rows, width), F32), ((rows, width), BF), ((rows, units), BF), ((rows, units), BF),
            ((rows, units), BF), ((rows, width), F32), ((rows, width), BF),
            ((rows, heads_wide), F32), ((rows, keys_wide), F32), ((rows, LANES), F32), *key_outs,
        ],
        [
            pltpu.VMEM((heads_wide, width), BF), pltpu.VMEM((width, units), BF),
            pltpu.VMEM((width, units), BF), pltpu.VMEM((units, width), BF),
            pltpu.VMEM((width, heads_wide), BF), pltpu.VMEM((width, keys_wide), BF),
            pltpu.VMEM((width, keys_wide), BF), pltpu.VMEM((rows, width), BF),
            pltpu.VMEM((rows, width), F32), pltpu.VMEM((rows, units), BF),
            pltpu.VMEM((rows, units), BF), pltpu.VMEM((rows, units), BF),
            pltpu.VMEM((rows, heads_wide), F32), pltpu.VMEM((rows, keys_wide), F32),
            pltpu.VMEM((rows, keys_wide), BF), pltpu.VMEM((rows, LANES), F32),
            dma(8), dma(11, GROUPS), pltpu.VMEM((key_heads, rows, HD), BF),
            pltpu.VMEM((key_heads, rows, HD), BF), dma(2, GROUPS), dma(2, GROUPS), dma(2, GROUPS),
        ]
        + pair_scratch,
        13_000_000_000,
    )(
        mixed_zero, stream_flat, output_weight, feed_gain, gate_weight, up_weight, down_weight,
        attention_gain, query_weight, key_weight, value_weight, heads_padded, key_gain, cos, sin,
    )
    saved_one = call(
        partial(attend_kernel, 1),
        5,
        [smem] + [WHOLE] * 5 + [ANY] * 2,
        attend_outs + key_outs,
        [dma(2, 2), dma(2), dma(2)] + attend_scratch(rows, heads_wide),
        1_000_000_000,
        WHOLE,
    )(prefixes, q_raw, logits, query_gain, cos, sin, *keys_one)
    mixed_one = saved_one[0]
    two_one, down_part, gate_low, up_low, grad, low, mixed_grad, feed_one, down_made = call(
        partial(turn_kernel, size, plane_sizes, 1, rows, width),
        1,
        [WHOLE, ANY, ANY, ANY, WHOLE, ANY, ANY, ANY],
        [
            ((rows, width), BF), ((rows, width), BF), ((rows, units), BF),
            ((rows, units), BF), ((rows, width), F32), ((rows, width), BF),
            ((rows, heads_wide), F32), ((8, width), F32), made_shapes[2],
        ],
        [
            pltpu.VMEM((heads_wide, width), BF), pltpu.VMEM((width, units), BF),
            pltpu.VMEM((width, units), BF), pltpu.VMEM((units, width), BF),
            pltpu.VMEM((rows, width), F32), pltpu.VMEM((rows, width), BF),
            pltpu.VMEM((rows, units), BF), pltpu.VMEM((rows, units), BF),
            pltpu.VMEM((rows, units), BF), pltpu.VMEM((rows, heads_wide), F32),
            pltpu.VMEM((rows, width), BF), pltpu.VMEM((8, width), F32),
            dma(6), dma(9, GROUPS),
        ]
        + pair_scratch + scatter_scratch,
        24_000_000_000,
    )(mixed_one, x_one, cot_flat, output_weight, feed_gain, gate_weight, up_weight, down_weight)
    (gate_low, up_low, first_low, grad, low, mixed_grad, gain_one, feed_zero, heads_one, q_gain_one,
     k_gain_one, *made_one) = call(
        partial(back_kernel, size, plane_sizes, 1, rows, width),
        2,
        [smem, ANY, WHOLE, ANY] + [WHOLE] * 4 + [ANY] + [WHOLE] * 5 + [ANY]
        + [ANY, ANY, ANY, WHOLE] + [ANY] * 9 + [WHOLE] + [ANY] * 6,
        [
            ((rows, units), BF), ((rows, units), BF), ((rows, width), BF), ((rows, width), F32),
            ((rows, width), BF), ((rows, heads_wide), F32), ((8, width), F32), ((8, width), F32),
            ((8, width), F32), ((8, HD), F32), ((8, HD), F32), *made_shapes[:2], *made_shapes[3:],
        ],
        [pltpu.VMEM(shape, kind) for shape, kind in attend_back_outs]
        + attend_back_scratch[:2] + attend_back_scratch[3:]
        + [
            pltpu.VMEM((width, heads_wide), BF), pltpu.VMEM((width, keys_wide), BF),
            pltpu.VMEM((width, keys_wide), BF), pltpu.VMEM((4, 512, width), BF),
            pltpu.VMEM((heads_wide, width), BF), pltpu.VMEM((span, width), F32),
            pltpu.VMEM((rows, width), F32), pltpu.VMEM((span, units), BF),
            pltpu.VMEM((span, units), BF), pltpu.VMEM((span, units), BF),
            pltpu.VMEM((span, units), BF), pltpu.VMEM((span, heads_wide), F32),
            pltpu.VMEM((8, width), F32), pltpu.VMEM((8, width), F32),
            pltpu.VMEM((rows, width), BF), pltpu.VMEM((rows, units), BF),
            pltpu.VMEM((width, LANES), BF),
            dma(6), dma(3), dma(2, PARTS - 1), dma(8, GROUPS), dma(4), dma(4),
        ]
        + pair_scratch + scatter_scratch,
        28_000_000_000,
    )(
        *attend_back_in(mixed_grad, logits, saved_one, q_raw, k_raw, normed_one),
        heads_padded, x_one, grad, attention_gain,
        query_weight, key_weight, value_weight, down_weight, gate_weight, up_weight, slope, silu,
        middle_zero, feed_gain, output_weight,
        two_one, gate_low, up_low, low, mixed_one,
    )
    made_one.insert(2, down_made)
    below_rows = 8
    stages = plane_count.bit_length() - 1 + size.bit_length() - 1
    stream_low, result, totals, *made_zero = call(
        partial(last_kernel, size, plane_sizes, 0, rows, width),
        3,
        [smem] + [WHOLE] * 14 + [WHOLE] * 7 + [ANY, ANY, WHOLE] + [ANY] * 11,
        [
            ((rows, width), BF), ((rows, width), BF), ((8 + below_rows, width), F32), *made_shapes,
        ],
        [pltpu.VMEM(shape, kind) for shape, kind in attend_back_outs]
        + attend_back_scratch
        + [
            pltpu.VMEM((width, heads_wide), BF), pltpu.VMEM((width, keys_wide), BF),
            pltpu.VMEM((width, keys_wide), BF), pltpu.VMEM((rows, width), BF),
            pltpu.VMEM((rows, width), F32), pltpu.VMEM((8, width), F32),
            pltpu.VMEM((rows, width), BF), pltpu.VMEM((rows, units), BF),
            pltpu.VMEM((8 + below_rows, width), F32), dma(6), dma(3, GROUPS),
        ]
        + landed + sum_scratch + landed + sum_scratch
        + Total.scratch(8 + below_rows, width, stages) + scatter_scratch,
        19_000_000_000,
    )(
        *attend_back_in(mixed_grad, logits_zero, saved_zero, q_raw_zero, k_raw_zero, normed_zero),
        heads_padded, gain_one, feed_zero, feed_one, q_gain_one, k_gain_one, heads_one, stream_flat,
        grad, attention_gain, query_weight, key_weight, value_weight, down_part,
        two_zero, gate_low, up_low, first_low, hidden_zero, low, mixed_zero,
    )
    attention_grad, feed_grad, stream_grad, result, *weights = widen(
        totals, plane_sizes[1], stream_low, result, made_zero, made_one, heads_wide, keys_wide)

    def own(array, wide_share):
        return lax.dynamic_slice_in_dim(array, here * wide_share, wide_share, array.ndim - 1)

    head_gains = own(totals[4, : 4 * HD].reshape(2, 2, HD), HD // plane_count)
    heads = own(totals[8:].reshape(LAYERS, 4, width)[:, :gates], share)
    return (
        result.reshape(seq_count, row_count, width),
        stream_grad.reshape(seq_count, row_count, width),
        attention_grad,
        weights[3],
        weights[4],
        weights[5],
        heads.transpose(0, 2, 1),
        head_gains[:, 0],
        head_gains[:, 1],
        weights[6],
        feed_grad,
        weights[0],
        weights[1],
        weights[2],
    )


def solution(mesh):
    return jax.shard_map(
        partial(shards, mesh.shape["tensor"]),
        mesh=mesh,
        in_specs=(
            P("dp", "ctx", None),
            P("dp", "ctx", None),
            P("dp"),
            P(),
            P(None, None, "tensor"),
            P(None, None, "tensor"),
            P(None, None, "tensor"),
            P(None, None, "tensor"),
            P(),
            P(),
            P(None, "tensor", None),
            P(),
            P(None, None, "tensor"),
            P(None, None, "tensor"),
            P(None, "tensor", None),
        ),
        out_specs=(
            P("dp", "ctx", None),
            P("dp", "ctx", None),
            P(None, ("dp", "ctx")),
            P(None, ("dp", "ctx"), "tensor"),
            P(None, ("dp", "ctx"), "tensor"),
            P(None, ("dp", "ctx"), "tensor"),
            P(None, ("dp", "ctx"), "tensor"),
            P(None, ("dp", "ctx")),
            P(None, ("dp", "ctx")),
            P(None, "tensor", ("dp", "ctx")),
            P(None, ("dp", "ctx")),
            P(None, ("dp", "ctx"), "tensor"),
            P(None, ("dp", "ctx"), "tensor"),
            P(None, "tensor", ("dp", "ctx")),
        ),
        check_vma=False,
    )
```
